32 devices in a mesh: section: 2 (over core), dp: 16 (over z, y, x).
Axes of the slice: x: 2, y: 2, z: 4, core: 2. Of those that a mesh axis runs over, the one named last changes fastest.
Arguments:
- inputs: bfloat16 [4, 64, 160, 400], P(None, 'dp'), may hold values from -6 to 6
- cotangent: bfloat16 [4, 64, 160, 400], P(None, 'dp'), may hold values from -6 to 6
- land: int32 [64, 160], P('dp'), may hold values from 0 to 1, as said below
- kernel: float32 [2, 49, 400], P('section'), may hold values from -0.875 to 0.875
- bn_gain: float32 [2, 400], P('section'), may hold values from 0.25 to 1.75
- bn_bias: float32 [2, 400], P('section'), may hold values from -3 to 3
- bias_in: float32 [2, 1600], P('section'), may hold values from -3 to 3
- bias_out: float32 [2, 400], P('section'), may hold values from -2 to 2
- w_in: float32 [2, 640000], P('section', 'dp'), may hold values from -0.3125 to 0.3125
- w_out: float32 [2, 640000], P('section', 'dp'), may hold values from -0.21875 to 0.21875
- resample: float32 [2, 1280000], P('section', 'dp'), may hold values from -0.15625 to 0.15625
- merge: float32 [320000], P(('section', 'dp')), may hold values from -0.21875 to 0.21875
Outputs:
- activations: bfloat16 [2, 4, 64, 160, 400], P('section', None, 'dp')
- grad_input: float32 [2, 4, 64, 160, 400], P('section', None, 'dp')
- grad_kernel: float32 [2, 49, 400], P('section')
- grad_gain: float32 [2, 400], P('section')
- grad_shift: float32 [2, 400], P('section')
- grad_bias_in: float32 [2, 1600], P('section')
- grad_bias_out: float32 [2, 400], P('section')
- grad_w_in: float32 [2, 640000], P('section', 'dp')
- grad_w_out: float32 [2, 640000], P('section', 'dp')
- grad_resample: float32 [2, 1280000], P('section', 'dp')
- grad_merge: float32 [320000], P(('section', 'dp'))
The draws below stay inside these ranges and needn't reach their ends.
Inputs may be any that keep to these rules, and one draw needn't show every extreme that they name: 1 marks an ocean cell and 0 a land cell.
All inputs are finite; a program needn't handle non-finite values.
Results may differ from the reference program's by a relative error of at most 0.015.
Values may be sent and summed in bfloat16 or wider, within the bound.
A program may use at most 320 MiB of HBM per device.

```python
import jax
import jax.numpy as jnp
from jax import lax

C = 400
HID = 1600
DEEP = 800
COLS = 160
MB = 4
ROWS = 64


def draw_land(key, part):
    key = jax.random.fold_in(key, 7)
    levels = 250 + 700 * jnp.arange(ROWS, dtype=jnp.int32) // ROWS
    rolled = jax.random.randint(key, (ROWS, COLS), 0, 1000)
    return (rolled < levels[:, None]).astype(jnp.int32)


def shard_levels(key, dims, cuts, low, largest):
    loudness = 1.0
    for axis_at, blocks in cuts:
        steps = jax.random.uniform(jax.random.fold_in(jax.random.fold_in(key, 6), axis_at), (blocks,), jnp.float32, low / len(cuts), largest / len(cuts))
        loudness = loudness * jnp.repeat(jnp.exp(steps), dims[axis_at] // blocks).reshape((-1,) + (1,) * (len(dims) - 1 - axis_at))
    return loudness


def scatter_about(rng, extent, scale, reach, split=(), kind=jnp.bfloat16):
    loudness = shard_levels(rng, extent, split, -0.22, 0.18) if split else 1.0
    drawn = jax.random.normal(rng, extent, jnp.float32) * scale * loudness
    return jnp.minimum(jnp.maximum(drawn, -reach), reach).astype(kind)


def setup_inputs(seed: int = 0) -> dict:
    keys = jax.random.split(jax.random.key(seed), 13)
    inputs = scatter_about(keys[0], (MB, ROWS, COLS, C), 1.0, 6.0, ((1, 16),))
    cotangent = scatter_about(keys[1], (MB, ROWS, COLS, C), 1.0, 6.0, ((1, 16),))
    land = draw_land(jax.random.fold_in(keys[12], 71), 0)
    kernel = scatter_about(keys[3], (2, 49, C), 49 ** -0.5, 0.875, ((0, 2),), jnp.float32)
    bn_gain = jnp.clip(1.0 + 0.15 * jax.random.normal(keys[4], (2, C), jnp.float32), 0.25, 1.75)
    bn_bias = scatter_about(keys[5], (2, C), 0.5, 3.0, ((0, 2),), jnp.float32)
    bias_in = scatter_about(keys[6], (2, HID), 0.5, 3.0, ((0, 2),), jnp.float32)
    bias_out = scatter_about(keys[7], (2, C), 0.3, 2.0, ((0, 2),), jnp.float32)
    w_in = scatter_about(keys[8], (2, C * HID), C ** -0.5, 0.3125, ((0, 2), (1, 16)), jnp.float32)
    w_out = scatter_about(keys[9], (2, HID * C), (HID // 2) ** -0.5, 0.21875, ((0, 2), (1, 16)), jnp.float32)
    resample = scatter_about(keys[10], (2, 4 * C * DEEP), (4 * C) ** -0.5, 0.15625, ((0, 2), (1, 16)), jnp.float32)
    merge = scatter_about(keys[11], (2 * C * C,), (2 * C) ** -0.5, 0.21875, ((0, 32),), jnp.float32)
    return dict(inputs=inputs, cotangent=cotangent, land=land, kernel=kernel, bn_gain=bn_gain, bn_bias=bn_bias, bias_in=bias_in, bias_out=bias_out, w_in=w_in, w_out=w_out, resample=resample, merge=merge)


@jax.custom_vjp
def low(v):
    return lax.optimization_barrier(v.astype(jnp.bfloat16)).astype(jnp.float32)

@jax.custom_vjp
def low_back(v):
    return v

def low_keep(v):
    return (low(v), None)

def low_pass(kept, grad):
    return (grad,)

def back_keep(v):
    return (v, None)

def back_low(kept, grad):
    return (low(grad),)
low.defvjp(low_keep, low_pass)
low_back.defvjp(back_keep, back_low)
eps_norm = 1e-05
highest = lax.Precision.HIGHEST

def wrap_pad(field):
    field = jnp.pad(field, ((3, 3), (0, 0), (0, 0)))
    return jnp.concatenate([field[:, -3:], field, field[:, :3]], axis=1)

def depthwise(padded, kernel_taps, height, across):
    summed = jnp.zeros((height, across, kernel_taps.shape[1]), jnp.float32)
    for offset in range(49):
        window = padded[offset // 7:offset // 7 + height, offset % 7:offset % 7 + across]
        summed = summed + window * kernel_taps[offset]
    return summed

def convnext(source, ocean, kernel_taps, norm_gain, norm_shift, weight_in, in_bias, weight_out, out_bias):
    height, across = ocean.shape
    lowered = low(source)
    depth_out = low_back(depthwise(wrap_pad(lowered), kernel_taps, height, across))
    ocean_cells = ocean[:, :, None]
    counted = jnp.sum(ocean)
    mean_value = lax.optimization_barrier(jnp.sum(depth_out * ocean_cells, axis=(0, 1))) / counted
    second = lax.optimization_barrier(jnp.sum(depth_out * depth_out * ocean_cells, axis=(0, 1))) / counted
    inverse = lax.rsqrt(second - mean_value * mean_value + eps_norm)
    normed = low((depth_out - mean_value) * inverse * norm_gain + norm_shift)
    expanded = low_back(jnp.einsum('hwc,ce->hwe', normed, weight_in, precision=highest) + in_bias)
    activated = low(jax.nn.gelu(expanded, approximate=False))
    branch = low_back(jnp.einsum('hwe,ec->hwc', activated, weight_out, precision=highest) + out_bias)
    return ocean_cells * (source + branch)

def encoder(source, ocean, coarse, params):
    kernel_taps, norm_gain, norm_shift, in_bias, out_bias, flat_in, flat_out, flat_res = params
    channels = source.shape[2]
    height, across = ocean.shape
    block_out = low(convnext(source, ocean, kernel_taps, norm_gain, norm_shift, low(flat_in.reshape(channels, -1)), in_bias, low(flat_out.reshape(-1, channels)), out_bias))
    down_map = low(flat_res.reshape(2, 2 * channels, -1))
    patches = block_out.reshape(height // 2, 2, across // 2, 2 * channels)
    deep_value = coarse[:, :, None] * jnp.einsum('aibk,ikn->abn', patches, down_map, precision=highest)
    return (block_out, low(deep_value))

def decoder(deep_value, skip_value, ocean, params, merge_flat):
    kernel_taps, norm_gain, norm_shift, in_bias, out_bias, flat_in, flat_out, flat_res = params
    channels = skip_value.shape[2]
    height, across = ocean.shape
    deep_in = low_back(deep_value)
    skip_in = low_back(skip_value)
    up_map = low(flat_res.reshape(-1, 2, 2 * channels))
    upsampled = jnp.einsum('abk,kin->aibn', deep_in, up_map, precision=highest).reshape(height, across, channels)
    upsampled = low(low_back(upsampled))
    merge_map = low(merge_flat.reshape(2 * channels, channels))
    joined = jnp.einsum('hwc,cn->hwn', upsampled, merge_map[:channels], precision=highest)
    joined = low_back(joined + jnp.einsum('hwc,cn->hwn', skip_in, merge_map[channels:], precision=highest))
    return convnext(joined, ocean, kernel_taps, norm_gain, norm_shift, low(flat_in.reshape(channels, -1)), in_bias, low(flat_out.reshape(-1, channels)), out_bias)

def reference(inputs, cotangent, land, kernel, bn_gain, bn_bias, bias_in, bias_out, w_in, w_out, resample, merge):
    ocean = land.astype(jnp.float32)
    height, across = land.shape
    coarse = lax.optimization_barrier(jnp.min(land.reshape(height // 2, 2, across // 2, 2), axis=(1, 3))).astype(jnp.float32)
    stacked = (kernel, bn_gain, bn_bias, bias_in, bias_out, w_in, w_out, resample)
    encoder_params = tuple((member[0] for member in stacked))
    decoder_params = tuple((member[1] for member in stacked))

    def one_batch(totals, batch_pair):
        enc_totals, dec_totals, merge_total = totals
        source, seed_grad = batch_pair
        enc_values, enc_back = jax.vjp(lambda source_in, params_in: encoder(source_in, ocean, coarse, params_in), source.astype(jnp.float32), encoder_params)
        skip_value, deep_value = enc_values
        dec_value, dec_back = jax.vjp(lambda deep_in, skip_in, params_in, merge_in: decoder(deep_in, skip_in, ocean, params_in, merge_in), deep_value, skip_value, decoder_params, merge)
        deep_grad, skip_grad, dec_grads, merge_grad = dec_back(seed_grad.astype(jnp.float32))
        source_grad, enc_grads = enc_back((skip_grad, deep_grad))
        new_totals = (jax.tree.map(jnp.add, enc_totals, enc_grads), jax.tree.map(jnp.add, dec_totals, dec_grads), merge_total + merge_grad)
        return (new_totals, (skip_value.astype(jnp.bfloat16), dec_value.astype(jnp.bfloat16), source_grad, skip_grad))
    start = (jax.tree.map(jnp.zeros_like, encoder_params), jax.tree.map(jnp.zeros_like, decoder_params), jnp.zeros_like(merge))
    totals, produced = lax.scan(one_batch, start, (inputs, cotangent))
    enc_totals, dec_totals, merge_total = totals
    skip_outs, dec_outs, source_grads, skip_grads = produced
    activations = jnp.stack([skip_outs, dec_outs])
    grad_input = jnp.stack([source_grads, skip_grads])
    grads = tuple((jnp.stack([first_grad, second_grad]) for first_grad, second_grad in zip(enc_totals, dec_totals)))
    return (activations, grad_input, grads[0], grads[1], grads[2], grads[3], grads[4], grads[5], grads[6], grads[7], merge_total)
```

```python
import functools

import jax
import jax.numpy as jnp
import ml_dtypes
import numpy as np
from jax import lax
from jax.experimental import pallas as pl
from jax.experimental.pallas import tpu as pltpu
from jax.sharding import PartitionSpec as P

BF = jnp.bfloat16
F32 = jnp.float32
MESH = pl.DeviceIdType.MESH
ANY = pl.BlockSpec(memory_space=pl.ANY)
VM = pl.BlockSpec(memory_space=pltpu.VMEM)
DMA = pltpu.SemaphoreType.DMA
EPS = 1e-05
GROUPS = 16
MEGA = 1 << 20


def padded(width):
    return -(-(width // GROUPS) // 16) * 16


def selector(rows, cols, pairs):
    out = np.zeros((rows, cols), np.float32)
    for r, c in pairs:
        out[r, c] = 1
    return out.astype(ml_dtypes.bfloat16)


def matrices(channels):
    group, wide = channels // GROUPS, padded(channels)
    spread = selector(channels, GROUPS * wide, [(c, c // group * wide + c % group) for c in range(channels)])
    natural = selector(896, 224, [(i * 128 + q * 8 + p, (p + i) * 16 + q) for i in range(7) for q in range(16) for p in range(8)])

    def place(q, row):
        if row < 0:
            return 128 + q * 3 + row + 3
        return q * 8 + row if row < 8 else 176 + q * 3 + row - 8

    shifts = selector(896, 224, [(i * 128 + q * 8 + p, place(q, p + i - 3)) for i in range(7) for q in range(16) for p in range(8)])
    turn = selector(128, 128, [(q * 8 + p, p * 16 + q) for q in range(16) for p in range(8)])
    edges = selector(96, 128, [(48 * e + q * 3 + k, q * 8 + 5 * e + k) for e in range(2) for q in range(16) for k in range(3)])
    patch = selector(
        256, 256,
        [((i * 2 + j) * 64 + b * 4 + a, (2 * b + j) * 8 + 2 * a + i) for i in range(2) for j in range(2) for b in range(16) for a in range(4)],
    )
    return dict(
        spread=spread, gather=np.ascontiguousarray(spread.T), natural=natural, shifts=shifts, turn=turn,
        back=np.ascontiguousarray(turn.T), edges=edges, patch=patch, unpatch=np.ascontiguousarray(patch.T),
    )


def grow(value, sizes):
    return jnp.pad(value, [(0, n - o) for n, o in zip(sizes, value.shape)])


def pack_in(value, parts, c, h):
    value = value.reshape(parts, c // GROUPS, GROUPS, h // GROUPS)
    return grow(value, (parts, padded(c), GROUPS, padded(h))).reshape(parts, padded(c), -1)


def pack_down(value, parts, c, n):
    value = value.reshape(parts, 4, c // GROUPS, GROUPS, n // GROUPS)
    return grow(value, (parts, 4, padded(c), GROUPS, padded(n))).reshape(parts, 4 * padded(c), -1)


def pack_up(value, parts, c, n):
    value = value.reshape(parts, n // GROUPS, 2, 2 * GROUPS, c // GROUPS)
    value = grow(value, (parts, padded(n), 2, 2 * GROUPS, padded(c)))
    return value.transpose(0, 2, 1, 3, 4).reshape(parts, 2 * padded(n), -1)


def unpack_in(value, c, h):
    value = value.reshape(-1, padded(c), GROUPS, padded(h))
    return value[:, : c // GROUPS, :, : h // GROUPS].reshape(-1)


def unpack_down(value, c, n):
    value = value.reshape(-1, 4, padded(c), GROUPS, padded(n))
    return value[:, :, : c // GROUPS, :, : n // GROUPS].reshape(-1)


def unpack_up(value, c, n):
    value = value.reshape(-1, 2, padded(n), 2 * GROUPS, padded(c))
    return value.transpose(0, 2, 1, 3, 4)[:, : n // GROUPS, :, :, : c // GROUPS].reshape(-1)


def where_am_i():
    s, d = lax.axis_index("section"), lax.axis_index("dp")
    return s, d, d // 4, d % 4, 2 * (d // 4) + s


def greet(peers):
    barrier = pltpu.get_barrier_semaphore()
    for peer in peers:
        pl.semaphore_signal(barrier, inc=1, device_id=peer, device_id_type=MESH)
    pl.semaphore_wait(barrier, len(peers))


def greet_line(count):
    s, d, g, m, p = where_am_i()
    barrier = pltpu.get_barrier_semaphore()

    def one(k, carry):
        q = (p + k) % count
        pl.semaphore_signal(barrier, inc=1, device_id=(q % 2, 4 * (q // 2) + m), device_id_type=MESH)
        return carry

    lax.fori_loop(1, count, one, 0)
    pl.semaphore_wait(barrier, count - 1)


def greet_all(sections, dps):
    s, d, g, m, p = where_am_i()
    barrier = pltpu.get_barrier_semaphore()
    me, count = s * dps + d, sections * dps

    def one(k, carry):
        q = (me + k) % count
        pl.semaphore_signal(barrier, inc=1, device_id=(q // dps, q % dps), device_id_type=MESH)
        return carry

    lax.fori_loop(1, count, one, 0)
    pl.semaphore_wait(barrier, count - 1)


def remote(src, dst, send, recv, peer):
    return pltpu.make_async_remote_copy(src_ref=src, dst_ref=dst, send_sem=send, recv_sem=recv, device_id=peer, device_id_type=MESH)


def arrived(ref, sem):
    pltpu.make_async_copy(ref, ref, sem).wait()


def all_sum(mine, slots, send, recv, count):
    s, d, g, m, p = where_am_i()

    def copy(k):
        q = (p + k) % count
        return remote(mine, slots.at[p], send.at[k], recv.at[k], (q % 2, 4 * (q // 2) + m))

    lax.fori_loop(1, count, lambda k, c: (copy(k).start(), c)[1], 0)
    slots[p] = mine[...]

    def wait(k, carry):
        arrived(slots.at[(p + count - k) % count], recv.at[k])
        copy(k).wait_send()
        return carry

    lax.fori_loop(1, count, wait, 0)
    return lax.fori_loop(0, count, lambda k, total: total + slots[k], jnp.zeros(mine.shape, F32))


def swap_rows(packed, halo, send, recv, count):
    s, d, g, m, p = where_am_i()

    def peer(q):
        return (q % 2, 4 * (q // 2) + m)

    @pl.when(p > 0)
    def _():
        remote(packed.at[0], halo.at[1], send.at[0], recv.at[1], peer(p - 1)).start()

    @pl.when(p < count - 1)
    def _():
        remote(packed.at[1], halo.at[0], send.at[1], recv.at[0], peer(p + 1)).start()

    @pl.when(p > 0)
    def _():
        arrived(halo.at[0], recv.at[0])
        remote(packed.at[0], halo.at[1], send.at[0], recv.at[1], peer(p - 1)).wait_send()

    @pl.when(p < count - 1)
    def _():
        arrived(halo.at[1], recv.at[1])
        remote(packed.at[1], halo.at[0], send.at[1], recv.at[0], peer(p + 1)).wait_send()

    @pl.when(p == 0)
    def _():
        halo[0] = jnp.zeros(halo.shape[1:], BF)

    @pl.when(p == count - 1)
    def _():
        halo[1] = jnp.zeros(halo.shape[1:], BF)


def dot(a, b):
    return jnp.dot(a, b, preferred_element_type=F32)


def dot_nt(a, b):
    return lax.dot_general(a, b, (((1,), (1,)), ((), ())), preferred_element_type=F32)


def dot_tn(a, b):
    return lax.dot_general(a, b, (((0,), (0,)), ((), ())), preferred_element_type=F32)


def lanes4(mask, width):
    return jnp.concatenate([mask] * (width // 128), axis=1)


def rows8(value):
    return value.reshape(-1, 8, value.shape[-1]).sum(0)


def to_natural(cells, back, gather):
    turned = dot(dot(back, cells).astype(BF), gather).astype(BF)
    return turned.reshape(8, 16, turned.shape[-1])


def shifted(chunk, perm, S, c):
    moved = dot(perm, chunk)
    for lane in range(S.shape[1]):
        S[:, lane, pl.ds(3 + 16 * c, 16)] = moved[:, lane * 128 : lane * 128 + 128].reshape(7, 16, 8, 128)
    return moved


def wrap(S, cols):
    S[:, :, 0:3] = S[:, :, cols : cols + 3]
    S[:, :, cols + 3 : cols + 6] = S[:, :, 3:6]


def taps_to(kb, par, flip):
    for k in range(49):
        kb[k] = jnp.broadcast_to(par[(48 - k if flip else k) : (48 - k if flip else k) + 1], kb.shape[1:])


def conv_tail(S, kb, ocean, z, stats, slots, out, send, recv, count, cols):
    wide = kb.shape[2]
    tally = jnp.zeros((8, 128), F32)
    tally = lax.fori_loop(0, cols // 8, lambda b, t: t + ocean[pl.ds(b * 8, 8)].sum(0), tally)
    for lane in range(wide // 128):
        at = slice(lane * 128, lane * 128 + 128)

        def step(b, carry):
            first, second = carry
            acc = jnp.zeros((8, 8, 128), F32)
            for i in range(7):
                window = S[i, lane, pl.ds(b * 8, 14)]
                for j in range(7):
                    acc = acc + window[j : j + 8] * kb[7 * i + j, :, at][None]
            z[pl.ds(b * 8, 8), :, at] = acc
            kept = acc * ocean[pl.ds(b * 8, 8)]
            return first + kept.sum(0), second + (kept * acc).sum(0)

        zero = jnp.zeros((8, 128), F32)
        first, second = lax.fori_loop(0, cols // 8, step, (zero, zero))
        stats[0:1, at] = first.sum(0, keepdims=True)
        stats[1:2, at] = second.sum(0, keepdims=True)
        stats[2:3, at] = tally.sum(0, keepdims=True)
        stats[3:8, at] = jnp.zeros((5, 128), F32)
    out[...] = all_sum(stats, slots, send, recv, count)


def enc_conv_kernel(count, cols, x14, spread, natural, par, ocean, z, a, out, S, kb, stats, slots, send, recv):
    greet_line(count)
    taps_to(kb, par, False)

    def chunk(c, carry):
        block = x14[:, c]
        block = dot(block.reshape(-1, block.shape[-1]), spread[...]).astype(BF)
        moved = shifted(block, natural[...], S, c)
        a[pl.ds(pl.multiple_of(c * 128, 128), 128)] = moved[384:512].astype(BF)
        return carry

    lax.fori_loop(0, cols // 16, chunk, 0)
    wrap(S, cols)
    conv_tail(S, kb, ocean, z, stats, slots, out, send, recv, count, cols)


def dec_conv_kernel(count, cols, a, halo, shifts, par, ocean, z, out, S, kb, stats, slots, send, recv):
    greet_line(count)
    taps_to(kb, par, False)

    def chunk(c, carry):
        block = jnp.concatenate([a[pl.ds(pl.multiple_of(c * 128, 128), 128)], halo[0, c], halo[1, c]], axis=0)
        shifted(block, shifts[...], S, c)
        return carry

    lax.fori_loop(0, cols // 16, chunk, 0)
    wrap(S, cols)
    conv_tail(S, kb, ocean, z, stats, slots, out, send, recv, count, cols)


def norm_terms(st, par):
    counted = st[2:3]
    mean = st[0:1] / counted
    inverse = lax.rsqrt(st[1:2] / counted - mean * mean + EPS)
    return counted, mean, inverse, par[49:50], par[50:51]


def ff_kernel(z, st, par, bias, w1, w2, res, ocean, back, gather, n, g, gp, y, nat):
    counted, mean, inverse, gain, shift = norm_terms(st, par)
    normed = ((z[...] - mean) * inverse * gain + shift).astype(BF)
    n[...] = normed
    acc = jnp.zeros(z.shape, F32)
    for h in range(0, w1.shape[1], 256):
        at = slice(h, h + 256)
        e = dot(normed, w1[:, at]) + bias[0:1, at]
        phi = 0.5 + 0.5 * lax.erf(e * np.float32(0.5**0.5))
        act = (e * phi).astype(BF)
        g[:, at] = act
        gp[:, at] = (phi + e * (np.float32((2 * np.pi) ** -0.5) * jnp.exp(-0.5 * e * e))).astype(BF)
        acc = acc + dot(act, w2[at])
    mask = lanes4(ocean[...], z.shape[1])
    out = (mask * (res[...].astype(F32) + (acc + par[51:52]))).astype(BF)
    y[...] = out
    for k in range(2):
        nat[:, k] = to_natural(out[128 * k : 128 * k + 128], back[...], gather[...])


def mid_kernel(count, skip, down, up_w, merge, coarse, patch, unpatch, edges, pieces, deep, up, h, a, halo, packed, send, recv):
    s, d, g, m, p = where_am_i()
    barrier = pltpu.get_barrier_semaphore()

    def peer(q):
        return (q % 2, 4 * (q // 2) + m)

    @pl.when(p > 0)
    def _():
        pl.semaphore_signal(barrier, inc=1, device_id=peer(p - 1), device_id_type=MESH)

    @pl.when(p < count - 1)
    def _():
        pl.semaphore_signal(barrier, inc=1, device_id=peer(p + 1), device_id_type=MESH)

    pl.semaphore_wait(barrier, jnp.where(p > 0, 1, 0) + jnp.where(p < count - 1, 1, 0))
    wide = skip.shape[1]
    blocks = skip.shape[0] // 256
    for b in range(blocks):
        moved = dot(patch[...], skip[256 * b : 256 * b + 256]).astype(BF)
        for k in range(4):
            pieces[k, 64 * b : 64 * b + 64] = moved[64 * k : 64 * k + 64]
    value = sum(dot(pieces[k], down[wide * k : wide * k + wide]) for k in range(4))
    deep_value = (lanes4(coarse[...], value.shape[1]) * value).astype(BF)
    deep[...] = deep_value
    rows = up_w.shape[0] * up_w.shape[2]
    lifted = [dot(deep_value, up_w[:, i].reshape(rows, -1)).astype(BF) for i in range(2)]
    for b in range(blocks):
        stacked = jnp.concatenate(
            [lifted[i][64 * b : 64 * b + 64, wide * j : wide * j + wide] for i in range(2) for j in range(2)], axis=0
        )
        up[256 * b : 256 * b + 256] = dot(unpatch[...], stacked).astype(BF)
    for b in range(blocks):
        at = slice(256 * b, 256 * b + 256)
        joined = dot(up[at], merge[0]) + dot(skip[at], merge[1])
        h[at] = joined
        low = joined.astype(BF)
        a[at] = low
        for k in range(2):
            ends = dot(edges[...], low[128 * k : 128 * k + 128]).astype(BF)
            packed[0, 2 * b + k] = ends[:48]
            packed[1, 2 * b + k] = ends[48:]
    swap_rows(packed, halo, send, recv, count)


def back_ff_kernel(
    count, natural_grad, top, z, st, par, w1, w2, n, g, gp, ocean, spread, turn, edges,
    dym, dw1, dw2, small, dz, halo, dn, dr, packed, stats, slots, send, recv, hsend, hrecv,
):
    greet_line(count)
    wide = z.shape[1]
    chunks = z.shape[0] // 128
    counted, mean, inverse, gain, shift = norm_terms(st, par)

    def begin(c, total):
        at = pl.ds(pl.multiple_of(c * 128, 128), 128)
        if natural_grad:
            block = top[:, c]
            block = dot(block.reshape(-1, block.shape[-1]), spread[...]).astype(BF)
            grad = dot(turn[...], block)
        else:
            grad = top[at]
        grad = grad * lanes4(ocean[at], wide)
        dym[at] = grad
        low = grad.astype(BF)
        dr[at] = low
        return total + rows8(low.astype(F32))

    total = lax.fori_loop(0, chunks, begin, jnp.zeros((8, wide), F32))
    small[2:3] = total.sum(0, keepdims=True)
    small[3:8] = jnp.zeros((5, wide), F32)
    for h in range(0, w1.shape[1], 256):
        at = slice(h, h + 256)
        dg = dot_nt(dr[...], w2[at])
        de = (dg * gp[:, at].astype(F32)).astype(BF)
        row, col = 3 + h // wide, h % wide
        small[row : row + 1, col : col + 256] = de.astype(F32).sum(0, keepdims=True)
        dw1[:, at] = dot_tn(n[...], de).astype(BF)
        dw2[at] = dot_tn(g[:, at], dr[...]).astype(BF)
        part = dot_nt(de, w1[:, at])
        if h == 0:
            dn[...] = part
        else:
            dn[...] += part

    def sums(c, carry):
        at = pl.ds(pl.multiple_of(c * 128, 128), 128)
        grad = dn[at]
        return carry[0] + rows8(grad), carry[1] + rows8(grad * ((z[at] - mean) * inverse))

    zero = jnp.zeros((8, wide), F32)
    plain, scaled = lax.fori_loop(0, chunks, sums, (zero, zero))
    small[0:1] = plain.sum(0, keepdims=True)
    small[1:2] = scaled.sum(0, keepdims=True)
    stats[...] = small[...]
    summed = all_sum(stats, slots, send, recv, count)
    first = -inverse * gain * summed[0:1] / counted
    second = -inverse * inverse * gain * summed[1:2] / counted

    def end(c, carry):
        at = pl.ds(pl.multiple_of(c * 128, 128), 128)
        grad = inverse * gain * dn[at] + lanes4(ocean[at], wide) * (first + second * (z[at] - mean))
        low = grad.astype(BF)
        dz[at] = low
        ends = dot(edges[...], low).astype(BF)
        packed[0, c] = ends[:48]
        packed[1, c] = ends[48:]
        return carry

    lax.fori_loop(0, chunks, end, 0)
    swap_rows(packed, halo, hsend, hrecv, count)


def back_conv_kernel(cols, natural_out, dz, halo, shifts, par, dym, a, back, gather, dh, dk, S, kb, acc_dk):
    taps_to(kb, par, True)
    wide = dz.shape[1]

    def chunk(c, carry):
        block = jnp.concatenate([dz[pl.ds(pl.multiple_of(c * 128, 128), 128)], halo[0, c], halo[1, c]], axis=0)
        shifted(block, shifts[...], S, c)
        return carry

    lax.fori_loop(0, cols // 16, chunk, 0)
    wrap(S, cols)
    acc_dk[...] = jnp.zeros(acc_dk.shape, F32)
    for lane in range(wide // 128):
        at = slice(lane * 128, lane * 128 + 128)

        def step(b, carry):
            cells = pl.ds(pl.multiple_of(b * 64, 64), 64)
            acc = dym[cells, at].reshape(8, 8, 128)
            field = a[cells, at].astype(F32).reshape(8, 8, 128)
            for i in range(7):
                window = S[i, lane, pl.ds(b * 8, 14)]
                for j in range(7):
                    acc = acc + window[j : j + 8] * kb[7 * i + j, :, at][None]
                    acc_dk[7 * i + j, :, at] += (window[j : j + 8] * field).sum(0)
            dh[cells, at] = acc.reshape(64, 128).astype(BF)
            return carry

        lax.fori_loop(0, cols // 8, step, 0)
    for k in range(49):
        dk[48 - k : 49 - k] = acc_dk[k].sum(0, keepdims=True)
    dk[49:56] = jnp.zeros((7, wide), F32)
    if natural_out is not None:

        def out(c, carry):
            cells = dh[pl.ds(pl.multiple_of(c * 128, 128), 128)]
            natural_out[:, c] = to_natural(cells, back[...], gather[...])
            return carry

        lax.fori_loop(0, cols // 16, out, 0)


def back_mid_kernel(dh, up, skip, deep, pieces, down, up_w, merge, coarse, patch, unpatch, back, gather,
                    dmerge, dup_w, ddown, dy, nat, dskip, dups, spreads):
    wide = dh.shape[1]
    blocks = dh.shape[0] // 256
    dmerge[0] = dot_tn(up[...], dh[...]).astype(BF)
    dmerge[1] = dot_tn(skip[...], dh[...]).astype(BF)
    for b in range(blocks):
        at = slice(256 * b, 256 * b + 256)
        low = dot_nt(dh[at], merge[1]).astype(BF)
        dskip[at] = low
        for k in range(2):
            nat[:, 2 * b + k] = to_natural(low[128 * k : 128 * k + 128], back[...], gather[...])
        lifted = dot_nt(dh[at], merge[0]).astype(BF)
        moved = dot(patch[...], lifted).astype(BF)
        for k in range(4):
            dups[k // 2, 64 * b : 64 * b + 64, wide * (k % 2) : wide * (k % 2) + wide] = moved[64 * k : 64 * k + 64]
    rows = up_w.shape[0] * up_w.shape[2]
    ddeep = dot_nt(dups[0], up_w[:, 0].reshape(rows, -1)) + dot_nt(dups[1], up_w[:, 1].reshape(rows, -1))
    for i in range(2):
        grad = dot_tn(deep[...], dups[i]).astype(BF)
        dup_w[:, i] = grad.reshape(up_w.shape[0], up_w.shape[2], -1)
    masked = (lanes4(coarse[...], ddeep.shape[1]) * ddeep).astype(BF)
    for k in range(4):
        ddown[wide * k : wide * k + wide] = dot_tn(pieces[k], masked).astype(BF)
        spreads[k] = dot_nt(masked, down[wide * k : wide * k + wide])
    for b in range(blocks):
        value = jnp.concatenate([spreads[k, 64 * b : 64 * b + 64] for k in range(4)], axis=0)
        high = value.astype(BF)
        rest = (value - high.astype(F32)).astype(BF)
        at = slice(256 * b, 256 * b + 256)
        dy[at] = dskip[at].astype(F32) + (dot(unpatch[...], high) + dot(unpatch[...], rest))


def share_kernel(sections, dps, x, cot, land, par, bias, zero, x14, cot8, land2, par2, bias2, xs, xr, hs, hr, cs, cr, ls, lr, ps, pr):
    s, d, g, m, p = where_am_i()
    count = 2 * (dps // 4)
    greet_all(sections, dps)
    pos, j = d // 2, d % 2

    def move(started, cond, src, dst, send, recv, peer):
        self = (peer[0] == s) & (peer[1] == d)
        far = remote(src, dst, send, recv, peer)
        pl.when(cond & jnp.logical_not(self))(lambda: far.start())
        pl.when(cond & self)(lambda: pltpu.make_async_copy(src, dst, recv).start())
        started.append((cond & jnp.logical_not(self), far))

    started = []
    yes = d >= 0
    for k in range(2):
        mb = 2 * k + s
        to = (pos % 2, 4 * (pos // 2) + mb)
        move(started, yes, x.at[mb], x14.at[pl.ds(3 + 4 * j, 4)], xs.at[k], xr.at[j], to)
        move(started, yes, cot.at[mb], cot8.at[pl.ds(4 * j, 4)], cs.at[k], cr.at[j], to)
        move(started, yes, land, land2.at[j], ls.at[k], lr.at[j], to)
        above, below = pos - 1, pos + 1
        move(started, (j == 0) & (pos > 0), x.at[mb, pl.ds(0, 3)], x14.at[pl.ds(11, 3)], hs.at[k], hr.at[1], (above % 2, 4 * (above // 2) + mb))
        move(started, (j == 1) & (pos < count - 1), x.at[mb, pl.ds(1, 3)], x14.at[pl.ds(0, 3)], hs.at[k], hr.at[0], (below % 2, 4 * (below // 2) + mb))
    pl.when(p == 0)(lambda: pltpu.make_async_copy(zero, x14.at[pl.ds(0, 3)], hr.at[0]).start())
    pl.when(p == count - 1)(lambda: pltpu.make_async_copy(zero, x14.at[pl.ds(11, 3)], hr.at[1]).start())
    other = (1 - s, d)
    far = [remote(par, par2.at[s], ps.at[0], pr.at[0], other), remote(bias, bias2.at[s], ps.at[1], pr.at[1], other)]
    near = [pltpu.make_async_copy(par, par2.at[s], ps.at[2]), pltpu.make_async_copy(bias, bias2.at[s], ps.at[3])]
    for c in far + near:
        c.start()
    for jj in range(2):
        arrived(x14.at[pl.ds(3 + 4 * jj, 4)], xr.at[jj])
        arrived(cot8.at[pl.ds(4 * jj, 4)], cr.at[jj])
        arrived(land2.at[jj], lr.at[jj])
    arrived(x14.at[pl.ds(0, 3)], hr.at[0])
    arrived(x14.at[pl.ds(11, 3)], hr.at[1])
    arrived(par2.at[1 - s], pr.at[0])
    arrived(bias2.at[1 - s], pr.at[1])
    for c in far:
        c.wait_send()
    for c in near:
        c.wait()
    for cond, c in started:
        pl.when(cond)(lambda c=c: c.wait_send())


def gather_kernel(*refs):
    ins, outs = refs[:4], refs[4:8]
    own, zs, zr, as_, ar, bs, br, cs, cr = refs[8:]
    s, d, g, m, p = where_am_i()
    greet_all(2, 16)
    zc, others = d // 4, []
    local, far_z = [], []
    for k in range(4):
        local.append(pltpu.make_async_copy(ins[k], outs[k].at[s, zc, m], own.at[k]))
        local[-1].start()
        for step in range(1, 4):
            peer = (s, 4 * ((zc + step) % 4) + m)
            far_z.append(remote(ins[k], outs[k].at[s, zc, m], zs.at[k, step], zr.at[k, step], peer))
            far_z[-1].start()
    first, second, last = [], [], []

    def hand_over(k, col, index):
        c = remote(outs[k].at[s, :, col], outs[k].at[s, :, col], cs.at[k, index], cr.at[k, index], (1 - s, d))
        c.start()
        last.append(c)

    for k in range(4):
        bit = 1 if k < 2 else 2
        local[k].wait()
        for step in range(1, 4):
            arrived(outs[k].at[s, (zc + 4 - step) % 4, m], zr.at[k, step])
        first.append(remote(outs[k].at[s, :, m], outs[k].at[s, :, m], as_.at[k], ar.at[k], (s, d ^ bit)))
        first[-1].start()
        second.append(remote(outs[k].at[s, :, m], outs[k].at[s, :, m], bs.at[k, 0], br.at[k, 0], (s, d ^ (3 - bit))))
        second[-1].start()
        hand_over(k, m, 0)
    for k in range(4):
        bit = 1 if k < 2 else 2
        arrived(outs[k].at[s, :, m ^ bit], ar.at[k])
        second.append(remote(outs[k].at[s, :, m ^ bit], outs[k].at[s, :, m ^ bit], bs.at[k, 1], br.at[k, 1], (s, d ^ (3 - bit))))
        second[-1].start()
        hand_over(k, m ^ bit, 1)
    for k in range(4):
        bit = 1 if k < 2 else 2
        arrived(outs[k].at[s, :, m ^ (3 - bit)], br.at[k, 0])
        hand_over(k, m ^ (3 - bit), 2)
        arrived(outs[k].at[s, :, m ^ 3], br.at[k, 1])
        hand_over(k, m ^ 3, 3)
    for k in range(4):
        bit = 1 if k < 2 else 2
        for index, col in enumerate((m, m ^ bit, m ^ (3 - bit), m ^ 3)):
            arrived(outs[k].at[1 - s, :, col], cr.at[k, index])
    for c in far_z + first + second + last:
        c.wait_send()


def deliver_kernel(dps, a0, a1, g0, g1, act, gi, send, recv):
    s, d, g, m, p = where_am_i()
    greet_all(2, dps)
    started = []
    for sec in range(2):
        for q, (src, dst) in enumerate((((a0, a1)[sec], act), ((g0, g1)[sec], gi))):
            for j in range(2):
                dp = 4 * g + 2 * s + j
                self = (s == sec) & (d == dp)
                part = src.at[pl.ds(4 * j, 4)]
                far = remote(part, dst.at[m], send.at[sec, q, j], recv.at[q, m], (sec, dp))
                pl.when(jnp.logical_not(self))(lambda far=far: far.start())
                pl.when(self)(lambda part=part, dst=dst, q=q: pltpu.make_async_copy(part, dst.at[m], recv.at[q, m]).start())
                started.append((jnp.logical_not(self), far))
    for q, dst in enumerate((act, gi)):
        for mb in range(4):
            arrived(dst.at[mb], recv.at[q, mb])
    for cond, far in started:
        pl.when(cond)(lambda far=far: far.wait_send())


def reduce_kernel(*refs):
    enc, dec, merge, small = refs[:3], refs[3:6], refs[6], refs[7]
    outs, small_out = refs[8:12], refs[12]
    own, core, plane1, plane2, line = refs[13:17], refs[17:21], refs[21:25], refs[25:29], refs[29:33]
    tiny, ls, cs, cr, as_, ar, bs, br, zs, zr, ts, tr = refs[33:]
    s, d, g, m, p = where_am_i()
    greet_all(2, 16)
    other = (1 - s, d)
    for k in range(4):
        for sec in range(2):

            @pl.when(s == sec)
            def _(k=k, sec=sec):
                mine = (enc, dec)[sec][k] if k < 3 else merge.at[sec]
                theirs = (enc, dec)[1 - sec][k] if k < 3 else merge.at[1 - sec]
                pltpu.make_async_copy(mine, own[k], ls.at[k]).start()
                remote(theirs, core[k], cs.at[k], cr.at[k], other).start()

    def theirs_of(k):
        return enc[k] if k < 3 else merge.at[0]

    t0 = remote(small.at[1 - s], tiny.at[0], ts.at[0], tr.at[0], other)
    t0.start()
    arrived(tiny.at[0], tr.at[0])
    t0.wait_send()
    tiny[1] = small[s] + tiny[0]
    sent = []
    for step in range(1, 4):
        sent.append(remote(tiny.at[1], tiny.at[1 + step], ts.at[step], tr.at[step], (s, 4 * ((g + step) % 4) + m)))
        sent[-1].start()
    for step in range(1, 4):
        arrived(tiny.at[1 + step], tr.at[step])
    for c in sent:
        c.wait_send()
    tiny[5] = tiny[1] + tiny[2] + tiny[3] + tiny[4]
    sent = []
    for step in range(1, 4):
        sent.append(remote(tiny.at[5], tiny.at[5 + step], ts.at[3 + step], tr.at[3 + step], (s, d ^ step)))
        sent[-1].start()
    for step in range(1, 4):
        arrived(tiny.at[5 + step], tr.at[3 + step])
    for c in sent:
        c.wait_send()
    small_out[...] = tiny[5] + tiny[6] + tiny[7] + tiny[8]

    sent = []
    for k in range(4):
        bit = 1 if k < 2 else 2
        pltpu.make_async_copy(own[k], own[k], ls.at[k]).wait()
        arrived(core[k], cr.at[k])

        def add(b, carry, k=k):
            own[k][b // 4, b % 4] = (own[k][b // 4, b % 4].astype(F32) + core[k][b // 4, b % 4].astype(F32)).astype(BF)
            return carry

        lax.fori_loop(0, 16, add, 0)
        for index, col in enumerate((m ^ bit, m ^ 3)):
            sent.append(remote(own[k].at[:, col], plane1[k].at[:, index], as_.at[k, index], ar.at[k, index], (s, d ^ bit)))
            sent[-1].start()
    for k in range(4):
        bit = 1 if k < 2 else 2
        rest = m ^ (3 - bit)
        arrived(plane1[k].at[:, 1], ar.at[k, 1])
        for z in range(4):
            own[k][z, rest] = (own[k][z, rest].astype(F32) + plane1[k][z, 1].astype(F32)).astype(BF)
        sent.append(remote(own[k].at[:, rest], plane2[k], bs.at[k], br.at[k], (s, d ^ (3 - bit))))
        sent[-1].start()
    for k in range(4):
        arrived(plane1[k].at[:, 0], ar.at[k, 0])
        arrived(plane2[k], br.at[k])
        for z in range(4):
            own[k][z, m] = (own[k][z, m].astype(F32) + plane1[k][z, 0].astype(F32) + plane2[k][z].astype(F32)).astype(BF)
        for step in range(1, 4):
            to = (g + step) % 4
            sent.append(remote(own[k].at[to, m], line[k].at[step - 1], zs.at[k, step], zr.at[k, step], (s, 4 * to + m)))
            sent[-1].start()
    for k in range(4):
        for step in range(1, 4):
            arrived(line[k].at[step - 1], zr.at[k, step])
        outs[k][...] = own[k][g, m].astype(F32) + line[k][0].astype(F32) + line[k][1].astype(F32) + line[k][2].astype(F32)
    for c in sent:
        c.wait_send()
    for k in range(4):
        remote(theirs_of(k), core[k], cs.at[k], cr.at[k], other).wait_send()


def call(name, body, outs, ins=None, out_specs=None, scratch=(), cid=None, limit=56, **more):
    params = dict(vmem_limit_bytes=limit * MEGA)
    if cid is not None:
        params.update(collective_id=cid, has_side_effects=True)
    shapes = [jax.ShapeDtypeStruct(s, t) for s, t in outs]
    return pl.pallas_call(
        body, out_shape=shapes, name=name, compiler_params=pltpu.CompilerParams(**params), scratch_shapes=list(scratch),
        out_specs=out_specs or [VM] * len(outs), **({"in_specs": ins} if ins else {}), **more,
    )


def on_device(sections, dps, inputs, cotangent, land, kernel, bn_gain, bn_bias, bias_in, bias_out, w_in, w_out, resample, merge):
    batches, height, cols, c = inputs.shape
    hid = bias_in.shape[1]
    n = resample.shape[1] * dps // (4 * c)
    cw, hw, nw = (GROUPS * padded(v) for v in (c, hid, n))
    cells, deep_cells = cols * 8, cols * 2
    count = 2 * (dps // 4)
    assert batches == 4 and height == 4 and dps % 4 == 0 and sections == 2 and cols % 32 == 0
    s = lax.axis_index("section")
    mats = {k: jnp.asarray(v) for k, v in matrices(c).items()}
    tiles = cols // 16

    rows = jnp.concatenate([kernel[0], bn_gain, bn_bias, bias_out], axis=0)
    par = grow(grow(rows.reshape(-1, GROUPS, c // GROUPS), (52, GROUPS, padded(c))).reshape(52, cw), (56, cw))
    bias = grow(grow(bias_in.reshape(GROUPS, -1), (GROUPS, padded(hid))).reshape(1, hw), (8, hw))
    x = inputs.reshape(batches, height, tiles, 16, c)
    cot = cotangent.reshape(batches, height, tiles, 16, c)
    land_cols = -(-cols // 128) * 128
    x14, cot8, land2, par2, bias2 = call(
        "share", functools.partial(share_kernel, sections, dps),
        [((14, tiles, 16, c), BF), ((8, tiles, 16, c), BF), ((2, 8, land_cols), jnp.int32), ((2, 56, cw), F32), ((2, 8, hw), F32)],
        [ANY] * 6, [ANY] * 5, [DMA((k,)) for k in (2, 2, 2, 2, 2, 2, 2, 2, 4, 2)], 1,
    )(x, cot, grow(land, (8, land_cols)), par, bias, jnp.zeros((3, tiles, 16, c), BF))

    def mine(parts, w1, w2, rd, ru):
        return (
            pack_in(w1, parts, c, hid), pack_in(w2, parts, hid, c),
            pack_down(rd, parts, c, n), pack_up(ru, parts, c, n),
        )

    if dps == GROUPS:
        w1, w2, rd, ru = mine(1, *(v.astype(BF) for v in (w_in, w_out, resample, resample)))
        mm = pack_in(merge.astype(BF), 1, c, c)
        shards = [w1[0], w2[0], jnp.where(s == 0, rd, ru)[0], mm[0]]
        full = call(
            "gather", gather_kernel, [((2, 4, 4) + v.shape, BF) for v in shards], [ANY] * 4, [ANY] * 4,
            [DMA((4,)), DMA((4, 4)), DMA((4, 4)), DMA((4,)), DMA((4,)), DMA((4, 2)), DMA((4, 2)), DMA((4, 4)), DMA((4, 4))], 2,
        )(*shards)
        W1, W2, R, M = (v.reshape((2, GROUPS) + v.shape[3:]) for v in full)
        R0, R1 = R[0], R[1]
    else:
        both = ("section", "dp")
        flat = [lax.all_gather(v.astype(BF).reshape(-1), both, axis=0, tiled=True) for v in (w_in, w_out, resample, merge)]
        halves = [v.reshape(2, -1) for v in flat]
        packs = [mine(GROUPS, halves[0][k], halves[1][k], halves[2][k], halves[2][k]) for k in range(2)]
        W1, W2 = (jnp.stack([packs[0][k], packs[1][k]]) for k in range(2))
        R0, R1 = packs[0][2], packs[1][3]
        M = jnp.stack([pack_in(halves[3][k], GROUPS, c, c) for k in range(2)])
    W1, W2, M = W1.reshape(2, cw, hw), W2.reshape(2, hw, cw), M.reshape(2, cw, cw)
    R0 = R0.reshape(4 * cw, nw)
    R1 = R1.reshape(GROUPS, 2, padded(n), 2 * cw)

    wet = land2[:, :height, :cols].reshape(8, cols)
    ocean = jnp.broadcast_to(wet.T.reshape(cells, 1), (cells, 128)).astype(F32)
    shallow = jnp.min(wet.reshape(4, 2, cols // 2, 2), axis=(1, 3))
    coarse = jnp.broadcast_to(shallow.T.reshape(deep_cells, 1), (deep_cells, 128)).astype(F32)
    ocean3 = ocean.reshape(cols, 8, 128)

    field = lambda t: ((cells, cw), t)
    exchange = [pltpu.VMEM((8, cw), F32), pltpu.VMEM((count, 8, cw), F32), DMA((count,)), DMA((count,))]
    shift_space = [pltpu.VMEM((7, cw // 128, cols + 6, 8, 128), F32), pltpu.VMEM((49, 8, cw), F32)]
    conv_out = [((cols, 8, cw), F32)]
    st_out = [((8, cw), F32)]

    def feed_forward(name, z, st, sec, res):
        full = lambda *shape: pl.BlockSpec(shape, lambda i: (0,) * len(shape))
        row = lambda w: pl.BlockSpec((256, w), lambda i: (i, 0))
        return call(
            name, ff_kernel, [field(BF), ((cells, hw), BF), ((cells, hw), BF), field(BF), ((8, tiles, 16, c), BF)],
            [row(cw), full(8, cw), full(56, cw), full(8, hw), full(cw, hw), full(hw, cw), row(cw), row(128), full(128, 128), full(cw, c)],
            [row(cw), row(hw), row(hw), row(cw), pl.BlockSpec((8, 2, 16, c), lambda i: (0, i, 0, 0))], grid=(cells // 256,),
        )(z.reshape(cells, cw), st, par2[sec], bias2[sec], W1[sec], W2[sec], res, ocean, mats["back"], mats["gather"])

    def backward(name, cid, natural_grad, top, z, st, sec, kept):
        nn, gg, gp = kept
        return call(
            name, functools.partial(back_ff_kernel, count, natural_grad),
            [field(F32), ((cw, hw), BF), ((hw, cw), BF), ((8, cw), F32), field(BF), ((2, tiles, 48, cw), BF)],
            scratch=[pltpu.VMEM((cells, cw), F32), pltpu.VMEM((cells, cw), BF), pltpu.VMEM((2, tiles, 48, cw), BF)] + exchange + [DMA((2,)), DMA((2,))],
            cid=cid, limit=60,
        )(top, z.reshape(cells, cw), st, par2[sec], W1[sec], W2[sec], nn, gg, gp, ocean, mats["spread"], mats["turn"], mats["edges"])

    def backward_conv(name, dz, halo, sec, dym, a, with_natural):
        def body(dz, halo, shifts, par, dym, a, back, gather, dh, dk, *rest):
            nat = rest[0] if with_natural else None
            back_conv_kernel(cols, nat, dz, halo, shifts, par, dym, a, back, gather, dh, dk, *rest[1 if with_natural else 0 :])

        return call(
            name, body, [field(BF), ((56, cw), F32)] + ([((8, tiles, 16, c), BF)] if with_natural else []),
            scratch=shift_space + [pltpu.VMEM((49, 8, cw), F32)],
        )(dz, halo, mats["shifts"], par2[sec], dym, a, mats["back"], mats["gather"])

    z0, a0, st0 = call(
        "enc_conv", functools.partial(enc_conv_kernel, count, cols), conv_out + [field(BF)] + st_out,
        scratch=shift_space + exchange, cid=3,
    )(x14, mats["spread"], mats["natural"], par2[0], ocean3)
    *kept0, skip, nat_act0 = feed_forward("enc_ff", z0, st0, 0, a0)
    pieces, deep, up, h, a1, halo1 = call(
        "mid", functools.partial(mid_kernel, count),
        [((4, deep_cells, cw), BF), ((deep_cells, nw), BF), field(BF), field(F32), field(BF), ((2, tiles, 48, cw), BF)],
        scratch=[pltpu.VMEM((2, tiles, 48, cw), BF), DMA((2,)), DMA((2,))], cid=4,
    )(skip, R0, R1, M, coarse, mats["patch"], mats["unpatch"], mats["edges"])
    z1, st1 = call(
        "dec_conv", functools.partial(dec_conv_kernel, count, cols), conv_out + st_out, scratch=shift_space + exchange, cid=5,
    )(a1, halo1, mats["shifts"], par2[1], ocean3)
    *kept1, _, nat_act1 = feed_forward("dec_ff", z1, st1, 1, h)

    dym1, dw1_1, dw2_1, small1, dz1, dhalo1 = backward("dec_back", 6, True, cot8, z1, st1, 1, kept1)
    dh1, dk1 = backward_conv("dec_back_conv", dz1, dhalo1, 1, dym1, a1, False)
    dm, dr1, dr0, dy0, nat_g1 = call(
        "back_mid", back_mid_kernel,
        [((2, cw, cw), BF), ((GROUPS, 2, padded(n), 2 * cw), BF), ((4 * cw, nw), BF), field(F32), ((8, tiles, 16, c), BF)],
        scratch=[pltpu.VMEM((cells, cw), BF), pltpu.VMEM((2, deep_cells, 2 * cw), BF), pltpu.VMEM((4, deep_cells, cw), F32)], limit=60,
    )(dh1, up, skip, deep, pieces, R0, R1, M, coarse, mats["patch"], mats["unpatch"], mats["back"], mats["gather"])
    dym0, dw1_0, dw2_0, small0, dz0, dhalo0 = backward("enc_back", 7, False, dy0, z0, st0, 0, kept0)
    _, dk0, nat_g0 = backward_conv("enc_back_conv", dz0, dhalo0, 0, dym0, a0, True)

    act, gi = call(
        "deliver", functools.partial(deliver_kernel, dps), [((4, 4, tiles, 16, c), BF)] * 2, [ANY] * 4, [ANY] * 2,
        [DMA((2, 2, 2)), DMA((2, 4))], 8,
    )(nat_act0, nat_act1, nat_g0, nat_g1)
    activations = act.reshape(1, batches, height, cols, c)
    grad_input = gi.astype(F32).reshape(1, batches, height, cols, c)
    tiny = jnp.stack([jnp.concatenate([dk, small], axis=0) for dk, small in ((dk0, small0), (dk1, small1))])
    shapes = [(padded(c), hw), (padded(hid), cw), (4 * padded(c), nw), (padded(c), cw)]
    if dps == GROUPS:
        view = lambda v, shape: v.reshape((4, 4) + shape)
        grids = lambda dw1, dw2, dr: [view(v, shape) for v, shape in zip((dw1, dw2, dr), shapes)]
        banks = [[pltpu.VMEM(lead + shape, BF) for shape in shapes] for lead in ((4, 4), (4, 4), (4, 2), (4,), (3,))]
        g1, g2, gr, gm, tiny = call(
            "reduce", reduce_kernel, [(shape, F32) for shape in shapes] + [((64, cw), F32)], [ANY] * 7 + [VM], None,
            sum(banks, []) + [pltpu.VMEM((9, 64, cw), F32)]
            + [DMA((4,)), DMA((4,)), DMA((4,)), DMA((4, 2)), DMA((4, 2)), DMA((4,)), DMA((4,)), DMA((4, 4)), DMA((4, 4)), DMA((7,)), DMA((7,))],
            9, 60,
        )(*grids(dw1_0, dw2_0, dr0), *grids(dw1_1, dw2_1, dr1), dm.reshape((2, 4, 4) + shapes[3]), tiny)
        gw1, gw2, gmm = unpack_in(g1, c, hid), unpack_in(g2, hid, c), unpack_in(gm, c, c)
        gres = jnp.where(s == 0, unpack_down(gr, c, n), unpack_up(gr, c, n))
    else:
        both = ("section", "dp")
        scatter = lambda v: lax.psum_scatter(v.astype(F32).reshape(-1), both, scatter_dimension=0, tiled=True)
        gw1 = scatter(jnp.stack([unpack_in(v, c, hid) for v in (dw1_0, dw1_1)]))
        gw2 = scatter(jnp.stack([unpack_in(v, hid, c) for v in (dw2_0, dw2_1)]))
        gres = scatter(jnp.stack([unpack_down(dr0, c, n), unpack_up(dr1, c, n)]))
        gmm = scatter(jnp.stack([unpack_in(dm[k], c, c) for k in range(2)]))
        tiny = lax.psum(tiny, both)[s]
    narrow = lambda v: v.reshape(-1, GROUPS, padded(c))[:, :, : c // GROUPS].reshape(-1, c)
    fine = narrow(tiny[:59])
    grad_bias_in = tiny[59:63].reshape(-1)[:hw].reshape(GROUPS, -1)[:, : hid // GROUPS].reshape(1, hid)
    return (
        activations, grad_input, fine[None, :49], fine[57:58], fine[56:57], grad_bias_in, fine[58:59],
        gw1[None], gw2[None], gres[None], gmm,
    )


def solution(mesh):
    sections, dps = mesh.shape["section"], mesh.shape["dp"]
    flat, both = P("section", "dp"), P(("section", "dp"))
    per = P("section", None)
    rows = P(None, "dp", None, None)
    taps = P("section", None, None)
    fields = P("section", None, "dp", None, None)
    return jax.shard_map(
        functools.partial(on_device, sections, dps), mesh=mesh,
        in_specs=(rows, rows, P("dp", None), taps, per, per, per, per, flat, flat, flat, both),
        out_specs=(fields, fields, taps, per, per, per, per, flat, flat, flat, both), check_vma=False,
    )
```

```python
import functools

import jax
import jax.numpy as jnp
import ml_dtypes
import numpy as np
from jax import lax
from jax.experimental import pallas as pl
from jax.experimental.pallas import tpu as pltpu
from jax.sharding import PartitionSpec as P

BF = jnp.bfloat16
F32 = jnp.float32
MESH = pl.DeviceIdType.MESH
ANY = pl.BlockSpec(memory_space=pl.ANY)
VM = pl.BlockSpec(memory_space=pltpu.VMEM)
DMA = pltpu.SemaphoreType.DMA
EPS = 1e-05
GROUPS = 16
MEGA = 1 << 20


def padded(width):
    return -(-(width // GROUPS) // 16) * 16


def selector(rows, cols, pairs):
    out = np.zeros((rows, cols), np.float32)
    for r, c in pairs:
        out[r, c] = 1
    return out.astype(ml_dtypes.bfloat16)


def matrices(channels):
    group, wide = channels // GROUPS, padded(channels)
    spread = selector(channels, GROUPS * wide, [(c, c // group * wide + c % group) for c in range(channels)])
    natural = selector(896, 224, [(i * 128 + q * 8 + p, (p + i) * 16 + q) for i in range(7) for q in range(16) for p in range(8)])

    def place(q, row):
        if row < 0:
            return 128 + q * 3 + row + 3
        return q * 8 + row if row < 8 else 176 + q * 3 + row - 8

    shifts = selector(896, 224, [(i * 128 + q * 8 + p, place(q, p + i - 3)) for i in range(7) for q in range(16) for p in range(8)])
    turn = selector(128, 128, [(q * 8 + p, p * 16 + q) for q in range(16) for p in range(8)])
    edges = selector(96, 128, [(48 * e + q * 3 + k, q * 8 + 5 * e + k) for e in range(2) for q in range(16) for k in range(3)])
    patch = selector(
        256, 256,
        [((i * 2 + j) * 64 + b * 4 + a, (2 * b + j) * 8 + 2 * a + i) for i in range(2) for j in range(2) for b in range(16) for a in range(4)],
    )
    pick = selector(128, 16, [(q * 8 + p, p // 4 * 8 + p % 4) for q in range(16) for p in range(8)])
    return dict(
        pick=pick, spread=spread, gather=np.ascontiguousarray(spread.T), natural=natural, shifts=shifts, turn=turn,
        back=np.ascontiguousarray(turn.T), edges=edges, patch=patch, unpatch=np.ascontiguousarray(patch.T),
    )


def grow(value, sizes):
    return jnp.pad(value, [(0, n - o) for n, o in zip(sizes, value.shape)])


def pack_in(value, parts, c, h):
    value = value.reshape(parts, c // GROUPS, GROUPS, h // GROUPS)
    return grow(value, (parts, padded(c), GROUPS, padded(h))).reshape(parts, padded(c), -1)


def pack_down(value, parts, c, n):
    value = value.reshape(parts, 4, c // GROUPS, GROUPS, n // GROUPS)
    return grow(value, (parts, 4, padded(c), GROUPS, padded(n))).reshape(parts, 4 * padded(c), -1)


def pack_up(value, parts, c, n):
    value = value.reshape(parts, n // GROUPS, 2, 2 * GROUPS, c // GROUPS)
    value = grow(value, (parts, padded(n), 2, 2 * GROUPS, padded(c)))
    return value.transpose(0, 2, 1, 3, 4).reshape(parts, 2 * padded(n), -1)


def unpack_in(value, c, h):
    value = value.reshape(-1, padded(c), GROUPS, padded(h))
    return value[:, : c // GROUPS, :, : h // GROUPS].reshape(-1)


def unpack_down(value, c, n):
    value = value.reshape(-1, 4, padded(c), GROUPS, padded(n))
    return value[:, :, : c // GROUPS, :, : n // GROUPS].reshape(-1)


def unpack_up(value, c, n):
    value = value.reshape(-1, 2, padded(n), 2 * GROUPS, padded(c))
    return value.transpose(0, 2, 1, 3, 4)[:, : n // GROUPS, :, :, : c // GROUPS].reshape(-1)


def device(p, m):
    g = p // 2
    return (p + g) % 2, 4 * g + m


def where_am_i():
    s, d = lax.axis_index("section"), lax.axis_index("dp")
    g = d // 4
    return s, d, g, d % 4, 2 * g + (s + g) % 2


def greet_near(count):
    s, d, g, m, p = where_am_i()
    barrier = pltpu.get_barrier_semaphore()

    def one(k, carry):
        q = (p + k) % count
        pl.semaphore_signal(barrier, inc=1, device_id=device(q, m), device_id_type=MESH)
        return carry

    lax.fori_loop(1, count, one, 0)
    for k in range(1, 4):
        for sec in range(2):
            pl.semaphore_signal(barrier, inc=1, device_id=(sec, 4 * g + (m + k) % 4), device_id_type=MESH)
    pl.semaphore_wait(barrier, count + 5)


def remote(src, dst, send, recv, peer):
    return pltpu.make_async_remote_copy(src_ref=src, dst_ref=dst, send_sem=send, recv_sem=recv, device_id=peer, device_id_type=MESH)


def arrived(ref, sem):
    pltpu.make_async_copy(ref, ref, sem).wait()


def all_sum(mine, slots, send, recv, count):
    s, d, g, m, p = where_am_i()
    groups = count // 2
    over = remote(mine, slots.at[groups], send.at[0], recv.at[0], (1 - s, d))
    over.start()
    arrived(slots.at[groups], recv.at[0])
    slots[g] = mine[...] + slots[groups]
    over.wait_send()

    def copy(k):
        return remote(slots.at[g], slots.at[g], send.at[k], recv.at[k], (s, 4 * ((g + k) % groups) + m))

    lax.fori_loop(1, groups, lambda k, c: (copy(k).start(), c)[1], 0)

    def wait(k, carry):
        arrived(slots.at[(g + groups - k) % groups], recv.at[k])
        copy(k).wait_send()
        return carry

    lax.fori_loop(1, groups, wait, 0)
    return lax.fori_loop(0, groups, lambda k, total: total + slots[k], jnp.zeros(mine.shape, F32))


def swap_rows(packed, halo, send, recv, count):
    s, d, g, m, p = where_am_i()

    def peer(q):
        return device(q, m)

    @pl.when(p > 0)
    def _():
        remote(packed.at[0], halo.at[1], send.at[0], recv.at[1], peer(p - 1)).start()

    @pl.when(p < count - 1)
    def _():
        remote(packed.at[1], halo.at[0], send.at[1], recv.at[0], peer(p + 1)).start()

    @pl.when(p > 0)
    def _():
        arrived(halo.at[0], recv.at[0])
        remote(packed.at[0], halo.at[1], send.at[0], recv.at[1], peer(p - 1)).wait_send()

    @pl.when(p < count - 1)
    def _():
        arrived(halo.at[1], recv.at[1])
        remote(packed.at[1], halo.at[0], send.at[1], recv.at[0], peer(p + 1)).wait_send()

    @pl.when(p == 0)
    def _():
        halo[0] = jnp.zeros(halo.shape[1:], BF)

    @pl.when(p == count - 1)
    def _():
        halo[1] = jnp.zeros(halo.shape[1:], BF)


def dot(a, b):
    return jnp.dot(a, b, preferred_element_type=F32)


def dot_nt(a, b):
    return lax.dot_general(a, b, (((1,), (1,)), ((), ())), preferred_element_type=F32)


def dot_tn(a, b):
    return lax.dot_general(a, b, (((0,), (0,)), ((), ())), preferred_element_type=F32)


def lanes4(mask, width):
    return jnp.concatenate([mask] * (width // 128), axis=1)


def rows8(value):
    return value.reshape(-1, 8, value.shape[-1]).sum(0)


def to_natural(cells, back, gather):
    turned = dot(dot(back, cells).astype(BF), gather).astype(BF)
    return turned.reshape(8, 16, turned.shape[-1])


def shifted(chunk, perm, S, c):
    moved = dot(perm, chunk)
    for lane in range(S.shape[1]):
        S[:, lane, pl.ds(3 + 16 * c, 16)] = moved[:, lane * 128 : lane * 128 + 128].reshape(7, 16, 8, 128)
    return moved


def wrap(S, cols):
    S[:, :, 0:3] = S[:, :, cols : cols + 3]
    S[:, :, cols + 3 : cols + 6] = S[:, :, 3:6]


def taps_to(kb, par, flip):
    for k in range(49):
        kb[k] = jnp.broadcast_to(par[(48 - k if flip else k) : (48 - k if flip else k) + 1], kb.shape[1:])


def norm_terms(st, par):
    counted = st[2:3]
    mean = st[0:1] / counted
    inverse = lax.rsqrt(st[1:2] / counted - mean * mean + EPS)
    return counted, mean, inverse, par[49:50], par[50:51]


def back_ff_kernel(sec, count, ns, hook):
    greet_near(count)
    hook(0)
    z, w1, w2, dn, dr, small, ocean, edges = ns.z, ns.w1, ns.w2, ns.dn, ns.dr, ns.small, ns.ocean, ns.edges
    wide = z.shape[1]
    chunks = z.shape[0] // 128
    counted, mean, inverse, gain, shift = norm_terms(ns.st, ns.par[sec])

    def begin(c, total):
        at = pl.ds(pl.multiple_of(c * 128, 128), 128)
        if sec == 1:
            block = ns.top[:, c]
            block = dot(block.reshape(-1, block.shape[-1]), ns.spread[...]).astype(BF)
            grad = dot(ns.turn[...], block)
        else:
            grad = ns.top[at]
        grad = grad * lanes4(ocean[at], wide)
        ns.dym[at] = grad
        low = grad.astype(BF)
        dr[at] = low
        return total + rows8(low.astype(F32))

    total = lax.fori_loop(0, chunks, begin, jnp.zeros((8, wide), F32))
    small[2:3] = total.sum(0, keepdims=True)
    small[3:8] = jnp.zeros((5, wide), F32)
    for h in range(0, w1.shape[1], 256):
        at = slice(h, h + 256)
        dg = dot_nt(dr[...], w2[at])
        de = (dg * ns.gp[:, at].astype(F32)).astype(BF)
        row, col = 3 + h // wide, h % wide
        small[row : row + 1, col : col + 256] = de.astype(F32).sum(0, keepdims=True)
        ns.dw1[:, at] = dot_tn(ns.n[...], de).astype(BF)
        ns.dw2[at] = dot_tn(ns.g[:, at], dr[...]).astype(BF)
        part = dot_nt(de, w1[:, at])
        if h == 0:
            dn[...] = part
        else:
            dn[...] += part
        if h == 512:
            hook(1)

    def sums(c, carry):
        at = pl.ds(pl.multiple_of(c * 128, 128), 128)
        grad = dn[at]
        return carry[0] + rows8(grad), carry[1] + rows8(grad * ((z[at] - mean) * inverse))

    zero = jnp.zeros((8, wide), F32)
    plain, scaled = lax.fori_loop(0, chunks, sums, (zero, zero))
    small[0:1] = plain.sum(0, keepdims=True)
    small[1:2] = scaled.sum(0, keepdims=True)
    ns.stats[...] = small[...]
    summed = all_sum(ns.stats, ns.slots, ns.send, ns.recv, count)
    first = -inverse * gain * summed[0:1] / counted
    second = -inverse * inverse * gain * summed[1:2] / counted
    hook(2)

    def end(c, carry):
        at = pl.ds(pl.multiple_of(c * 128, 128), 128)
        grad = inverse * gain * dn[at] + lanes4(ocean[at], wide) * (first + second * (z[at] - mean))
        low = grad.astype(BF)
        ns.dz[at] = low
        ends = dot(edges[...], low).astype(BF)
        ns.packed[0, c] = ends[:48]
        ns.packed[1, c] = ends[48:]
        return carry

    lax.fori_loop(0, chunks, end, 0)
    swap_rows(ns.packed, ns.halo, ns.hsend, ns.hrecv, count)
    hook(3)


def back_conv_kernel(sec, count, cols, ns, hook):
    greet_near(count)
    hook(0)
    taps_to(ns.kb, ns.par[sec], True)
    wide = ns.dz.shape[1]
    S, kb, acc_dk = ns.S, ns.kb, ns.acc_dk

    def chunk(c, carry):
        block = jnp.concatenate([ns.dz[pl.ds(pl.multiple_of(c * 128, 128), 128)], ns.halo[0, c], ns.halo[1, c]], axis=0)
        shifted(block, ns.perm[...], S, c)
        return carry

    lax.fori_loop(0, cols // 16, chunk, 0)
    wrap(S, cols)
    acc_dk[...] = jnp.zeros(acc_dk.shape, F32)
    for lane in range(wide // 128):
        at = slice(lane * 128, lane * 128 + 128)

        def step(b, carry):
            cells = pl.ds(pl.multiple_of(b * 64, 64), 64)
            acc = ns.dym[cells, at].reshape(8, 8, 128)
            field = ns.a[cells, at].astype(F32).reshape(8, 8, 128)
            for i in range(7):
                window = S[i, lane, pl.ds(b * 8, 14)]
                for j in range(7):
                    acc = acc + window[j : j + 8] * kb[7 * i + j, :, at][None]
                    acc_dk[7 * i + j, :, at] += (window[j : j + 8] * field).sum(0)
            ns.dh[cells, at] = acc.reshape(64, 128).astype(BF)
            return carry

        lax.fori_loop(0, cols // 8, step, 0)
        if lane in (1, 2):
            hook(lane)
    for k in range(49):
        ns.dk[48 - k : 49 - k] = acc_dk[k].sum(0, keepdims=True)
    ns.dk[49:56] = jnp.zeros((7, wide), F32)
    if sec == 0:

        def out(c, carry):
            cells = ns.dh[pl.ds(pl.multiple_of(c * 128, 128), 128)]
            ns.nat[:, c] = to_natural(cells, ns.back[...], ns.gather[...])
            return carry

        lax.fori_loop(0, cols // 16, out, 0)
    hook(3)


def back_mid_kernel(count, ns, hook):
    greet_near(count)
    hook(0)
    dh, up, skip, deep, pieces, down, up_w, merge = ns.dh, ns.up, ns.skip, ns.deep, ns.pieces, ns.down, ns.up_w, ns.merge
    dskip, dups, spreads = ns.dskip, ns.dups, ns.spreads
    wide = dh.shape[1]
    blocks = dh.shape[0] // 256
    ns.dmerge[0] = dot_tn(up[...], dh[...]).astype(BF)
    ns.dmerge[1] = dot_tn(skip[...], dh[...]).astype(BF)
    for b in range(blocks):
        at = slice(256 * b, 256 * b + 256)
        low = dot_nt(dh[at], merge[1]).astype(BF)
        dskip[at] = low
        for k in range(2):
            ns.nat[:, 2 * b + k] = to_natural(low[128 * k : 128 * k + 128], ns.back[...], ns.gather[...])
        lifted = dot_nt(dh[at], merge[0]).astype(BF)
        moved = dot(ns.patch[...], lifted).astype(BF)
        for k in range(4):
            dups[k // 2, 64 * b : 64 * b + 64, wide * (k % 2) : wide * (k % 2) + wide] = moved[64 * k : 64 * k + 64]
    hook(1)
    rows = up_w.shape[0] * up_w.shape[2]
    ddeep = dot_nt(dups[0], up_w[:, 0].reshape(rows, -1)) + dot_nt(dups[1], up_w[:, 1].reshape(rows, -1))
    for i in range(2):
        grad = dot_tn(deep[...], dups[i]).astype(BF)
        ns.dup_w[:, i] = grad.reshape(up_w.shape[0], up_w.shape[2], -1)
    masked = (lanes4(ns.coarse[...], ddeep.shape[1]) * ddeep).astype(BF)
    hook(2)
    for k in range(4):
        ns.ddown[wide * k : wide * k + wide] = dot_tn(pieces[k], masked).astype(BF)
        spreads[k] = dot_nt(masked, down[wide * k : wide * k + wide])
    for b in range(blocks):
        value = jnp.concatenate([spreads[k, 64 * b : 64 * b + 64] for k in range(4)], axis=0)
        high = value.astype(BF)
        rest = (value - high.astype(F32)).astype(BF)
        at = slice(256 * b, 256 * b + 256)
        ns.dy[at] = dskip[at].astype(F32) + (dot(ns.unpatch[...], high) + dot(ns.unpatch[...], rest))
    hook(3)


class Job:
    def __init__(self, name):
        self.name, self.ins, self.outs, self.scratch, self.alias = name, {}, {}, {}, {}

    def add(self, kind, name, value):
        getattr(self, kind)[self.name + name] = value

    def ref(self, ns, name):
        return getattr(ns, self.name + name)

    def steps(self, ns):
        return [lambda: None] * 4


def start_either(self, src, dst, send, recv, peer):
    pl.when(jnp.logical_not(self))(lambda: remote(src, dst, send, recv, peer).start())
    pl.when(self)(lambda: pltpu.make_async_copy(src, dst, recv).start())


class Deliver(Job):
    def __init__(self, name, sec, natural, before=None):
        super().__init__(name)
        self.sec = sec
        rows, tiles, q, c = natural.shape
        self.add("ins", "nat", (natural, ANY))
        self.add("outs", "out", ((4, 4, tiles, q, c), BF, ANY))
        self.add("outs", "bounce", ((rows, tiles, q, c), BF, ANY))
        self.add("scratch", "s", DMA((2, 2)))
        self.add("scratch", "r", DMA((4,)))
        self.add("scratch", "b", DMA((2,)))
        if before is not None:
            self.add("ins", "before", (before, ANY))
            self.alias = {name + "before": name + "out"}

    def steps(self, ns):
        return deliver(self.sec, *(self.ref(ns, k) for k in ("nat", "out", "bounce", "s", "r", "b")))


def deliver(sec, nat, out, bounce, send, recv, b):
    s, d, g, m, p = where_am_i()

    def target(which, j):
        dp = 4 * g + 2 * ((p + which) % 2) + j
        part = (nat, bounce)[which].at[pl.ds(4 * j, 4)]
        return dp == d, part, out.at[m], send.at[which, j], recv.at[m], (s, dp)

    def over():
        return remote(nat, bounce, b.at[0], b.at[1], (1 - s, d))

    def sends(which):
        for j in range(2):
            start_either(*target(which, j))

    def begin():
        pl.when(s != sec)(lambda: over().start())
        pl.when(s == sec)(lambda: sends(0))

    def middle():
        @pl.when(s == sec)
        def _():
            arrived(bounce, b.at[1])
            sends(1)

    def end():
        @pl.when(s == sec)
        def _():
            for mb in range(4):
                arrived(out.at[mb], recv.at[mb])
            for which in range(2):
                for j in range(2):
                    self_, *rest = target(which, j)
                    pl.when(jnp.logical_not(self_))(lambda rest=rest: remote(*rest).wait_send())

        pl.when(s != sec)(lambda: over().wait_send())

    return [begin, middle, lambda: None, end]


def collect(field, out, first, send, recv):
    s, d, g, m, p = where_am_i()
    core, dp = device(d // 2, 0)
    j = d % 2

    def parts(step):
        mb = (m + step) % 4
        return field.at[mb], out.at[pl.ds(first + 4 * j, 4)], send.at[step], recv.at[j], (s, dp + mb)

    def begin():
        @pl.when(s == core)
        def _():
            for step in range(1, 4):
                remote(*parts(step)).start()
            src, dst, _, sem, _ = parts(0)
            pltpu.make_async_copy(src, dst, sem).start()

    def end():
        for jj in range(2):
            arrived(out.at[pl.ds(first + 4 * jj, 4)], recv.at[jj])

        @pl.when(s == core)
        def _():
            for step in range(1, 4):
                remote(*parts(step)).wait_send()

    return begin, end


def half(ref, c):
    rows, lanes = ref.shape[-2:]
    lead = (slice(None),) * (len(ref.shape) - 2)
    if rows % 32 == 0:
        return ref.at[lead + (pl.ds(pl.multiple_of(c * (rows // 2), 16), rows // 2),)]
    return ref.at[lead + (slice(None), pl.ds(pl.multiple_of(c * (lanes // 2), 128), lanes // 2))]


def half_shape(shape):
    rows, lanes = shape[-2:]
    return shape[:-2] + ((rows // 2, lanes) if rows % 32 == 0 else (rows, lanes // 2))


class PlaneSum(Job):
    def __init__(self, name, parts):
        super().__init__(name)
        self.parts, n = parts, len(parts)
        for k, v in enumerate(parts):
            array = v[0] if isinstance(v, tuple) else v
            self.add("ins", f"in{k}", (array, ANY))
            shape = half_shape(array.shape[-2:])
            for bank, lead in (("own", (4, 4)), ("core", (4, 4)), ("one", (4, 2)), ("two", (4,))):
                self.add("scratch", f"{bank}{k}", pltpu.VMEM(lead + shape, BF))
            self.add("outs", f"out{k}", ((4,) + shape, BF, VM))
        for k, width in (("l", 1), ("cs", 1), ("cr", 1), ("as", 2), ("ar", 2), ("bs", 1), ("br", 1)):
            self.add("scratch", k, DMA((n, width)))

    def steps(self, ns):
        s, d, g, m, p = where_am_i()
        sem = {k: self.ref(ns, k) for k in ("l", "cs", "cr", "as", "ar", "bs", "br")}
        bank = lambda kind, k: self.ref(ns, f"{kind}{k}")
        bit, every = 1 + s, range(len(self.parts))

        def source(k, c):
            v, ref = self.parts[k], self.ref(ns, f"in{k}")
            return half(ref.at[v[1]] if isinstance(v, tuple) else ref, c)

        def near(k):
            return pltpu.make_async_copy(source(k, s), bank("own", k), sem["l"].at[k, 0])

        def over(k):
            return remote(source(k, 1 - s), bank("core", k), sem["cs"].at[k, 0], sem["cr"].at[k, 0], (1 - s, d))

        def first(k, index):
            col = (m ^ bit, m ^ 3)[index]
            return remote(bank("own", k).at[:, col], bank("one", k).at[:, index], sem["as"].at[k, index], sem["ar"].at[k, index], (s, d ^ bit))

        def second(k):
            return remote(bank("own", k).at[:, m ^ (3 - bit)], bank("two", k), sem["bs"].at[k, 0], sem["br"].at[k, 0], (s, d ^ (3 - bit)))

        def h0():
            for k in every:
                over(k).start()
                near(k).start()

        def h1():
            for k in every:
                own, core = bank("own", k), bank("core", k)
                near(k).wait()
                arrived(core, sem["cr"].at[k, 0])

                def add(b, carry, own=own, core=core):
                    own[b // 4, b % 4] = (own[b // 4, b % 4].astype(F32) + core[b // 4, b % 4].astype(F32)).astype(BF)
                    return carry

                lax.fori_loop(0, 16, add, 0)
                first(k, 1).start()
                first(k, 0).start()

        def h2():
            for k in every:
                own, one, rest = bank("own", k), bank("one", k), m ^ (3 - bit)
                arrived(one.at[:, 1], sem["ar"].at[k, 1])
                for z in range(4):
                    own[z, rest] = (own[z, rest].astype(F32) + one[z, 1].astype(F32)).astype(BF)
                second(k).start()

        def h3():
            for k in every:
                own, one, two, out = (bank(n, k) for n in ("own", "one", "two", "out"))
                arrived(one.at[:, 0], sem["ar"].at[k, 0])
                arrived(two, sem["br"].at[k, 0])
                for z in range(4):
                    out[z] = (own[z, m].astype(F32) + one[z, 0].astype(F32) + two[z].astype(F32)).astype(BF)
                first(k, 0).wait_send()
                first(k, 1).wait_send()
                second(k).wait_send()
                over(k).wait_send()

        return [h0, h1, h2, h3]


class LineSum(Job):
    def __init__(self, name, columns):
        super().__init__(name)
        self.secs = [sec for _, sec in columns]
        n = len(columns)
        for k, (v, _) in enumerate(columns):
            self.add("ins", f"in{k}", (v, ANY))
            self.add("outs", f"out{k}", ((2,) + v.shape[1:], F32, VM))
            self.add("scratch", f"line{k}", pltpu.VMEM(v.shape, BF))
            self.add("scratch", f"mine{k}", pltpu.VMEM(v.shape[1:], F32))
        for k, width in (("s", 4), ("r", 4), ("c", 2)):
            self.add("scratch", k, DMA((n, width)))

    def steps(self, ns):
        s, d, g, m, p = where_am_i()
        send, recv, sem = self.ref(ns, "s"), self.ref(ns, "r"), self.ref(ns, "c")
        every = list(enumerate(self.secs))

        def near(k):
            return pltpu.make_async_copy(self.ref(ns, f"in{k}").at[g], self.ref(ns, f"line{k}").at[0], send.at[k, 0])

        def far(k, step):
            to = (g + step) % 4
            return remote(self.ref(ns, f"in{k}").at[to], self.ref(ns, f"line{k}").at[step], send.at[k, step], recv.at[k, step], (s, 4 * to + m))

        def give(k):
            return remote(self.ref(ns, f"mine{k}"), self.ref(ns, f"out{k}").at[s], sem.at[k, 0], sem.at[k, 1], (1 - s, d))

        def begin():
            for k, _ in every:
                near(k).start()
                for step in range(1, 4):
                    far(k, step).start()

        def end():
            for k, sec in every:
                line, mine, out = (self.ref(ns, f"{n}{k}") for n in ("line", "mine", "out"))
                near(k).wait()
                for step in range(1, 4):
                    arrived(line.at[step], recv.at[k, step])
                    far(k, step).wait_send()
                mine[...] = sum(line[z].astype(F32) for z in range(4))
                pl.when(s != sec)(give(k).start)

                @pl.when(s == sec)
                def _(out=out, mine=mine):
                    out[s] = mine[...]

            for k, sec in every:
                pl.when(s != sec)(give(k).wait_send)
                pl.when(s == sec)(lambda k=k: arrived(self.ref(ns, f"out{k}").at[1 - s], sem.at[k, 1]))

        return [begin, lambda: None, lambda: None, end]


def collect_land(land, out, send, recv):
    s, d, g, m, p = where_am_i()
    core, dp = device(d // 2, 0)

    def part(step):
        return remote(land, out.at[d % 2], send.at[step], recv.at[d % 2], (s, dp + (m + step) % 4))

    def begin():
        @pl.when(s == core)
        def _():
            for step in range(1, 4):
                part(step).start()
            pltpu.make_async_copy(land, out.at[d % 2], recv.at[d % 2]).start()

    def end():
        for jj in range(2):
            arrived(out.at[jj], recv.at[jj])

        @pl.when(s == core)
        def _():
            for step in range(1, 4):
                part(step).wait_send()

    return begin, end


def last_kernel(count, ns, hook):
    s, d, g, m, p = where_am_i()
    greet_near(count)
    hook(0)
    tiny, small, ts, tr = ns.tiny, ns.small, ns.ts, ns.tr
    over = remote(small.at[1 - s], tiny.at[0], ts.at[0], tr.at[0], (1 - s, d))
    over.start()
    arrived(tiny.at[0], tr.at[0])
    over.wait_send()
    tiny[1] = small[s] + tiny[0]
    for base, peer in ((1, lambda step: (s, 4 * ((g + step) % 4) + m)), (5, lambda step: (s, d ^ step))):
        sent = [remote(tiny.at[base], tiny.at[base + step], ts.at[base + step], tr.at[base + step], peer(step)) for step in range(1, 4)]
        for c in sent:
            c.start()
        for step in range(1, 4):
            arrived(tiny.at[base + step], tr.at[base + step])
        for c in sent:
            c.wait_send()
        total = tiny[base] + tiny[base + 1] + tiny[base + 2] + tiny[base + 3]
        if base == 1:
            tiny[5] = total
        else:
            ns.total[...] = total
    hook(1)
    hook(2)
    hook(3)


class Gather:
    def __init__(self, shard, full, send, recv):
        self.shard, self.full, self.send, self.recv = shard, full, send, recv
        self.s, self.d, self.g, self.m, _ = where_am_i()
        self.bit = 1 + self.s

    def block(self, col, c):
        return half(self.full.at[:, col], c)

    def near(self):
        return pltpu.make_async_copy(half(self.shard, self.s), half(self.full.at[self.g, self.m], self.s), self.send.at[0])

    def line(self, step):
        src, dst = half(self.shard, self.s), half(self.full.at[self.g, self.m], self.s)
        return remote(src, dst, self.send.at[step], self.recv.at[step], (self.s, 4 * ((self.g + step) % 4) + self.m))

    def column(self, slot, col, peer):
        block = self.block(col, self.s)
        return remote(block, block, self.send.at[slot], self.recv.at[slot], peer)

    def first(self):
        return self.column(4, self.m, (self.s, self.d ^ self.bit))

    def second(self, index):
        return self.column(5 + index, (self.m, self.m ^ self.bit)[index], (self.s, self.d ^ (3 - self.bit)))

    def cols(self, way):
        return (self.m, self.m ^ way, self.m ^ (3 - way), self.m ^ 3)

    def hand(self, index):
        return self.column(7 + index, self.cols(self.bit)[index], (1 - self.s, self.d))

    def start(self):
        self.near().start()
        for step in range(1, 4):
            self.line(step).start()

    def plane(self):
        self.near().wait()
        for step in range(1, 4):
            arrived(half(self.full.at[(self.g + 4 - step) % 4, self.m], self.s), self.recv.at[step])
        self.first().start()
        self.second(0).start()
        self.hand(0).start()

    def onward(self):
        arrived(self.block(self.m ^ self.bit, self.s), self.recv.at[4])
        self.second(1).start()
        self.hand(1).start()

    def over(self):
        for index in range(2):
            arrived(self.block((self.m ^ (3 - self.bit), self.m ^ 3)[index], self.s), self.recv.at[5 + index])
            self.hand(2 + index).start()

    def whole(self):
        for index, col in enumerate(self.cols(3 - self.bit)):
            arrived(self.block(col, 1 - self.s), self.recv.at[7 + index])

    def finish(self):
        for step in range(1, 4):
            self.line(step).wait_send()
        self.first().wait_send()
        for index in range(2):
            self.second(index).wait_send()
        for index in range(4):
            self.hand(index).wait_send()


class Load:
    def __init__(self, src, full, sem):
        self.copy = lambda: pltpu.make_async_copy(src, full, sem.at[0])

    def start(self):
        self.copy().start()

    def whole(self):
        self.copy().wait()

    def plane(self):
        pass

    onward = over = finish = plane


def masks(land, ocean, coarse, pick, patch):
    rows, across = land.shape[0] * land.shape[1], land.shape[2]
    flat = land[...].reshape(rows, across).astype(F32).astype(BF)
    spread = dot(pick, flat)
    at = lax.broadcasted_iota(jnp.int32, spread.shape, 1) - lax.broadcasted_iota(jnp.int32, spread.shape, 0) // 8
    ones = jnp.ones((across, 128), BF)

    def chunk(c, carry):
        ocean[pl.ds(pl.multiple_of(c * 128, 128), 128)] = dot(jnp.where(at == 16 * c, spread, 0.0).astype(BF), ones)
        return carry

    lax.fori_loop(0, ocean.shape[0] // 128, chunk, 0)
    for b in range(ocean.shape[0] // 256):
        moved = dot(patch, ocean[256 * b : 256 * b + 256].astype(BF))
        coarse[64 * b : 64 * b + 64] = moved[:64] * moved[64:128] * moved[128:192] * moved[192:]


def conv_phase(sec, cols, ns, hook):
    S, kb, ocean, z, stats = ns.S, ns.kb, ns.ocean, ns.z, ns.stats
    taps_to(kb, ns.par[sec], False)
    lanes = S.shape[1]
    wide = kb.shape[2]

    def count_cells(b, t):
        return t + ocean[pl.ds(pl.multiple_of(b * 64, 64), 64)].reshape(8, 8, 128).sum(0)

    tally = lax.fori_loop(0, cols // 8, count_cells, jnp.zeros((8, 128), F32))
    for group in range(wide // 128 // lanes):
        part = slice(group * lanes * 128, (group + 1) * lanes * 128)

        def chunk(c, carry):
            cells = pl.ds(pl.multiple_of(c * 128, 128), 128)
            if sec == 0:
                block = ns.x14[:, c]
                block = dot(block.reshape(-1, block.shape[-1]), ns.spread[:, part]).astype(BF)
                moved = shifted(block, ns.natural[...], S, c)
                ns.a0[cells, part] = moved[384:512].astype(BF)
            else:
                shifted(jnp.concatenate([ns.a1[cells, part], ns.halo[0, c, :, part], ns.halo[1, c, :, part]], axis=0), ns.shifts[...], S, c)
            return carry

        lax.fori_loop(0, cols // 16, chunk, 0)
        wrap(S, cols)
        hook()
        for lane in range(lanes):
            at = slice((group * lanes + lane) * 128, (group * lanes + lane + 1) * 128)

            def step(b, carry):
                first, second = carry
                acc = jnp.zeros((8, 8, 128), F32)
                for i in range(7):
                    window = S[i, lane, pl.ds(b * 8, 14)]
                    for j in range(7):
                        acc = acc + window[j : j + 8] * kb[7 * i + j, :, at][None]
                z[pl.ds(b * 8, 8), :, at] = acc
                kept = acc * ocean[pl.ds(pl.multiple_of(b * 64, 64), 64)].reshape(8, 8, 128)
                return first + kept.sum(0), second + (kept * acc).sum(0)

            zero = jnp.zeros((8, 128), F32)
            first, second = lax.fori_loop(0, cols // 8, step, (zero, zero))
            stats[0:1, at] = first.sum(0, keepdims=True)
            stats[1:2, at] = second.sum(0, keepdims=True)
            stats[2:3, at] = tally.sum(0, keepdims=True)
            stats[3:8, at] = jnp.zeros((5, 128), F32)
            hook()


def ff_phase(sec, ns, st, w1, w2, res, y, nat, kept, hook):
    par = ns.par[sec]
    counted, mean, inverse, gain, shift = norm_terms(st, par)
    wide = ns.z.shape[2]
    steps = ns.z.shape[0] // 32
    stage, sems = (ns.n_st, ns.g_st, ns.gp_st), ns.ff_sem
    w1, w2 = w1.reshape(wide, -1), w2.reshape(-1, wide)
    hidden = w1.shape[1]

    def outs(b, slot):
        at = pl.ds(pl.multiple_of(b * 256, 256), 256)
        return [pltpu.make_async_copy(src.at[slot], dst.at[at], sems.at[k, slot]) for k, (src, dst) in enumerate(zip(stage, kept))]

    def block(b, carry):
        slot = b % 2

        @pl.when(b >= 2)
        def _():
            for copy in outs(b - 2, slot):
                copy.wait()

        z = ns.z[pl.ds(b * 32, 32)].reshape(256, wide)
        at = pl.ds(pl.multiple_of(b * 256, 256), 256)
        normed = ((z - mean) * inverse * gain + shift).astype(BF)
        ns.n_st[slot] = normed
        acc = jnp.zeros((256, wide), F32)
        for h in range(0, hidden, 256):
            cut = slice(h, h + 256)
            e = dot(normed, w1[:, cut]) + ns.bias[sec, 0:1, cut]
            phi = 0.5 + 0.5 * lax.erf(e * np.float32(0.5**0.5))
            act = (e * phi).astype(BF)
            ns.g_st[slot, :, cut] = act
            ns.gp_st[slot, :, cut] = (phi + e * (np.float32((2 * np.pi) ** -0.5) * jnp.exp(-0.5 * e * e))).astype(BF)
            acc = acc + dot(act, w2[cut])
        out = (lanes4(ns.ocean[at], wide) * (res[at].astype(F32) + (acc + par[51:52]))).astype(BF)
        if y is not None:
            y[at] = out
        for k in range(2):
            nat[:, 2 * b + k] = to_natural(out[128 * k : 128 * k + 128], ns.back[...], ns.gather[...])
        for copy in outs(b, slot):
            copy.start()
        for k in range(steps):
            pl.when(b == k)(functools.partial(hook, k))
        return carry

    lax.fori_loop(0, steps, block, 0)
    for b in (steps - 2, steps - 1):
        for copy in outs(b, b % 2):
            copy.wait()


def forward_kernel(fast, count, cols, ns):
    s, d, g, m, p = where_am_i()
    greet_near(count)
    x14 = ns.x14
    x_begin, x_end = collect(ns.x, x14, 3, ns.xs, ns.xr)
    land_begin, land_end = collect_land(ns.land, ns.land2, ns.ls, ns.lr)
    x_begin()
    land_begin()
    pairs = [(ns.mine, ns.par), (ns.mine_bias, ns.bias)] + [(getattr(ns, f"mine{k}"), getattr(ns, f"shard{k}")) for k in range(4) if fast]
    far = [remote(src, dst.at[s], ns.ps.at[k, 0], ns.pr.at[k], (1 - s, d)) for k, (src, dst) in enumerate(pairs)]
    near = [pltpu.make_async_copy(src, dst.at[s], ns.ps.at[k, 1]) for k, (src, dst) in enumerate(pairs)]
    for c in far + near:
        c.start()
    fulls = dict(w1_0=ns.w1_0, w2_0=ns.w2_0, r0=ns.r0, m0=ns.m0, m1=ns.m1, r1=ns.r1, w1_1=ns.w1_1, w2_1=ns.w2_1)
    which = dict(w1_0=(0, 0), w2_0=(1, 0), r0=(2, 0), r1=(2, 1), m0=(3, 0), m1=(3, 1), w1_1=(0, 1), w2_1=(1, 1))
    mats = {}
    for k, (name, full) in enumerate(fulls.items()):
        if fast:
            index, sec = which[name]
            mats[name] = Gather(getattr(ns, f"shard{index}").at[sec], full, ns.gs.at[k], ns.gr.at[k])
        else:
            mats[name] = Load(getattr(ns, name + "_in"), full, ns.gs.at[k])
    saves = {name: lambda k=k, name=name, full=full: pltpu.make_async_copy(full, getattr(ns, name + "_out"), ns.save.at[k]) for k, (name, full) in enumerate(fulls.items())}

    def do(step, *names):
        for name in names:
            getattr(mats[name], step)()

    def whole(*names):
        do("whole", *names)
        for name in names:
            saves[name]().start()

    if fast:
        for k in range(2, 6):
            near[k].wait()
            arrived(pairs[k][1].at[1 - s], ns.pr.at[k])
    do("start", "w1_0", "w2_0")
    do("start", "r0")
    land_end()
    masks(ns.land2, ns.ocean, ns.coarse, ns.pick[...], ns.patch[...])
    x_end()

    def edge(up):
        src, dst = (x14.at[pl.ds(3, 3)], x14.at[pl.ds(11, 3)]) if up else (x14.at[pl.ds(8, 3)], x14.at[pl.ds(0, 3)])
        return remote(src, dst, ns.hs.at[int(up)], ns.hr.at[int(up)], device(p - 1 if up else p + 1, m))

    pl.when(p > 0)(edge(True).start)
    pl.when(p < count - 1)(edge(False).start)
    do("plane", "w1_0", "w2_0")
    for k in range(2):
        near[k].wait()
        arrived(pairs[k][1].at[1 - s], ns.pr.at[k])

    @pl.when(p == 0)
    def _():
        x14[0:3] = jnp.zeros((3,) + x14.shape[1:], BF)

    @pl.when(p == count - 1)
    def _():
        x14[11:14] = jnp.zeros((3,) + x14.shape[1:], BF)

    pl.when(p > 0)(lambda: arrived(x14.at[pl.ds(0, 3)], ns.hr.at[0]))
    pl.when(p < count - 1)(lambda: arrived(x14.at[pl.ds(11, 3)], ns.hr.at[1]))

    def script(*actions):
        queue = list(actions)

        def hook(*_):
            if queue:
                queue.pop(0)()

        return hook

    cot_begin, cot_end = collect(ns.cot, ns.cot8, 0, ns.cs, ns.cr)
    act = deliver(0, ns.nat0, ns.act, ns.bounce, ns.ds_, ns.dr_, ns.db)

    conv_phase(0, cols, ns, script(
        lambda: (do("onward", "w1_0", "w2_0"), do("start", "m0", "m1", "r1")),
        lambda: do("plane", "r0"),
        lambda: do("over", "w1_0", "w2_0"),
        lambda: do("onward", "r0"),
        lambda: do("start", "w1_1", "w2_1"),
        lambda: do("plane", "m0", "m1", "r1"),
    ))
    ns.st0[...] = all_sum(ns.stats, ns.slots, ns.send, ns.recv, count)
    keep_z = pltpu.make_async_copy(ns.z, ns.z0, ns.keep.at[0])
    keep_z.start()
    whole("w1_0", "w2_0")
    ff0 = {0: lambda: do("over", "r0"), 1: lambda: do("onward", "m0", "m1", "r1"), 4: lambda: do("plane", "w1_1", "w2_1")}
    ff_phase(0, ns, ns.st0, ns.w1_0, ns.w2_0, ns.a0, ns.skip, ns.nat0, (ns.n0, ns.g0, ns.gp0), lambda k: ff0.get(k, lambda: None)())

    whole("r0")
    skip, pieces, wide = ns.skip, ns.pieces, ns.skip.shape[1]
    blocks = skip.shape[0] // 256
    down, up_w = ns.r0.reshape(4 * wide, -1), ns.r1.reshape(GROUPS, 2, ns.r1.shape[2] // 2, -1)
    merge = [v.reshape(wide, wide) for v in (ns.m0, ns.m1)]
    for b in range(blocks):
        moved = dot(ns.patch[...], skip[256 * b : 256 * b + 256]).astype(BF)
        for k in range(4):
            pieces[k, 64 * b : 64 * b + 64] = moved[64 * k : 64 * k + 64]
    value = sum(dot(pieces[k], down[wide * k : wide * k + wide]) for k in range(4))
    deep_value = (lanes4(ns.coarse[...], value.shape[1]) * value).astype(BF)
    ns.deep[...] = deep_value
    do("over", "m0", "m1", "r1")
    do("onward", "w1_1", "w2_1")
    act[0]()
    whole("m0", "m1", "r1")
    rows = up_w.shape[0] * up_w.shape[2]
    lifted = [dot(deep_value, up_w[:, i].reshape(rows, -1)).astype(BF) for i in range(2)]
    for b in range(blocks):
        at = slice(256 * b, 256 * b + 256)
        stacked = jnp.concatenate(
            [lifted[i][64 * b : 64 * b + 64, wide * j : wide * j + wide] for i in range(2) for j in range(2)], axis=0
        )
        ns.up[at] = dot(ns.unpatch[...], stacked).astype(BF)
        joined = dot(ns.up[at], merge[0][...]) + dot(skip[at], merge[1][...])
        ns.h[at] = joined
        low = joined.astype(BF)
        ns.a1[at] = low
        for k in range(2):
            ends = dot(ns.edges[...], low[128 * k : 128 * k + 128]).astype(BF)
            ns.packed[0, 2 * b + k] = ends[:48]
            ns.packed[1, 2 * b + k] = ends[48:]
    swap_rows(ns.packed, ns.halo, ns.es, ns.er, count)
    keep_z.wait()
    cot_begin()

    conv_phase(1, cols, ns, script(
        act[1],
        lambda: do("over", "w1_1", "w2_1"),
        lambda: whole("w1_1", "w2_1"),
    ))
    ns.st1[...] = all_sum(ns.stats, ns.slots1, ns.send1, ns.recv1, count)
    keep_z1 = pltpu.make_async_copy(ns.z, ns.z1, ns.keep.at[0])
    keep_z1.start()
    ff_phase(1, ns, ns.st1, ns.w1_1, ns.w2_1, ns.h, None, ns.nat1, (ns.n1, ns.g1, ns.gp1), lambda k: None)

    cot_end()
    act[3]()
    for name, save in saves.items():
        save().wait()
        do("finish", name)
    keep_z1.wait()
    for c in far:
        c.wait_send()
    pl.when(p > 0)(edge(True).wait_send)
    pl.when(p < count - 1)(edge(False).wait_send)


class Names:
    pass


def build(name, body, ins, outs, scratch=None, jobs=(), cid=None, limit=60, **more):
    ins, outs, scratch, alias = dict(ins), dict(outs), dict(scratch or {}), {}
    for job in jobs:
        ins.update(job.ins)
        outs.update(job.outs)
        scratch.update(job.scratch)
        alias.update(job.alias)
    ins = {k: v if isinstance(v, tuple) else (v, VM) for k, v in ins.items()}
    outs = {k: v if len(v) == 3 else v + (VM,) for k, v in outs.items()}
    names = list(ins) + list(outs) + list(scratch)

    def kernel(*refs):
        ns = Names()
        for k, ref in zip(names, refs):
            setattr(ns, k, ref)
        steps = [job.steps(ns) for job in jobs]

        def hook(k):
            for step in steps:
                step[k]()

        body(ns, hook)

    params = dict(vmem_limit_bytes=limit * MEGA)
    if cid is not None:
        params.update(collective_id=cid, has_side_effects=True)
    order_in, order_out = list(ins), list(outs)
    results = pl.pallas_call(
        kernel, name=name, out_shape=[jax.ShapeDtypeStruct(v[0], v[1]) for v in outs.values()],
        in_specs=[v[1] for v in ins.values()], out_specs=[v[2] for v in outs.values()], scratch_shapes=list(scratch.values()),
        input_output_aliases={order_in.index(a): order_out.index(b) for a, b in alias.items()},
        compiler_params=pltpu.CompilerParams(**params), **more,
    )(*[v[0] for v in ins.values()])
    out = Names()
    for k, v in zip(order_out, results):
        setattr(out, k, v)
    return out


def on_device(sections, dps, inputs, cotangent, land, kernel, bn_gain, bn_bias, bias_in, bias_out, w_in, w_out, resample, merge):
    batches, height, cols, c = inputs.shape
    hid = bias_in.shape[1]
    n = resample.shape[1] * dps // (4 * c)
    cw, hw, nw = (GROUPS * padded(v) for v in (c, hid, n))
    cells, deep_cells = cols * 8, cols * 2
    count = 2 * (dps // 4)
    fast = dps == GROUPS
    assert batches == 4 and height == 4 and dps % 4 == 0 and sections == 2 and cols % 32 == 0
    s = lax.axis_index("section")
    mats = {k: jnp.asarray(v) for k, v in matrices(c).items()}
    tiles = cols // 16
    both = ("section", "dp")

    def packs(parts, w1, w2, rd, ru):
        return pack_in(w1, parts, c, hid), pack_in(w2, parts, hid, c), pack_down(rd, parts, c, n), pack_up(ru, parts, c, n)

    shards = []
    if fast:
        w1, w2, rd, ru = packs(1, *(v.astype(BF) for v in (w_in, w_out, resample, resample)))
        shards = [w1[0], w2[0], jnp.where(s == 0, rd, ru)[0], pack_in(merge.astype(BF), 1, c, c)[0]]
    else:
        flat = [lax.all_gather(v.astype(BF).reshape(-1), both, axis=0, tiled=True) for v in (w_in, w_out, resample, merge)]
        halves = [v.reshape(2, -1) for v in flat]
        whole = [packs(GROUPS, halves[0][k], halves[1][k], halves[2][k], halves[2][k]) for k in range(2)]

    rows = jnp.concatenate([kernel[0], bn_gain, bn_bias, bias_out], axis=0)
    mine = grow(grow(rows.reshape(-1, GROUPS, c // GROUPS), (52, GROUPS, padded(c))).reshape(52, cw), (56, cw))
    mine_bias = grow(grow(bias_in.reshape(GROUPS, -1), (GROUPS, padded(hid))).reshape(1, hw), (8, hw))
    x = inputs.reshape(batches, height, tiles, 16, c)
    cot = cotangent.reshape(batches, height, tiles, 16, c)
    land_cols = -(-cols // 128) * 128
    at_any = lambda v: (v, ANY)
    field = lambda t: ((cells, cw), t)
    natural = ((8, tiles, 16, c), BF)
    edge_rows = ((2, tiles, 48, cw), BF)
    exchange = dict(stats=pltpu.VMEM((8, cw), F32), slots=pltpu.VMEM((count // 2 + 1, 8, cw), F32), send=DMA((count,)), recv=DMA((count,)))
    shift_space = dict(S=pltpu.VMEM((7, cw // 128, cols + 6, 8, 128), F32), kb=pltpu.VMEM((49, 8, cw), F32))
    conv_outs = dict(z=((cols, 8, cw), F32), st=((8, cw), F32))

    def only(ns, hook):
        greet_near(count)
        for k in range(4):
            hook(k)


    def backward(name, cid, jobs, sec, top, conv, w1, w2, kept):
        return build(
            name, functools.partial(back_ff_kernel, sec, count),
            dict(top=top, z=conv.z.reshape(cells, cw), st=conv.st, par=par, w1=w1, w2=w2, n=kept.n, g=kept.g, gp=kept.gp, ocean=ocean,
                 spread=mats["spread"], turn=mats["turn"], edges=mats["edges"]),
            dict(dym=field(F32), dw1=((cw, hw), BF), dw2=((hw, cw), BF), small=((8, cw), F32), dz=field(BF), halo=edge_rows),
            dict(dn=pltpu.VMEM((cells, cw), F32), dr=pltpu.VMEM((cells, cw), BF), packed=pltpu.VMEM(*edge_rows), hsend=DMA((2,)), hrecv=DMA((2,)), **exchange),
            jobs, cid,
        )

    def backward_conv(name, cid, jobs, sec, back, a):
        outs = dict(dh=field(BF), dk=((56, cw), F32))
        if sec == 0:
            outs["nat"] = natural
        return build(
            name, functools.partial(back_conv_kernel, sec, count, cols),
            dict(dz=back.dz, halo=back.halo, perm=mats["shifts"], par=par, dym=back.dym, a=a, back=mats["back"], gather=mats["gather"]),
            outs, dict(acc_dk=pltpu.VMEM((49, 8, cw), F32), **shift_space), jobs, cid,
        )

    shapes = [(padded(c), hw), (padded(hid), cw), (4 * padded(c), nw), (padded(c), cw)]
    names = dict(w1_0=0, w2_0=1, r0=2, m0=3, m1=3, r1=2, w1_1=0, w2_1=1)
    ins = dict(x=x, land=grow(land, (8, land_cols)), mine=mine, mine_bias=mine_bias, cot=cot)
    if fast:
        ins.update({f"mine{k}": v for k, v in enumerate(shards)})
    else:
        given = dict(w1_0=whole[0][0], w2_0=whole[0][1], r0=whole[0][2], r1=whole[1][3], w1_1=whole[1][0], w2_1=whole[1][1])
        given.update(m0=pack_in(halves[3][0], GROUPS, c, c), m1=pack_in(halves[3][1], GROUPS, c, c))
        ins.update({k + "_in": v.reshape((4, 4) + shapes[names[k]]) for k, v in given.items()})
    ins = {k: at_any(v) for k, v in ins.items()}
    ins.update({k: mats[k] for k in ("spread", "gather", "natural", "shifts", "patch", "unpatch", "edges", "back", "pick")})
    outs = dict(
        par=((2, 56, cw), F32), bias=((2, 8, hw), F32), ocean=((cells, 128), F32), coarse=((deep_cells, 128), F32),
        st0=((8, cw), F32), st1=((8, cw), F32), a0=field(BF), a1=field(BF), skip=field(BF), up=field(BF),
        pieces=((4, deep_cells, cw), BF), deep=((deep_cells, nw), BF), nat1=natural,
        z0=((cols, 8, cw), F32, ANY), z1=((cols, 8, cw), F32, ANY), cot8=natural + (ANY,), act=((4, 4, tiles, 16, c), BF, ANY),
    )
    for k in range(2):
        outs.update({f"n{k}": field(BF) + (ANY,), f"g{k}": ((cells, hw), BF, ANY), f"gp{k}": ((cells, hw), BF, ANY)})
    outs.update({k + "_out": ((4, 4) + shapes[v], BF, ANY) for k, v in names.items()})
    scratch = dict(
        x14=pltpu.VMEM((14, tiles, 16, c), BF), land2=pltpu.VMEM((2, 8, land_cols), jnp.int32),
        S=pltpu.VMEM((7, 2, cols + 6, 8, 128), F32), kb=pltpu.VMEM((49, 8, cw), F32), z=pltpu.VMEM((cols, 8, cw), F32),
        h=pltpu.VMEM((cells, cw), F32), n_st=pltpu.VMEM((2, 256, cw), BF), g_st=pltpu.VMEM((2, 256, hw), BF), gp_st=pltpu.VMEM((2, 256, hw), BF),
        nat0=pltpu.VMEM(*natural), bounce=pltpu.VMEM(*natural), halo=pltpu.VMEM(*edge_rows), packed=pltpu.VMEM(*edge_rows),
        stats=pltpu.VMEM((8, cw), F32), slots=pltpu.VMEM((count // 2 + 1, 8, cw), F32), slots1=pltpu.VMEM((count // 2 + 1, 8, cw), F32),
        send=DMA((count,)), recv=DMA((count,)), send1=DMA((count,)), recv1=DMA((count,)),
        xs=DMA((4,)), xr=DMA((2,)), ls=DMA((4,)), lr=DMA((2,)), hs=DMA((2,)), hr=DMA((2,)), ps=DMA((6, 2)), pr=DMA((6,)), cs=DMA((4,)), cr=DMA((2,)),
        ds_=DMA((2, 2)), dr_=DMA((4,)), db=DMA((2,)), es=DMA((2,)), er=DMA((2,)), gs=DMA((8, 12)), gr=DMA((8, 12)), save=DMA((8,)), keep=DMA((2,)),
        ff_sem=DMA((3, 2)),
    )
    scratch.update({k: pltpu.VMEM((4, 4) + shapes[v], BF) for k, v in names.items()})
    if fast:
        scratch.update({f"shard{k}": pltpu.VMEM((2,) + shapes[k], BF) for k in range(4)})
    fw = build("forward", lambda ns, hook: forward_kernel(fast, count, cols, ns), ins, outs, scratch, (), 1, 63)
    par, ocean, coarse, bias = fw.par, fw.ocean, fw.coarse, fw.bias
    w1_0, w2_0, w1_1, w2_1 = (v.reshape(r) for v, r in zip((fw.w1_0_out, fw.w2_0_out, fw.w1_1_out, fw.w2_1_out), ((cw, hw), (hw, cw)) * 2))
    r0, r1 = fw.r0_out.reshape(4 * cw, nw), fw.r1_out.reshape(GROUPS, 2, padded(n), 2 * cw)
    mm = jnp.stack([fw.m0_out.reshape(cw, cw), fw.m1_out.reshape(cw, cw)])

    class Kept:
        def __init__(self, k):
            self.z, self.st, self.n, self.g, self.gp, self.a = (getattr(fw, f"{v}{k}") for v in ("z", "st", "n", "g", "gp", "a"))

    conv0, conv1 = Kept(0), Kept(1)
    ff0, ff1 = conv0, conv1

    view = lambda v, k: v.reshape((4, 4) + shapes[k])
    back1 = backward("dec_back", 6, [Deliver("act", 1, fw.nat1, fw.act)], 1, fw.cot8, conv1, w1_1, w2_1, ff1)
    jobs = [PlaneSum("ps", [view(back1.dw1, 0), view(back1.dw2, 1)])] if fast else []
    bconv1 = backward_conv("dec_back_conv", 7, jobs, 1, back1, conv1.a)
    jobs = [LineSum("ls", [(bconv1.psout0, 1), (bconv1.psout1, 1)])] if fast else []
    bmid = build(
        "back_mid", functools.partial(back_mid_kernel, count),
        dict(dh=bconv1.dh, up=fw.up, skip=fw.skip, deep=fw.deep, pieces=fw.pieces, down=r0, up_w=r1, merge=mm, coarse=coarse,
             patch=mats["patch"], unpatch=mats["unpatch"], back=mats["back"], gather=mats["gather"]),
        dict(dmerge=((2, cw, cw), BF), dup_w=((GROUPS, 2, padded(n), 2 * cw), BF), ddown=((4 * cw, nw), BF), dy=field(F32), nat=natural),
        dict(dskip=pltpu.VMEM((cells, cw), BF), dups=pltpu.VMEM((2, deep_cells, 2 * cw), BF), spreads=pltpu.VMEM((4, deep_cells, cw), F32)), jobs, 8,
    )
    jobs = []
    if fast:
        dm = bmid.dmerge.reshape((2, 4, 4) + shapes[3])
        jobs = [PlaneSum("ps", [view(bmid.ddown, 2), view(bmid.dup_w, 2), (dm, 0), (dm, 1)])]
    back0 = backward("enc_back", 9, jobs, 0, bmid.dy, conv0, w1_0, w2_0, ff0)
    jobs = [Deliver("gi", 1, bmid.nat)]
    if fast:
        jobs += [PlaneSum("ps", [view(back0.dw1, 0), view(back0.dw2, 1)]), LineSum("ls", [(getattr(back0, f"psout{k}"), k % 2) for k in range(4)])]
    bconv0 = backward_conv("enc_back_conv", 10, jobs, 0, back0, conv0.a)

    tiny = jnp.stack([jnp.concatenate([dk, small], axis=0) for dk, small in ((bconv0.dk, back0.small), (bconv1.dk, back1.small))])
    jobs = [Deliver("gi", 0, bconv0.nat, bconv0.giout)]
    if fast:
        jobs += [LineSum("ls", [(bconv0.psout0, 0), (bconv0.psout1, 0)])]
        last = build(
            "last", functools.partial(last_kernel, count), dict(small=tiny), dict(total=((64, cw), F32)),
            dict(tiny=pltpu.VMEM((9, 64, cw), F32), ts=DMA((9,)), tr=DMA((9,))), jobs, 11,
        )
        tiny = last.total
        rows_of = lambda v: v.reshape(-1, v.shape[-1])
        gw1 = unpack_in(rows_of(jnp.where(s == 0, last.lsout0, bmid.lsout0)), c, hid)
        gw2 = unpack_in(jnp.where(s == 0, last.lsout1, bmid.lsout1).transpose(1, 0, 2).reshape(padded(hid), cw), hid, c)
        gres = jnp.where(s == 0, unpack_down(rows_of(bconv0.lsout0), c, n), unpack_up(rows_of(bconv0.lsout1), c, n))
        gmm = unpack_in(rows_of(jnp.where(s == 0, bconv0.lsout2, bconv0.lsout3)), c, c)
    else:
        last = build("last", only, {}, {}, {}, jobs, 11)
        scatter = lambda v: lax.psum_scatter(v.astype(F32).reshape(-1), both, scatter_dimension=0, tiled=True)
        gw1 = scatter(jnp.stack([unpack_in(v, c, hid) for v in (back0.dw1, back1.dw1)]))
        gw2 = scatter(jnp.stack([unpack_in(v, hid, c) for v in (back0.dw2, back1.dw2)]))
        gres = scatter(jnp.stack([unpack_down(bmid.ddown, c, n), unpack_up(bmid.dup_w, c, n)]))
        gmm = scatter(jnp.stack([unpack_in(bmid.dmerge[k], c, c) for k in range(2)]))
        tiny = lax.psum(tiny, both)[s]
    activations = back1.actout.reshape(1, batches, height, cols, c)
    grad_input = last.giout.astype(F32).reshape(1, batches, height, cols, c)
    narrow = lambda v: v.reshape(-1, GROUPS, padded(c))[:, :, : c // GROUPS].reshape(-1, c)
    fine = narrow(tiny[:59])
    grad_bias_in = tiny[59:63].reshape(-1)[:hw].reshape(GROUPS, -1)[:, : hid // GROUPS].reshape(1, hid)
    return (
        activations, grad_input, fine[None, :49], fine[57:58], fine[56:57], grad_bias_in, fine[58:59],
        gw1[None], gw2[None], gres[None], gmm,
    )


def solution(mesh):
    sections, dps = mesh.shape["section"], mesh.shape["dp"]
    flat, both = P("section", "dp"), P(("section", "dp"))
    per = P("section", None)
    rows = P(None, "dp", None, None)
    taps = P("section", None, None)
    fields = P("section", None, "dp", None, None)
    return jax.shard_map(
        functools.partial(on_device, sections, dps), mesh=mesh,
        in_specs=(rows, rows, P("dp", None), taps, per, per, per, per, flat, flat, flat, both),
        out_specs=(fields, fields, taps, per, per, per, per, flat, flat, flat, both), check_vma=False,
    )
```

```python
import functools

import jax
import jax.numpy as jnp
import ml_dtypes
import numpy as np
from jax import lax
from jax.experimental import pallas as pl
from jax.experimental.pallas import tpu as pltpu
from jax.sharding import PartitionSpec as P

BF = jnp.bfloat16
F32 = jnp.float32
MESH = pl.DeviceIdType.MESH
ANY = pl.BlockSpec(memory_space=pl.ANY)
VM = pl.BlockSpec(memory_space=pltpu.VMEM)
DMA = pltpu.SemaphoreType.DMA
EPS = 1e-05
GROUPS = 16
MEGA = 1 << 20


def padded(width):
    return -(-(width // GROUPS) // 16) * 16


def selector(rows, cols, pairs):
    out = np.zeros((rows, cols), np.float32)
    for r, c in pairs:
        out[r, c] = 1
    return out.astype(ml_dtypes.bfloat16)


def matrices(channels):
    group, wide = channels // GROUPS, padded(channels)
    spread = selector(channels, GROUPS * wide, [(c, c // group * wide + c % group) for c in range(channels)])
    natural = selector(896, 224, [(i * 128 + q * 8 + p, (p + i) * 16 + q) for i in range(7) for q in range(16) for p in range(8)])

    def place(q, row):
        if row < 0:
            return 128 + q * 3 + row + 3
        return q * 8 + row if row < 8 else 176 + q * 3 + row - 8

    shifts = selector(896, 224, [(i * 128 + q * 8 + p, place(q, p + i - 3)) for i in range(7) for q in range(16) for p in range(8)])
    turn = selector(128, 128, [(q * 8 + p, p * 16 + q) for q in range(16) for p in range(8)])
    edges = selector(96, 128, [(48 * e + q * 3 + k, q * 8 + 5 * e + k) for e in range(2) for q in range(16) for k in range(3)])
    patch = selector(
        256, 256,
        [((i * 2 + j) * 64 + b * 4 + a, (2 * b + j) * 8 + 2 * a + i) for i in range(2) for j in range(2) for b in range(16) for a in range(4)],
    )
    pick = selector(128, 16, [(q * 8 + p, p // 4 * 8 + p % 4) for q in range(16) for p in range(8)])
    return dict(
        pick=pick, spread=spread, gather=np.ascontiguousarray(spread.T), natural=natural, shifts=shifts, turn=turn,
        back=np.ascontiguousarray(turn.T), edges=edges, patch=patch, unpatch=np.ascontiguousarray(patch.T),
    )


def grow(value, sizes):
    return jnp.pad(value, [(0, n - o) for n, o in zip(sizes, value.shape)])


def pack_in(value, parts, c, h):
    value = value.reshape(parts, c // GROUPS, GROUPS, h // GROUPS)
    return grow(value, (parts, padded(c), GROUPS, padded(h))).reshape(parts, padded(c), -1)


def pack_down(value, parts, c, n):
    value = value.reshape(parts, 4, c // GROUPS, GROUPS, n // GROUPS)
    return grow(value, (parts, 4, padded(c), GROUPS, padded(n))).reshape(parts, 4 * padded(c), -1)


def pack_up(value, parts, c, n):
    value = value.reshape(parts, n // GROUPS, 2, 2 * GROUPS, c // GROUPS)
    value = grow(value, (parts, padded(n), 2, 2 * GROUPS, padded(c)))
    return value.transpose(0, 2, 1, 3, 4).reshape(parts, 2 * padded(n), -1)


def unpack_in(value, c, h):
    value = value.reshape(-1, padded(c), GROUPS, padded(h))
    return value[:, : c // GROUPS, :, : h // GROUPS].reshape(-1)


def unpack_down(value, c, n):
    value = value.reshape(-1, 4, padded(c), GROUPS, padded(n))
    return value[:, :, : c // GROUPS, :, : n // GROUPS].reshape(-1)


def unpack_up(value, c, n):
    value = value.reshape(-1, 2, padded(n), 2 * GROUPS, padded(c))
    return value.transpose(0, 2, 1, 3, 4)[:, : n // GROUPS, :, :, : c // GROUPS].reshape(-1)


def device(p, m):
    g = p // 2
    return (p + g) % 2, 4 * g + m


def where_am_i():
    s, d = lax.axis_index("section"), lax.axis_index("dp")
    g = d // 4
    return s, d, g, d % 4, 2 * g + (s + g) % 2


def greet_near(count):
    s, d, g, m, p = where_am_i()
    barrier = pltpu.get_barrier_semaphore()

    def one(k, carry):
        q = (p + k) % count
        pl.semaphore_signal(barrier, inc=1, device_id=device(q, m), device_id_type=MESH)
        return carry

    lax.fori_loop(1, count, one, 0)
    for k in range(1, 4):
        for sec in range(2):
            pl.semaphore_signal(barrier, inc=1, device_id=(sec, 4 * g + (m + k) % 4), device_id_type=MESH)
    pl.semaphore_wait(barrier, count + 5)


def remote(src, dst, send, recv, peer):
    return pltpu.make_async_remote_copy(src_ref=src, dst_ref=dst, send_sem=send, recv_sem=recv, device_id=peer, device_id_type=MESH)


def arrived(ref, sem):
    pltpu.make_async_copy(ref, ref, sem).wait()


def all_sum(mine, slots, send, recv, count):
    s, d, g, m, p = where_am_i()
    groups = count // 2
    over = remote(mine, slots.at[groups], send.at[0], recv.at[0], (1 - s, d))
    over.start()
    arrived(slots.at[groups], recv.at[0])
    slots[g] = mine[...] + slots[groups]
    over.wait_send()

    def copy(k):
        return remote(slots.at[g], slots.at[g], send.at[k], recv.at[k], (s, 4 * ((g + k) % groups) + m))

    lax.fori_loop(1, groups, lambda k, c: (copy(k).start(), c)[1], 0)

    def wait(k, carry):
        arrived(slots.at[(g + groups - k) % groups], recv.at[k])
        copy(k).wait_send()
        return carry

    lax.fori_loop(1, groups, wait, 0)
    return lax.fori_loop(0, groups, lambda k, total: total + slots[k], jnp.zeros(mine.shape, F32))


def swap_rows(packed, halo, send, recv, count):
    s, d, g, m, p = where_am_i()

    def peer(q):
        return device(q, m)

    @pl.when(p > 0)
    def _():
        remote(packed.at[0], halo.at[1], send.at[0], recv.at[1], peer(p - 1)).start()

    @pl.when(p < count - 1)
    def _():
        remote(packed.at[1], halo.at[0], send.at[1], recv.at[0], peer(p + 1)).start()

    @pl.when(p > 0)
    def _():
        arrived(halo.at[0], recv.at[0])
        remote(packed.at[0], halo.at[1], send.at[0], recv.at[1], peer(p - 1)).wait_send()

    @pl.when(p < count - 1)
    def _():
        arrived(halo.at[1], recv.at[1])
        remote(packed.at[1], halo.at[0], send.at[1], recv.at[0], peer(p + 1)).wait_send()

    @pl.when(p == 0)
    def _():
        halo[0] = jnp.zeros(halo.shape[1:], BF)

    @pl.when(p == count - 1)
    def _():
        halo[1] = jnp.zeros(halo.shape[1:], BF)


def dot(a, b):
    return jnp.dot(a, b, preferred_element_type=F32)


def dot_nt(a, b):
    return lax.dot_general(a, b, (((1,), (1,)), ((), ())), preferred_element_type=F32)


def dot_tn(a, b):
    return lax.dot_general(a, b, (((0,), (0,)), ((), ())), preferred_element_type=F32)


def lanes4(mask, width):
    return jnp.concatenate([mask] * (width // 128), axis=1)


def rows8(value):
    return value.reshape(-1, 8, value.shape[-1]).sum(0)


def to_natural(cells, back, gather):
    turned = dot(dot(back, cells).astype(BF), gather).astype(BF)
    return turned.reshape(8, 16, turned.shape[-1])


def shifted(chunk, perm, S, c):
    moved = dot(perm, chunk)
    for lane in range(S.shape[1]):
        S[:, lane, pl.ds(3 + 16 * c, 16)] = moved[:, lane * 128 : lane * 128 + 128].reshape(7, 16, 8, 128)
    return moved


def wrap(S, cols):
    S[:, :, 0:3] = S[:, :, cols : cols + 3]
    S[:, :, cols + 3 : cols + 6] = S[:, :, 3:6]


def taps_to(kb, par, flip):
    for k in range(49):
        kb[k] = jnp.broadcast_to(par[(48 - k if flip else k) : (48 - k if flip else k) + 1], kb.shape[1:])


def norm_terms(st, par):
    counted = st[2:3]
    mean = st[0:1] / counted
    inverse = lax.rsqrt(st[1:2] / counted - mean * mean + EPS)
    return counted, mean, inverse, par[49:50], par[50:51]


def start_either(self, src, dst, send, recv, peer):
    pl.when(jnp.logical_not(self))(lambda: remote(src, dst, send, recv, peer).start())
    pl.when(self)(lambda: pltpu.make_async_copy(src, dst, recv).start())


def deliver(sec, nat, out, bounce, send, recv, b):
    s, d, g, m, p = where_am_i()

    def target(which, j):
        dp = 4 * g + 2 * ((p + which) % 2) + j
        part = (nat, bounce)[which].at[pl.ds(4 * j, 4)]
        return dp == d, part, out.at[m], send.at[which, j], recv.at[m], (s, dp)

    def over():
        return remote(nat, bounce, b.at[0], b.at[1], (1 - s, d))

    def sends(which):
        for j in range(2):
            start_either(*target(which, j))

    def begin():
        pl.when(s != sec)(lambda: over().start())
        pl.when(s == sec)(lambda: sends(0))

    def middle():
        @pl.when(s == sec)
        def _():
            arrived(bounce, b.at[1])
            sends(1)

    def end():
        @pl.when(s == sec)
        def _():
            for mb in range(4):
                arrived(out.at[mb], recv.at[mb])
            for which in range(2):
                for j in range(2):
                    self_, *rest = target(which, j)
                    pl.when(jnp.logical_not(self_))(lambda rest=rest: remote(*rest).wait_send())

        pl.when(s != sec)(lambda: over().wait_send())

    return [begin, middle, lambda: None, end]


def collect(field, out, first, send, recv):
    s, d, g, m, p = where_am_i()
    core, dp = device(d // 2, 0)
    j = d % 2

    def parts(step):
        mb = (m + step) % 4
        return field.at[mb], out.at[pl.ds(first + 4 * j, 4)], send.at[step], recv.at[j], (s, dp + mb)

    def begin():
        @pl.when(s == core)
        def _():
            for step in range(1, 4):
                remote(*parts(step)).start()
            src, dst, _, sem, _ = parts(0)
            pltpu.make_async_copy(src, dst, sem).start()

    def end():
        for jj in range(2):
            arrived(out.at[pl.ds(first + 4 * jj, 4)], recv.at[jj])

        @pl.when(s == core)
        def _():
            for step in range(1, 4):
                remote(*parts(step)).wait_send()

    return begin, end


def half(ref, c):
    rows, lanes = ref.shape[-2:]
    lead = (slice(None),) * (len(ref.shape) - 2)
    if rows % 32 == 0:
        return ref.at[lead + (pl.ds(pl.multiple_of(c * (rows // 2), 16), rows // 2),)]
    return ref.at[lead + (slice(None), pl.ds(pl.multiple_of(c * (lanes // 2), 128), lanes // 2))]


def half_shape(shape):
    rows, lanes = shape[-2:]
    return shape[:-2] + ((rows // 2, lanes) if rows % 32 == 0 else (rows, lanes // 2))


def collect_land(land, out, send, recv):
    s, d, g, m, p = where_am_i()
    core, dp = device(d // 2, 0)

    def part(step):
        return remote(land, out.at[d % 2], send.at[step], recv.at[d % 2], (s, dp + (m + step) % 4))

    def begin():
        @pl.when(s == core)
        def _():
            for step in range(1, 4):
                part(step).start()
            pltpu.make_async_copy(land, out.at[d % 2], recv.at[d % 2]).start()

    def end():
        for jj in range(2):
            arrived(out.at[jj], recv.at[jj])

        @pl.when(s == core)
        def _():
            for step in range(1, 4):
                part(step).wait_send()

    return begin, end


def script(*actions):
    queue = list(actions)

    def hook(*_):
        if queue:
            queue.pop(0)()

    return hook


def nothing():
    pass


class Gather:
    def __init__(self, shard, full, send, recv):
        self.shard, self.full, self.send, self.recv = shard, full, send, recv
        self.s, self.d, self.g, self.m, _ = where_am_i()
        self.bit = 1 + self.s

    def block(self, col, c):
        return half(self.full.at[:, col], c)

    def near(self):
        return pltpu.make_async_copy(half(self.shard, self.s), half(self.full.at[self.g, self.m], self.s), self.send.at[0])

    def line(self, step):
        src, dst = half(self.shard, self.s), half(self.full.at[self.g, self.m], self.s)
        return remote(src, dst, self.send.at[step], self.recv.at[step], (self.s, 4 * ((self.g + step) % 4) + self.m))

    def column(self, slot, col, peer):
        block = self.block(col, self.s)
        return remote(block, block, self.send.at[slot], self.recv.at[slot], peer)

    def first(self):
        return self.column(4, self.m, (self.s, self.d ^ self.bit))

    def second(self, index):
        return self.column(5 + index, (self.m, self.m ^ self.bit)[index], (self.s, self.d ^ (3 - self.bit)))

    def cols(self, way):
        return (self.m, self.m ^ way, self.m ^ (3 - way), self.m ^ 3)

    def hand(self, index):
        return self.column(7 + index, self.cols(self.bit)[index], (1 - self.s, self.d))

    def start(self):
        self.near().start()
        for step in range(1, 4):
            self.line(step).start()

    def plane(self):
        self.near().wait()
        for step in range(1, 4):
            arrived(half(self.full.at[(self.g + 4 - step) % 4, self.m], self.s), self.recv.at[step])
        self.first().start()
        self.second(0).start()
        self.hand(0).start()

    def onward(self):
        arrived(self.block(self.m ^ self.bit, self.s), self.recv.at[4])
        self.second(1).start()
        self.hand(1).start()

    def over(self):
        for index in range(2):
            arrived(self.block((self.m ^ (3 - self.bit), self.m ^ 3)[index], self.s), self.recv.at[5 + index])
            self.hand(2 + index).start()

    def whole(self):
        for index, col in enumerate(self.cols(3 - self.bit)):
            arrived(self.block(col, 1 - self.s), self.recv.at[7 + index])

    def finish(self):
        for step in range(1, 4):
            self.line(step).wait_send()
        self.first().wait_send()
        for index in range(2):
            self.second(index).wait_send()
        for index in range(4):
            self.hand(index).wait_send()


class Load:
    def __init__(self, src, full, sem):
        self.copy = lambda: pltpu.make_async_copy(src, full, sem.at[0])

    def start(self):
        self.copy().start()

    def whole(self):
        self.copy().wait()

    def plane(self):
        pass

    onward = over = finish = plane


def masks(land, ocean, coarse, pick, patch):
    rows, across = land.shape[0] * land.shape[1], land.shape[2]
    flat = land[...].reshape(rows, across).astype(F32).astype(BF)
    spread = dot(pick, flat)
    at = lax.broadcasted_iota(jnp.int32, spread.shape, 1) - lax.broadcasted_iota(jnp.int32, spread.shape, 0) // 8
    ones = jnp.ones((across, 128), BF)

    def chunk(c, carry):
        ocean[pl.ds(pl.multiple_of(c * 128, 128), 128)] = dot(jnp.where(at == 16 * c, spread, 0.0).astype(BF), ones)
        return carry

    lax.fori_loop(0, ocean.shape[0] // 128, chunk, 0)
    for b in range(ocean.shape[0] // 256):
        moved = dot(patch, ocean[256 * b : 256 * b + 256].astype(BF))
        coarse[64 * b : 64 * b + 64] = moved[:64] * moved[64:128] * moved[128:192] * moved[192:]


def conv_phase(sec, cols, ns, hook):
    S, kb, ocean, z, stats = ns.S, ns.kb, ns.ocean, ns.z, ns.stats
    taps_to(kb, ns.par[sec], False)
    lanes = S.shape[1]
    wide = kb.shape[2]

    def count_cells(b, t):
        return t + ocean[pl.ds(pl.multiple_of(b * 64, 64), 64)].reshape(8, 8, 128).sum(0)

    tally = lax.fori_loop(0, cols // 8, count_cells, jnp.zeros((8, 128), F32))
    for group in range(wide // 128 // lanes):
        part = slice(group * lanes * 128, (group + 1) * lanes * 128)

        def chunk(c, carry):
            cells = pl.ds(pl.multiple_of(c * 128, 128), 128)
            if sec == 0:
                block = ns.x14[:, c]
                block = dot(block.reshape(-1, block.shape[-1]), ns.spread[:, part]).astype(BF)
                moved = shifted(block, ns.natural[...], S, c)
                ns.a0[cells, part] = moved[384:512].astype(BF)
            else:
                shifted(jnp.concatenate([ns.a1[cells, part], ns.halo[0, c, :, part], ns.halo[1, c, :, part]], axis=0), ns.shifts[...], S, c)
            return carry

        lax.fori_loop(0, cols // 16, chunk, 0)
        wrap(S, cols)
        hook()
        for lane in range(lanes):
            at = slice((group * lanes + lane) * 128, (group * lanes + lane + 1) * 128)

            def step(b, carry):
                first, second = carry
                acc = jnp.zeros((8, 8, 128), F32)
                for i in range(7):
                    window = S[i, lane, pl.ds(b * 8, 14)]
                    for j in range(7):
                        acc = acc + window[j : j + 8] * kb[7 * i + j, :, at][None]
                z[pl.ds(b * 8, 8), :, at] = acc
                kept = acc * ocean[pl.ds(pl.multiple_of(b * 64, 64), 64)].reshape(8, 8, 128)
                return first + kept.sum(0), second + (kept * acc).sum(0)

            zero = jnp.zeros((8, 128), F32)
            first, second = lax.fori_loop(0, cols // 8, step, (zero, zero))
            stats[0:1, at] = first.sum(0, keepdims=True)
            stats[1:2, at] = second.sum(0, keepdims=True)
            stats[2:3, at] = tally.sum(0, keepdims=True)
            stats[3:8, at] = jnp.zeros((5, 128), F32)
            hook()


def ff_phase(sec, ns, st, w1, w2, res, y, nat, kept, hook):
    par = ns.par[sec]
    counted, mean, inverse, gain, shift = norm_terms(st, par)
    wide = ns.z.shape[2]
    steps = ns.z.shape[0] // 32
    stage, sems = (ns.n_st, ns.g_st, ns.gp_st), ns.ff_sem
    w1, w2 = w1.reshape(wide, -1), w2.reshape(-1, wide)
    hidden = w1.shape[1]

    def outs(b, slot):
        at = pl.ds(pl.multiple_of(b * 256, 256), 256)
        return [pltpu.make_async_copy(src.at[slot], dst.at[at], sems.at[k, slot]) for k, (src, dst) in enumerate(zip(stage, kept))]

    def block(b, carry):
        slot = b % 2

        @pl.when(b >= 2)
        def _():
            for copy in outs(b - 2, slot):
                copy.wait()

        z = ns.z[pl.ds(b * 32, 32)].reshape(256, wide)
        at = pl.ds(pl.multiple_of(b * 256, 256), 256)
        normed = ((z - mean) * inverse * gain + shift).astype(BF)
        ns.n_st[slot] = normed
        acc = jnp.zeros((256, wide), F32)
        for h in range(0, hidden, 256):
            cut = slice(h, h + 256)
            e = dot(normed, w1[:, cut]) + ns.bias[sec, 0:1, cut]
            phi = 0.5 + 0.5 * lax.erf(e * np.float32(0.5**0.5))
            act = (e * phi).astype(BF)
            ns.g_st[slot, :, cut] = act
            ns.gp_st[slot, :, cut] = (phi + e * (np.float32((2 * np.pi) ** -0.5) * jnp.exp(-0.5 * e * e))).astype(BF)
            acc = acc + dot(act, w2[cut])
        out = (lanes4(ns.ocean[at], wide) * (res[at].astype(F32) + (acc + par[51:52]))).astype(BF)
        if y is not None:
            y[at] = out
        for k in range(2):
            nat[:, 2 * b + k] = to_natural(out[128 * k : 128 * k + 128], ns.back[...], ns.gather[...])
        for copy in outs(b, slot):
            copy.start()
        for k in range(steps):
            pl.when(b == k)(functools.partial(hook, k))
        return carry

    lax.fori_loop(0, steps, block, 0)
    for b in (steps - 2, steps - 1):
        for copy in outs(b, b % 2):
            copy.wait()


def forward_kernel(fast, count, cols, ns):
    s, d, g, m, p = where_am_i()
    greet_near(count)
    x14 = ns.x14
    x_begin, x_end = collect(ns.x, x14, 3, ns.xs, ns.xr)
    land_begin, land_end = collect_land(ns.land, ns.land2, ns.ls, ns.lr)
    x_begin()
    land_begin()
    pairs = [(ns.mine, ns.par), (ns.mine_bias, ns.bias)] + [(getattr(ns, f"mine{k}"), getattr(ns, f"shard{k}")) for k in range(4) if fast]
    far = [remote(src, dst.at[s], ns.ps.at[k, 0], ns.pr.at[k], (1 - s, d)) for k, (src, dst) in enumerate(pairs)]
    near = [pltpu.make_async_copy(src, dst.at[s], ns.ps.at[k, 1]) for k, (src, dst) in enumerate(pairs)]
    for c in far + near:
        c.start()
    fulls = dict(w1_0=ns.w1_0, w2_0=ns.w2_0, r0=ns.r0, m0=ns.m0, m1=ns.m1, r1=ns.r1, w1_1=ns.w1_1, w2_1=ns.w2_1)
    which = dict(w1_0=(0, 0), w2_0=(1, 0), r0=(2, 0), r1=(2, 1), m0=(3, 0), m1=(3, 1), w1_1=(0, 1), w2_1=(1, 1))
    mats = {}
    for k, (name, full) in enumerate(fulls.items()):
        if fast:
            index, sec = which[name]
            mats[name] = Gather(getattr(ns, f"shard{index}").at[sec], full, ns.gs.at[k], ns.gr.at[k])
        else:
            mats[name] = Load(getattr(ns, name + "_in"), full, ns.gs.at[k])
    saves = {name: lambda k=k, name=name, full=full: pltpu.make_async_copy(full, getattr(ns, name + "_out"), ns.save.at[k]) for k, (name, full) in enumerate(fulls.items())}

    def do(step, *names):
        for name in names:
            getattr(mats[name], step)()

    def whole(*names):
        do("whole", *names)
        for name in names:
            saves[name]().start()

    if fast:
        for k in range(2, 6):
            near[k].wait()
            arrived(pairs[k][1].at[1 - s], ns.pr.at[k])
    do("start", "w1_0", "w2_0")
    do("start", "r0")
    land_end()
    masks(ns.land2, ns.ocean, ns.coarse, ns.pick[...], ns.patch[...])
    x_end()

    def edge(up):
        src, dst = (x14.at[pl.ds(3, 3)], x14.at[pl.ds(11, 3)]) if up else (x14.at[pl.ds(8, 3)], x14.at[pl.ds(0, 3)])
        return remote(src, dst, ns.hs.at[int(up)], ns.hr.at[int(up)], device(p - 1 if up else p + 1, m))

    pl.when(p > 0)(edge(True).start)
    pl.when(p < count - 1)(edge(False).start)
    do("plane", "w1_0", "w2_0")
    for k in range(2):
        near[k].wait()
        arrived(pairs[k][1].at[1 - s], ns.pr.at[k])

    @pl.when(p == 0)
    def _():
        x14[0:3] = jnp.zeros((3,) + x14.shape[1:], BF)

    @pl.when(p == count - 1)
    def _():
        x14[11:14] = jnp.zeros((3,) + x14.shape[1:], BF)

    pl.when(p > 0)(lambda: arrived(x14.at[pl.ds(0, 3)], ns.hr.at[0]))
    pl.when(p < count - 1)(lambda: arrived(x14.at[pl.ds(11, 3)], ns.hr.at[1]))

    cot_begin, cot_end = collect(ns.cot, ns.cot8, 0, ns.cs, ns.cr)
    act = deliver(0, ns.nat0, ns.act, ns.bounce, ns.ds_, ns.dr_, ns.db)

    conv_phase(0, cols, ns, script(
        lambda: (do("onward", "w1_0", "w2_0"), do("start", "m0", "m1", "r1")),
        lambda: do("plane", "r0"),
        lambda: do("over", "w1_0", "w2_0"),
        lambda: do("onward", "r0"),
        lambda: do("start", "w1_1", "w2_1"),
        lambda: do("plane", "m0", "m1", "r1"),
    ))
    ns.st0[...] = all_sum(ns.stats, ns.slots, ns.send, ns.recv, count)
    keep_z = pltpu.make_async_copy(ns.z, ns.z0, ns.keep.at[0])
    keep_z.start()
    whole("w1_0", "w2_0")
    ff0 = {0: lambda: do("over", "r0"), 1: lambda: do("onward", "m0", "m1", "r1"), 4: lambda: do("plane", "w1_1", "w2_1")}
    ff_phase(0, ns, ns.st0, ns.w1_0, ns.w2_0, ns.a0, ns.skip, ns.nat0, (ns.n0, ns.g0, ns.gp0), lambda k: ff0.get(k, lambda: None)())

    whole("r0")
    skip, pieces, wide = ns.skip, ns.pieces, ns.skip.shape[1]
    blocks = skip.shape[0] // 256
    down, up_w = ns.r0.reshape(4 * wide, -1), ns.r1.reshape(GROUPS, 2, ns.r1.shape[2] // 2, -1)
    merge = [v.reshape(wide, wide) for v in (ns.m0, ns.m1)]
    for b in range(blocks):
        moved = dot(ns.patch[...], skip[256 * b : 256 * b + 256]).astype(BF)
        for k in range(4):
            pieces[k, 64 * b : 64 * b + 64] = moved[64 * k : 64 * k + 64]
    value = sum(dot(pieces[k], down[wide * k : wide * k + wide]) for k in range(4))
    deep_value = (lanes4(ns.coarse[...], value.shape[1]) * value).astype(BF)
    ns.deep[...] = deep_value
    do("over", "m0", "m1", "r1")
    do("onward", "w1_1", "w2_1")
    act[0]()
    whole("m0", "m1", "r1")
    rows = up_w.shape[0] * up_w.shape[2]
    lifted = [dot(deep_value, up_w[:, i].reshape(rows, -1)).astype(BF) for i in range(2)]
    for b in range(blocks):
        at = slice(256 * b, 256 * b + 256)
        stacked = jnp.concatenate(
            [lifted[i][64 * b : 64 * b + 64, wide * j : wide * j + wide] for i in range(2) for j in range(2)], axis=0
        )
        ns.up[at] = dot(ns.unpatch[...], stacked).astype(BF)
        joined = dot(ns.up[at], merge[0][...]) + dot(skip[at], merge[1][...])
        ns.h[at] = joined
        low = joined.astype(BF)
        ns.a1[at] = low
        for k in range(2):
            ends = dot(ns.edges[...], low[128 * k : 128 * k + 128]).astype(BF)
            ns.packed[0, 2 * b + k] = ends[:48]
            ns.packed[1, 2 * b + k] = ends[48:]
    swap_rows(ns.packed, ns.halo, ns.es, ns.er, count)
    keep_z.wait()
    cot_begin()

    conv_phase(1, cols, ns, script(
        act[1],
        lambda: do("over", "w1_1", "w2_1"),
        lambda: whole("w1_1", "w2_1"),
    ))
    ns.st1[...] = all_sum(ns.stats, ns.slots1, ns.send1, ns.recv1, count)
    keep_z1 = pltpu.make_async_copy(ns.z, ns.z1, ns.keep.at[0])
    keep_z1.start()
    ff_phase(1, ns, ns.st1, ns.w1_1, ns.w2_1, ns.h, None, ns.nat1, (ns.n1, ns.g1, ns.gp1), lambda k: None)

    cot_end()
    act[3]()
    for name, save in saves.items():
        save().wait()
        do("finish", name)
    keep_z1.wait()
    for c in far:
        c.wait_send()
    pl.when(p > 0)(edge(True).wait_send)
    pl.when(p < count - 1)(edge(False).wait_send)


class Reduce:
    def __init__(self, sec, partial, bank, out, send, recv):
        self.sec, self.partial, self.out, self.send, self.recv = sec, partial, out, send, recv
        self.own, self.core, self.one, self.two, self.row, self.mine = bank
        self.s, self.d, self.g, self.m, _ = where_am_i()
        self.bit = 1 + self.s
        self.rest = self.m ^ (3 - self.bit)

    def near(self):
        return pltpu.make_async_copy(half(self.partial, self.s), self.own, self.send.at[0])

    def over(self):
        return remote(half(self.partial, 1 - self.s), self.core, self.send.at[1], self.recv.at[1], (1 - self.s, self.d))

    def first(self, index):
        col = (self.m ^ self.bit, self.m ^ 3)[index]
        return remote(self.own.at[:, col], self.one.at[:, index], self.send.at[2 + index], self.recv.at[2 + index], (self.s, self.d ^ self.bit))

    def second(self):
        return remote(self.own.at[:, self.rest], self.two, self.send.at[4], self.recv.at[4], (self.s, self.d ^ (3 - self.bit)))

    def along(self, step):
        to = (self.g + step) % 4
        return remote(self.own.at[to, self.m], self.row.at[step - 1], self.send.at[4 + step], self.recv.at[4 + step], (self.s, 4 * to + self.m))

    def give(self):
        return remote(self.mine, self.out.at[self.s], self.send.at[8], self.recv.at[8], (1 - self.s, self.d))

    def start(self):
        self.over().start()
        self.near().start()

    def plane(self):
        self.near().wait()
        arrived(self.core, self.recv.at[1])
        own, core, m, bit = self.own, self.core, self.m, self.bit

        def add(k, carry):
            z, col = k % 4, (m ^ 3, m ^ bit, m ^ (3 - bit), m)
            for c in col:
                own[z, c] = (own[z, c].astype(F32) + core[z, c].astype(F32)).astype(BF)
            return carry

        lax.fori_loop(0, 4, add, 0)
        self.first(1).start()
        self.first(0).start()

    def onward(self):
        own, one, rest = self.own, self.one, self.rest
        arrived(one.at[:, 1], self.recv.at[3])

        def add(z, carry):
            own[z, rest] = (own[z, rest].astype(F32) + one[z, 1].astype(F32)).astype(BF)
            return carry

        lax.fori_loop(0, 4, add, 0)
        self.second().start()

    def line(self):
        own, one, two, m = self.own, self.one, self.two, self.m
        arrived(one.at[:, 0], self.recv.at[2])
        arrived(two, self.recv.at[4])

        def add(z, carry):
            own[z, m] = (own[z, m].astype(F32) + one[z, 0].astype(F32) + two[z].astype(F32)).astype(BF)
            return carry

        lax.fori_loop(0, 4, add, 0)
        for step in range(1, 4):
            self.along(step).start()

    def total(self):
        for step in range(1, 4):
            arrived(self.row.at[step - 1], self.recv.at[4 + step])
        row = self.row
        self.mine[...] = self.own[self.g, self.m].astype(F32) + row[0].astype(F32) + row[1].astype(F32) + row[2].astype(F32)
        pl.when(self.s != self.sec)(lambda: self.give().start())

        @pl.when(self.s == self.sec)
        def _():
            self.out[self.s] = self.mine[...]

    def finish(self):
        self.over().wait_send()
        for index in range(2):
            self.first(index).wait_send()
        self.second().wait_send()
        for step in range(1, 4):
            self.along(step).wait_send()
        pl.when(self.s != self.sec)(lambda: self.give().wait_send())
        pl.when(self.s == self.sec)(lambda: arrived(self.out.at[1 - self.s], self.recv.at[8]))


def reduce_bank(name, shape):
    part = half_shape(shape)
    out = {f"{name}_{k}": pltpu.VMEM(lead + part, BF) for k, lead in (("own", (4, 4)), ("core", (4, 4)), ("one", (4, 2)), ("two", (4,)), ("row", (3,)))}
    out.update({f"{name}_mine": pltpu.VMEM(part, F32), f"{name}_s": DMA((9,)), f"{name}_r": DMA((9,))})
    return out


def reducer(ns, name, sec, partial, out):
    bank = [getattr(ns, f"{name}_{k}") for k in ("own", "core", "one", "two", "row", "mine")]
    return Reduce(sec, partial, bank, out, getattr(ns, f"{name}_s"), getattr(ns, f"{name}_r"))


def loads(pairs, sems, first=0):
    copies = [pltpu.make_async_copy(src, dst, sems.at[first + k]) for k, (src, dst) in enumerate(pairs)]
    for c in copies:
        c.start()
    return [c.wait for c in copies]


def back_ff_phase(sec, count, ns, top, kept, w_in, w_out, hook, done):
    z_in, st, n_in, g_in, gp_in = kept
    cells, wide = ns.dym.shape
    hidden = w_in.shape[1]
    chunks = cells // 128
    ocean, small, dr_rows, dym = ns.ocean, ns.small, None, ns.dym
    counted, mean, inverse, gain, shift = norm_terms(st, ns.par[sec])

    def phase(w1, w2, z, n, g, gp, dn, dr):
        def columns(h):
            at, slot = pl.ds(256 * h, 256), h % 2
            return [pltpu.make_async_copy(src.at[:, at], dst.at[slot], ns.col_sem.at[k, slot]) for k, (src, dst) in enumerate(((g_in, g), (gp_in, gp)))]

        got_w2, got_w1, got_n, got_z = loads([(w_out, w2), (w_in, w1), (n_in, n), (z_in, z)], ns.load_sem)
        for copy in columns(0):
            copy.start()

        def begin(c, total):
            at = pl.ds(pl.multiple_of(c * 128, 128), 128)
            if sec == 1:
                block = top[:, c]
                block = dot(block.reshape(-1, block.shape[-1]), ns.spread[...]).astype(BF)
                grad = dot(ns.turn[...], block)
            else:
                grad = top[at]
            grad = grad * lanes4(ocean[at], wide)
            dym[at] = grad
            low = grad.astype(BF)
            dr[at] = low
            return total + rows8(low.astype(F32))

        total = lax.fori_loop(0, chunks, begin, jnp.zeros((8, wide), F32))
        small[2:3] = total.sum(0, keepdims=True)
        small[3:8] = jnp.zeros((5, wide), F32)
        got_w2()
        for h in range(hidden // 256):
            at, slot = slice(256 * h, 256 * h + 256), h % 2
            if h + 1 < hidden // 256:
                for copy in columns(h + 1):
                    copy.start()
            dg = dot_nt(dr[...], w2[at])
            if h == 0:
                got_n()
                got_w1()
            for copy in columns(h):
                copy.wait()
            de = (dg * gp[slot].astype(F32)).astype(BF)
            row, col = 3 + 256 * h // wide, 256 * h % wide
            small[row : row + 1, col : col + 256] = de.astype(F32).sum(0, keepdims=True)
            ns.dw1[:, at] = dot_tn(n[...], de).astype(BF)
            ns.dw2[at] = dot_tn(g[slot], dr[...]).astype(BF)
            part = dot_nt(de, w1[:, at])
            if h == 0:
                dn[...] = part
            else:
                dn[...] += part
            hook(h)
        done()
        got_z()

        def sums(c, carry):
            at = pl.ds(pl.multiple_of(c * 128, 128), 128)
            grad = dn[at]
            return carry[0] + rows8(grad), carry[1] + rows8(grad * ((z[at] - mean) * inverse))

        zero = jnp.zeros((8, wide), F32)
        plain, scaled = lax.fori_loop(0, chunks, sums, (zero, zero))
        small[0:1] = plain.sum(0, keepdims=True)
        small[1:2] = scaled.sum(0, keepdims=True)
        ns.stats[...] = small[...]
        summed = all_sum(ns.stats, ns.slots, ns.send, ns.recv, count)
        first = -inverse * gain * summed[0:1] / counted
        second = -inverse * inverse * gain * summed[1:2] / counted

        def end(c, carry):
            at = pl.ds(pl.multiple_of(c * 128, 128), 128)
            grad = inverse * gain * dn[at] + lanes4(ocean[at], wide) * (first + second * (z[at] - mean))
            low = grad.astype(BF)
            ns.dz[at] = low
            ends = dot(ns.edges[...], low).astype(BF)
            ns.packed[0, c] = ends[:48]
            ns.packed[1, c] = ends[48:]
            return carry

        lax.fori_loop(0, chunks, end, 0)

    field = lambda t: pltpu.VMEM((cells, wide), t)
    pl.run_scoped(
        phase, pltpu.VMEM(w_in.shape, BF), pltpu.VMEM(w_out.shape, BF), field(F32), field(BF),
        pltpu.VMEM((2, cells, 256), BF), pltpu.VMEM((2, cells, 256), BF), field(F32), field(BF),
    )
    swap_rows(ns.packed, ns.halo, ns.hsend, ns.hrecv, count)


def back_conv_phase(sec, cols, ns, a_in, tiny, hook):
    cells, wide = ns.dz.shape
    dz = ns.dz

    def phase(S, kb, acc_dk, a):
        (got_a,) = loads([(a_in, a)], ns.load_sem)
        taps_to(kb, ns.par[sec], True)
        acc_dk[...] = jnp.zeros(acc_dk.shape, F32)
        lanes = S.shape[1]
        for group in range(wide // 128 // lanes):
            part = slice(group * lanes * 128, (group + 1) * lanes * 128)

            def chunk(c, carry):
                block = jnp.concatenate([dz[pl.ds(pl.multiple_of(c * 128, 128), 128), part], ns.halo[0, c, :, part], ns.halo[1, c, :, part]], axis=0)
                shifted(block, ns.shifts[...], S, c)
                return carry

            lax.fori_loop(0, cols // 16, chunk, 0)
            wrap(S, cols)
            hook()
            if group == 0:
                got_a()
            for lane in range(lanes):
                at = slice((group * lanes + lane) * 128, (group * lanes + lane + 1) * 128)

                def step(b, carry):
                    rows = pl.ds(pl.multiple_of(b * 64, 64), 64)
                    acc = ns.dym[rows, at].reshape(8, 8, 128)
                    field = a[rows, at].astype(F32).reshape(8, 8, 128)
                    for i in range(7):
                        window = S[i, lane, pl.ds(b * 8, 14)]
                        for j in range(7):
                            acc = acc + window[j : j + 8] * kb[7 * i + j, :, at][None]
                            acc_dk[7 * i + j, :, at] += (window[j : j + 8] * field).sum(0)
                    dz[rows, at] = acc.reshape(64, 128).astype(BF)
                    return carry

                lax.fori_loop(0, cols // 8, step, 0)
                hook()
        for k in range(49):
            tiny[48 - k : 49 - k] = acc_dk[k].sum(0, keepdims=True)
        tiny[49:56] = jnp.zeros((7, wide), F32)

    pl.run_scoped(
        phase, pltpu.VMEM((7, 2, cols + 6, 8, 128), F32), pltpu.VMEM((49, 8, wide), F32), pltpu.VMEM((49, 8, wide), F32), pltpu.VMEM((cells, wide), BF)
    )


def back_mid_phase(ns, hook):
    dh = ns.dz
    cells, wide = dh.shape
    blocks = cells // 256

    def phase(skip, up, merge0, merge1, up_w, deep, down, pieces, dups, spreads):
        got = loads(
            [(ns.up, up), (ns.skip, skip), (ns.m1, merge1), (ns.m0, merge0), (ns.r1, up_w), (ns.deep, deep), (ns.pieces, pieces), (ns.r0, down)],
            ns.load_sem,
        )
        for k in range(4):
            got[k]()
        ns.dm0[...] = dot_tn(up[...], dh[...]).astype(BF)
        ns.dm1[...] = dot_tn(skip[...], dh[...]).astype(BF)
        hook(0)
        for b in range(blocks):
            at = slice(256 * b, 256 * b + 256)
            low = dot_nt(dh[at], merge1[...]).astype(BF)
            ns.dym[at] = low.astype(F32)
            for k in range(2):
                ns.nat[:, 2 * b + k] = to_natural(low[128 * k : 128 * k + 128], ns.back[...], ns.gather[...])
            lifted = dot_nt(dh[at], merge0[...]).astype(BF)
            moved = dot(ns.patch[...], lifted).astype(BF)
            for k in range(4):
                dups[k // 2, 64 * b : 64 * b + 64, wide * (k % 2) : wide * (k % 2) + wide] = moved[64 * k : 64 * k + 64]
        hook(1)
        rows = up_w.shape[0] * up_w.shape[2]
        got[4]()
        ddeep = dot_nt(dups[0], up_w[:, 0].reshape(rows, -1)) + dot_nt(dups[1], up_w[:, 1].reshape(rows, -1))
        got[5]()
        for i in range(2):
            ns.dr1[:, i] = dot_tn(deep[...], dups[i]).astype(BF).reshape(up_w.shape[0], up_w.shape[2], -1)
        masked = (lanes4(ns.coarse[...], ddeep.shape[1]) * ddeep).astype(BF)
        hook(2)
        got[6]()
        got[7]()
        for k in range(4):
            ns.dr0[wide * k : wide * k + wide] = dot_tn(pieces[k], masked).astype(BF)
            spreads[k] = dot_nt(masked, down[wide * k : wide * k + wide])
        hook(3)
        for b in range(blocks):
            value = jnp.concatenate([spreads[k, 64 * b : 64 * b + 64] for k in range(4)], axis=0)
            high = value.astype(BF)
            rest = (value - high.astype(F32)).astype(BF)
            at = slice(256 * b, 256 * b + 256)
            ns.dym[at] += dot(ns.unpatch[...], high) + dot(ns.unpatch[...], rest)

    like = lambda ref: pltpu.VMEM(ref.shape, BF)
    deep_cells = ns.deep.shape[0]
    pl.run_scoped(
        phase, like(ns.skip), like(ns.up), like(ns.m0), like(ns.m1), like(ns.r1), like(ns.deep), like(ns.r0), like(ns.pieces),
        pltpu.VMEM((2, deep_cells, 2 * wide), BF), pltpu.VMEM((4, deep_cells, wide), F32),
    )


def back_decoder_kernel(fast, count, cols, ns):
    greet_near(count)
    act = deliver(1, ns.nat1, ns.act, ns.bounce, ns.ds_, ns.dr_, ns.db)
    act[0]()
    sums = []
    if fast:
        grid = lambda ref, like: ref.reshape((4, 4) + like.shape[-2:])
        sums = [reducer(ns, f"w{k}", 1, ref, out) for k, (ref, out) in enumerate(((ns.dw1.reshape(4, 4, -1, ns.dw1.shape[1]), ns.gw1), (ns.dw2.reshape(4, 4, -1, ns.dw2.shape[1]), ns.gw2)))]

    def all_(step):
        return lambda: [getattr(r, step)() for r in sums]

    back_ff_phase(1, count, ns, ns.top, (ns.z, ns.st, ns.n, ns.g, ns.gp), ns.w1, ns.w2, lambda h: act[1]() if h == 2 else None, all_("start"))
    back_conv_phase(1, cols, ns, ns.a, ns.tiny, script(all_("plane"), nothing, all_("onward"), act[3], nothing, all_("line")))
    ns.tiny[56:64] = ns.small[...]
    back_mid_phase(ns, script(nothing, all_("total"), nothing, nothing))
    all_("finish")()


def back_encoder_kernel(fast, count, cols, ns):
    s, d, g, m, p = where_am_i()
    greet_near(count)
    gi1 = deliver(1, ns.nat1, ns.gi, ns.bounce1, ns.ds1, ns.dr1_, ns.db1)
    gi0 = deliver(0, ns.nat0, ns.gi, ns.bounce0, ns.ds0, ns.dr0_, ns.db0)
    deep, mats = [], []
    if fast:
        deep = [reducer(ns, f"r{k}", sec, getattr(ns, part), getattr(ns, out)) for k, (sec, part, out) in enumerate(
            ((0, "pr0", "gr0"), (1, "pr1", "gr1"), (0, "pm0", "gm0"), (1, "pm1", "gm1")))]
        mats = [reducer(ns, f"w{k}", 0, ref, out) for k, (ref, out) in enumerate(((ns.dw1.reshape(4, 4, -1, ns.dw1.shape[1]), ns.gw1), (ns.dw2.reshape(4, 4, -1, ns.dw2.shape[1]), ns.gw2)))]

    def all_(step, group):
        return lambda: [getattr(r, step)() for r in group]

    all_("start", deep)()
    gi1[0]()
    steps = {1: all_("plane", deep), 3: gi1[1]}
    back_ff_phase(0, count, ns, ns.top, (ns.z, ns.st, ns.n, ns.g, ns.gp), ns.w1, ns.w2, lambda h: steps.get(h, nothing)(), all_("start", mats))
    back_conv_phase(0, cols, ns, ns.a, ns.tiny0, script(
        all_("onward", deep), all_("plane", mats), all_("line", deep), lambda: (all_("onward", mats)(), gi1[3]()), nothing, all_("line", mats)))
    ns.tiny0[56:64] = ns.small[...]

    def out(c, carry):
        cells = ns.dz[pl.ds(pl.multiple_of(c * 128, 128), 128)]
        ns.nat0[:, c] = to_natural(cells, ns.back[...], ns.gather[...])
        return carry

    lax.fori_loop(0, cols // 16, out, 0)
    gi0[0]()
    all_("total", deep)()
    if fast:
        sm, tiny, ts, tr = ns.sm, ns.tiny, ns.ts, ns.tr
        sm[0] = ns.tiny0[...]
        sm[1] = ns.tiny1[...]
        over = remote(sm.at[1 - s], tiny.at[0], ts.at[0], tr.at[0], (1 - s, d))
        over.start()
        arrived(tiny.at[0], tr.at[0])
        over.wait_send()
        tiny[1] = sm[s] + tiny[0]
        for base, peer in ((1, lambda step: (s, 4 * ((g + step) % 4) + m)), (5, lambda step: (s, d ^ step))):
            sent = [remote(tiny.at[base], tiny.at[base + step], ts.at[base + step], tr.at[base + step], peer(step)) for step in range(1, 4)]
            for c in sent:
                c.start()
            if base == 1:
                gi0[1]()
            for step in range(1, 4):
                arrived(tiny.at[base + step], tr.at[base + step])
            for c in sent:
                c.wait_send()
            total = tiny[base] + tiny[base + 1] + tiny[base + 2] + tiny[base + 3]
            if base == 1:
                tiny[5] = total
            else:
                ns.total[...] = total
    else:
        gi0[1]()
        ns.total[...] = ns.tiny0[...]
    all_("total", mats)()
    all_("finish", deep + mats)()
    gi0[3]()


class Names:
    pass


def build(name, body, ins, outs, scratch, alias, cid, limit):
    ins = {k: v if isinstance(v, tuple) else (v, VM) for k, v in ins.items()}
    outs = {k: v if len(v) == 3 else v + (VM,) for k, v in outs.items()}
    names = list(ins) + list(outs) + list(scratch)

    def kernel(*refs):
        ns = Names()
        for k, ref in zip(names, refs):
            setattr(ns, k, ref)
        body(ns)

    order_in, order_out = list(ins), list(outs)
    results = pl.pallas_call(
        kernel, name=name, out_shape=[jax.ShapeDtypeStruct(v[0], v[1]) for v in outs.values()],
        in_specs=[v[1] for v in ins.values()], out_specs=[v[2] for v in outs.values()], scratch_shapes=list(scratch.values()),
        input_output_aliases={order_in.index(a): order_out.index(b) for a, b in alias.items()},
        compiler_params=pltpu.CompilerParams(vmem_limit_bytes=limit * MEGA, collective_id=cid, has_side_effects=True),
    )(*[v[0] for v in ins.values()])
    out = Names()
    for k, v in zip(order_out, results):
        setattr(out, k, v)
    return out


def on_device(sections, dps, inputs, cotangent, land, kernel, bn_gain, bn_bias, bias_in, bias_out, w_in, w_out, resample, merge):
    batches, height, cols, c = inputs.shape
    hid = bias_in.shape[1]
    n = resample.shape[1] * dps // (4 * c)
    cw, hw, nw = (GROUPS * padded(v) for v in (c, hid, n))
    cells, deep_cells = cols * 8, cols * 2
    count = 2 * (dps // 4)
    fast = dps == GROUPS
    assert batches == 4 and height == 4 and dps % 4 == 0 and sections == 2 and cols % 32 == 0
    s = lax.axis_index("section")
    mats = {k: jnp.asarray(v) for k, v in matrices(c).items()}
    tiles = cols // 16
    both = ("section", "dp")

    def packs(parts, w1, w2, rd, ru):
        return pack_in(w1, parts, c, hid), pack_in(w2, parts, hid, c), pack_down(rd, parts, c, n), pack_up(ru, parts, c, n)

    shards = []
    if fast:
        w1, w2, rd, ru = packs(1, *(v.astype(BF) for v in (w_in, w_out, resample, resample)))
        shards = [w1[0], w2[0], jnp.where(s == 0, rd, ru)[0], pack_in(merge.astype(BF), 1, c, c)[0]]
    else:
        flat = [lax.all_gather(v.astype(BF).reshape(-1), both, axis=0, tiled=True) for v in (w_in, w_out, resample, merge)]
        halves = [v.reshape(2, -1) for v in flat]
        whole = [packs(GROUPS, halves[0][k], halves[1][k], halves[2][k], halves[2][k]) for k in range(2)]

    rows = jnp.concatenate([kernel[0], bn_gain, bn_bias, bias_out], axis=0)
    mine = grow(grow(rows.reshape(-1, GROUPS, c // GROUPS), (52, GROUPS, padded(c))).reshape(52, cw), (56, cw))
    mine_bias = grow(grow(bias_in.reshape(GROUPS, -1), (GROUPS, padded(hid))).reshape(1, hw), (8, hw))
    x = inputs.reshape(batches, height, tiles, 16, c)
    cot = cotangent.reshape(batches, height, tiles, 16, c)
    land_cols = -(-cols // 128) * 128
    at_any = lambda v: (v, ANY)
    field = lambda t: ((cells, cw), t)
    natural = ((8, tiles, 16, c), BF)
    edge_rows = ((2, tiles, 48, cw), BF)
    shapes = [(padded(c), hw), (padded(hid), cw), (4 * padded(c), nw), (padded(c), cw)]
    names = dict(w1_0=0, w2_0=1, r0=2, m0=3, m1=3, r1=2, w1_1=0, w2_1=1)
    ins = dict(x=x, land=grow(land, (8, land_cols)), mine=mine, mine_bias=mine_bias, cot=cot)
    if fast:
        ins.update({f"mine{k}": v for k, v in enumerate(shards)})
    else:
        given = dict(w1_0=whole[0][0], w2_0=whole[0][1], r0=whole[0][2], r1=whole[1][3], w1_1=whole[1][0], w2_1=whole[1][1])
        given.update(m0=pack_in(halves[3][0], GROUPS, c, c), m1=pack_in(halves[3][1], GROUPS, c, c))
        ins.update({k + "_in": v.reshape((4, 4) + shapes[names[k]]) for k, v in given.items()})
    ins = {k: at_any(v) for k, v in ins.items()}
    ins.update({k: mats[k] for k in ("spread", "gather", "natural", "shifts", "patch", "unpatch", "edges", "back", "pick")})
    outs = dict(
        par=((2, 56, cw), F32), bias=((2, 8, hw), F32), ocean=((cells, 128), F32), coarse=((deep_cells, 128), F32),
        st0=((8, cw), F32), st1=((8, cw), F32), a0=field(BF), a1=field(BF), skip=field(BF), up=field(BF),
        pieces=((4, deep_cells, cw), BF), deep=((deep_cells, nw), BF), nat1=natural,
        z0=((cols, 8, cw), F32, ANY), z1=((cols, 8, cw), F32, ANY), cot8=natural + (ANY,), act=((4, 4, tiles, 16, c), BF, ANY),
    )
    for k in range(2):
        outs.update({f"n{k}": field(BF) + (ANY,), f"g{k}": ((cells, hw), BF, ANY), f"gp{k}": ((cells, hw), BF, ANY)})
    outs.update({k + "_out": ((4, 4) + shapes[v], BF, ANY) for k, v in names.items()})
    scratch = dict(
        x14=pltpu.VMEM((14, tiles, 16, c), BF), land2=pltpu.VMEM((2, 8, land_cols), jnp.int32),
        S=pltpu.VMEM((7, 2, cols + 6, 8, 128), F32), kb=pltpu.VMEM((49, 8, cw), F32), z=pltpu.VMEM((cols, 8, cw), F32),
        h=pltpu.VMEM((cells, cw), F32), n_st=pltpu.VMEM((2, 256, cw), BF), g_st=pltpu.VMEM((2, 256, hw), BF), gp_st=pltpu.VMEM((2, 256, hw), BF),
        nat0=pltpu.VMEM(*natural), bounce=pltpu.VMEM(*natural), halo=pltpu.VMEM(*edge_rows), packed=pltpu.VMEM(*edge_rows),
        stats=pltpu.VMEM((8, cw), F32), slots=pltpu.VMEM((count // 2 + 1, 8, cw), F32), slots1=pltpu.VMEM((count // 2 + 1, 8, cw), F32),
        send=DMA((count,)), recv=DMA((count,)), send1=DMA((count,)), recv1=DMA((count,)),
        xs=DMA((4,)), xr=DMA((2,)), ls=DMA((4,)), lr=DMA((2,)), hs=DMA((2,)), hr=DMA((2,)), ps=DMA((6, 2)), pr=DMA((6,)), cs=DMA((4,)), cr=DMA((2,)),
        ds_=DMA((2, 2)), dr_=DMA((4,)), db=DMA((2,)), es=DMA((2,)), er=DMA((2,)), gs=DMA((8, 12)), gr=DMA((8, 12)), save=DMA((8,)), keep=DMA((2,)),
        ff_sem=DMA((3, 2)),
    )
    scratch.update({k: pltpu.VMEM((4, 4) + shapes[v], BF) for k, v in names.items()})
    if fast:
        scratch.update({f"shard{k}": pltpu.VMEM((2,) + shapes[k], BF) for k in range(4)})
    fw = build("forward", lambda ns: forward_kernel(fast, count, cols, ns), ins, outs, scratch, {}, 1, 63)
    par, ocean, coarse, bias = fw.par, fw.ocean, fw.coarse, fw.bias
    w1_0, w2_0, w1_1, w2_1 = (v.reshape(r) for v, r in zip((fw.w1_0_out, fw.w2_0_out, fw.w1_1_out, fw.w2_1_out), ((cw, hw), (hw, cw)) * 2))
    r0, r1 = fw.r0_out.reshape(4 * cw, nw), fw.r1_out.reshape(GROUPS, 2, padded(n), 2 * cw)

    def kept(k):
        names = ("z", "st", "n", "g", "gp", "a")
        ins = {v: at_any(getattr(fw, f"{v}{k}")) for v in names}
        ins["z"] = at_any(ins["z"][0].reshape(cells, cw))
        ins["st"] = getattr(fw, f"st{k}")
        return ins

    mats_of = lambda *names: {k: mats[k] for k in names}
    common = dict(par=par, ocean=ocean, **mats_of("shifts", "edges", "back", "gather"))
    outs_w = dict(gw1=((2,) + half_shape(shapes[0]), F32), gw2=((2,) + half_shape(shapes[1]), F32)) if fast else {}
    wide_w = dict(dw1=((cw, hw), BF), dw2=((hw, cw), BF))
    rows_of = lambda names: {k: pltpu.VMEM(*v) for k, v in names.items()}
    small_space = dict(
        dz=pltpu.VMEM(*field(BF)), packed=pltpu.VMEM(*edge_rows), halo=pltpu.VMEM(*edge_rows), small=pltpu.VMEM((8, cw), F32),
        stats=pltpu.VMEM((8, cw), F32), slots=pltpu.VMEM((count // 2 + 1, 8, cw), F32), send=DMA((count,)), recv=DMA((count,)),
        hsend=DMA((2,)), hrecv=DMA((2,)), load_sem=DMA((8,)), col_sem=DMA((2, 2)),
    )
    banks = {}
    if fast:
        banks = {**reduce_bank("w0", shapes[0]), **reduce_bank("w1", shapes[1])}
    give_w = not fast
    bounce = natural + (ANY,)
    dec_outs = dict(
        act=((4, 4, tiles, 16, c), BF, ANY), bounce=bounce, tiny=((64, cw), F32), dym=field(F32), nat=natural,
        dm0=((cw, cw), BF), dm1=((cw, cw), BF), dr1=((GROUPS, 2, padded(n), 2 * cw), BF), dr0=((4 * cw, nw), BF), **outs_w,
    )
    if give_w:
        dec_outs.update(wide_w)
    dec = build(
        "decoder_back", lambda ns: back_decoder_kernel(fast, count, cols, ns),
        dict(
            nat1=at_any(fw.nat1), act_in=at_any(fw.act), top=fw.cot8, w1=at_any(w1_1), w2=at_any(w2_1), **kept(1),
            up=at_any(fw.up), skip=at_any(fw.skip), deep=at_any(fw.deep), pieces=at_any(fw.pieces), r0=at_any(r0), r1=at_any(r1),
            m0=at_any(fw.m0_out.reshape(cw, cw)), m1=at_any(fw.m1_out.reshape(cw, cw)), coarse=coarse,
            **common, **mats_of("spread", "turn", "patch", "unpatch"),
        ),
        dec_outs, dict(ds_=DMA((2, 2)), dr_=DMA((4,)), db=DMA((2,)), **small_space, **banks, **({} if give_w else rows_of(wide_w))), {"act_in": "act"}, 2, 63,
    )
    enc_ins = dict(
        nat1=at_any(dec.nat), top=dec.dym, tiny1=dec.tiny, w1=at_any(w1_0), w2=at_any(w2_0), **kept(0), **common,
    )
    enc_outs = dict(gi=((4, 4, tiles, 16, c), BF, ANY), bounce0=bounce, bounce1=bounce, total=((64, cw), F32), **outs_w)
    enc_banks = dict(banks)
    if fast:
        view = lambda v, k: at_any(v.reshape((4, 4) + shapes[k]))
        enc_ins.update(pr0=view(dec.dr0, 2), pr1=view(dec.dr1, 2), pm0=view(dec.dm0, 3), pm1=view(dec.dm1, 3))
        for name, k in (("r0", 2), ("r1", 2), ("r2", 3), ("r3", 3)):
            enc_banks.update(reduce_bank(name, shapes[k]))
        for name, k in (("gr0", 2), ("gr1", 2), ("gm0", 3), ("gm1", 3)):
            enc_outs[name] = ((2,) + half_shape(shapes[k]), F32)
        enc_banks.update(sm=pltpu.VMEM((2, 64, cw), F32), tiny=pltpu.VMEM((9, 64, cw), F32), ts=DMA((9,)), tr=DMA((9,)))
    if give_w:
        enc_outs.update(wide_w)
    enc = build(
        "encoder_back", lambda ns: back_encoder_kernel(fast, count, cols, ns), enc_ins, enc_outs,
        dict(
            nat0=pltpu.VMEM(*natural), dym=pltpu.VMEM(*field(F32)), tiny0=pltpu.VMEM((64, cw), F32), ds0=DMA((2, 2)), dr0_=DMA((4,)), db0=DMA((2,)),
            ds1=DMA((2, 2)), dr1_=DMA((4,)), db1=DMA((2,)), **small_space, **enc_banks, **({} if give_w else rows_of(wide_w)),
        ),
        {}, 3, 63,
    )
    last, tiny = enc, enc.total
    if fast:
        rows_of = lambda v: v.reshape(-1, v.shape[-1])
        gw1 = unpack_in(rows_of(jnp.where(s == 0, enc.gw1, dec.gw1)), c, hid)
        gw2 = unpack_in(jnp.where(s == 0, enc.gw2, dec.gw2).transpose(1, 0, 2).reshape(padded(hid), cw), hid, c)
        gres = jnp.where(s == 0, unpack_down(rows_of(enc.gr0), c, n), unpack_up(rows_of(enc.gr1), c, n))
        gmm = unpack_in(rows_of(jnp.where(s == 0, enc.gm0, enc.gm1)), c, c)
    else:
        scatter = lambda v: lax.psum_scatter(v.astype(F32).reshape(-1), both, scatter_dimension=0, tiled=True)
        gw1 = scatter(jnp.stack([unpack_in(v, c, hid) for v in (enc.dw1, dec.dw1)]))
        gw2 = scatter(jnp.stack([unpack_in(v, hid, c) for v in (enc.dw2, dec.dw2)]))
        gres = scatter(jnp.stack([unpack_down(dec.dr0, c, n), unpack_up(dec.dr1, c, n)]))
        gmm = scatter(jnp.stack([unpack_in(v, c, c) for v in (dec.dm0, dec.dm1)]))
        tiny = lax.psum(jnp.stack([enc.total, dec.tiny]), both)[s]
    activations = dec.act.reshape(1, batches, height, cols, c)
    grad_input = last.gi.astype(F32).reshape(1, batches, height, cols, c)
    narrow = lambda v: v.reshape(-1, GROUPS, padded(c))[:, :, : c // GROUPS].reshape(-1, c)
    fine = narrow(tiny[:59])
    grad_bias_in = tiny[59:63].reshape(-1)[:hw].reshape(GROUPS, -1)[:, : hid // GROUPS].reshape(1, hid)
    return (
        activations, grad_input, fine[None, :49], fine[57:58], fine[56:57], grad_bias_in, fine[58:59],
        gw1[None], gw2[None], gres[None], gmm,
    )


def solution(mesh):
    sections, dps = mesh.shape["section"], mesh.shape["dp"]
    flat, both = P("section", "dp"), P(("section", "dp"))
    per = P("section", None)
    rows = P(None, "dp", None, None)
    taps = P("section", None, None)
    fields = P("section", None, "dp", None, None)
    return jax.shard_map(
        functools.partial(on_device, sections, dps), mesh=mesh,
        in_specs=(rows, rows, P("dp", None), taps, per, per, per, per, flat, flat, flat, both),
        out_specs=(fields, fields, taps, per, per, per, per, flat, flat, flat, both), check_vma=False,
    )
```

```python
import functools

import jax
import jax.numpy as jnp
import ml_dtypes
import numpy as np
from jax import lax
from jax.experimental import pallas as pl
from jax.experimental.pallas import tpu as pltpu
from jax.sharding import PartitionSpec as P

BF = jnp.bfloat16
F32 = jnp.float32
MESH = pl.DeviceIdType.MESH
ANY = pl.BlockSpec(memory_space=pl.ANY)
VM = pl.BlockSpec(memory_space=pltpu.VMEM)
DMA = pltpu.SemaphoreType.DMA
EPS = 1e-05
GROUPS = 16
MEGA = 1 << 20


def padded(width):
    return -(-(width // GROUPS) // 16) * 16


def selector(rows, cols, pairs):
    out = np.zeros((rows, cols), np.float32)
    for r, c in pairs:
        out[r, c] = 1
    return out.astype(ml_dtypes.bfloat16)


def matrices(channels):
    group, wide = channels // GROUPS, padded(channels)
    spread = selector(channels, GROUPS * wide, [(c, c // group * wide + c % group) for c in range(channels)])
    natural = selector(896, 224, [(i * 128 + q * 8 + p, (p + i) * 16 + q) for i in range(7) for q in range(16) for p in range(8)])

    def place(q, row):
        if row < 0:
            return 128 + q * 3 + row + 3
        return q * 8 + row if row < 8 else 176 + q * 3 + row - 8

    shifts = selector(896, 224, [(i * 128 + q * 8 + p, place(q, p + i - 3)) for i in range(7) for q in range(16) for p in range(8)])
    turn = selector(128, 128, [(q * 8 + p, p * 16 + q) for q in range(16) for p in range(8)])
    edges = selector(96, 128, [(48 * e + q * 3 + k, q * 8 + 5 * e + k) for e in range(2) for q in range(16) for k in range(3)])
    patch = selector(
        256, 256,
        [((i * 2 + j) * 64 + b * 4 + a, (2 * b + j) * 8 + 2 * a + i) for i in range(2) for j in range(2) for b in range(16) for a in range(4)],
    )
    pick = selector(128, 16, [(q * 8 + p, p // 4 * 8 + p % 4) for q in range(16) for p in range(8)])
    return dict(
        pick=pick, spread=spread, gather=np.ascontiguousarray(spread.T), natural=natural, shifts=shifts, turn=turn,
        back=np.ascontiguousarray(turn.T), edges=edges, patch=patch, unpatch=np.ascontiguousarray(patch.T),
    )


def grow(value, sizes):
    return jnp.pad(value, [(0, n - o) for n, o in zip(sizes, value.shape)])


def pack_in(value, parts, c, h):
    value = value.reshape(parts, c // GROUPS, GROUPS, h // GROUPS)
    return grow(value, (parts, padded(c), GROUPS, padded(h))).reshape(parts, padded(c), -1)


def pack_down(value, parts, c, n):
    value = value.reshape(parts, 4, c // GROUPS, GROUPS, n // GROUPS)
    return grow(value, (parts, 4, padded(c), GROUPS, padded(n))).reshape(parts, 4 * padded(c), -1)


def pack_up(value, parts, c, n):
    value = value.reshape(parts, n // GROUPS, 2, 2 * GROUPS, c // GROUPS)
    value = grow(value, (parts, padded(n), 2, 2 * GROUPS, padded(c)))
    return value.transpose(0, 2, 1, 3, 4).reshape(parts, 2 * padded(n), -1)


def unpack_in(value, c, h):
    value = value.reshape(-1, padded(c), GROUPS, padded(h))
    return value[:, : c // GROUPS, :, : h // GROUPS].reshape(-1)


def unpack_down(value, c, n):
    value = value.reshape(-1, 4, padded(c), GROUPS, padded(n))
    return value[:, :, : c // GROUPS, :, : n // GROUPS].reshape(-1)


def unpack_up(value, c, n):
    value = value.reshape(-1, 2, padded(n), 2 * GROUPS, padded(c))
    return value.transpose(0, 2, 1, 3, 4)[:, : n // GROUPS, :, :, : c // GROUPS].reshape(-1)


def device(p, m):
    g = p // 2
    return (p + g) % 2, 4 * g + m


def where_am_i():
    s, d = lax.axis_index("section"), lax.axis_index("dp")
    g = d // 4
    return s, d, g, d % 4, 2 * g + (s + g) % 2


def greet_near(count):
    s, d, g, m, p = where_am_i()
    barrier = pltpu.get_barrier_semaphore()

    def one(k, carry):
        q = (p + k) % count
        pl.semaphore_signal(barrier, inc=1, device_id=device(q, m), device_id_type=MESH)
        return carry

    lax.fori_loop(1, count, one, 0)
    for k in range(1, 4):
        for sec in range(2):
            pl.semaphore_signal(barrier, inc=1, device_id=(sec, 4 * g + (m + k) % 4), device_id_type=MESH)
    pl.semaphore_wait(barrier, count + 5)


def remote(src, dst, send, recv, peer):
    return pltpu.make_async_remote_copy(src_ref=src, dst_ref=dst, send_sem=send, recv_sem=recv, device_id=peer, device_id_type=MESH)


def arrived(ref, sem):
    pltpu.make_async_copy(ref, ref, sem).wait()


def all_sum(mine, slots, send, recv, count):
    s, d, g, m, p = where_am_i()
    groups = count // 2
    over = remote(mine, slots.at[groups], send.at[0], recv.at[0], (1 - s, d))
    over.start()
    arrived(slots.at[groups], recv.at[0])
    slots[g] = mine[...] + slots[groups]
    over.wait_send()

    def copy(k):
        return remote(slots.at[g], slots.at[g], send.at[k], recv.at[k], (s, 4 * ((g + k) % groups) + m))

    lax.fori_loop(1, groups, lambda k, c: (copy(k).start(), c)[1], 0)

    def wait(k, carry):
        arrived(slots.at[(g + groups - k) % groups], recv.at[k])
        copy(k).wait_send()
        return carry

    lax.fori_loop(1, groups, wait, 0)
    return lax.fori_loop(0, groups, lambda k, total: total + slots[k], jnp.zeros(mine.shape, F32))


def swap_rows(packed, halo, send, recv, count):
    s, d, g, m, p = where_am_i()

    def peer(q):
        return device(q, m)

    @pl.when(p > 0)
    def _():
        remote(packed.at[0], halo.at[1], send.at[0], recv.at[1], peer(p - 1)).start()

    @pl.when(p < count - 1)
    def _():
        remote(packed.at[1], halo.at[0], send.at[1], recv.at[0], peer(p + 1)).start()

    @pl.when(p > 0)
    def _():
        arrived(halo.at[0], recv.at[0])
        remote(packed.at[0], halo.at[1], send.at[0], recv.at[1], peer(p - 1)).wait_send()

    @pl.when(p < count - 1)
    def _():
        arrived(halo.at[1], recv.at[1])
        remote(packed.at[1], halo.at[0], send.at[1], recv.at[0], peer(p + 1)).wait_send()

    @pl.when(p == 0)
    def _():
        halo[0] = jnp.zeros(halo.shape[1:], BF)

    @pl.when(p == count - 1)
    def _():
        halo[1] = jnp.zeros(halo.shape[1:], BF)


def dot(a, b):
    return jnp.dot(a, b, preferred_element_type=F32)


def dot_nt(a, b):
    return lax.dot_general(a, b, (((1,), (1,)), ((), ())), preferred_element_type=F32)


def dot_tn(a, b):
    return lax.dot_general(a, b, (((0,), (0,)), ((), ())), preferred_element_type=F32)


def lanes4(mask, width):
    return jnp.concatenate([mask] * (width // 128), axis=1)


def rows8(value):
    return value.reshape(-1, 8, value.shape[-1]).sum(0)


def to_natural(cells, back, gather, out):
    narrow = dot(cells, gather).astype(BF)
    for c in range(out.shape[1]):
        out[:, c] = dot(back, narrow[128 * c : 128 * c + 128]).astype(BF).reshape(8, 16, narrow.shape[1])


def shifted(chunk, perm, S, c):
    moved = dot(perm, chunk)
    for lane in range(S.shape[1]):
        S[:, lane, pl.ds(3 + 16 * c, 16)] = moved[:, lane * 128 : lane * 128 + 128].reshape(7, 16, 8, 128)
    return moved


def wrap(S, cols):
    S[:, :, 0:3] = S[:, :, cols : cols + 3]
    S[:, :, cols + 3 : cols + 6] = S[:, :, 3:6]


def taps_to(kb, par, flip):
    for lane in range(kb.shape[0]):
        at = slice(128 * lane, 128 * lane + 128)
        for k in range(49):
            tap = 48 - k if flip else k
            kb[lane, k] = jnp.broadcast_to(par[tap : tap + 1, at], (8, 128))


def taps_at(S, kb, lane, tile, first, sums):
    for i in range(7):
        window = [S[i, lane, first + t] for t in range(len(sums) + 6)]
        taps = [kb[tile, 7 * i + j] for j in range(7)]
        for k in range(len(sums)):
            total = window[k] * taps[0]
            for j in range(1, 7):
                total = total + window[k + j] * taps[j]
            sums[k] = sums[k] + total
    return sums


def norm_terms(st, par):
    counted = st[2:3]
    mean = st[0:1] / counted
    inverse = lax.rsqrt(st[1:2] / counted - mean * mean + EPS)
    return counted, mean, inverse, par[49:50], par[50:51]


def start_either(self, src, dst, send, recv, peer):
    pl.when(jnp.logical_not(self))(lambda: remote(src, dst, send, recv, peer).start())
    pl.when(self)(lambda: pltpu.make_async_copy(src, dst, recv).start())


def deliver(sec, nat, out, bounce, send, recv, b):
    s, d, g, m, p = where_am_i()

    def target(which, j):
        dp = 4 * g + 2 * ((p + which) % 2) + j
        part = (nat, bounce)[which].at[pl.ds(4 * j, 4)]
        return dp == d, part, out.at[m], send.at[which, j], recv.at[m], (s, dp)

    def over():
        return remote(nat, bounce, b.at[0], b.at[1], (1 - s, d))

    def sends(which):
        for j in range(2):
            start_either(*target(which, j))

    def begin():
        pl.when(s != sec)(lambda: over().start())
        pl.when(s == sec)(lambda: sends(0))

    def middle():
        @pl.when(s == sec)
        def _():
            arrived(bounce, b.at[1])
            sends(1)

    def end():
        @pl.when(s == sec)
        def _():
            for mb in range(4):
                arrived(out.at[mb], recv.at[mb])
            for which in range(2):
                for j in range(2):
                    self_, *rest = target(which, j)
                    pl.when(jnp.logical_not(self_))(lambda rest=rest: remote(*rest).wait_send())

        pl.when(s != sec)(lambda: over().wait_send())

    return [begin, middle, lambda: None, end]


def collect(field, out, first, send, recv):
    s, d, g, m, p = where_am_i()
    core, dp = device(d // 2, 0)
    j = d % 2

    def parts(step):
        mb = (m + step) % 4
        return field.at[mb], out.at[pl.ds(first + 4 * j, 4)], send.at[step], recv.at[j], (s, dp + mb)

    def begin():
        @pl.when(s == core)
        def _():
            for step in range(1, 4):
                remote(*parts(step)).start()
            src, dst, _, sem, _ = parts(0)
            pltpu.make_async_copy(src, dst, sem).start()

    def end():
        for jj in range(2):
            arrived(out.at[pl.ds(first + 4 * jj, 4)], recv.at[jj])

        @pl.when(s == core)
        def _():
            for step in range(1, 4):
                remote(*parts(step)).wait_send()

    return begin, end


def half(ref, c):
    rows, lanes = ref.shape[-2:]
    lead = (slice(None),) * (len(ref.shape) - 2)
    if rows % 32 == 0:
        return ref.at[lead + (pl.ds(pl.multiple_of(c * (rows // 2), 16), rows // 2),)]
    return ref.at[lead + (slice(None), pl.ds(pl.multiple_of(c * (lanes // 2), 128), lanes // 2))]


def half_shape(shape):
    rows, lanes = shape[-2:]
    return shape[:-2] + ((rows // 2, lanes) if rows % 32 == 0 else (rows, lanes // 2))


def collect_land(land, out, send, recv):
    s, d, g, m, p = where_am_i()
    core, dp = device(d // 2, 0)

    def part(step):
        return remote(land, out.at[d % 2], send.at[step], recv.at[d % 2], (s, dp + (m + step) % 4))

    def begin():
        @pl.when(s == core)
        def _():
            for step in range(1, 4):
                part(step).start()
            pltpu.make_async_copy(land, out.at[d % 2], recv.at[d % 2]).start()

    def end():
        for jj in range(2):
            arrived(out.at[jj], recv.at[jj])

        @pl.when(s == core)
        def _():
            for step in range(1, 4):
                part(step).wait_send()

    return begin, end


def script(*actions):
    queue = list(actions)

    def hook(*_):
        if queue:
            queue.pop(0)()

    return hook


def nothing(*_):
    pass


class Gather:
    def __init__(self, shard, full, send, recv):
        self.shard, self.full, self.send, self.recv = shard, full, send, recv
        self.s, self.d, self.g, self.m, _ = where_am_i()
        self.bit = 1 + self.s

    def block(self, col, c):
        return half(self.full.at[:, col], c)

    def near(self):
        return pltpu.make_async_copy(half(self.shard, self.s), half(self.full.at[self.g, self.m], self.s), self.send.at[0])

    def line(self, step):
        src, dst = half(self.shard, self.s), half(self.full.at[self.g, self.m], self.s)
        return remote(src, dst, self.send.at[step], self.recv.at[step], (self.s, 4 * ((self.g + step) % 4) + self.m))

    def column(self, slot, col, peer):
        block = self.block(col, self.s)
        return remote(block, block, self.send.at[slot], self.recv.at[slot], peer)

    def first(self):
        return self.column(4, self.m, (self.s, self.d ^ self.bit))

    def second(self, index):
        return self.column(5 + index, (self.m, self.m ^ self.bit)[index], (self.s, self.d ^ (3 - self.bit)))

    def cols(self, way):
        return (self.m, self.m ^ way, self.m ^ (3 - way), self.m ^ 3)

    def hand(self, index):
        return self.column(7 + index, self.cols(self.bit)[index], (1 - self.s, self.d))

    def start(self):
        self.near().start()
        for step in range(1, 4):
            self.line(step).start()

    def plane(self):
        self.near().wait()
        for step in range(1, 4):
            arrived(half(self.full.at[(self.g + 4 - step) % 4, self.m], self.s), self.recv.at[step])
        self.first().start()
        self.second(0).start()
        self.hand(0).start()

    def onward(self):
        arrived(self.block(self.m ^ self.bit, self.s), self.recv.at[4])
        self.second(1).start()
        self.hand(1).start()

    def over(self):
        for index in range(2):
            arrived(self.block((self.m ^ (3 - self.bit), self.m ^ 3)[index], self.s), self.recv.at[5 + index])
            self.hand(2 + index).start()

    def whole(self):
        for index, col in enumerate(self.cols(3 - self.bit)):
            arrived(self.block(col, 1 - self.s), self.recv.at[7 + index])

    def finish(self):
        for step in range(1, 4):
            self.line(step).wait_send()
        self.first().wait_send()
        for index in range(2):
            self.second(index).wait_send()
        for index in range(4):
            self.hand(index).wait_send()


class Load:
    def __init__(self, src, full, sem):
        self.copy = lambda: pltpu.make_async_copy(src, full, sem.at[0])

    def start(self):
        self.copy().start()

    def whole(self):
        self.copy().wait()

    def plane(self):
        pass

    onward = over = finish = plane


def masks(land, ocean, coarse, pick, patch):
    rows, across = land.shape[0] * land.shape[1], land.shape[2]
    flat = land[...].reshape(rows, across).astype(F32).astype(BF)
    spread = dot(pick, flat)
    at = lax.broadcasted_iota(jnp.int32, spread.shape, 1) - lax.broadcasted_iota(jnp.int32, spread.shape, 0) // 8
    ones = jnp.ones((across, 128), BF)

    def chunk(c, carry):
        ocean[pl.ds(pl.multiple_of(c * 128, 128), 128)] = dot(jnp.where(at == 16 * c, spread, 0.0).astype(BF), ones)
        return carry

    lax.fori_loop(0, ocean.shape[0] // 128, chunk, 0, unroll=True)
    for b in range(ocean.shape[0] // 256):
        moved = dot(patch, ocean[256 * b : 256 * b + 256].astype(BF))
        coarse[64 * b : 64 * b + 64] = moved[:64] * moved[64:128] * moved[128:192] * moved[192:]


def conv_phase(sec, cols, ns, hook):
    ocean, z, stats = ns.ocean, ns.z, ns.stats
    wide, tiles = z.shape[2], cols // 16

    def count_cells(b, t):
        return t + ocean[pl.ds(pl.multiple_of(b * 64, 64), 64)].reshape(8, 8, 128).sum(0)

    def phase(S, kb, *laid):
        taps_to(kb, ns.par[sec], False)
        tally = lax.fori_loop(0, cols // 8, count_cells, jnp.zeros((8, 128), F32))
        lanes = S.shape[1]
        if sec == 0:
            (laid,) = laid

            def lay(r, carry):
                row = ns.x14[r]
                laid[r] = dot(row.reshape(cols, row.shape[2]), ns.spread[...]).astype(BF).reshape(tiles, 16, wide)
                return carry

            lax.fori_loop(0, 14, lay, 0, unroll=True)
        for group in range(wide // 128 // lanes):
            part = slice(group * lanes * 128, (group + 1) * lanes * 128)

            def chunk(c, carry):
                cells = pl.ds(pl.multiple_of(c * 128, 128), 128)
                if sec == 0:
                    moved = shifted(laid[:, c, :, part].reshape(224, lanes * 128), ns.natural[...], S, c)
                    ns.a0[cells, part] = moved[384:512].astype(BF)
                else:
                    shifted(jnp.concatenate([ns.a1[cells, part], ns.halo[0, c, :, part], ns.halo[1, c, :, part]], axis=0), ns.shifts[...], S, c)
                return carry

            lax.fori_loop(0, tiles, chunk, 0)
            wrap(S, cols)
            hook()
            for lane in range(lanes):
                at = slice((group * lanes + lane) * 128, (group * lanes + lane + 1) * 128)

                def step(b, carry):
                    first, second = carry
                    sums = taps_at(S, kb, lane, group * lanes + lane, b * 16, [jnp.zeros((8, 128), F32)] * 16)
                    for k, total in enumerate(sums):
                        z[b * 16 + k, :, at] = total
                        kept = total * ocean[pl.ds(pl.multiple_of(b * 128 + 8 * k, 8), 8)]
                        first = first + kept
                        second = second + kept * total
                    return first, second

                zero = jnp.zeros((8, 128), F32)
                first, second = lax.fori_loop(0, tiles, step, (zero, zero))
                stats[0:1, at] = first.sum(0, keepdims=True)
                stats[1:2, at] = second.sum(0, keepdims=True)
                stats[2:3, at] = tally.sum(0, keepdims=True)
                stats[3:8, at] = jnp.zeros((5, 128), F32)
                hook()

    space = [pltpu.VMEM((7, 2, cols + 6, 8, 128), F32), pltpu.VMEM((wide // 128, 49, 8, 128), F32)]
    pl.run_scoped(phase, *space, *([pltpu.VMEM((14, tiles, 16, wide), BF)] if sec == 0 else []))


def gelu_terms(e):
    phi = 0.5 + 0.5 * lax.erf(e * np.float32(0.5**0.5))
    return phi, phi + e * (np.float32((2 * np.pi) ** -0.5) * jnp.exp(-0.5 * e * e))


def ff_phase(sec, ns, st, w1, w2, res, y, nat, hook):
    par = ns.par[sec]
    counted, mean, inverse, gain, shift = norm_terms(st, par)
    cells, wide = res.shape
    w1, w2 = w1.reshape(wide, -1), w2.reshape(-1, wide)
    hidden = w1.shape[1]

    def phase(n, g, r):
        def norm(b, carry):
            z = ns.z[pl.ds(b * 32, 32)].reshape(256, wide)
            n[pl.ds(pl.multiple_of(b * 256, 256), 256)] = ((z - mean) * inverse * gain + shift).astype(BF)
            return carry

        lax.fori_loop(0, cells // 256, norm, 0, unroll=True)
        for h in range(hidden // 256):
            at = slice(256 * h, 256 * h + 256)
            e = dot(n[...], w1[:, at]) + ns.bias[sec, 0:1, at]
            g[:, at] = (e * gelu_terms(e)[0]).astype(BF)
            hook(h)
        r[...] = dot(g[...], w2[...])
        hook(hidden // 256)

        def end(b, carry):
            at = pl.ds(pl.multiple_of(b * 256, 256), 256)
            y[at] = (lanes4(ns.ocean[at], wide) * (res[at].astype(F32) + (r[at] + par[51:52]))).astype(BF)
            return carry

        lax.fori_loop(0, cells // 256, end, 0, unroll=True)
        to_natural(y[...], ns.back[...], ns.gather[...], nat)

    pl.run_scoped(phase, pltpu.VMEM((cells, wide), BF), pltpu.VMEM((cells, hidden), BF), pltpu.VMEM((cells, wide), F32))


def forward_kernel(fast, count, cols, ns):
    s, d, g, m, p = where_am_i()
    greet_near(count)
    x14 = ns.x14
    x_begin, x_end = collect(ns.x, x14, 3, ns.xs, ns.xr)
    land_begin, land_end = collect_land(ns.land, ns.land2, ns.ls, ns.lr)
    x_begin()
    land_begin()
    pairs = [(ns.mine, ns.par), (ns.mine_bias, ns.bias)] + [(getattr(ns, f"mine{k}"), getattr(ns, f"shard{k}")) for k in range(4) if fast]
    far = [remote(src, dst.at[s], ns.ps.at[k, 0], ns.pr.at[k], (1 - s, d)) for k, (src, dst) in enumerate(pairs)]
    near = [pltpu.make_async_copy(src, dst.at[s], ns.ps.at[k, 1]) for k, (src, dst) in enumerate(pairs)]
    for c in far + near:
        c.start()
    fulls = dict(w1_0=ns.w1_0, w2_0=ns.w2_0, r0=ns.r0, m0=ns.m0, m1=ns.m1, r1=ns.r1, w1_1=ns.w1_1, w2_1=ns.w2_1)
    which = dict(w1_0=(0, 0), w2_0=(1, 0), r0=(2, 0), r1=(2, 1), m0=(3, 0), m1=(3, 1), w1_1=(0, 1), w2_1=(1, 1))
    mats = {}
    for k, (name, full) in enumerate(fulls.items()):
        if fast:
            index, sec = which[name]
            mats[name] = Gather(getattr(ns, f"shard{index}").at[sec], full, ns.gs.at[k], ns.gr.at[k])
        else:
            mats[name] = Load(getattr(ns, name + "_in"), full, ns.gs.at[k])
    kept = dict(z0=ns.z, z1=ns.z, a0=ns.a0, a1=ns.a1, skip=ns.skip, up=ns.up, pieces=ns.pieces, deep=ns.deep, nat0=ns.nat0, nat1=ns.nat1)
    keeps = {name: lambda k=k, name=name, ref=ref: pltpu.make_async_copy(ref, getattr(ns, name + "_out"), ns.keep.at[k]) for k, (name, ref) in enumerate(kept.items())}

    def keep(*names):
        for name in names:
            keeps[name]().start()

    saves = {name: lambda k=k, name=name, full=full: pltpu.make_async_copy(full, getattr(ns, name + "_out"), ns.save.at[k]) for k, (name, full) in enumerate(fulls.items())}

    def do(step, *names):
        for name in names:
            getattr(mats[name], step)()

    def whole(*names):
        do("whole", *names)
        for name in names:
            saves[name]().start()

    for k in range(2, len(pairs)):
        near[k].wait()
        arrived(pairs[k][1].at[1 - s], ns.pr.at[k])
        if k == 3:
            do("start", "w1_0", "w2_0")
    if not fast:
        do("start", "w1_0", "w2_0")
    do("start", "r0")
    land_end()
    masks(ns.land2, ns.ocean, ns.coarse, ns.pick[...], ns.patch[...])
    x_end()

    def edge(up):
        src, dst = (x14.at[pl.ds(3, 3)], x14.at[pl.ds(11, 3)]) if up else (x14.at[pl.ds(8, 3)], x14.at[pl.ds(0, 3)])
        return remote(src, dst, ns.hs.at[int(up)], ns.hr.at[int(up)], device(p - 1 if up else p + 1, m))

    pl.when(p > 0)(edge(True).start)
    pl.when(p < count - 1)(edge(False).start)
    do("plane", "w1_0", "w2_0")
    for k in range(2):
        near[k].wait()
        arrived(pairs[k][1].at[1 - s], ns.pr.at[k])

    @pl.when(p == 0)
    def _():
        x14[0:3] = jnp.zeros((3,) + x14.shape[1:], BF)

    @pl.when(p == count - 1)
    def _():
        x14[11:14] = jnp.zeros((3,) + x14.shape[1:], BF)

    pl.when(p > 0)(lambda: arrived(x14.at[pl.ds(0, 3)], ns.hr.at[0]))
    pl.when(p < count - 1)(lambda: arrived(x14.at[pl.ds(11, 3)], ns.hr.at[1]))

    cot_begin, cot_end = collect(ns.cot, ns.cot8, 0, ns.cs, ns.cr)

    do("onward", "w1_0", "w2_0")

    conv_phase(0, cols, ns, script(
        nothing,
        lambda: (do("plane", "r0"), do("start", "r1", "m0", "m1")),
        nothing,
        nothing,
        lambda: do("over", "w1_0", "w2_0"),
        lambda: do("onward", "r0"),
    ))
    ns.st0[...] = all_sum(ns.stats, ns.slots, ns.send, ns.recv, count)
    keep("z0", "a0")
    whole("w1_0", "w2_0")
    ff0 = {1: lambda: (do("plane", "r1", "m0", "m1"), do("start", "w1_1", "w2_1")), 7: lambda: do("over", "r0")}
    ff_phase(0, ns, ns.st0, ns.w1_0, ns.w2_0, ns.a0, ns.skip, ns.nat0, lambda k: ff0.get(k, nothing)())
    keep("skip", "nat0")

    skip, pieces, wide = ns.skip, ns.pieces, ns.skip.shape[1]
    blocks = skip.shape[0] // 256
    down, up_w = ns.r0.reshape(4 * wide, -1), ns.r1.reshape(GROUPS, 2, ns.r1.shape[2] // 2, -1)
    merge = [v.reshape(wide, wide) for v in (ns.m0, ns.m1)]
    for b in range(blocks):
        moved = dot(ns.patch[...], skip[256 * b : 256 * b + 256]).astype(BF)
        for k in range(4):
            pieces[k, 64 * b : 64 * b + 64] = moved[64 * k : 64 * k + 64]
    do("onward", "r1", "m0", "m1")
    do("plane", "w1_1", "w2_1")
    whole("r0")
    value = sum(dot(pieces[k], down[wide * k : wide * k + wide]) for k in range(4))
    deep_value = (lanes4(ns.coarse[...], value.shape[1]) * value).astype(BF)
    ns.deep[...] = deep_value
    keep("pieces", "deep")
    do("over", "m0", "m1", "r1")
    do("onward", "w1_1", "w2_1")
    cot_begin()
    whole("m0", "m1", "r1")
    rows = up_w.shape[0] * up_w.shape[2]
    lifted = [dot(deep_value, up_w[:, i].reshape(rows, -1)).astype(BF) for i in range(2)]
    for b in range(blocks):
        at = slice(256 * b, 256 * b + 256)
        stacked = jnp.concatenate(
            [lifted[i][64 * b : 64 * b + 64, wide * j : wide * j + wide] for i in range(2) for j in range(2)], axis=0
        )
        ns.up[at] = dot(ns.unpatch[...], stacked).astype(BF)
    for b in range(blocks):
        at = slice(256 * b, 256 * b + 256)
        joined = dot(ns.up[at], merge[0][...]) + dot(skip[at], merge[1][...])
        ns.h[at] = joined
        low = joined.astype(BF)
        ns.a1[at] = low
        for k in range(2):
            ends = dot(ns.edges[...], low[128 * k : 128 * k + 128]).astype(BF)
            ns.packed[0, 2 * b + k] = ends[:48]
            ns.packed[1, 2 * b + k] = ends[48:]
    swap_rows(ns.packed, ns.halo, ns.es, ns.er, count)
    keep("up", "a1")
    keeps["z0"]().wait()

    conv_phase(1, cols, ns, script(nothing, nothing, lambda: do("over", "w1_1", "w2_1")))
    ns.st1[...] = all_sum(ns.stats, ns.slots1, ns.send1, ns.recv1, count)
    keep("z1")
    whole("w1_1", "w2_1")
    ff_phase(1, ns, ns.st1, ns.w1_1, ns.w2_1, ns.h, ns.y1, ns.nat1, nothing)
    keep("nat1")

    cot_end()
    for name, save in saves.items():
        save().wait()
        do("finish", name)
    for name, copy in keeps.items():
        if name != "z0":
            copy().wait()
    for c in far:
        c.wait_send()
    pl.when(p > 0)(edge(True).wait_send)
    pl.when(p < count - 1)(edge(False).wait_send)


class Reduce:
    def __init__(self, sec, partial, bank, out, send, recv):
        self.sec, self.partial, self.out, self.send, self.recv = sec, partial, out, send, recv
        self.own, self.core, self.one, self.two, self.row, self.mine = bank
        self.s, self.d, self.g, self.m, _ = where_am_i()
        self.bit = 1 + self.s
        self.rest = self.m ^ (3 - self.bit)

    def near(self):
        return pltpu.make_async_copy(half(self.partial, self.s), self.own, self.send.at[0])

    def over(self):
        return remote(half(self.partial, 1 - self.s), self.core, self.send.at[1], self.recv.at[1], (1 - self.s, self.d))

    def first(self, index):
        col = (self.m ^ self.bit, self.m ^ 3)[index]
        return remote(self.own.at[:, col], self.one.at[:, index], self.send.at[2 + index], self.recv.at[2 + index], (self.s, self.d ^ self.bit))

    def second(self):
        return remote(self.own.at[:, self.rest], self.two, self.send.at[4], self.recv.at[4], (self.s, self.d ^ (3 - self.bit)))

    def along(self, step):
        to = (self.g + step) % 4
        return remote(self.own.at[to, self.m], self.row.at[step - 1], self.send.at[4 + step], self.recv.at[4 + step], (self.s, 4 * to + self.m))

    def give(self):
        return remote(self.mine, self.out.at[self.s], self.send.at[8], self.recv.at[8], (1 - self.s, self.d))

    def start(self):
        self.over().start()
        self.near().start()

    def plane(self):
        self.near().wait()
        arrived(self.core, self.recv.at[1])
        own, core, m, bit = self.own, self.core, self.m, self.bit

        def add(k, carry):
            z, col = k % 4, (m ^ 3, m ^ bit, m ^ (3 - bit), m)
            for c in col:
                own[z, c] = (own[z, c].astype(F32) + core[z, c].astype(F32)).astype(BF)
            return carry

        lax.fori_loop(0, 4, add, 0)
        self.first(1).start()
        self.first(0).start()

    def onward(self):
        own, one, rest = self.own, self.one, self.rest
        arrived(one.at[:, 1], self.recv.at[3])

        def add(z, carry):
            own[z, rest] = (own[z, rest].astype(F32) + one[z, 1].astype(F32)).astype(BF)
            return carry

        lax.fori_loop(0, 4, add, 0)
        self.second().start()

    def line(self):
        own, one, two, m = self.own, self.one, self.two, self.m
        arrived(one.at[:, 0], self.recv.at[2])
        arrived(two, self.recv.at[4])

        def add(z, carry):
            own[z, m] = (own[z, m].astype(F32) + one[z, 0].astype(F32) + two[z].astype(F32)).astype(BF)
            return carry

        lax.fori_loop(0, 4, add, 0)
        for step in range(1, 4):
            self.along(step).start()

    def total(self):
        for step in range(1, 4):
            arrived(self.row.at[step - 1], self.recv.at[4 + step])
        row = self.row
        self.mine[...] = self.own[self.g, self.m].astype(F32) + row[0].astype(F32) + row[1].astype(F32) + row[2].astype(F32)
        pl.when(self.s != self.sec)(lambda: self.give().start())

        @pl.when(self.s == self.sec)
        def _():
            self.out[self.s] = self.mine[...]

    def finish(self):
        self.over().wait_send()
        for index in range(2):
            self.first(index).wait_send()
        self.second().wait_send()
        for step in range(1, 4):
            self.along(step).wait_send()
        pl.when(self.s != self.sec)(lambda: self.give().wait_send())
        pl.when(self.s == self.sec)(lambda: arrived(self.out.at[1 - self.s], self.recv.at[8]))


def reduce_bank(name, shape):
    part = half_shape(shape)
    out = {f"{name}_{k}": pltpu.VMEM(lead + part, BF) for k, lead in (("own", (4, 4)), ("core", (4, 4)), ("one", (4, 2)), ("two", (4,)), ("row", (3,)))}
    out.update({f"{name}_mine": pltpu.VMEM(part, F32), f"{name}_s": DMA((9,)), f"{name}_r": DMA((9,))})
    return out


def reducer(ns, name, sec, partial, out):
    bank = [getattr(ns, f"{name}_{k}") for k in ("own", "core", "one", "two", "row", "mine")]
    return Reduce(sec, partial, bank, out, getattr(ns, f"{name}_s"), getattr(ns, f"{name}_r"))


def loads(pairs, sems, first=0):
    copies = [pltpu.make_async_copy(src, dst, sems.at[first + k]) for k, (src, dst) in enumerate(pairs)]
    for c in copies:
        c.start()
    return [c.wait for c in copies]


def back_ff_phase(sec, count, ns, top, kept, w_in, w_out, hook, done):
    z_in, st = kept
    cells, wide = ns.dym.shape
    hidden = w_in.shape[1]
    chunks = cells // 128
    ocean, small, dym = ns.ocean, ns.small, ns.dym
    counted, mean, inverse, gain, shift = norm_terms(st, ns.par[sec])

    def phase(w1, w2, z, n, de, dn, dr):
        got_z, got_w1, got_w2 = loads([(z_in, z), (w_in, w1), (w_out, w2)], ns.load_sem)

        def begin(c, total):
            at = pl.ds(pl.multiple_of(c * 128, 128), 128)
            if sec == 1:
                block = top[:, c]
                block = dot(block.reshape(-1, block.shape[-1]), ns.spread[...]).astype(BF)
                grad = dot(ns.turn[...], block)
            else:
                grad = top[at]
            grad = grad * lanes4(ocean[at], wide)
            dym[at] = grad
            low = grad.astype(BF)
            dr[at] = low
            return total + rows8(low.astype(F32))

        total = lax.fori_loop(0, chunks, begin, jnp.zeros((8, wide), F32), unroll=True)
        small[2:3] = total.sum(0, keepdims=True)
        small[3:8] = jnp.zeros((5, wide), F32)
        got_z()

        def norm(c, carry):
            at = pl.ds(pl.multiple_of(c * 128, 128), 128)
            n[at] = ((z[at] - mean) * inverse * gain + shift).astype(BF)
            return carry

        lax.fori_loop(0, chunks, norm, 0, unroll=True)
        got_w1()
        got_w2()
        for h in range(hidden // 256):
            at = slice(256 * h, 256 * h + 256)
            e = dot(n[...], w1[:, at]) + ns.bias[sec, 0:1, at]
            phi, slope = gelu_terms(e)
            ns.dw2[at] = dot_tn((e * phi).astype(BF), dr[...]).astype(BF)
            low = (dot_nt(dr[...], w2[at]) * slope).astype(BF)
            de[:, at] = low
            row, col = 3 + 256 * h // wide, 256 * h % wide
            small[row : row + 1, col : col + 256] = low.astype(F32).sum(0, keepdims=True)
            ns.dw1[:, at] = dot_tn(n[...], low).astype(BF)
            hook(h)
        done()
        dn[...] = dot_nt(de[...], w1[...])

        def sums(c, carry):
            at = pl.ds(pl.multiple_of(c * 128, 128), 128)
            grad = dn[at]
            return carry[0] + rows8(grad), carry[1] + rows8(grad * ((z[at] - mean) * inverse))

        zero = jnp.zeros((8, wide), F32)
        plain, scaled = lax.fori_loop(0, chunks, sums, (zero, zero), unroll=True)
        small[0:1] = plain.sum(0, keepdims=True)
        small[1:2] = scaled.sum(0, keepdims=True)
        ns.stats[...] = small[...]
        summed = all_sum(ns.stats, ns.slots, ns.send, ns.recv, count)
        first = -inverse * gain * summed[0:1] / counted
        second = -inverse * inverse * gain * summed[1:2] / counted

        def end(c, carry):
            at = pl.ds(pl.multiple_of(c * 128, 128), 128)
            grad = inverse * gain * dn[at] + lanes4(ocean[at], wide) * (first + second * (z[at] - mean))
            low = grad.astype(BF)
            ns.dz[at] = low
            ends = dot(ns.edges[...], low).astype(BF)
            ns.packed[0, c] = ends[:48]
            ns.packed[1, c] = ends[48:]
            return carry

        lax.fori_loop(0, chunks, end, 0, unroll=True)

    field = lambda t: pltpu.VMEM((cells, wide), t)
    pl.run_scoped(
        phase, pltpu.VMEM(w_in.shape, BF), pltpu.VMEM(w_out.shape, BF), field(F32), field(BF), pltpu.VMEM((cells, hidden), BF), field(F32), field(BF),
    )
    swap_rows(ns.packed, ns.halo, ns.hsend, ns.hrecv, count)


def back_conv_phase(sec, cols, ns, a_in, tiny, hook):
    cells, wide = ns.dz.shape
    dz = ns.dz

    def phase(S, kb, a, field, acc_dk):
        (got_a,) = loads([(a_in, a)], ns.load_sem)
        taps_to(kb, ns.par[sec], True)
        lanes = S.shape[1]
        for group in range(wide // 128 // lanes):
            part = slice(group * lanes * 128, (group + 1) * lanes * 128)

            def chunk(c, carry):
                block = jnp.concatenate([dz[pl.ds(pl.multiple_of(c * 128, 128), 128), part], ns.halo[0, c, :, part], ns.halo[1, c, :, part]], axis=0)
                shifted(block, ns.shifts[...], S, c)
                return carry

            lax.fori_loop(0, cols // 16, chunk, 0)
            wrap(S, cols)
            hook()
            if group == 0:
                got_a()
            for lane in range(lanes):
                at = slice((group * lanes + lane) * 128, (group * lanes + lane + 1) * 128)

                field[...] = a[:, at].astype(F32).reshape(field.shape)

                def step(b, carry):
                    rows = pl.ds(pl.multiple_of(b * 128, 128), 128)
                    above = ns.dym[rows, at].reshape(16, 8, 128)
                    sums = taps_at(S, kb, lane, group * lanes + lane, b * 16, [above[k] for k in range(16)])
                    dz[rows, at] = jnp.concatenate(sums, axis=0).astype(BF)
                    return carry

                lax.fori_loop(0, cols // 16, step, 0)
                acc_dk[...] = jnp.zeros(acc_dk.shape, F32)

                def tap_sums(b, carry):
                    here = [field[b * 16 + k] for k in range(16)]
                    for i in range(7):
                        window = [S[i, lane, b * 16 + t] for t in range(22)]
                        for j in range(7):
                            total = window[j] * here[0]
                            for k in range(1, 16):
                                total = total + window[j + k] * here[k]
                            acc_dk[7 * i + j] += total
                    return carry

                lax.fori_loop(0, cols // 16, tap_sums, 0)
                for k in range(49):
                    tiny[48 - k : 49 - k, at] = acc_dk[k].sum(0, keepdims=True)
                hook()
        tiny[49:56] = jnp.zeros((7, wide), F32)

    pl.run_scoped(
        phase, pltpu.VMEM((7, 2, cols + 6, 8, 128), F32), pltpu.VMEM((wide // 128, 49, 8, 128), F32), pltpu.VMEM((cells, wide), BF),
        pltpu.VMEM((cols, 8, 128), F32), pltpu.VMEM((49, 8, 128), F32),
    )


def back_mid_phase(ns, hook):
    dh = ns.dz
    cells, wide = dh.shape
    blocks = cells // 256

    def phase(skip, up, merge0, merge1, up_w, deep, down, pieces, dups, spreads, dskip):
        got = loads(
            [(ns.m1, merge1), (ns.m0, merge0), (ns.up, up), (ns.skip, skip), (ns.r1, up_w), (ns.deep, deep), (ns.pieces, pieces), (ns.r0, down)],
            ns.load_sem,
        )
        for k in range(2):
            got[k]()
        for b in range(blocks):
            at = slice(256 * b, 256 * b + 256)
            low = dot_nt(dh[at], merge1[...]).astype(BF)
            ns.dym[at] = low.astype(F32)
            dskip[at] = low
            lifted = dot_nt(dh[at], merge0[...]).astype(BF)
            moved = dot(ns.patch[...], lifted).astype(BF)
            for k in range(4):
                dups[k // 2, 64 * b : 64 * b + 64, wide * (k % 2) : wide * (k % 2) + wide] = moved[64 * k : 64 * k + 64]
        to_natural(dskip[...], ns.back[...], ns.gather[...], ns.nat)
        hook(0)
        got[2]()
        got[3]()
        ns.dm0[...] = dot_tn(up[...], dh[...]).astype(BF)
        ns.dm1[...] = dot_tn(skip[...], dh[...]).astype(BF)
        hook(1)
        rows = up_w.shape[0] * up_w.shape[2]
        got[4]()
        ddeep = dot_nt(dups[0], up_w[:, 0].reshape(rows, -1)) + dot_nt(dups[1], up_w[:, 1].reshape(rows, -1))
        got[5]()
        for i in range(2):
            up_w[:, i] = dot_tn(deep[...], dups[i]).astype(BF).reshape(up_w.shape[0], up_w.shape[2], -1)
        saves = [pltpu.make_async_copy(up_w, ns.dr1, ns.load_sem.at[0]), pltpu.make_async_copy(down, ns.dr0, ns.load_sem.at[1])]
        saves[0].start()
        masked = (lanes4(ns.coarse[...], ddeep.shape[1]) * ddeep).astype(BF)
        hook(2)
        got[6]()
        got[7]()
        for k in range(4):
            spreads[k] = dot_nt(masked, down[wide * k : wide * k + wide])
            down[wide * k : wide * k + wide] = dot_tn(pieces[k], masked).astype(BF)
        saves[1].start()
        saves[0].wait()
        hook(3)
        for b in range(blocks):
            value = jnp.concatenate([spreads[k, 64 * b : 64 * b + 64] for k in range(4)], axis=0)
            high = value.astype(BF)
            rest = (value - high.astype(F32)).astype(BF)
            at = slice(256 * b, 256 * b + 256)
            ns.dym[at] += dot(ns.unpatch[...], high) + dot(ns.unpatch[...], rest)
        saves[1].wait()

    like = lambda ref: pltpu.VMEM(ref.shape, BF)
    deep_cells = ns.deep.shape[0]
    pl.run_scoped(
        phase, like(ns.skip), like(ns.up), like(ns.m0), like(ns.m1), like(ns.r1), like(ns.deep), like(ns.r0), like(ns.pieces),
        pltpu.VMEM((2, deep_cells, 2 * wide), BF), pltpu.VMEM((4, deep_cells, wide), F32), pltpu.VMEM((cells, wide), BF),
    )


def with_names(ns, **names):
    out = Names()
    out.__dict__.update(ns.__dict__)
    out.__dict__.update(names)
    return out


def back_kernel(fast, count, cols, ns):
    s, d, g, m, p = where_am_i()
    greet_near(count)
    acts = [deliver(k, getattr(ns, f"nat{k}"), ns.act, getattr(ns, f"bounce{k}"), ns.ds.at[k], ns.dr.at[k], ns.db.at[k]) for k in range(2)]
    gi1, gi0 = (deliver(1 - k, ns.nat, ns.gi, getattr(ns, f"bounce{2 + k}"), ns.ds.at[2 + k], ns.dr.at[2 + k], ns.db.at[2 + k]) for k in range(2))
    w_dec = w_enc = m_all = r_up = r_down = []
    if fast:
        cut = lambda ref: ref.reshape(4, 4, ref.shape[0] // 16, ref.shape[1])
        w_dec = [reducer(ns, "w0", 1, cut(ns.dw1), ns.gw1_1), reducer(ns, "w1", 1, cut(ns.dw2), ns.gw2_1)]
        w_enc = [reducer(ns, "w0", 0, cut(ns.dw1), ns.gw1_0), reducer(ns, "w1", 0, cut(ns.dw2), ns.gw2_0)]
        m_all = [reducer(ns, f"m{k}", k, cut(getattr(ns, f"dm{k}")), getattr(ns, f"gm{k}")) for k in range(2)]
        r_up = [reducer(ns, "r1", 1, ns.dr1.reshape(4, 4, -1, ns.dr1.shape[3]), ns.gr1)]
        r_down = [reducer(ns, "r0", 0, ns.dr0.reshape(4, 4, -1, ns.dr0.shape[1]), ns.gr0)]

    def do(*steps):
        def action(*_):
            for step in steps:
                if isinstance(step, tuple):
                    for r in step[0]:
                        getattr(r, step[1])()
                else:
                    step()

        return action

    def keep_dw(sec):
        if not fast:
            copies = [pltpu.make_async_copy(ns.dw1, getattr(ns, f"dw1_{sec}"), ns.ps.at[0]), pltpu.make_async_copy(ns.dw2, getattr(ns, f"dw2_{sec}"), ns.ps.at[1])]
            for copy in copies:
                copy.start()
            for copy in copies:
                copy.wait()

    def at_step(**actions):
        return lambda h: actions.get(f"h{h}", nothing)()

    do(*(act[0] for act in acts))()
    dec = with_names(ns, halo=ns.halo1, slots=ns.slots1, send=ns.send1, recv=ns.recv1, hsend=ns.hsend1, hrecv=ns.hrecv1)
    back_ff_phase(1, count, dec, ns.top, (ns.z1, ns.st1), ns.w1_1, ns.w2_1, at_step(h3=do(*(act[1] for act in acts))), do((w_dec, "start"), lambda: keep_dw(1)))
    back_conv_phase(1, cols, dec, ns.a1, ns.tiny1, script(
        do((w_dec, "plane")), nothing, do(*(act[3] for act in acts)), do((w_dec, "onward")), nothing, do((w_dec, "line"))))
    ns.tiny1[56:64] = ns.small[...]
    back_mid_phase(ns, script(gi1[0], do((m_all, "start")), do((w_dec, "total"), gi1[1]), do((r_up, "start"), (m_all, "plane"))))
    do((r_down, "start"), (w_dec, "finish"))()

    back_ff_phase(0, count, ns, ns.dym, (ns.z0, ns.st0), ns.w1_0, ns.w2_0, at_step(
        h0=do((r_up, "plane")), h2=do((m_all, "onward")), h4=do((r_down, "plane")),
    ), do((w_enc, "start"), (m_all, "line"), lambda: keep_dw(0)))
    do((r_up, "onward"), (w_enc, "plane"))()
    back_conv_phase(0, cols, ns, ns.a0, ns.tiny0, script(
        do((r_down, "onward"), (r_up, "line")), do((m_all, "total")), do((w_enc, "onward")), do((r_down, "line"), gi1[3]), do((r_up, "total")), do((w_enc, "line"))))
    ns.tiny0[56:64] = ns.small[...]
    to_natural(ns.dz[...], ns.back[...], ns.gather[...], ns.nat)
    gi0[0]()
    if fast:
        sm, tiny, ts, tr = ns.sm, ns.tiny, ns.ts, ns.tr
        sm[0] = ns.tiny0[...]
        sm[1] = ns.tiny1[...]
        over = remote(sm.at[1 - s], tiny.at[0], ts.at[0], tr.at[0], (1 - s, d))
        over.start()
        arrived(tiny.at[0], tr.at[0])
        over.wait_send()
        tiny[1] = sm[s] + tiny[0]
        for base, peer in ((1, lambda step: (s, 4 * ((g + step) % 4) + m)), (5, lambda step: (s, d ^ step))):
            sent = [remote(tiny.at[base], tiny.at[base + step], ts.at[base + step], tr.at[base + step], peer(step)) for step in range(1, 4)]
            for c in sent:
                c.start()
            if base == 1:
                gi0[1]()
                do((r_down, "total"))()
            for step in range(1, 4):
                arrived(tiny.at[base + step], tr.at[base + step])
            for c in sent:
                c.wait_send()
            total = tiny[base] + tiny[base + 1] + tiny[base + 2] + tiny[base + 3]
            if base == 1:
                tiny[5] = total
            else:
                ns.total[...] = total
    else:
        gi0[1]()
    do((w_enc, "total"), (m_all + r_up + r_down + w_enc, "finish"), gi0[3])()


class Names:
    pass


def build(name, body, ins, outs, scratch, alias, cid, limit):
    ins = {k: v if isinstance(v, tuple) else (v, VM) for k, v in ins.items()}
    outs = {k: v if len(v) == 3 else v + (VM,) for k, v in outs.items()}
    names = list(ins) + list(outs) + list(scratch)

    def kernel(*refs):
        ns = Names()
        for k, ref in zip(names, refs):
            setattr(ns, k, ref)
        body(ns)

    order_in, order_out = list(ins), list(outs)
    results = pl.pallas_call(
        kernel, name=name, out_shape=[jax.ShapeDtypeStruct(v[0], v[1]) for v in outs.values()],
        in_specs=[v[1] for v in ins.values()], out_specs=[v[2] for v in outs.values()], scratch_shapes=list(scratch.values()),
        input_output_aliases={order_in.index(a): order_out.index(b) for a, b in alias.items()},
        compiler_params=pltpu.CompilerParams(vmem_limit_bytes=limit * MEGA, collective_id=cid, has_side_effects=True),
    )(*[v[0] for v in ins.values()])
    out = Names()
    for k, v in zip(order_out, results):
        setattr(out, k, v)
    return out


def on_device(sections, dps, inputs, cotangent, land, kernel, bn_gain, bn_bias, bias_in, bias_out, w_in, w_out, resample, merge):
    batches, height, cols, c = inputs.shape
    hid = bias_in.shape[1]
    n = resample.shape[1] * dps // (4 * c)
    cw, hw, nw = (GROUPS * padded(v) for v in (c, hid, n))
    cells, deep_cells = cols * 8, cols * 2
    count = 2 * (dps // 4)
    fast = dps == GROUPS
    assert batches == 4 and height == 4 and dps % 4 == 0 and sections == 2 and cols % 32 == 0
    s = lax.axis_index("section")
    mats = {k: jnp.asarray(v) for k, v in matrices(c).items()}
    tiles = cols // 16
    both = ("section", "dp")

    def packs(parts, w1, w2, rd, ru):
        return pack_in(w1, parts, c, hid), pack_in(w2, parts, hid, c), pack_down(rd, parts, c, n), pack_up(ru, parts, c, n)

    shards = []
    if fast:
        w1, w2, rd, ru = packs(1, *(v.astype(BF) for v in (w_in, w_out, resample, resample)))
        shards = [w1[0], w2[0], jnp.where(s == 0, rd, ru)[0], pack_in(merge.astype(BF), 1, c, c)[0]]
    else:
        flat = [lax.all_gather(v.astype(BF).reshape(-1), both, axis=0, tiled=True) for v in (w_in, w_out, resample, merge)]
        halves = [v.reshape(2, -1) for v in flat]
        whole = [packs(GROUPS, halves[0][k], halves[1][k], halves[2][k], halves[2][k]) for k in range(2)]

    rows = jnp.concatenate([kernel[0], bn_gain, bn_bias, bias_out], axis=0)
    mine = grow(grow(rows.reshape(-1, GROUPS, c // GROUPS), (52, GROUPS, padded(c))).reshape(52, cw), (56, cw))
    mine_bias = grow(grow(bias_in.reshape(GROUPS, -1), (GROUPS, padded(hid))).reshape(1, hw), (8, hw))
    x = inputs.reshape(batches, height, tiles, 16, c)
    cot = cotangent.reshape(batches, height, tiles, 16, c)
    land_cols = -(-cols // 128) * 128
    at_any = lambda v: (v, ANY)
    field = lambda t: ((cells, cw), t)
    natural = ((8, tiles, 16, c), BF)
    edge_rows = ((2, tiles, 48, cw), BF)
    shapes = [(padded(c), hw), (padded(hid), cw), (4 * padded(c), nw), (padded(c), cw)]
    names = dict(w1_0=0, w2_0=1, r0=2, m0=3, m1=3, r1=2, w1_1=0, w2_1=1)
    ins = dict(x=x, land=grow(land, (8, land_cols)), mine=mine, mine_bias=mine_bias, cot=cot)
    if fast:
        ins.update({f"mine{k}": v for k, v in enumerate(shards)})
    else:
        given = dict(w1_0=whole[0][0], w2_0=whole[0][1], r0=whole[0][2], r1=whole[1][3], w1_1=whole[1][0], w2_1=whole[1][1])
        given.update(m0=pack_in(halves[3][0], GROUPS, c, c), m1=pack_in(halves[3][1], GROUPS, c, c))
        ins.update({k + "_in": v.reshape((4, 4) + shapes[names[k]]) for k, v in given.items()})
    ins = {k: at_any(v) for k, v in ins.items()}
    ins.update({k: mats[k] for k in ("spread", "gather", "natural", "shifts", "patch", "unpatch", "edges", "back", "pick")})
    outs = dict(
        par=((2, 56, cw), F32), bias=((2, 8, hw), F32), ocean=((cells, 128), F32), coarse=((deep_cells, 128), F32),
        st0=((8, cw), F32), st1=((8, cw), F32), cot8=natural + (ANY,),
    )
    held = dict(
        a0=field(BF), a1=field(BF), skip=field(BF), up=field(BF), pieces=((4, deep_cells, cw), BF), deep=((deep_cells, nw), BF), nat0=natural, nat1=natural,
    )
    outs.update({k + "_out": v + (ANY,) for k, v in held.items()}, z0_out=((cols, 8, cw), F32, ANY), z1_out=((cols, 8, cw), F32, ANY))
    outs.update({k + "_out": ((4, 4) + shapes[v], BF, ANY) for k, v in names.items()})
    scratch = dict(
        x14=pltpu.VMEM((14, tiles, 16, c), BF), land2=pltpu.VMEM((2, 8, land_cols), jnp.int32),
        z=pltpu.VMEM((cols, 8, cw), F32),
        h=pltpu.VMEM((cells, cw), F32),
        halo=pltpu.VMEM(*edge_rows), packed=pltpu.VMEM(*edge_rows), y1=pltpu.VMEM(*field(BF)),
        stats=pltpu.VMEM((8, cw), F32), slots=pltpu.VMEM((count // 2 + 1, 8, cw), F32), slots1=pltpu.VMEM((count // 2 + 1, 8, cw), F32),
        send=DMA((count,)), recv=DMA((count,)), send1=DMA((count,)), recv1=DMA((count,)),
        xs=DMA((4,)), xr=DMA((2,)), ls=DMA((4,)), lr=DMA((2,)), hs=DMA((2,)), hr=DMA((2,)), ps=DMA((6, 2)), pr=DMA((6,)), cs=DMA((4,)), cr=DMA((2,)),
        es=DMA((2,)), er=DMA((2,)), gs=DMA((8, 12)), gr=DMA((8, 12)), save=DMA((8,)), keep=DMA((10,)),
    )
    scratch.update({k: pltpu.VMEM((4, 4) + shapes[v], BF) for k, v in names.items()}, **{k: pltpu.VMEM(*v) for k, v in held.items()})
    if fast:
        scratch.update({f"shard{k}": pltpu.VMEM((2,) + shapes[k], BF) for k in range(4)})
    fw = build("forward", lambda ns: forward_kernel(fast, count, cols, ns), ins, outs, scratch, {}, 1, 63)
    wide_w = dict(dw1=((cw, hw), BF), dw2=((hw, cw), BF))
    bounce = natural + (ANY,)
    names = ("par", "ocean", "coarse", "bias", "st0", "st1")
    ins = dict(top=fw.cot8, **{k: getattr(fw, k) for k in names})
    ins.update({k: mats[k] for k in ("shifts", "edges", "back", "gather", "spread", "turn", "patch", "unpatch")})
    ins.update({k: at_any(getattr(fw, k + "_out")) for k in ("nat0", "nat1", "a0", "a1", "up", "skip", "deep", "pieces")})
    ins.update({k: at_any(getattr(fw, k + "_out").reshape(cells, cw)) for k in ("z0", "z1")})
    views = dict(w1_0=(cw, hw), w2_0=(hw, cw), w1_1=(cw, hw), w2_1=(hw, cw), m0=(cw, cw), m1=(cw, cw), r0=(4 * cw, nw), r1=(GROUPS, 2, padded(n), 2 * cw))
    ins.update({k: at_any(getattr(fw, k + "_out").reshape(v)) for k, v in views.items()})
    outs = dict(
        act=((4, 4, tiles, 16, c), BF, ANY), gi=((4, 4, tiles, 16, c), BF, ANY), tiny0=((64, cw), F32), tiny1=((64, cw), F32),
        dm0=((cw, cw), BF), dm1=((cw, cw), BF), dr0=(views["r0"], BF, ANY), dr1=(views["r1"], BF, ANY), **{f"bounce{k}": bounce for k in range(4)},
    )
    space = {k: pltpu.VMEM(*v) for k, v in dict(dym=field(F32), dz=field(BF), packed=edge_rows, halo=edge_rows, halo1=edge_rows, nat=natural, **wide_w).items()}
    space.update(small=pltpu.VMEM((8, cw), F32), stats=pltpu.VMEM((8, cw), F32))
    for k in ("", "1"):
        space.update({"slots" + k: pltpu.VMEM((count // 2 + 1, 8, cw), F32), "send" + k: DMA((count,)), "recv" + k: DMA((count,)), "hsend" + k: DMA((2,)), "hrecv" + k: DMA((2,))})
    space.update(load_sem=DMA((8,)), ds=DMA((4, 2, 2)), dr=DMA((4, 4)), db=DMA((4, 2)), ps=DMA((2,)))
    if fast:
        for name, k in (("w0", 0), ("w1", 1), ("m0", 3), ("m1", 3), ("r0", 2), ("r1", 2)):
            space.update(reduce_bank(name, shapes[k]))
        for name, k in (("gw1_0", 0), ("gw2_0", 1), ("gw1_1", 0), ("gw2_1", 1), ("gr0", 2), ("gr1", 2), ("gm0", 3), ("gm1", 3)):
            outs[name] = ((2,) + half_shape(shapes[k]), F32)
        outs["total"] = ((64, cw), F32)
        space.update(sm=pltpu.VMEM((2, 64, cw), F32), tiny=pltpu.VMEM((9, 64, cw), F32), ts=DMA((9,)), tr=DMA((9,)))
    else:
        outs.update({f"{k}_{sec}": v + (ANY,) for k, v in wide_w.items() for sec in range(2)})
    bw = build("backward", lambda ns: back_kernel(fast, count, cols, ns), ins, outs, space, {}, 2, 63)
    if fast:
        rows_of = lambda v: v.reshape(-1, v.shape[-1])
        tiny = bw.total
        gw1 = unpack_in(rows_of(jnp.where(s == 0, bw.gw1_0, bw.gw1_1)), c, hid)
        gw2 = unpack_in(jnp.where(s == 0, bw.gw2_0, bw.gw2_1).transpose(1, 0, 2).reshape(padded(hid), cw), hid, c)
        gres = jnp.where(s == 0, unpack_down(rows_of(bw.gr0), c, n), unpack_up(rows_of(bw.gr1), c, n))
        gmm = unpack_in(rows_of(jnp.where(s == 0, bw.gm0, bw.gm1)), c, c)
    else:
        scatter = lambda v: lax.psum_scatter(v.astype(F32).reshape(-1), both, scatter_dimension=0, tiled=True)
        gw1 = scatter(jnp.stack([unpack_in(v, c, hid) for v in (bw.dw1_0, bw.dw1_1)]))
        gw2 = scatter(jnp.stack([unpack_in(v, hid, c) for v in (bw.dw2_0, bw.dw2_1)]))
        gres = scatter(jnp.stack([unpack_down(bw.dr0, c, n), unpack_up(bw.dr1, c, n)]))
        gmm = scatter(jnp.stack([unpack_in(v, c, c) for v in (bw.dm0, bw.dm1)]))
        tiny = lax.psum(jnp.stack([bw.tiny0, bw.tiny1]), both)[s]
    activations = bw.act.reshape(1, batches, height, cols, c)
    grad_input = bw.gi.astype(F32).reshape(1, batches, height, cols, c)
    narrow = lambda v: v.reshape(-1, GROUPS, padded(c))[:, :, : c // GROUPS].reshape(-1, c)
    fine = narrow(tiny[:59])
    grad_bias_in = tiny[59:63].reshape(-1)[:hw].reshape(GROUPS, -1)[:, : hid // GROUPS].reshape(1, hid)
    return (
        activations, grad_input, fine[None, :49], fine[57:58], fine[56:57], grad_bias_in, fine[58:59],
        gw1[None], gw2[None], gres[None], gmm,
    )


def solution(mesh):
    sections, dps = mesh.shape["section"], mesh.shape["dp"]
    flat, both = P("section", "dp"), P(("section", "dp"))
    per = P("section", None)
    rows = P(None, "dp", None, None)
    taps = P("section", None, None)
    fields = P("section", None, "dp", None, None)
    return jax.shard_map(
        functools.partial(on_device, sections, dps), mesh=mesh,
        in_specs=(rows, rows, P("dp", None), taps, per, per, per, per, flat, flat, flat, both),
        out_specs=(fields, fields, taps, per, per, per, per, flat, flat, flat, both), check_vma=False,
    )
```

```python
import functools

import jax
import jax.numpy as jnp
import ml_dtypes
import numpy as np
from jax import lax
from jax.experimental import pallas as pl
from jax.experimental.pallas import tpu as pltpu
from jax.sharding import PartitionSpec as P

BF = jnp.bfloat16
F32 = jnp.float32
MESH = pl.DeviceIdType.MESH
ANY = pl.BlockSpec(memory_space=pl.ANY)
VM = pl.BlockSpec(memory_space=pltpu.VMEM)
DMA = pltpu.SemaphoreType.DMA
EPS = 1e-05
GROUPS = 16
MEGA = 1 << 20


def padded(width):
    return -(-(width // GROUPS) // 16) * 16


def selector(rows, cols, pairs):
    out = np.zeros((rows, cols), np.float32)
    for r, c in pairs:
        out[r, c] = 1
    return out.astype(ml_dtypes.bfloat16)


def matrices(channels, hidden, deep):
    group, wide = channels // GROUPS, padded(channels)
    spread = selector(channels, GROUPS * wide, [(c, c // group * wide + c % group) for c in range(channels)])
    natural = selector(896, 224, [(i * 128 + q * 8 + p, (p + i) * 16 + q) for i in range(7) for q in range(16) for p in range(8)])

    def place(q, row):
        if row < 0:
            return 128 + q * 3 + row + 3
        return q * 8 + row if row < 8 else 176 + q * 3 + row - 8

    shifts = selector(896, 224, [(i * 128 + q * 8 + p, place(q, p + i - 3)) for i in range(7) for q in range(16) for p in range(8)])
    turn = selector(128, 128, [(q * 8 + p, p * 16 + q) for q in range(16) for p in range(8)])
    edges = selector(96, 128, [(48 * e + q * 3 + k, q * 8 + 5 * e + k) for e in range(2) for q in range(16) for k in range(3)])
    patch = selector(
        256, 256,
        [((i * 2 + j) * 64 + b * 4 + a, (2 * b + j) * 8 + 2 * a + i) for i in range(2) for j in range(2) for b in range(16) for a in range(4)],
    )
    pick = selector(128, 16, [(q * 8 + p, p // 4 * 8 + p % 4) for q in range(16) for p in range(8)])

    def widen(width):
        group, wide = width // GROUPS, padded(width)
        return selector(width, GROUPS * wide, [(v, v // group * wide + v % group) for v in range(width)])

    half_hidden = widen(hidden)[: hidden // 2, : GROUPS * padded(hidden) // 2]
    deep_spread = widen(deep)
    band = channels // GROUPS
    rows = selector(4 * wide, -(-4 * band // 16) * 16, [(k * wide + r, k * band + r) for k in range(4) for r in range(band)])
    return dict(
        half_hidden=half_hidden, half_hidden_back=np.ascontiguousarray(half_hidden.T), deep_spread=deep_spread,
        deep_back=np.ascontiguousarray(deep_spread.T), rows=rows, pick=pick, spread=spread, gather=np.ascontiguousarray(spread.T), natural=natural, shifts=shifts, turn=turn,
        back=np.ascontiguousarray(turn.T), edges=edges, patch=patch, unpatch=np.ascontiguousarray(patch.T),
    )


def grow(value, sizes):
    return jnp.pad(value, [(0, n - o) for n, o in zip(sizes, value.shape)])


def pack_in(value, parts, c, h):
    value = value.reshape(parts, c // GROUPS, GROUPS, h // GROUPS)
    return grow(value, (parts, padded(c), GROUPS, padded(h))).reshape(parts, padded(c), -1)


def pack_down(value, parts, c, n):
    value = value.reshape(parts, 4, c // GROUPS, GROUPS, n // GROUPS)
    return grow(value, (parts, 4, padded(c), GROUPS, padded(n))).reshape(parts, 4 * padded(c), -1)


def pack_up(value, parts, c, n):
    value = value.reshape(parts, n // GROUPS, 2, 2 * GROUPS, c // GROUPS)
    value = grow(value, (parts, padded(n), 2, 2 * GROUPS, padded(c)))
    return value.transpose(0, 2, 1, 3, 4).reshape(parts, 2 * padded(n), -1)


def unpack_in(value, c, h):
    value = value.reshape(-1, padded(c), GROUPS, padded(h))
    return value[:, : c // GROUPS, :, : h // GROUPS].reshape(-1)


def unpack_down(value, c, n):
    value = value.reshape(-1, 4, padded(c), GROUPS, padded(n))
    return value[:, :, : c // GROUPS, :, : n // GROUPS].reshape(-1)


def unpack_up(value, c, n):
    value = value.reshape(-1, 2, padded(n), 2 * GROUPS, padded(c))
    return value.transpose(0, 2, 1, 3, 4)[:, : n // GROUPS, :, :, : c // GROUPS].reshape(-1)


def device(p, m):
    g = p // 2
    return (p + g) % 2, 4 * g + m


def where_am_i():
    s, d = lax.axis_index("section"), lax.axis_index("dp")
    g = d // 4
    return s, d, g, d % 4, 2 * g + (s + g) % 2


def greet_near(count):
    s, d, g, m, p = where_am_i()
    barrier = pltpu.get_barrier_semaphore()

    def one(k, carry):
        q = (p + k) % count
        pl.semaphore_signal(barrier, inc=1, device_id=device(q, m), device_id_type=MESH)
        return carry

    lax.fori_loop(1, count, one, 0)
    for k in range(1, 4):
        for sec in range(2):
            pl.semaphore_signal(barrier, inc=1, device_id=(sec, 4 * g + (m + k) % 4), device_id_type=MESH)
    pl.semaphore_wait(barrier, count + 5)


def remote(src, dst, send, recv, peer):
    return pltpu.make_async_remote_copy(src_ref=src, dst_ref=dst, send_sem=send, recv_sem=recv, device_id=peer, device_id_type=MESH)


def arrived(ref, sem):
    pltpu.make_async_copy(ref, ref, sem).wait()


def all_sum(mine, slots, send, recv, count):
    s, d, g, m, p = where_am_i()
    groups = count // 2
    over = remote(mine, slots.at[groups], send.at[0], recv.at[0], (1 - s, d))
    over.start()
    arrived(slots.at[groups], recv.at[0])
    slots[g] = mine[...] + slots[groups]
    over.wait_send()

    def copy(k):
        return remote(slots.at[g], slots.at[g], send.at[k], recv.at[k], (s, 4 * ((g + k) % groups) + m))

    lax.fori_loop(1, groups, lambda k, c: (copy(k).start(), c)[1], 0)

    def wait(k, carry):
        arrived(slots.at[(g + groups - k) % groups], recv.at[k])
        copy(k).wait_send()
        return carry

    lax.fori_loop(1, groups, wait, 0)
    return lax.fori_loop(0, groups, lambda k, total: total + slots[k], jnp.zeros(mine.shape, F32))


def swap_rows(packed, halo, send, recv, count):
    s, d, g, m, p = where_am_i()

    def peer(q):
        return device(q, m)

    @pl.when(p > 0)
    def _():
        remote(packed.at[0], halo.at[1], send.at[0], recv.at[1], peer(p - 1)).start()

    @pl.when(p < count - 1)
    def _():
        remote(packed.at[1], halo.at[0], send.at[1], recv.at[0], peer(p + 1)).start()

    @pl.when(p > 0)
    def _():
        arrived(halo.at[0], recv.at[0])
        remote(packed.at[0], halo.at[1], send.at[0], recv.at[1], peer(p - 1)).wait_send()

    @pl.when(p < count - 1)
    def _():
        arrived(halo.at[1], recv.at[1])
        remote(packed.at[1], halo.at[0], send.at[1], recv.at[0], peer(p + 1)).wait_send()

    @pl.when(p == 0)
    def _():
        halo[0] = jnp.zeros(halo.shape[1:], BF)

    @pl.when(p == count - 1)
    def _():
        halo[1] = jnp.zeros(halo.shape[1:], BF)


def dot(a, b):
    return jnp.dot(a, b, preferred_element_type=F32)


def dot_nt(a, b):
    return lax.dot_general(a, b, (((1,), (1,)), ((), ())), preferred_element_type=F32)


def dot_tn(a, b):
    return lax.dot_general(a, b, (((0,), (0,)), ((), ())), preferred_element_type=F32)


def lanes4(mask, width):
    return jnp.concatenate([mask] * (width // 128), axis=1)


def rows8(value):
    return value.reshape(-1, 8, value.shape[-1]).sum(0)


def to_natural(cells, back, gather, out):
    narrow = dot(cells, gather).astype(BF)
    for c in range(out.shape[1]):
        out[:, c] = dot(back, narrow[128 * c : 128 * c + 128]).astype(BF).reshape(8, 16, narrow.shape[1])


def shifted(chunk, perm, S, c):
    moved = dot(perm, chunk)
    for lane in range(S.shape[1]):
        S[:, lane, pl.ds(3 + 16 * c, 16)] = moved[:, lane * 128 : lane * 128 + 128].reshape(7, 16, 8, 128)
    return moved


def wrap(S, cols):
    S[:, :, 0:3] = S[:, :, cols : cols + 3]
    S[:, :, cols + 3 : cols + 6] = S[:, :, 3:6]


def taps_to(kb, par, flip):
    for lane in range(kb.shape[0]):
        at = slice(128 * lane, 128 * lane + 128)
        for k in range(49):
            tap = 48 - k if flip else k
            kb[lane, k] = jnp.broadcast_to(par[tap : tap + 1, at], (8, 128))


def taps_at(S, kb, lane, tile, first, sums):
    for i in range(7):
        window = [S[i, lane, first + t] for t in range(len(sums) + 6)]
        taps = [kb[tile, 7 * i + j] for j in range(7)]
        for k in range(len(sums)):
            total = window[k] * taps[0]
            for j in range(1, 7):
                total = total + window[k + j] * taps[j]
            sums[k] = sums[k] + total
    return sums


def norm_terms(st, par):
    counted = st[2:3]
    mean = st[0:1] / counted
    inverse = lax.rsqrt(st[1:2] / counted - mean * mean + EPS)
    return counted, mean, inverse, par[49:50], par[50:51]


def start_either(self, src, dst, send, recv, peer):
    pl.when(jnp.logical_not(self))(lambda: remote(src, dst, send, recv, peer).start())
    pl.when(self)(lambda: pltpu.make_async_copy(src, dst, recv).start())


def deliver(sec, nat, out, bounce, send, recv, b):
    s, d, g, m, p = where_am_i()

    def target(which, j):
        dp = 4 * g + 2 * ((p + which) % 2) + j
        part = (nat, bounce)[which].at[pl.ds(4 * j, 4)]
        return dp == d, part, out.at[m], send.at[which, j], recv.at[m], (s, dp)

    def over():
        return remote(nat, bounce, b.at[0], b.at[1], (1 - s, d))

    def sends(which):
        for j in range(2):
            start_either(*target(which, j))

    def begin():
        pl.when(s != sec)(lambda: over().start())
        pl.when(s == sec)(lambda: sends(0))

    def middle():
        @pl.when(s == sec)
        def _():
            arrived(bounce, b.at[1])
            sends(1)

    def end():
        @pl.when(s == sec)
        def _():
            for mb in range(4):
                arrived(out.at[mb], recv.at[mb])
            for which in range(2):
                for j in range(2):
                    self_, *rest = target(which, j)
                    pl.when(jnp.logical_not(self_))(lambda rest=rest: remote(*rest).wait_send())

        pl.when(s != sec)(lambda: over().wait_send())

    return [begin, middle, lambda: None, end]


def collect(field, out, first, send, recv):
    s, d, g, m, p = where_am_i()
    core, dp = device(d // 2, 0)
    j = d % 2

    def parts(step):
        mb = (m + step) % 4
        return field.at[mb], out.at[pl.ds(first + 4 * j, 4)], send.at[step], recv.at[j], (s, dp + mb)

    def begin():
        @pl.when(s == core)
        def _():
            for step in range(1, 4):
                remote(*parts(step)).start()
            src, dst, _, sem, _ = parts(0)
            pltpu.make_async_copy(src, dst, sem).start()

    def end():
        for jj in range(2):
            arrived(out.at[pl.ds(first + 4 * jj, 4)], recv.at[jj])

        @pl.when(s == core)
        def _():
            for step in range(1, 4):
                remote(*parts(step)).wait_send()

    return begin, end


def half(ref, c):
    rows, lanes = ref.shape[-2:]
    lead = (slice(None),) * (len(ref.shape) - 2)
    if rows % 32 == 0:
        return ref.at[lead + (pl.ds(pl.multiple_of(c * (rows // 2), 16), rows // 2),)]
    return ref.at[lead + (slice(None), pl.ds(pl.multiple_of(c * (lanes // 2), 128), lanes // 2))]


def half_shape(shape):
    rows, lanes = shape[-2:]
    return shape[:-2] + ((rows // 2, lanes) if rows % 32 == 0 else (rows, lanes // 2))


def collect_land(land, out, send, recv):
    s, d, g, m, p = where_am_i()
    core, dp = device(d // 2, 0)

    def part(step):
        return remote(land, out.at[d % 2], send.at[step], recv.at[d % 2], (s, dp + (m + step) % 4))

    def begin():
        @pl.when(s == core)
        def _():
            for step in range(1, 4):
                part(step).start()
            pltpu.make_async_copy(land, out.at[d % 2], recv.at[d % 2]).start()

    def end():
        for jj in range(2):
            arrived(out.at[jj], recv.at[jj])

        @pl.when(s == core)
        def _():
            for step in range(1, 4):
                part(step).wait_send()

    return begin, end


def script(*actions):
    queue = list(actions)

    def hook(*_):
        if queue:
            queue.pop(0)()

    return hook


def nothing(*_):
    pass


class Gather:
    def __init__(self, shard, full, send, recv):
        self.shard, self.full, self.send, self.recv = shard, full, send, recv
        self.s, self.d, self.g, self.m, _ = where_am_i()
        self.bit = 1 + self.s

    def block(self, col, c):
        return half(self.full.at[:, col], c)

    def near(self):
        return pltpu.make_async_copy(half(self.shard, self.s), half(self.full.at[self.g, self.m], self.s), self.send.at[0])

    def line(self, step):
        src, dst = half(self.shard, self.s), half(self.full.at[self.g, self.m], self.s)
        return remote(src, dst, self.send.at[step], self.recv.at[step], (self.s, 4 * ((self.g + step) % 4) + self.m))

    def column(self, slot, col, peer):
        block = self.block(col, self.s)
        return remote(block, block, self.send.at[slot], self.recv.at[slot], peer)

    def first(self):
        return self.column(4, self.m, (self.s, self.d ^ self.bit))

    def second(self, index):
        return self.column(5 + index, (self.m, self.m ^ self.bit)[index], (self.s, self.d ^ (3 - self.bit)))

    def cols(self, way):
        return (self.m, self.m ^ way, self.m ^ (3 - way), self.m ^ 3)

    def hand(self, index):
        return self.column(7 + index, self.cols(self.bit)[index], (1 - self.s, self.d))

    def start(self):
        self.near().start()
        for step in range(1, 4):
            self.line(step).start()

    def plane(self):
        self.near().wait()
        for step in range(1, 4):
            arrived(half(self.full.at[(self.g + 4 - step) % 4, self.m], self.s), self.recv.at[step])
        self.first().start()
        self.second(0).start()
        self.hand(0).start()

    def onward(self):
        arrived(self.block(self.m ^ self.bit, self.s), self.recv.at[4])
        self.second(1).start()
        self.hand(1).start()

    def over(self):
        for index in range(2):
            arrived(self.block((self.m ^ (3 - self.bit), self.m ^ 3)[index], self.s), self.recv.at[5 + index])
            self.hand(2 + index).start()

    def whole(self):
        for index, col in enumerate(self.cols(3 - self.bit)):
            arrived(self.block(col, 1 - self.s), self.recv.at[7 + index])

    def finish(self):
        for step in range(1, 4):
            self.line(step).wait_send()
        self.first().wait_send()
        for index in range(2):
            self.second(index).wait_send()
        for index in range(4):
            self.hand(index).wait_send()


class Load:
    def __init__(self, src, full, sem):
        self.copy = lambda: pltpu.make_async_copy(src, full, sem.at[0])

    def start(self):
        self.copy().start()

    def whole(self):
        self.copy().wait()

    def plane(self):
        pass

    onward = over = finish = plane


def masks(land, ocean, coarse, pick, patch):
    rows, across = land.shape[0] * land.shape[1], land.shape[2]
    flat = land[...].reshape(rows, across).astype(F32).astype(BF)
    spread = dot(pick, flat)
    at = lax.broadcasted_iota(jnp.int32, spread.shape, 1) - lax.broadcasted_iota(jnp.int32, spread.shape, 0) // 8
    ones = jnp.ones((across, 128), BF)

    def chunk(c, carry):
        ocean[pl.ds(pl.multiple_of(c * 128, 128), 128)] = dot(jnp.where(at == 16 * c, spread, 0.0).astype(BF), ones)
        return carry

    lax.fori_loop(0, ocean.shape[0] // 128, chunk, 0, unroll=True)
    for b in range(ocean.shape[0] // 256):
        moved = dot(patch, ocean[256 * b : 256 * b + 256].astype(BF))
        coarse[64 * b : 64 * b + 64] = moved[:64] * moved[64:128] * moved[128:192] * moved[192:]


def conv_phase(sec, cols, ns, hook):
    ocean, z, stats = ns.ocean, ns.z, ns.stats
    wide, tiles = z.shape[2], cols // 16

    def count_cells(b, t):
        return t + ocean[pl.ds(pl.multiple_of(b * 64, 64), 64)].reshape(8, 8, 128).sum(0)

    def phase(S, kb, *laid):
        taps_to(kb, ns.par[sec], False)
        tally = lax.fori_loop(0, cols // 8, count_cells, jnp.zeros((8, 128), F32))
        lanes = S.shape[1]
        if sec == 0:
            (laid,) = laid

            def lay(r, carry):
                row = ns.x14[r]
                laid[r] = dot(row.reshape(cols, row.shape[2]), ns.spread[...]).astype(BF).reshape(tiles, 16, wide)
                return carry

            lax.fori_loop(0, 14, lay, 0, unroll=True)
        for group in range(wide // 128 // lanes):
            part = slice(group * lanes * 128, (group + 1) * lanes * 128)

            def chunk(c, carry):
                cells = pl.ds(pl.multiple_of(c * 128, 128), 128)
                if sec == 0:
                    moved = shifted(laid[:, c, :, part].reshape(224, lanes * 128), ns.natural[...], S, c)
                    ns.a0[cells, part] = moved[384:512].astype(BF)
                else:
                    shifted(jnp.concatenate([ns.a1[cells, part], ns.halo[0, c, :, part], ns.halo[1, c, :, part]], axis=0), ns.shifts[...], S, c)
                return carry

            lax.fori_loop(0, tiles, chunk, 0)
            wrap(S, cols)
            hook()
            for lane in range(lanes):
                at = slice((group * lanes + lane) * 128, (group * lanes + lane + 1) * 128)

                def step(b, carry):
                    first, second = carry
                    sums = taps_at(S, kb, lane, group * lanes + lane, b * 16, [jnp.zeros((8, 128), F32)] * 16)
                    for k, total in enumerate(sums):
                        z[b * 16 + k, :, at] = total
                        kept = total * ocean[pl.ds(pl.multiple_of(b * 128 + 8 * k, 8), 8)]
                        first = first + kept
                        second = second + kept * total
                    return first, second

                zero = jnp.zeros((8, 128), F32)
                first, second = lax.fori_loop(0, tiles, step, (zero, zero))
                stats[0:1, at] = first.sum(0, keepdims=True)
                stats[1:2, at] = second.sum(0, keepdims=True)
                stats[2:3, at] = tally.sum(0, keepdims=True)
                stats[3:8, at] = jnp.zeros((5, 128), F32)
                hook()

    space = [pltpu.VMEM((7, 2, cols + 6, 8, 128), F32), pltpu.VMEM((wide // 128, 49, 8, 128), F32)]
    pl.run_scoped(phase, *space, *([pltpu.VMEM((14, tiles, 16, wide), BF)] if sec == 0 else []))


def gelu_terms(e):
    phi = 0.5 + 0.5 * lax.erf(e * np.float32(0.5**0.5))
    return phi, phi + e * (np.float32((2 * np.pi) ** -0.5) * jnp.exp(-0.5 * e * e))


def ff_phase(sec, ns, st, w1, w2, res, y, nat, hook):
    par = ns.par[sec]
    counted, mean, inverse, gain, shift = norm_terms(st, par)
    cells, wide = res.shape
    w1, w2 = w1.reshape(wide, -1), w2.reshape(-1, wide)
    hidden = w1.shape[1]

    def phase(n, g, r):
        def norm(b, carry):
            z = ns.z[pl.ds(b * 32, 32)].reshape(256, wide)
            n[pl.ds(pl.multiple_of(b * 256, 256), 256)] = ((z - mean) * inverse * gain + shift).astype(BF)
            return carry

        lax.fori_loop(0, cells // 256, norm, 0, unroll=True)
        for h in range(hidden // 256):
            at = slice(256 * h, 256 * h + 256)
            e = dot(n[...], w1[:, at]) + ns.bias[sec, 0:1, at]
            g[:, at] = (e * gelu_terms(e)[0]).astype(BF)
            hook(h)
        r[...] = dot(g[...], w2[...])
        hook(hidden // 256)

        def end(b, carry):
            at = pl.ds(pl.multiple_of(b * 256, 256), 256)
            y[at] = (lanes4(ns.ocean[at], wide) * (res[at].astype(F32) + (r[at] + par[51:52]))).astype(BF)
            return carry

        lax.fori_loop(0, cells // 256, end, 0, unroll=True)
        to_natural(y[...], ns.back[...], ns.gather[...], nat)

    pl.run_scoped(phase, pltpu.VMEM((cells, wide), BF), pltpu.VMEM((cells, hidden), BF), pltpu.VMEM((cells, wide), F32))


def parts3(value):
    high = value.astype(BF)
    rest = value - high.astype(F32)
    middle = rest.astype(BF)
    return high, middle, (rest - middle.astype(F32)).astype(BF)


def select(value, matrix):
    return sum(dot(v, matrix) for v in parts3(value))


def pack_shards(ns, swap):
    s = lax.axis_index("section")
    c, wide = ns.spread.shape
    hid, n = 2 * ns.half_hidden.shape[0], ns.deep_spread.shape[0]

    def phase(nat, half_hidden, deep_spread):
        got = loads([(ns.half_hidden, half_hidden), (ns.deep_spread, deep_spread)], ns.keep)

        def rows(flat, width):
            count = flat.shape[1] // width
            tall = -(-count // 16) * 16
            nat[tall - 16 : tall] = jnp.zeros((16, nat.shape[1]), F32)
            for r in range(count):
                nat[r : r + 1, 0:width] = flat[0:1, r * width : r * width + width]
            return tall

        tall = rows(ns.w_in, hid)
        got[0]()
        size = half_hidden.shape[1]
        for q in range(2):
            ns.shard0[s, :, size * q : size * q + size] = dot(nat[0:tall, hid // 2 * q : hid // 2 * q + hid // 2].astype(BF), half_hidden[...]).astype(BF)
        swap(0)
        tall = rows(ns.w_out, c)
        ns.shard1[s] = dot(nat[0:tall, 0:c].astype(BF), ns.spread[...]).astype(BF)
        swap(1)
        got[1]()

        @pl.when(s == 0)
        def _():
            tall = rows(ns.resample, n)
            laid = dot(nat[0:tall, 0:n].astype(BF), deep_spread[...]).astype(BF)
            ns.shard2[0] = dot(ns.rows[...], laid).astype(BF)

        @pl.when(s == 1)
        def _():
            tall = rows(ns.resample, 4 * c)
            for q in range(4):
                ns.shard2[1, tall * (q // 2) : tall * (q // 2) + tall, wide * (q % 2) : wide * (q % 2) + wide] = dot(
                    nat[0:tall, c * q : c * q + c].astype(BF), ns.spread[...]).astype(BF)

        swap(2)
        tall = rows(ns.merge, c)
        ns.shard3[s] = dot(nat[0:tall, 0:c].astype(BF), ns.spread[...]).astype(BF)
        swap(3)
        nat[48:64] = jnp.zeros((16, nat.shape[1]), F32)
        nat[0:49, 0:c] = ns.kernel[0]
        for k, ref in enumerate((ns.bn_gain, ns.bn_bias, ns.bias_out)):
            nat[49 + k : 50 + k, 0:c] = ref[...]
        ns.par[s] = select(nat[0:56, 0:c], ns.spread[...])
        swap(4)
        nat[0:8] = jnp.zeros((8, nat.shape[1]), F32)
        nat[0:1, 0:hid] = ns.bias_in[...]
        for q in range(2):
            ns.bias[s, :, size * q : size * q + size] = select(nat[0:8, hid // 2 * q : hid // 2 * q + hid // 2], half_hidden[...])
        swap(5)

    pl.run_scoped(phase, pltpu.VMEM((112, max(hid, 4 * c)), F32), pltpu.VMEM(ns.half_hidden.shape, BF), pltpu.VMEM(ns.deep_spread.shape, BF))


def unpack_sums(ns, first, second):
    s = lax.axis_index("section")
    wide, c = ns.gather.shape
    hid, n = 2 * ns.half_hidden_back.shape[1], ns.deep_back.shape[1]

    def phase(nat, half_back, deep_back):
        got = loads([(ns.half_hidden_back, half_back), (ns.deep_back, deep_back)], ns.load_sem)
        got[0]()
        got[1]()

        def narrow(value, matrix):
            return dot(value.astype(BF), matrix) + dot((value - value.astype(BF).astype(F32)).astype(BF), matrix)

        def rows(out, width, count):
            for r in range(count):
                out[0:1, r * width : r * width + width] = nat[r : r + 1, 0:width]

        first()
        nat[0:64, 0:c] = narrow(ns.total[...], ns.gather[...])
        ns.gk[0] = nat[0:49, 0:c]
        ns.gs[...] = nat[56:57, 0:c]
        ns.gg[...] = nat[57:58, 0:c]
        ns.gbo[...] = nat[58:59, 0:c]
        size = half_back.shape[0]
        flat = jnp.concatenate([ns.total[59 + k : 60 + k] for k in range(-(-2 * size // wide))], axis=1)
        for q in range(2):
            ns.gbi[0:1, hid // 2 * q : hid // 2 * q + hid // 2] = narrow(jnp.broadcast_to(flat[:, size * q : size * q + size], (8, size)), half_back[...])[0:1]
        merge = ns.gm.reshape(-1, wide)
        nat[0 : merge.shape[0], 0:c] = narrow(merge[...], ns.gather[...])
        rows(ns.gmm, c, ns.gmm.shape[1] // c)
        deep = ns.gr.reshape(-1, ns.gr.shape[2])

        @pl.when(s == 0)
        def _():
            nat[0 : deep.shape[0], 0:n] = narrow(deep[...], deep_back[...])
            band, high = c // GROUPS, deep.shape[0] // 4
            for k in range(4):
                for r in range(band):
                    at = n * (band * k + r)
                    ns.gres[0:1, at : at + n] = nat[high * k + r : high * k + r + 1, 0:n]

        @pl.when(s == 1)
        def _():
            high = deep.shape[0] // 2
            for j in range(2):
                nat[0 : deep.shape[0], 0:c] = narrow(deep[:, wide * j : wide * j + wide], ns.gather[...])
                for i in range(2):
                    for r in range(n // GROUPS):
                        at = 4 * c * r + c * (2 * i + j)
                        ns.gres[0:1, at : at + c] = nat[high * i + r : high * i + r + 1, 0:c]

        second()
        grad = ns.gw1.reshape(-1, ns.gw1.shape[2])
        for q in range(2):
            nat[0 : grad.shape[0], hid // 2 * q : hid // 2 * q + hid // 2] = narrow(grad[:, size * q : size * q + size], half_back[...])
        rows(ns.gwi, hid, ns.gwi.shape[1] // hid)
        for k in range(2):
            lanes = wide // 2
            part = narrow(ns.gw2[k], ns.gather[lanes * k : lanes * k + lanes])
            if k == 0:
                nat[0 : ns.gw2.shape[1], 0:c] = part
            else:
                nat[0 : ns.gw2.shape[1], 0:c] += part
        rows(ns.gwo, c, ns.gwo.shape[1] // c)

    pl.run_scoped(phase, pltpu.VMEM((128, max(hid, 4 * c)), F32), pltpu.VMEM(ns.half_hidden_back.shape, BF), pltpu.VMEM(ns.deep_back.shape, BF))


def forward_kernel(fast, count, cols, ns):
    s, d, g, m, p = where_am_i()
    greet_near(count)
    x14 = ns.x14
    x_begin, x_end = collect(ns.x, x14, 3, ns.xs, ns.xr)
    land_begin, land_end = collect_land(ns.land, ns.land2, ns.ls, ns.lr)
    x_begin()
    land_begin()
    swapped = [getattr(ns, f"shard{k}") for k in range(4)] + [ns.par, ns.bias] if fast else [ns.par, ns.bias]

    def swap(k):
        return remote(swapped[k].at[s], swapped[k].at[s], ns.ps.at[k], ns.pr.at[k], (1 - s, d))

    def swap_in(k):
        arrived(swapped[k].at[1 - s], ns.pr.at[k])

    fulls = dict(w1_0=ns.w1_0, w2_0=ns.w2_0, r0=ns.r0, m0=ns.m0, m1=ns.m1, r1=ns.r1, w1_1=ns.w1_1, w2_1=ns.w2_1)
    which = dict(w1_0=(0, 0), w2_0=(1, 0), r0=(2, 0), r1=(2, 1), m0=(3, 0), m1=(3, 1), w1_1=(0, 1), w2_1=(1, 1))
    mats = {}
    for k, (name, full) in enumerate(fulls.items()):
        if fast:
            index, sec = which[name]
            mats[name] = Gather(getattr(ns, f"shard{index}").at[sec], full, ns.gs.at[k], ns.gr.at[k])
        else:
            mats[name] = Load(getattr(ns, name + "_in"), full, ns.gs.at[k])
    kept = dict(z0=ns.z, z1=ns.z, a0=ns.a0, a1=ns.a1, skip=ns.skip, up=ns.up, pieces=ns.pieces, deep=ns.deep, nat0=ns.nat0, nat1=ns.nat1)
    keeps = {name: lambda k=k, name=name, ref=ref: pltpu.make_async_copy(ref, getattr(ns, name + "_out"), ns.keep.at[k]) for k, (name, ref) in enumerate(kept.items())}

    def keep(*names):
        for name in names:
            keeps[name]().start()

    saves = {name: lambda k=k, name=name, full=full: pltpu.make_async_copy(full, getattr(ns, name + "_out"), ns.save.at[k]) for k, (name, full) in enumerate(fulls.items())}

    def do(step, *names):
        for name in names:
            getattr(mats[name], step)()

    def whole(*names):
        do("whole", *names)
        for name in names:
            saves[name]().start()

    def give(k):
        swap(k).start()
        if k == 1:
            swap_in(0)
            do("start", "w1_0")
        if k == 2:
            swap_in(1)
            do("start", "w2_0")

    if fast:
        pack_shards(ns, give)
        swap_in(2)
        swap_in(3)
    else:
        near = [pltpu.make_async_copy(src, dst.at[s], ns.keep.at[k]) for k, (src, dst) in enumerate(((ns.mine, ns.par), (ns.mine_bias, ns.bias)))]
        for c in near:
            c.start()
        for c in near:
            c.wait()
        for k in range(2):
            swap(k).start()
        do("start", "w1_0", "w2_0")
    do("start", "r0")
    land_end()
    masks(ns.land2, ns.ocean, ns.coarse, ns.pick[...], ns.patch[...])
    x_end()

    def edge(up):
        src, dst = (x14.at[pl.ds(3, 3)], x14.at[pl.ds(11, 3)]) if up else (x14.at[pl.ds(8, 3)], x14.at[pl.ds(0, 3)])
        return remote(src, dst, ns.hs.at[int(up)], ns.hr.at[int(up)], device(p - 1 if up else p + 1, m))

    pl.when(p > 0)(edge(True).start)
    pl.when(p < count - 1)(edge(False).start)
    do("plane", "w1_0", "w2_0")
    swap_in(len(swapped) - 2)
    swap_in(len(swapped) - 1)

    @pl.when(p == 0)
    def _():
        x14[0:3] = jnp.zeros((3,) + x14.shape[1:], BF)

    @pl.when(p == count - 1)
    def _():
        x14[11:14] = jnp.zeros((3,) + x14.shape[1:], BF)

    pl.when(p > 0)(lambda: arrived(x14.at[pl.ds(0, 3)], ns.hr.at[0]))
    pl.when(p < count - 1)(lambda: arrived(x14.at[pl.ds(11, 3)], ns.hr.at[1]))

    cot_begin, cot_end = collect(ns.cot, ns.cot8, 0, ns.cs, ns.cr)

    do("onward", "w1_0", "w2_0")

    conv_phase(0, cols, ns, script(
        nothing,
        lambda: (do("plane", "r0"), do("start", "r1", "m0", "m1")),
        nothing,
        nothing,
        lambda: do("over", "w1_0", "w2_0"),
        lambda: do("onward", "r0"),
    ))
    ns.st0[...] = all_sum(ns.stats, ns.slots, ns.send, ns.recv, count)
    keep("z0", "a0")
    whole("w1_0", "w2_0")
    ff0 = {1: lambda: (do("plane", "r1", "m0", "m1"), do("start", "w1_1", "w2_1")), 7: lambda: do("over", "r0")}
    ff_phase(0, ns, ns.st0, ns.w1_0, ns.w2_0, ns.a0, ns.skip, ns.nat0, lambda k: ff0.get(k, nothing)())
    keep("skip", "nat0")

    skip, pieces, wide = ns.skip, ns.pieces, ns.skip.shape[1]
    blocks = skip.shape[0] // 256
    down, up_w = ns.r0.reshape(4 * wide, -1), ns.r1.reshape(GROUPS, 2, ns.r1.shape[2] // 2, -1)
    merge = [v.reshape(wide, wide) for v in (ns.m0, ns.m1)]
    for b in range(blocks):
        moved = dot(ns.patch[...], skip[256 * b : 256 * b + 256]).astype(BF)
        for k in range(4):
            pieces[k, 64 * b : 64 * b + 64] = moved[64 * k : 64 * k + 64]
    do("onward", "r1", "m0", "m1")
    do("plane", "w1_1", "w2_1")
    whole("r0")
    value = sum(dot(pieces[k], down[wide * k : wide * k + wide]) for k in range(4))
    deep_value = (lanes4(ns.coarse[...], value.shape[1]) * value).astype(BF)
    ns.deep[...] = deep_value
    keep("pieces", "deep")
    do("over", "m0", "m1", "r1")
    do("onward", "w1_1", "w2_1")
    cot_begin()
    whole("m0", "m1", "r1")
    rows = up_w.shape[0] * up_w.shape[2]
    lifted = [dot(deep_value, up_w[:, i].reshape(rows, -1)).astype(BF) for i in range(2)]
    for b in range(blocks):
        at = slice(256 * b, 256 * b + 256)
        stacked = jnp.concatenate(
            [lifted[i][64 * b : 64 * b + 64, wide * j : wide * j + wide] for i in range(2) for j in range(2)], axis=0
        )
        ns.up[at] = dot(ns.unpatch[...], stacked).astype(BF)
    for b in range(blocks):
        at = slice(256 * b, 256 * b + 256)
        joined = dot(ns.up[at], merge[0][...]) + dot(skip[at], merge[1][...])
        ns.h[at] = joined
        low = joined.astype(BF)
        ns.a1[at] = low
        for k in range(2):
            ends = dot(ns.edges[...], low[128 * k : 128 * k + 128]).astype(BF)
            ns.packed[0, 2 * b + k] = ends[:48]
            ns.packed[1, 2 * b + k] = ends[48:]
    swap_rows(ns.packed, ns.halo, ns.es, ns.er, count)
    keep("up", "a1")
    keeps["z0"]().wait()

    conv_phase(1, cols, ns, script(nothing, nothing, lambda: do("over", "w1_1", "w2_1")))
    ns.st1[...] = all_sum(ns.stats, ns.slots1, ns.send1, ns.recv1, count)
    keep("z1")
    whole("w1_1", "w2_1")
    ff_phase(1, ns, ns.st1, ns.w1_1, ns.w2_1, ns.h, ns.y1, ns.nat1, nothing)
    keep("nat1")

    cot_end()
    for name, save in saves.items():
        save().wait()
        do("finish", name)
    for name, copy in keeps.items():
        if name != "z0":
            copy().wait()
    for k in range(len(swapped)):
        swap(k).wait_send()
    pl.when(p > 0)(edge(True).wait_send)
    pl.when(p < count - 1)(edge(False).wait_send)


class Reduce:
    def __init__(self, sec, partial, bank, out, send, recv):
        self.sec, self.partial, self.out, self.send, self.recv = sec, partial, out, send, recv
        self.own, self.core, self.one, self.two, self.row, self.mine = bank
        self.s, self.d, self.g, self.m, _ = where_am_i()
        self.bit = 1 + self.s
        self.rest = self.m ^ (3 - self.bit)

    def near(self):
        return pltpu.make_async_copy(half(self.partial, self.s), self.own, self.send.at[0])

    def over(self):
        return remote(half(self.partial, 1 - self.s), self.core, self.send.at[1], self.recv.at[1], (1 - self.s, self.d))

    def first(self, index):
        col = (self.m ^ self.bit, self.m ^ 3)[index]
        return remote(self.own.at[:, col], self.one.at[:, index], self.send.at[2 + index], self.recv.at[2 + index], (self.s, self.d ^ self.bit))

    def second(self):
        return remote(self.own.at[:, self.rest], self.two, self.send.at[4], self.recv.at[4], (self.s, self.d ^ (3 - self.bit)))

    def along(self, step):
        to = (self.g + step) % 4
        return remote(self.own.at[to, self.m], self.row.at[step - 1], self.send.at[4 + step], self.recv.at[4 + step], (self.s, 4 * to + self.m))

    def give(self):
        return remote(self.mine, self.out.at[self.s], self.send.at[8], self.recv.at[8], (1 - self.s, self.d))

    def start(self):
        self.over().start()
        self.near().start()

    def plane(self):
        self.near().wait()
        arrived(self.core, self.recv.at[1])
        own, core, m, bit = self.own, self.core, self.m, self.bit

        def add(k, carry):
            z, col = k % 4, (m ^ 3, m ^ bit, m ^ (3 - bit), m)
            for c in col:
                own[z, c] = (own[z, c].astype(F32) + core[z, c].astype(F32)).astype(BF)
            return carry

        lax.fori_loop(0, 4, add, 0)
        self.first(1).start()
        self.first(0).start()

    def onward(self):
        own, one, rest = self.own, self.one, self.rest
        arrived(one.at[:, 1], self.recv.at[3])

        def add(z, carry):
            own[z, rest] = (own[z, rest].astype(F32) + one[z, 1].astype(F32)).astype(BF)
            return carry

        lax.fori_loop(0, 4, add, 0)
        self.second().start()

    def line(self):
        own, one, two, m = self.own, self.one, self.two, self.m
        arrived(one.at[:, 0], self.recv.at[2])
        arrived(two, self.recv.at[4])

        def add(z, carry):
            own[z, m] = (own[z, m].astype(F32) + one[z, 0].astype(F32) + two[z].astype(F32)).astype(BF)
            return carry

        lax.fori_loop(0, 4, add, 0)
        for step in range(1, 4):
            self.along(step).start()

    def total(self):
        for step in range(1, 4):
            arrived(self.row.at[step - 1], self.recv.at[4 + step])
        row = self.row
        self.mine[...] = self.own[self.g, self.m].astype(F32) + row[0].astype(F32) + row[1].astype(F32) + row[2].astype(F32)
        pl.when(self.s != self.sec)(lambda: self.give().start())

        @pl.when(self.s == self.sec)
        def _():
            self.out[self.s] = self.mine[...]

    def finish(self):
        self.over().wait_send()
        for index in range(2):
            self.first(index).wait_send()
        self.second().wait_send()
        for step in range(1, 4):
            self.along(step).wait_send()
        pl.when(self.s != self.sec)(lambda: self.give().wait_send())
        pl.when(self.s == self.sec)(lambda: arrived(self.out.at[1 - self.s], self.recv.at[8]))


def reduce_bank(name, shape):
    part = half_shape(shape)
    out = {f"{name}_{k}": pltpu.VMEM(lead + part, BF) for k, lead in (("own", (4, 4)), ("core", (4, 4)), ("one", (4, 2)), ("two", (4,)), ("row", (3,)))}
    out.update({f"{name}_mine": pltpu.VMEM(part, F32), f"{name}_s": DMA((9,)), f"{name}_r": DMA((9,))})
    return out


def reducer(ns, name, sec, partial, out):
    bank = [getattr(ns, f"{name}_{k}") for k in ("own", "core", "one", "two", "row", "mine")]
    return Reduce(sec, partial, bank, out, getattr(ns, f"{name}_s"), getattr(ns, f"{name}_r"))


def loads(pairs, sems, first=0):
    copies = [pltpu.make_async_copy(src, dst, sems.at[first + k]) for k, (src, dst) in enumerate(pairs)]
    for c in copies:
        c.start()
    return [c.wait for c in copies]


def back_ff_phase(sec, count, ns, top, kept, w_in, w_out, hook, done):
    z_in, st = kept
    cells, wide = ns.dym.shape
    hidden = w_in.shape[1]
    chunks = cells // 128
    ocean, small, dym = ns.ocean, ns.small, ns.dym
    counted, mean, inverse, gain, shift = norm_terms(st, ns.par[sec])

    def phase(w1, w2, z, n, de, dn, dr):
        got_z, got_w1, got_w2 = loads([(z_in, z), (w_in, w1), (w_out, w2)], ns.load_sem)

        def begin(c, total):
            at = pl.ds(pl.multiple_of(c * 128, 128), 128)
            if sec == 1:
                block = top[:, c]
                block = dot(block.reshape(-1, block.shape[-1]), ns.spread[...]).astype(BF)
                grad = dot(ns.turn[...], block)
            else:
                grad = top[at]
            grad = grad * lanes4(ocean[at], wide)
            dym[at] = grad
            low = grad.astype(BF)
            dr[at] = low
            return total + rows8(low.astype(F32))

        total = lax.fori_loop(0, chunks, begin, jnp.zeros((8, wide), F32), unroll=True)
        small[2:3] = total.sum(0, keepdims=True)
        small[3:8] = jnp.zeros((5, wide), F32)
        got_z()

        def norm(c, carry):
            at = pl.ds(pl.multiple_of(c * 128, 128), 128)
            n[at] = ((z[at] - mean) * inverse * gain + shift).astype(BF)
            return carry

        lax.fori_loop(0, chunks, norm, 0, unroll=True)
        got_w1()
        got_w2()
        for h in range(hidden // 256):
            at = slice(256 * h, 256 * h + 256)
            e = dot(n[...], w1[:, at]) + ns.bias[sec, 0:1, at]
            phi, slope = gelu_terms(e)
            ns.dw2[at] = dot_tn((e * phi).astype(BF), dr[...]).astype(BF)
            low = (dot_nt(dr[...], w2[at]) * slope).astype(BF)
            de[:, at] = low
            row, col = 3 + 256 * h // wide, 256 * h % wide
            small[row : row + 1, col : col + 256] = low.astype(F32).sum(0, keepdims=True)
            ns.dw1[:, at] = dot_tn(n[...], low).astype(BF)
            hook(h)
        done()
        dn[...] = dot_nt(de[...], w1[...])

        def sums(c, carry):
            at = pl.ds(pl.multiple_of(c * 128, 128), 128)
            grad = dn[at]
            return carry[0] + rows8(grad), carry[1] + rows8(grad * ((z[at] - mean) * inverse))

        zero = jnp.zeros((8, wide), F32)
        plain, scaled = lax.fori_loop(0, chunks, sums, (zero, zero), unroll=True)
        small[0:1] = plain.sum(0, keepdims=True)
        small[1:2] = scaled.sum(0, keepdims=True)
        ns.stats[...] = small[...]
        summed = all_sum(ns.stats, ns.slots, ns.send, ns.recv, count)
        first = -inverse * gain * summed[0:1] / counted
        second = -inverse * inverse * gain * summed[1:2] / counted

        def end(c, carry):
            at = pl.ds(pl.multiple_of(c * 128, 128), 128)
            grad = inverse * gain * dn[at] + lanes4(ocean[at], wide) * (first + second * (z[at] - mean))
            low = grad.astype(BF)
            ns.dz[at] = low
            ends = dot(ns.edges[...], low).astype(BF)
            ns.packed[0, c] = ends[:48]
            ns.packed[1, c] = ends[48:]
            return carry

        lax.fori_loop(0, chunks, end, 0, unroll=True)

    field = lambda t: pltpu.VMEM((cells, wide), t)
    pl.run_scoped(
        phase, pltpu.VMEM(w_in.shape, BF), pltpu.VMEM(w_out.shape, BF), field(F32), field(BF), pltpu.VMEM((cells, hidden), BF), field(F32), field(BF),
    )
    swap_rows(ns.packed, ns.halo, ns.hsend, ns.hrecv, count)


def back_conv_phase(sec, cols, ns, a_in, tiny, hook):
    cells, wide = ns.dz.shape
    dz = ns.dz

    def phase(S, kb, a, field, acc_dk):
        (got_a,) = loads([(a_in, a)], ns.load_sem)
        taps_to(kb, ns.par[sec], True)
        lanes = S.shape[1]
        for group in range(wide // 128 // lanes):
            part = slice(group * lanes * 128, (group + 1) * lanes * 128)

            def chunk(c, carry):
                block = jnp.concatenate([dz[pl.ds(pl.multiple_of(c * 128, 128), 128), part], ns.halo[0, c, :, part], ns.halo[1, c, :, part]], axis=0)
                shifted(block, ns.shifts[...], S, c)
                return carry

            lax.fori_loop(0, cols // 16, chunk, 0)
            wrap(S, cols)
            hook()
            if group == 0:
                got_a()
            tiles = [(lane, slice((group * lanes + lane) * 128, (group * lanes + lane + 1) * 128)) for lane in range(lanes)]
            for lane, at in tiles:

                def step(b, carry):
                    rows = pl.ds(pl.multiple_of(b * 128, 128), 128)
                    above = ns.dym[rows, at].reshape(16, 8, 128)
                    sums = taps_at(S, kb, lane, group * lanes + lane, b * 16, [above[k] for k in range(16)])
                    dz[rows, at] = jnp.concatenate(sums, axis=0).astype(BF)
                    return carry

                lax.fori_loop(0, cols // 16, step, 0)
            hook()
            for lane, at in tiles:
                field[...] = a[:, at].astype(F32).reshape(field.shape)
                acc_dk[...] = jnp.zeros(acc_dk.shape, F32)

                def tap_sums(b, carry):
                    here = [field[b * 16 + k] for k in range(16)]
                    for i in range(7):
                        window = [S[i, lane, b * 16 + t] for t in range(22)]
                        for j in range(7):
                            total = window[j] * here[0]
                            for k in range(1, 16):
                                total = total + window[j + k] * here[k]
                            acc_dk[7 * i + j] += total
                    return carry

                lax.fori_loop(0, cols // 16, tap_sums, 0)
                for k in range(49):
                    tiny[48 - k : 49 - k, at] = acc_dk[k].sum(0, keepdims=True)
            hook()
        tiny[49:56] = jnp.zeros((7, wide), F32)

    pl.run_scoped(
        phase, pltpu.VMEM((7, 2, cols + 6, 8, 128), F32), pltpu.VMEM((wide // 128, 49, 8, 128), F32), pltpu.VMEM((cells, wide), BF),
        pltpu.VMEM((cols, 8, 128), F32), pltpu.VMEM((49, 8, 128), F32),
    )


def back_mid_phase(ns, hook):
    dh = ns.dz
    cells, wide = dh.shape
    blocks = cells // 256

    def phase(skip, up, merge0, merge1, up_w, deep, down, pieces, dups, spreads, dskip):
        got = loads(
            [(ns.m1, merge1), (ns.m0, merge0), (ns.up, up), (ns.skip, skip), (ns.r1, up_w), (ns.deep, deep), (ns.pieces, pieces), (ns.r0, down)],
            ns.load_sem,
        )
        for k in range(2):
            got[k]()
        for b in range(blocks):
            at = slice(256 * b, 256 * b + 256)
            low = dot_nt(dh[at], merge1[...]).astype(BF)
            ns.dym[at] = low.astype(F32)
            dskip[at] = low
            lifted = dot_nt(dh[at], merge0[...]).astype(BF)
            moved = dot(ns.patch[...], lifted).astype(BF)
            for k in range(4):
                dups[k // 2, 64 * b : 64 * b + 64, wide * (k % 2) : wide * (k % 2) + wide] = moved[64 * k : 64 * k + 64]
        to_natural(dskip[...], ns.back[...], ns.gather[...], ns.nat)
        hook(0)
        got[2]()
        got[3]()
        ns.dm0[...] = dot_tn(up[...], dh[...]).astype(BF)
        ns.dm1[...] = dot_tn(skip[...], dh[...]).astype(BF)
        hook(1)
        rows = up_w.shape[0] * up_w.shape[2]
        got[4]()
        ddeep = dot_nt(dups[0], up_w[:, 0].reshape(rows, -1)) + dot_nt(dups[1], up_w[:, 1].reshape(rows, -1))
        got[5]()
        for i in range(2):
            up_w[:, i] = dot_tn(deep[...], dups[i]).astype(BF).reshape(up_w.shape[0], up_w.shape[2], -1)
        saves = [pltpu.make_async_copy(up_w, ns.dr1, ns.load_sem.at[0]), pltpu.make_async_copy(down, ns.dr0, ns.load_sem.at[1])]
        saves[0].start()
        masked = (lanes4(ns.coarse[...], ddeep.shape[1]) * ddeep).astype(BF)
        hook(2)
        got[6]()
        got[7]()
        for k in range(4):
            spreads[k] = dot_nt(masked, down[wide * k : wide * k + wide])
            down[wide * k : wide * k + wide] = dot_tn(pieces[k], masked).astype(BF)
        saves[1].start()
        saves[0].wait()
        hook(3)
        for b in range(blocks):
            value = jnp.concatenate([spreads[k, 64 * b : 64 * b + 64] for k in range(4)], axis=0)
            high = value.astype(BF)
            rest = (value - high.astype(F32)).astype(BF)
            at = slice(256 * b, 256 * b + 256)
            ns.dym[at] += dot(ns.unpatch[...], high) + dot(ns.unpatch[...], rest)
        saves[1].wait()

    like = lambda ref: pltpu.VMEM(ref.shape, BF)
    deep_cells = ns.deep.shape[0]
    pl.run_scoped(
        phase, like(ns.skip), like(ns.up), like(ns.m0), like(ns.m1), like(ns.r1), like(ns.deep), like(ns.r0), like(ns.pieces),
        pltpu.VMEM((2, deep_cells, 2 * wide), BF), pltpu.VMEM((4, deep_cells, wide), F32), pltpu.VMEM((cells, wide), BF),
    )


def with_names(ns, **names):
    out = Names()
    out.__dict__.update(ns.__dict__)
    out.__dict__.update(names)
    return out


def back_kernel(fast, count, cols, ns):
    s, d, g, m, p = where_am_i()
    greet_near(count)
    acts = [deliver(k, getattr(ns, f"nat{k}"), ns.act, getattr(ns, f"bounce{k}"), ns.ds.at[k], ns.dr.at[k], ns.db.at[k]) for k in range(2)]
    gi1, gi0 = (deliver(1 - k, ns.nat, ns.gi, getattr(ns, f"bounce{2 + k}"), ns.ds.at[2 + k], ns.dr.at[2 + k], ns.db.at[2 + k]) for k in range(2))
    w_dec = w_enc = m_all = r_up = r_down = []
    if fast:
        cut = lambda ref: ref.reshape(4, 4, ref.shape[0] // 16, ref.shape[1])
        w_dec = [reducer(ns, "w0", 1, cut(ns.dw1), ns.gw1), reducer(ns, "w1", 1, cut(ns.dw2), ns.gw2)]
        w_enc = [reducer(ns, "w0", 0, cut(ns.dw1), ns.gw1), reducer(ns, "w1", 0, cut(ns.dw2), ns.gw2)]
        m_all = [reducer(ns, f"m{k}", k, cut(getattr(ns, f"dm{k}")), ns.gm) for k in range(2)]
        r_up = [reducer(ns, "r1", 1, ns.dr1.reshape(4, 4, -1, ns.dr1.shape[3]), ns.gr)]
        r_down = [reducer(ns, "r0", 0, ns.dr0.reshape(4, 4, -1, ns.dr0.shape[1]), ns.gr)]

    def do(*steps):
        def action(*_):
            for step in steps:
                if isinstance(step, tuple):
                    for r in step[0]:
                        getattr(r, step[1])()
                else:
                    step()

        return action

    def keep_dw(sec):
        if not fast:
            copies = [pltpu.make_async_copy(ns.dw1, getattr(ns, f"dw1_{sec}"), ns.ps.at[0]), pltpu.make_async_copy(ns.dw2, getattr(ns, f"dw2_{sec}"), ns.ps.at[1])]
            for copy in copies:
                copy.start()
            for copy in copies:
                copy.wait()

    def at_step(**actions):
        return lambda h: actions.get(f"h{h}", nothing)()

    do(*(act[0] for act in acts))()
    dec = with_names(ns, halo=ns.halo1, slots=ns.slots1, send=ns.send1, recv=ns.recv1, hsend=ns.hsend1, hrecv=ns.hrecv1)
    back_ff_phase(1, count, dec, ns.top, (ns.z1, ns.st1), ns.w1_1, ns.w2_1, at_step(h3=do(*(act[1] for act in acts))), do((w_dec, "start"), lambda: keep_dw(1)))
    back_conv_phase(1, cols, dec, ns.a1, ns.tiny1, script(
        do((w_dec, "plane")), nothing, do(*(act[3] for act in acts)), do((w_dec, "onward")), nothing, do((w_dec, "line"))))
    ns.tiny1[56:64] = ns.small[...]
    back_mid_phase(ns, script(gi1[0], do((m_all, "start")), do((w_dec, "total"), gi1[1]), do((r_up, "start"), (m_all, "plane"))))
    do((r_down, "start"), (w_dec, "finish"))()

    back_ff_phase(0, count, ns, ns.dym, (ns.z0, ns.st0), ns.w1_0, ns.w2_0, at_step(
        h0=do((r_up, "plane")), h2=do((m_all, "onward")), h4=do((r_down, "plane")),
    ), do((w_enc, "start"), (m_all, "line"), lambda: keep_dw(0)))
    do((r_up, "onward"), (w_enc, "plane"))()
    def give_dh():
        to_natural(ns.dz[...], ns.back[...], ns.gather[...], ns.nat)
        gi0[0]()

    back_conv_phase(0, cols, ns, ns.a0, ns.tiny0, script(
        do((r_down, "onward"), (r_up, "line")), do((m_all, "total"), gi1[3]), do((w_enc, "onward"), (r_down, "line")), do((r_up, "total")),
        do(give_dh, (w_enc, "line")), gi0[1]))
    ns.tiny0[56:64] = ns.small[...]
    if fast:
        sm, tiny, ts, tr = ns.sm, ns.tiny, ns.ts, ns.tr
        sm[0] = ns.tiny0[...]
        sm[1] = ns.tiny1[...]
        over = remote(sm.at[1 - s], tiny.at[0], ts.at[0], tr.at[0], (1 - s, d))
        over.start()
        arrived(tiny.at[0], tr.at[0])
        over.wait_send()
        tiny[1] = sm[s] + tiny[0]
        for base, peer in ((1, lambda step: (s, 4 * ((g + step) % 4) + m)), (5, lambda step: (s, d ^ step))):
            sent = [remote(tiny.at[base], tiny.at[base + step], ts.at[base + step], tr.at[base + step], peer(step)) for step in range(1, 4)]
            for c in sent:
                c.start()
            if base == 1:
                do((r_down, "total"))()
            for step in range(1, 4):
                arrived(tiny.at[base + step], tr.at[base + step])
            for c in sent:
                c.wait_send()
            total = tiny[base] + tiny[base + 1] + tiny[base + 2] + tiny[base + 3]
            if base == 1:
                tiny[5] = total
            else:
                ns.total[...] = total
    if fast:
        unpack_sums(ns, do((m_all + r_up + r_down, "finish")), do((w_enc, "total"), (w_enc, "finish")))
    gi0[3]()


class Names:
    pass


def build(name, body, ins, outs, scratch, alias, cid, limit):
    ins = {k: v if isinstance(v, tuple) else (v, VM) for k, v in ins.items()}
    outs = {k: v if len(v) == 3 else v + (VM,) for k, v in outs.items()}
    names = list(ins) + list(outs) + list(scratch)

    def kernel(*refs):
        ns = Names()
        for k, ref in zip(names, refs):
            setattr(ns, k, ref)
        body(ns)

    order_in, order_out = list(ins), list(outs)
    results = pl.pallas_call(
        kernel, name=name, out_shape=[jax.ShapeDtypeStruct(v[0], v[1]) for v in outs.values()],
        in_specs=[v[1] for v in ins.values()], out_specs=[v[2] for v in outs.values()], scratch_shapes=list(scratch.values()),
        input_output_aliases={order_in.index(a): order_out.index(b) for a, b in alias.items()},
        compiler_params=pltpu.CompilerParams(vmem_limit_bytes=limit * MEGA, collective_id=cid, has_side_effects=True),
    )(*[v[0] for v in ins.values()])
    out = Names()
    for k, v in zip(order_out, results):
        setattr(out, k, v)
    return out


def on_device(sections, dps, inputs, cotangent, land, kernel, bn_gain, bn_bias, bias_in, bias_out, w_in, w_out, resample, merge):
    batches, height, cols, c = inputs.shape
    hid = bias_in.shape[1]
    n = resample.shape[1] * dps // (4 * c)
    cw, hw, nw = (GROUPS * padded(v) for v in (c, hid, n))
    cells, deep_cells = cols * 8, cols * 2
    count = 2 * (dps // 4)
    fast = dps == GROUPS
    assert batches == 4 and height == 4 and dps % 4 == 0 and sections == 2 and cols % 32 == 0
    s = lax.axis_index("section")
    mats = {k: jnp.asarray(v) for k, v in matrices(c, hid, n).items()}
    tiles = cols // 16
    both = ("section", "dp")

    def packs(parts, w1, w2, rd, ru):
        return pack_in(w1, parts, c, hid), pack_in(w2, parts, hid, c), pack_down(rd, parts, c, n), pack_up(ru, parts, c, n)

    if not fast:
        flat = [lax.all_gather(v.astype(BF).reshape(-1), both, axis=0, tiled=True) for v in (w_in, w_out, resample, merge)]
        halves = [v.reshape(2, -1) for v in flat]
        whole = [packs(GROUPS, halves[0][k], halves[1][k], halves[2][k], halves[2][k]) for k in range(2)]
        rows = jnp.concatenate([kernel[0], bn_gain, bn_bias, bias_out], axis=0)
        mine = grow(grow(rows.reshape(-1, GROUPS, c // GROUPS), (52, GROUPS, padded(c))).reshape(52, cw), (56, cw))
        mine_bias = grow(grow(bias_in.reshape(GROUPS, -1), (GROUPS, padded(hid))).reshape(1, hw), (8, hw))

    x = inputs.reshape(batches, height, tiles, 16, c)
    cot = cotangent.reshape(batches, height, tiles, 16, c)
    land_cols = -(-cols // 128) * 128
    at_any = lambda v: (v, ANY)
    field = lambda t: ((cells, cw), t)
    natural = ((8, tiles, 16, c), BF)
    edge_rows = ((2, tiles, 48, cw), BF)
    shapes = [(padded(c), hw), (padded(hid), cw), (4 * padded(c), nw), (padded(c), cw)]
    names = dict(w1_0=0, w2_0=1, r0=2, m0=3, m1=3, r1=2, w1_1=0, w2_1=1)
    ins = dict(x=x, land=grow(land, (8, land_cols)), cot=cot)
    if fast:
        ins.update(half_hidden=mats["half_hidden"], deep_spread=mats["deep_spread"])
    else:
        ins.update(mine=mine, mine_bias=mine_bias)
        given = dict(w1_0=whole[0][0], w2_0=whole[0][1], r0=whole[0][2], r1=whole[1][3], w1_1=whole[1][0], w2_1=whole[1][1])
        given.update(m0=pack_in(halves[3][0], GROUPS, c, c), m1=pack_in(halves[3][1], GROUPS, c, c))
        ins.update({k + "_in": v.reshape((4, 4) + shapes[names[k]]) for k, v in given.items()})
    ins = {k: at_any(v) for k, v in ins.items()}
    ins.update({k: mats[k] for k in ("spread", "gather", "natural", "shifts", "patch", "unpatch", "edges", "back", "pick", "rows")})
    if fast:
        ins.update(w_in=w_in, w_out=w_out, resample=resample, merge=merge.reshape(1, -1), kernel=kernel, bn_gain=bn_gain, bn_bias=bn_bias, bias_in=bias_in, bias_out=bias_out)
    outs = dict(
        par=((2, 56, cw), F32), bias=((2, 8, hw), F32), ocean=((cells, 128), F32), coarse=((deep_cells, 128), F32),
        st0=((8, cw), F32), st1=((8, cw), F32), cot8=natural + (ANY,),
    )
    held = dict(
        a0=field(BF), a1=field(BF), skip=field(BF), up=field(BF), pieces=((4, deep_cells, cw), BF), deep=((deep_cells, nw), BF), nat0=natural, nat1=natural,
    )
    outs.update({k + "_out": v + (ANY,) for k, v in held.items()}, z0_out=((cols, 8, cw), F32, ANY), z1_out=((cols, 8, cw), F32, ANY))
    outs.update({k + "_out": ((4, 4) + shapes[v], BF, ANY) for k, v in names.items()})
    scratch = dict(
        x14=pltpu.VMEM((14, tiles, 16, c), BF), land2=pltpu.VMEM((2, 8, land_cols), jnp.int32),
        z=pltpu.VMEM((cols, 8, cw), F32),
        h=pltpu.VMEM((cells, cw), F32),
        halo=pltpu.VMEM(*edge_rows), packed=pltpu.VMEM(*edge_rows), y1=pltpu.VMEM(*field(BF)),
        stats=pltpu.VMEM((8, cw), F32), slots=pltpu.VMEM((count // 2 + 1, 8, cw), F32), slots1=pltpu.VMEM((count // 2 + 1, 8, cw), F32),
        send=DMA((count,)), recv=DMA((count,)), send1=DMA((count,)), recv1=DMA((count,)),
        xs=DMA((4,)), xr=DMA((2,)), ls=DMA((4,)), lr=DMA((2,)), hs=DMA((2,)), hr=DMA((2,)), ps=DMA((6,)), pr=DMA((6,)), cs=DMA((4,)), cr=DMA((2,)),
        es=DMA((2,)), er=DMA((2,)), gs=DMA((8, 12)), gr=DMA((8, 12)), save=DMA((8,)), keep=DMA((10,)),
    )
    scratch.update({k: pltpu.VMEM((4, 4) + shapes[v], BF) for k, v in names.items()}, **{k: pltpu.VMEM(*v) for k, v in held.items()})
    if fast:
        scratch.update({f"shard{k}": pltpu.VMEM((2,) + shapes[k], BF) for k in range(4)})
    fw = build("forward", lambda ns: forward_kernel(fast, count, cols, ns), ins, outs, scratch, {}, 1, 63)
    wide_w = dict(dw1=((cw, hw), BF), dw2=((hw, cw), BF))
    bounce = natural + (ANY,)
    names = ("par", "ocean", "coarse", "bias", "st0", "st1")
    ins = dict(top=fw.cot8, **{k: getattr(fw, k) for k in names})
    ins.update({k: mats[k] for k in ("shifts", "edges", "back", "gather", "spread", "turn", "patch", "unpatch")})
    ins.update({k: at_any(getattr(fw, k + "_out")) for k in ("nat0", "nat1", "a0", "a1", "up", "skip", "deep", "pieces")})
    ins.update({k: at_any(getattr(fw, k + "_out").reshape(cells, cw)) for k in ("z0", "z1")})
    views = dict(w1_0=(cw, hw), w2_0=(hw, cw), w1_1=(cw, hw), w2_1=(hw, cw), m0=(cw, cw), m1=(cw, cw), r0=(4 * cw, nw), r1=(GROUPS, 2, padded(n), 2 * cw))
    ins.update({k: at_any(getattr(fw, k + "_out").reshape(v)) for k, v in views.items()})
    outs = dict(
        act=((4, 4, tiles, 16, c), BF, ANY), gi=((4, 4, tiles, 16, c), BF, ANY), tiny0=((64, cw), F32), tiny1=((64, cw), F32),
        dm0=((cw, cw), BF), dm1=((cw, cw), BF), dr0=(views["r0"], BF, ANY), dr1=(views["r1"], BF, ANY), **{f"bounce{k}": bounce for k in range(4)},
    )
    space = {k: pltpu.VMEM(*v) for k, v in dict(dym=field(F32), dz=field(BF), packed=edge_rows, halo=edge_rows, halo1=edge_rows, nat=natural, **wide_w).items()}
    space.update(small=pltpu.VMEM((8, cw), F32), stats=pltpu.VMEM((8, cw), F32))
    for k in ("", "1"):
        space.update({"slots" + k: pltpu.VMEM((count // 2 + 1, 8, cw), F32), "send" + k: DMA((count,)), "recv" + k: DMA((count,)), "hsend" + k: DMA((2,)), "hrecv" + k: DMA((2,))})
    space.update(load_sem=DMA((8,)), ds=DMA((4, 2, 2)), dr=DMA((4, 4)), db=DMA((4, 2)), ps=DMA((2,)))
    if fast:
        for name, k in (("w0", 0), ("w1", 1), ("m0", 3), ("m1", 3), ("r0", 2), ("r1", 2)):
            space.update(reduce_bank(name, shapes[k]))
        for name, k in (("gw1", 0), ("gw2", 1), ("gr", 2), ("gm", 3)):
            space[name] = pltpu.VMEM((2,) + half_shape(shapes[k]), F32)
        space["total"] = pltpu.VMEM((64, cw), F32)
        outs.update(gwi=(w_in.shape, F32), gwo=(w_out.shape, F32), gres=(resample.shape, F32), gmm=((1, merge.shape[0]), F32))
        outs.update(gk=((1, 49, c), F32), gg=((1, c), F32), gs=((1, c), F32), gbo=((1, c), F32), gbi=((1, hid), F32))
        ins.update(half_hidden_back=at_any(mats["half_hidden_back"]), deep_back=at_any(mats["deep_back"]))
        space.update(sm=pltpu.VMEM((2, 64, cw), F32), tiny=pltpu.VMEM((9, 64, cw), F32), ts=DMA((9,)), tr=DMA((9,)))
    else:
        outs.update({f"{k}_{sec}": v + (ANY,) for k, v in wide_w.items() for sec in range(2)})
    bw = build("backward", lambda ns: back_kernel(fast, count, cols, ns), ins, outs, space, {}, 2, 63)
    activations = bw.act.reshape(1, batches, height, cols, c)
    grad_input = bw.gi.astype(F32).reshape(1, batches, height, cols, c)
    if fast:
        return activations, grad_input, bw.gk, bw.gg, bw.gs, bw.gbi, bw.gbo, bw.gwi, bw.gwo, bw.gres, bw.gmm.reshape(-1)
    scatter = lambda v: lax.psum_scatter(v.astype(F32).reshape(-1), both, scatter_dimension=0, tiled=True)
    gw1 = scatter(jnp.stack([unpack_in(v, c, hid) for v in (bw.dw1_0, bw.dw1_1)]))
    gw2 = scatter(jnp.stack([unpack_in(v, hid, c) for v in (bw.dw2_0, bw.dw2_1)]))
    gres = scatter(jnp.stack([unpack_down(bw.dr0, c, n), unpack_up(bw.dr1, c, n)]))
    gmm = scatter(jnp.stack([unpack_in(v, c, c) for v in (bw.dm0, bw.dm1)]))
    tiny = lax.psum(jnp.stack([bw.tiny0, bw.tiny1]), both)[s]
    narrow = lambda v: v.reshape(-1, GROUPS, padded(c))[:, :, : c // GROUPS].reshape(-1, c)
    fine = narrow(tiny[:59])
    grad_bias_in = tiny[59:63].reshape(-1)[:hw].reshape(GROUPS, -1)[:, : hid // GROUPS].reshape(1, hid)
    return (
        activations, grad_input, fine[None, :49], fine[57:58], fine[56:57], grad_bias_in, fine[58:59],
        gw1[None], gw2[None], gres[None], gmm,
    )


def solution(mesh):
    sections, dps = mesh.shape["section"], mesh.shape["dp"]
    flat, both = P("section", "dp"), P(("section", "dp"))
    per = P("section", None)
    rows = P(None, "dp", None, None)
    taps = P("section", None, None)
    fields = P("section", None, "dp", None, None)
    return jax.shard_map(
        functools.partial(on_device, sections, dps), mesh=mesh,
        in_specs=(rows, rows, P("dp", None), taps, per, per, per, per, flat, flat, flat, both),
        out_specs=(fields, fields, taps, per, per, per, per, flat, flat, flat, both), check_vma=False,
    )
```

```python
import functools

import jax
import jax.numpy as jnp
import ml_dtypes
import numpy as np
from jax import lax
from jax.experimental import pallas as pl
from jax.experimental.pallas import tpu as pltpu
from jax.sharding import PartitionSpec as P

BF = jnp.bfloat16
F32 = jnp.float32
MESH = pl.DeviceIdType.MESH
ANY = pl.BlockSpec(memory_space=pl.ANY)
VM = pl.BlockSpec(memory_space=pltpu.VMEM)
DMA = pltpu.SemaphoreType.DMA
EPS = 1e-05
GROUPS = 16
MEGA = 1 << 20


def padded(width):
    return -(-(width // GROUPS) // 16) * 16


def selector(rows, cols, pairs):
    out = np.zeros((rows, cols), np.float32)
    for r, c in pairs:
        out[r, c] = 1
    return out.astype(ml_dtypes.bfloat16)


def matrices(channels, hidden, deep):
    group, wide = channels // GROUPS, padded(channels)
    spread = selector(channels, GROUPS * wide, [(c, c // group * wide + c % group) for c in range(channels)])
    natural = selector(896, 224, [(i * 128 + q * 8 + p, (p + i) * 16 + q) for i in range(7) for q in range(16) for p in range(8)])

    def place(q, row):
        if row < 0:
            return 128 + q * 3 + row + 3
        return q * 8 + row if row < 8 else 176 + q * 3 + row - 8

    shifts = selector(896, 224, [(i * 128 + q * 8 + p, place(q, p + i - 3)) for i in range(7) for q in range(16) for p in range(8)])
    turn = selector(128, 128, [(q * 8 + p, p * 16 + q) for q in range(16) for p in range(8)])
    edges = selector(96, 128, [(48 * e + q * 3 + k, q * 8 + 5 * e + k) for e in range(2) for q in range(16) for k in range(3)])
    patch = selector(
        256, 256,
        [((i * 2 + j) * 64 + b * 4 + a, (2 * b + j) * 8 + 2 * a + i) for i in range(2) for j in range(2) for b in range(16) for a in range(4)],
    )
    pick = selector(128, 16, [(q * 8 + p, p // 4 * 8 + p % 4) for q in range(16) for p in range(8)])

    def widen(width):
        group, wide = width // GROUPS, padded(width)
        return selector(width, GROUPS * wide, [(v, v // group * wide + v % group) for v in range(width)])

    half_hidden = widen(hidden)[: hidden // 2, : GROUPS * padded(hidden) // 2]
    deep_spread = widen(deep)
    band = channels // GROUPS
    rows = selector(4 * wide, -(-4 * band // 16) * 16, [(k * wide + r, k * band + r) for k in range(4) for r in range(band)])
    return dict(
        half_hidden=half_hidden, half_hidden_back=np.ascontiguousarray(half_hidden.T), deep_spread=deep_spread,
        deep_back=np.ascontiguousarray(deep_spread.T), rows=rows, pick=pick, spread=spread, gather=np.ascontiguousarray(spread.T), natural=natural, shifts=shifts, turn=turn,
        back=np.ascontiguousarray(turn.T), edges=edges, patch=patch, unpatch=np.ascontiguousarray(patch.T),
    )


def grow(value, sizes):
    return jnp.pad(value, [(0, n - o) for n, o in zip(sizes, value.shape)])


def pack_in(value, parts, c, h):
    value = value.reshape(parts, c // GROUPS, GROUPS, h // GROUPS)
    return grow(value, (parts, padded(c), GROUPS, padded(h))).reshape(parts, padded(c), -1)


def pack_down(value, parts, c, n):
    value = value.reshape(parts, 4, c // GROUPS, GROUPS, n // GROUPS)
    return grow(value, (parts, 4, padded(c), GROUPS, padded(n))).reshape(parts, 4 * padded(c), -1)


def pack_up(value, parts, c, n):
    value = value.reshape(parts, n // GROUPS, 2, 2 * GROUPS, c // GROUPS)
    value = grow(value, (parts, padded(n), 2, 2 * GROUPS, padded(c)))
    return value.transpose(0, 2, 1, 3, 4).reshape(parts, 2 * padded(n), -1)


def unpack_in(value, c, h):
    value = value.reshape(-1, padded(c), GROUPS, padded(h))
    return value[:, : c // GROUPS, :, : h // GROUPS].reshape(-1)


def unpack_down(value, c, n):
    value = value.reshape(-1, 4, padded(c), GROUPS, padded(n))
    return value[:, :, : c // GROUPS, :, : n // GROUPS].reshape(-1)


def unpack_up(value, c, n):
    value = value.reshape(-1, 2, padded(n), 2 * GROUPS, padded(c))
    return value.transpose(0, 2, 1, 3, 4)[:, : n // GROUPS, :, :, : c // GROUPS].reshape(-1)


def device(p, m):
    g = p // 2
    return (p + g) % 2, 4 * g + m


def where_am_i():
    s, d = lax.axis_index("section"), lax.axis_index("dp")
    g = d // 4
    return s, d, g, d % 4, 2 * g + (s + g) % 2


def greet_near(count):
    s, d, g, m, p = where_am_i()
    barrier = pltpu.get_barrier_semaphore()

    def one(k, carry):
        q = (p + k) % count
        pl.semaphore_signal(barrier, inc=1, device_id=device(q, m), device_id_type=MESH)
        return carry

    lax.fori_loop(1, count, one, 0)
    for k in range(1, 4):
        for sec in range(2):
            pl.semaphore_signal(barrier, inc=1, device_id=(sec, 4 * g + (m + k) % 4), device_id_type=MESH)
    pl.semaphore_wait(barrier, count + 5)


def remote(src, dst, send, recv, peer):
    return pltpu.make_async_remote_copy(src_ref=src, dst_ref=dst, send_sem=send, recv_sem=recv, device_id=peer, device_id_type=MESH)


def arrived(ref, sem):
    pltpu.make_async_copy(ref, ref, sem).wait()


def all_sum(mine, slots, send, recv, count):
    s, d, g, m, p = where_am_i()
    groups = count // 2
    over = remote(mine, slots.at[groups], send.at[0], recv.at[0], (1 - s, d))
    over.start()
    arrived(slots.at[groups], recv.at[0])
    slots[g] = mine[...] + slots[groups]
    over.wait_send()

    def copy(k):
        return remote(slots.at[g], slots.at[g], send.at[k], recv.at[k], (s, 4 * ((g + k) % groups) + m))

    lax.fori_loop(1, groups, lambda k, c: (copy(k).start(), c)[1], 0)

    def wait(k, carry):
        arrived(slots.at[(g + groups - k) % groups], recv.at[k])
        copy(k).wait_send()
        return carry

    lax.fori_loop(1, groups, wait, 0)
    return lax.fori_loop(0, groups, lambda k, total: total + slots[k], jnp.zeros(mine.shape, F32))


def swap_rows(packed, halo, send, recv, count, between=None):
    s, d, g, m, p = where_am_i()

    def peer(q):
        return device(q, m)

    @pl.when(p > 0)
    def _():
        remote(packed.at[0], halo.at[1], send.at[0], recv.at[1], peer(p - 1)).start()

    @pl.when(p < count - 1)
    def _():
        remote(packed.at[1], halo.at[0], send.at[1], recv.at[0], peer(p + 1)).start()

    if between is not None:
        between()

    @pl.when(p > 0)
    def _():
        arrived(halo.at[0], recv.at[0])
        remote(packed.at[0], halo.at[1], send.at[0], recv.at[1], peer(p - 1)).wait_send()

    @pl.when(p < count - 1)
    def _():
        arrived(halo.at[1], recv.at[1])
        remote(packed.at[1], halo.at[0], send.at[1], recv.at[0], peer(p + 1)).wait_send()

    @pl.when(p == 0)
    def _():
        halo[0] = jnp.zeros(halo.shape[1:], BF)

    @pl.when(p == count - 1)
    def _():
        halo[1] = jnp.zeros(halo.shape[1:], BF)


def dot(a, b):
    return jnp.dot(a, b, preferred_element_type=F32)


def dot_nt(a, b):
    return lax.dot_general(a, b, (((1,), (1,)), ((), ())), preferred_element_type=F32)


def dot_tn(a, b):
    return lax.dot_general(a, b, (((0,), (0,)), ((), ())), preferred_element_type=F32)


def lanes4(mask, width):
    return jnp.concatenate([mask] * (width // 128), axis=1)


def rows8(value):
    return value.reshape(-1, 8, value.shape[-1]).sum(0)


def to_natural(cells, back, gather, out):
    narrow = dot(cells, gather).astype(BF)
    for c in range(out.shape[1]):
        out[:, c] = dot(back, narrow[128 * c : 128 * c + 128]).astype(BF).reshape(8, 16, narrow.shape[1])


def shifted(chunk, perm, S, c):
    moved = dot(perm, chunk)
    for lane in range(S.shape[1]):
        S[:, lane, pl.ds(3 + 16 * c, 16)] = moved[:, lane * 128 : lane * 128 + 128].reshape(7, 16, 8, 128)
    return moved


def wrap(S, cols):
    S[:, :, 0:3] = S[:, :, cols : cols + 3]
    S[:, :, cols + 3 : cols + 6] = S[:, :, 3:6]


def taps_to(kb, par, flip):
    for lane in range(kb.shape[0]):
        at = slice(128 * lane, 128 * lane + 128)
        for k in range(49):
            tap = 48 - k if flip else k
            kb[lane, k] = jnp.broadcast_to(par[tap : tap + 1, at], (8, 128))


def taps_at(S, kb, lane, tile, first, sums):
    for i in range(7):
        window = [S[i, lane, first + t] for t in range(len(sums) + 6)]
        taps = [kb[tile, 7 * i + j] for j in range(7)]
        for k in range(len(sums)):
            total = window[k] * taps[0]
            for j in range(1, 7):
                total = total + window[k + j] * taps[j]
            sums[k] = sums[k] + total
    return sums


def norm_terms(st, par):
    counted = st[2:3]
    mean = st[0:1] / counted
    inverse = lax.rsqrt(st[1:2] / counted - mean * mean + EPS)
    return counted, mean, inverse, par[49:50], par[50:51]


def start_either(self, src, dst, send, recv, peer):
    pl.when(jnp.logical_not(self))(lambda: remote(src, dst, send, recv, peer).start())
    pl.when(self)(lambda: pltpu.make_async_copy(src, dst, recv).start())


def deliver(sec, nat, out, bounce, send, recv, b):
    s, d, g, m, p = where_am_i()

    def target(which, j):
        dp = 4 * g + 2 * ((p + which) % 2) + j
        part = (nat, bounce)[which].at[pl.ds(4 * j, 4)]
        return dp == d, part, out.at[m], send.at[which, j], recv.at[m], (s, dp)

    def over():
        return remote(nat, bounce, b.at[0], b.at[1], (1 - s, d))

    def sends(which):
        for j in range(2):
            start_either(*target(which, j))

    def begin():
        pl.when(s != sec)(lambda: over().start())
        pl.when(s == sec)(lambda: sends(0))

    def middle():
        @pl.when(s == sec)
        def _():
            arrived(bounce, b.at[1])
            sends(1)

    def end():
        @pl.when(s == sec)
        def _():
            for mb in range(4):
                arrived(out.at[mb], recv.at[mb])
            for which in range(2):
                for j in range(2):
                    self_, *rest = target(which, j)
                    pl.when(jnp.logical_not(self_))(lambda rest=rest: remote(*rest).wait_send())

        pl.when(s != sec)(lambda: over().wait_send())

    return [begin, middle, lambda: None, end]


def collect(field, out, first, send, recv):
    s, d, g, m, p = where_am_i()
    core, dp = device(d // 2, 0)
    j = d % 2

    def parts(step):
        mb = (m + step) % 4
        return field.at[mb], out.at[pl.ds(first + 4 * j, 4)], send.at[step], recv.at[j], (s, dp + mb)

    def begin():
        @pl.when(s == core)
        def _():
            for step in range(1, 4):
                remote(*parts(step)).start()
            src, dst, _, sem, _ = parts(0)
            pltpu.make_async_copy(src, dst, sem).start()

    def end():
        for jj in range(2):
            arrived(out.at[pl.ds(first + 4 * jj, 4)], recv.at[jj])

        @pl.when(s == core)
        def _():
            for step in range(1, 4):
                remote(*parts(step)).wait_send()

    return begin, end


def half(ref, c):
    rows, lanes = ref.shape[-2:]
    lead = (slice(None),) * (len(ref.shape) - 2)
    if rows % 32 == 0:
        return ref.at[lead + (pl.ds(pl.multiple_of(c * (rows // 2), 16), rows // 2),)]
    return ref.at[lead + (slice(None), pl.ds(pl.multiple_of(c * (lanes // 2), 128), lanes // 2))]


def half_shape(shape):
    rows, lanes = shape[-2:]
    return shape[:-2] + ((rows // 2, lanes) if rows % 32 == 0 else (rows, lanes // 2))


def collect_land(land, out, send, recv):
    s, d, g, m, p = where_am_i()
    core, dp = device(d // 2, 0)

    def part(step):
        return remote(land, out.at[d % 2], send.at[step], recv.at[d % 2], (s, dp + (m + step) % 4))

    def begin():
        @pl.when(s == core)
        def _():
            for step in range(1, 4):
                part(step).start()
            pltpu.make_async_copy(land, out.at[d % 2], recv.at[d % 2]).start()

    def end():
        for jj in range(2):
            arrived(out.at[jj], recv.at[jj])

        @pl.when(s == core)
        def _():
            for step in range(1, 4):
                part(step).wait_send()

    return begin, end


def script(*actions):
    queue = list(actions)

    def hook(*_):
        if queue:
            queue.pop(0)()

    return hook


def nothing(*_):
    pass


class Gather:
    def __init__(self, shard, full, send, recv):
        self.shard, self.full, self.send, self.recv = shard, full, send, recv
        self.s, self.d, self.g, self.m, _ = where_am_i()
        self.bit = 1 + self.s

    def block(self, col, c):
        return half(self.full.at[:, col], c)

    def near(self):
        return pltpu.make_async_copy(half(self.shard, self.s), half(self.full.at[self.g, self.m], self.s), self.send.at[0])

    def line(self, step):
        src, dst = half(self.shard, self.s), half(self.full.at[self.g, self.m], self.s)
        return remote(src, dst, self.send.at[step], self.recv.at[step], (self.s, 4 * ((self.g + step) % 4) + self.m))

    def column(self, slot, col, peer):
        block = self.block(col, self.s)
        return remote(block, block, self.send.at[slot], self.recv.at[slot], peer)

    def first(self):
        return self.column(4, self.m, (self.s, self.d ^ self.bit))

    def second(self, index):
        return self.column(5 + index, (self.m, self.m ^ self.bit)[index], (self.s, self.d ^ (3 - self.bit)))

    def cols(self, way):
        return (self.m, self.m ^ way, self.m ^ (3 - way), self.m ^ 3)

    def hand(self, index):
        return self.column(7 + index, self.cols(self.bit)[index], (1 - self.s, self.d))

    def start(self):
        self.near().start()
        for step in range(1, 4):
            self.line(step).start()

    def plane(self):
        self.near().wait()
        for step in range(1, 4):
            arrived(half(self.full.at[(self.g + 4 - step) % 4, self.m], self.s), self.recv.at[step])
        self.first().start()
        self.second(0).start()
        self.hand(0).start()

    def onward(self):
        arrived(self.block(self.m ^ self.bit, self.s), self.recv.at[4])
        self.second(1).start()
        self.hand(1).start()

    def over(self):
        for index in range(2):
            arrived(self.block((self.m ^ (3 - self.bit), self.m ^ 3)[index], self.s), self.recv.at[5 + index])
            self.hand(2 + index).start()

    def whole(self):
        for index, col in enumerate(self.cols(3 - self.bit)):
            arrived(self.block(col, 1 - self.s), self.recv.at[7 + index])

    def finish(self):
        for step in range(1, 4):
            self.line(step).wait_send()
        self.first().wait_send()
        for index in range(2):
            self.second(index).wait_send()
        for index in range(4):
            self.hand(index).wait_send()


class Load:
    def __init__(self, src, full, sem):
        self.copy = lambda: pltpu.make_async_copy(src, full, sem.at[0])

    def start(self):
        self.copy().start()

    def whole(self):
        self.copy().wait()

    def plane(self):
        pass

    onward = over = finish = plane


def masks(land, ocean, coarse, pick, patch):
    rows, across = land.shape[0] * land.shape[1], land.shape[2]
    flat = land[...].reshape(rows, across).astype(F32).astype(BF)
    spread = dot(pick, flat)
    at = lax.broadcasted_iota(jnp.int32, spread.shape, 1) - lax.broadcasted_iota(jnp.int32, spread.shape, 0) // 8
    ones = jnp.ones((across, 128), BF)

    def chunk(c, carry):
        ocean[pl.ds(pl.multiple_of(c * 128, 128), 128)] = dot(jnp.where(at == 16 * c, spread, 0.0).astype(BF), ones)
        return carry

    lax.fori_loop(0, ocean.shape[0] // 128, chunk, 0, unroll=True)
    for b in range(ocean.shape[0] // 256):
        moved = dot(patch, ocean[256 * b : 256 * b + 256].astype(BF))
        coarse[64 * b : 64 * b + 64] = moved[:64] * moved[64:128] * moved[128:192] * moved[192:]


def conv_phase(sec, cols, ns, hook):
    ocean, z, stats = ns.ocean, ns.z, ns.stats
    wide, tiles = z.shape[2], cols // 16

    def count_cells(b, t):
        return t + ocean[pl.ds(pl.multiple_of(b * 64, 64), 64)].reshape(8, 8, 128).sum(0)

    def phase(S, kb, *laid):
        taps_to(kb, ns.par[sec], False)
        tally = lax.fori_loop(0, cols // 8, count_cells, jnp.zeros((8, 128), F32))
        lanes = S.shape[1]
        if sec == 0:
            (laid,) = laid

            def lay(r, carry):
                row = ns.x14[r]
                laid[r] = dot(row.reshape(cols, row.shape[2]), ns.spread[...]).astype(BF).reshape(tiles, 16, wide)
                return carry

            lax.fori_loop(0, 14, lay, 0, unroll=True)
        for group in range(wide // 128 // lanes):
            part = slice(group * lanes * 128, (group + 1) * lanes * 128)

            def chunk(c, carry):
                cells = pl.ds(pl.multiple_of(c * 128, 128), 128)
                if sec == 0:
                    moved = shifted(laid[:, c, :, part].reshape(224, lanes * 128), ns.natural[...], S, c)
                    ns.a0[cells, part] = moved[384:512].astype(BF)
                else:
                    shifted(jnp.concatenate([ns.a1[cells, part], ns.halo[0, c, :, part], ns.halo[1, c, :, part]], axis=0), ns.shifts[...], S, c)
                return carry

            lax.fori_loop(0, tiles, chunk, 0, unroll=5)
            wrap(S, cols)
            hook()
            for lane in range(lanes):
                at = slice((group * lanes + lane) * 128, (group * lanes + lane + 1) * 128)

                def step(b, carry):
                    first, second = carry
                    sums = taps_at(S, kb, lane, group * lanes + lane, b * 16, [jnp.zeros((8, 128), F32)] * 16)
                    for k, total in enumerate(sums):
                        z[b * 16 + k, :, at] = total
                        kept = total * ocean[pl.ds(pl.multiple_of(b * 128 + 8 * k, 8), 8)]
                        first = first + kept
                        second = second + kept * total
                    return first, second

                zero = jnp.zeros((8, 128), F32)
                first, second = lax.fori_loop(0, tiles, step, (zero, zero), unroll=2)
                stats[0:1, at] = first.sum(0, keepdims=True)
                stats[1:2, at] = second.sum(0, keepdims=True)
                stats[2:3, at] = tally.sum(0, keepdims=True)
                stats[3:8, at] = jnp.zeros((5, 128), F32)
                hook()

    space = [pltpu.VMEM((7, 2, cols + 6, 8, 128), F32), pltpu.VMEM((wide // 128, 49, 8, 128), F32)]
    pl.run_scoped(phase, *space, *([pltpu.VMEM((14, tiles, 16, wide), BF)] if sec == 0 else []))


def gelu_terms(e):
    phi = 0.5 + 0.5 * lax.erf(e * np.float32(0.5**0.5))
    return phi, phi + e * (np.float32((2 * np.pi) ** -0.5) * jnp.exp(-0.5 * e * e))


def ff_phase(sec, ns, st, w1, w2, res, y, nat, hook):
    par = ns.par[sec]
    counted, mean, inverse, gain, shift = norm_terms(st, par)
    cells, wide = res.shape
    w1, w2 = w1.reshape(wide, -1), w2.reshape(-1, wide)
    hidden = w1.shape[1]

    def phase(n, g, r):
        def norm(b, carry):
            z = ns.z[pl.ds(b * 32, 32)].reshape(256, wide)
            n[pl.ds(pl.multiple_of(b * 256, 256), 256)] = ((z - mean) * inverse * gain + shift).astype(BF)
            return carry

        lax.fori_loop(0, cells // 256, norm, 0, unroll=True)
        for h in range(hidden // 256):
            at = slice(256 * h, 256 * h + 256)
            e = dot(n[...], w1[:, at]) + ns.bias[sec, 0:1, at]
            g[:, at] = (e * gelu_terms(e)[0]).astype(BF)
            hook(h)
        r[...] = dot(g[...], w2[...])
        hook(hidden // 256)

        def end(b, carry):
            at = pl.ds(pl.multiple_of(b * 256, 256), 256)
            y[at] = (lanes4(ns.ocean[at], wide) * (res[at].astype(F32) + (r[at] + par[51:52]))).astype(BF)
            return carry

        lax.fori_loop(0, cells // 256, end, 0, unroll=True)
        to_natural(y[...], ns.back[...], ns.gather[...], nat)

    pl.run_scoped(phase, pltpu.VMEM((cells, wide), BF), pltpu.VMEM((cells, hidden), BF), pltpu.VMEM((cells, wide), F32))


def parts3(value):
    high = value.astype(BF)
    rest = value - high.astype(F32)
    middle = rest.astype(BF)
    return high, middle, (rest - middle.astype(F32)).astype(BF)


def select(value, matrix):
    return sum(dot(v, matrix) for v in parts3(value))


def pack_shards(ns, swap):
    s = lax.axis_index("section")
    c, wide = ns.spread.shape
    hid, n = 2 * ns.half_hidden.shape[0], ns.deep_spread.shape[0]

    def phase(nat, half_hidden, deep_spread):
        got = loads([(ns.half_hidden, half_hidden), (ns.deep_spread, deep_spread)], ns.keep)

        def rows(flat, width):
            count = flat.shape[1] // width
            tall = -(-count // 16) * 16
            nat[tall - 16 : tall] = jnp.zeros((16, nat.shape[1]), F32)
            for r in range(count):
                nat[r : r + 1, 0:width] = flat[0:1, r * width : r * width + width]
            return tall

        tall = rows(ns.w_in, hid)
        got[0]()
        size = half_hidden.shape[1]
        for q in range(2):
            ns.shard0[s, :, size * q : size * q + size] = dot(nat[0:tall, hid // 2 * q : hid // 2 * q + hid // 2].astype(BF), half_hidden[...]).astype(BF)
        swap(0)
        tall = rows(ns.w_out, c)
        ns.shard1[s] = dot(nat[0:tall, 0:c].astype(BF), ns.spread[...]).astype(BF)
        swap(1)
        got[1]()

        @pl.when(s == 0)
        def _():
            tall = rows(ns.resample, n)
            laid = dot(nat[0:tall, 0:n].astype(BF), deep_spread[...]).astype(BF)
            ns.shard2[0] = dot(ns.rows[...], laid).astype(BF)

        @pl.when(s == 1)
        def _():
            tall = rows(ns.resample, 4 * c)
            for q in range(4):
                ns.shard2[1, tall * (q // 2) : tall * (q // 2) + tall, wide * (q % 2) : wide * (q % 2) + wide] = dot(
                    nat[0:tall, c * q : c * q + c].astype(BF), ns.spread[...]).astype(BF)

        swap(2)
        tall = rows(ns.merge, c)
        ns.shard3[s] = dot(nat[0:tall, 0:c].astype(BF), ns.spread[...]).astype(BF)
        swap(3)
        nat[48:64] = jnp.zeros((16, nat.shape[1]), F32)
        nat[0:49, 0:c] = ns.kernel[0]
        for k, ref in enumerate((ns.bn_gain, ns.bn_bias, ns.bias_out)):
            nat[49 + k : 50 + k, 0:c] = ref[...]
        ns.par[s] = select(nat[0:56, 0:c], ns.spread[...])
        swap(4)
        nat[0:8] = jnp.zeros((8, nat.shape[1]), F32)
        nat[0:1, 0:hid] = ns.bias_in[...]
        for q in range(2):
            ns.bias[s, :, size * q : size * q + size] = select(nat[0:8, hid // 2 * q : hid // 2 * q + hid // 2], half_hidden[...])
        swap(5)

    pl.run_scoped(phase, pltpu.VMEM((112, max(hid, 4 * c)), F32), pltpu.VMEM(ns.half_hidden.shape, BF), pltpu.VMEM(ns.deep_spread.shape, BF))


def unpack_sums(ns, deep_ready, mats_ready, small_ready):
    s = lax.axis_index("section")
    wide, c = ns.gather.shape
    hid, n = 2 * ns.half_hidden_back.shape[1], ns.deep_back.shape[1]

    def phase(nat, half_back, deep_back):
        got = loads([(ns.half_hidden_back, half_back), (ns.deep_back, deep_back)], ns.load_sem)
        got[0]()
        got[1]()

        def narrow(value, matrix):
            return dot(value.astype(BF), matrix) + dot((value - value.astype(BF).astype(F32)).astype(BF), matrix)

        def rows(out, width, count):
            for r in range(count):
                out[0:1, r * width : r * width + width] = nat[r : r + 1, 0:width]

        size = half_back.shape[0]
        deep_ready()
        merge = ns.gm.reshape(-1, wide)
        nat[0 : merge.shape[0], 0:c] = narrow(merge[...], ns.gather[...])
        rows(ns.gmm, c, ns.gmm.shape[1] // c)
        deep = ns.gr.reshape(-1, ns.gr.shape[2])

        @pl.when(s == 0)
        def _():
            nat[0 : deep.shape[0], 0:n] = narrow(deep[...], deep_back[...])
            band, high = c // GROUPS, deep.shape[0] // 4
            for k in range(4):
                for r in range(band):
                    at = n * (band * k + r)
                    ns.gres[0:1, at : at + n] = nat[high * k + r : high * k + r + 1, 0:n]

        @pl.when(s == 1)
        def _():
            high = deep.shape[0] // 2
            for j in range(2):
                nat[0 : deep.shape[0], 0:c] = narrow(deep[:, wide * j : wide * j + wide], ns.gather[...])
                for i in range(2):
                    for r in range(n // GROUPS):
                        at = 4 * c * r + c * (2 * i + j)
                        ns.gres[0:1, at : at + c] = nat[high * i + r : high * i + r + 1, 0:c]

        mats_ready()
        grad = ns.gw1.reshape(-1, ns.gw1.shape[2])
        for q in range(2):
            nat[0 : grad.shape[0], hid // 2 * q : hid // 2 * q + hid // 2] = narrow(grad[:, size * q : size * q + size], half_back[...])
        rows(ns.gwi, hid, ns.gwi.shape[1] // hid)
        for k in range(2):
            lanes = wide // 2
            part = narrow(ns.gw2[k], ns.gather[lanes * k : lanes * k + lanes])
            if k == 0:
                nat[0 : ns.gw2.shape[1], 0:c] = part
            else:
                nat[0 : ns.gw2.shape[1], 0:c] += part
        rows(ns.gwo, c, ns.gwo.shape[1] // c)
        small_ready()
        nat[0:64, 0:c] = narrow(ns.total[...], ns.gather[...])
        ns.gk[0] = nat[0:49, 0:c]
        ns.gs[...] = nat[56:57, 0:c]
        ns.gg[...] = nat[57:58, 0:c]
        ns.gbo[...] = nat[58:59, 0:c]
        flat = jnp.concatenate([ns.total[59 + k : 60 + k] for k in range(-(-2 * size // wide))], axis=1)
        for q in range(2):
            ns.gbi[0:1, hid // 2 * q : hid // 2 * q + hid // 2] = narrow(jnp.broadcast_to(flat[:, size * q : size * q + size], (8, size)), half_back[...])[0:1]

    pl.run_scoped(phase, pltpu.VMEM((128, max(hid, 4 * c)), F32), pltpu.VMEM(ns.half_hidden_back.shape, BF), pltpu.VMEM(ns.deep_back.shape, BF))


def forward_kernel(fast, count, cols, ns):
    s, d, g, m, p = where_am_i()
    greet_near(count)
    x14 = ns.x14
    x_begin, x_end = collect(ns.x, x14, 3, ns.xs, ns.xr)
    land_begin, land_end = collect_land(ns.land, ns.land2, ns.ls, ns.lr)
    x_begin()
    land_begin()
    swapped = [getattr(ns, f"shard{k}") for k in range(4)] + [ns.par, ns.bias] if fast else [ns.par, ns.bias]

    def swap(k):
        return remote(swapped[k].at[s], swapped[k].at[s], ns.ps.at[k], ns.pr.at[k], (1 - s, d))

    def swap_in(k):
        arrived(swapped[k].at[1 - s], ns.pr.at[k])

    fulls = dict(w1_0=ns.w1_0, w2_0=ns.w2_0, r0=ns.r0, m0=ns.m0, m1=ns.m1, r1=ns.r1, w1_1=ns.w1_1, w2_1=ns.w2_1)
    which = dict(w1_0=(0, 0), w2_0=(1, 0), r0=(2, 0), r1=(2, 1), m0=(3, 0), m1=(3, 1), w1_1=(0, 1), w2_1=(1, 1))
    mats = {}
    for k, (name, full) in enumerate(fulls.items()):
        if fast:
            index, sec = which[name]
            mats[name] = Gather(getattr(ns, f"shard{index}").at[sec], full, ns.gs.at[k], ns.gr.at[k])
        else:
            mats[name] = Load(getattr(ns, name + "_in"), full, ns.gs.at[k])
    kept = dict(z0=ns.z, z1=ns.z, a0=ns.a0, a1=ns.a1, skip=ns.skip, up=ns.up, pieces=ns.pieces, deep=ns.deep, nat0=ns.nat0, nat1=ns.nat1)
    keeps = {name: lambda k=k, name=name, ref=ref: pltpu.make_async_copy(ref, getattr(ns, name + "_out"), ns.keep.at[k]) for k, (name, ref) in enumerate(kept.items())}

    def keep(*names):
        for name in names:
            keeps[name]().start()

    saves = {name: lambda k=k, name=name, full=full: pltpu.make_async_copy(full, getattr(ns, name + "_out"), ns.save.at[k]) for k, (name, full) in enumerate(fulls.items())}

    def do(step, *names):
        for name in names:
            getattr(mats[name], step)()

    def whole(*names):
        do("whole", *names)
        for name in names:
            saves[name]().start()

    def give(k):
        swap(k).start()
        if k == 1:
            swap_in(0)
            do("start", "w1_0")
        if k == 2:
            swap_in(1)
            do("start", "w2_0")

    if fast:
        pack_shards(ns, give)
        swap_in(2)
        swap_in(3)
    else:
        near = [pltpu.make_async_copy(src, dst.at[s], ns.keep.at[k]) for k, (src, dst) in enumerate(((ns.mine, ns.par), (ns.mine_bias, ns.bias)))]
        for c in near:
            c.start()
        for c in near:
            c.wait()
        for k in range(2):
            swap(k).start()
        do("start", "w1_0", "w2_0")
    do("start", "r0")
    land_end()
    masks(ns.land2, ns.ocean, ns.coarse, ns.pick[...], ns.patch[...])
    x_end()

    def edge(up):
        src, dst = (x14.at[pl.ds(3, 3)], x14.at[pl.ds(11, 3)]) if up else (x14.at[pl.ds(8, 3)], x14.at[pl.ds(0, 3)])
        return remote(src, dst, ns.hs.at[int(up)], ns.hr.at[int(up)], device(p - 1 if up else p + 1, m))

    pl.when(p > 0)(edge(True).start)
    pl.when(p < count - 1)(edge(False).start)
    do("plane", "w1_0", "w2_0")
    swap_in(len(swapped) - 2)
    swap_in(len(swapped) - 1)

    @pl.when(p == 0)
    def _():
        x14[0:3] = jnp.zeros((3,) + x14.shape[1:], BF)

    @pl.when(p == count - 1)
    def _():
        x14[11:14] = jnp.zeros((3,) + x14.shape[1:], BF)

    pl.when(p > 0)(lambda: arrived(x14.at[pl.ds(0, 3)], ns.hr.at[0]))
    pl.when(p < count - 1)(lambda: arrived(x14.at[pl.ds(11, 3)], ns.hr.at[1]))

    cot_begin, cot_end = collect(ns.cot, ns.cot8, 0, ns.cs, ns.cr)

    do("onward", "w1_0", "w2_0")

    conv_phase(0, cols, ns, script(
        nothing,
        lambda: (do("plane", "r0"), do("start", "r1", "m0", "m1")),
        nothing,
        lambda: do("over", "w1_0", "w2_0"),
        lambda: do("onward", "r0"),
        nothing,
    ))
    ns.st0[...] = all_sum(ns.stats, ns.slots, ns.send, ns.recv, count)
    keep("z0", "a0")
    whole("w1_0", "w2_0")
    ff0 = {1: lambda: (do("plane", "r1", "m0", "m1"), do("start", "w1_1", "w2_1")), 7: lambda: do("over", "r0")}
    ff_phase(0, ns, ns.st0, ns.w1_0, ns.w2_0, ns.a0, ns.skip, ns.nat0, lambda k: ff0.get(k, nothing)())
    keep("skip", "nat0")

    skip, pieces, wide = ns.skip, ns.pieces, ns.skip.shape[1]
    blocks = skip.shape[0] // 256
    down, up_w = ns.r0.reshape(4 * wide, -1), ns.r1.reshape(GROUPS, 2, ns.r1.shape[2] // 2, -1)
    merge = [v.reshape(wide, wide) for v in (ns.m0, ns.m1)]
    for b in range(blocks):
        moved = dot(ns.patch[...], skip[256 * b : 256 * b + 256]).astype(BF)
        for k in range(4):
            pieces[k, 64 * b : 64 * b + 64] = moved[64 * k : 64 * k + 64]
    do("onward", "r1", "m0", "m1")
    whole("r0")
    value = sum(dot(pieces[k], down[wide * k : wide * k + wide]) for k in range(4))
    deep_value = (lanes4(ns.coarse[...], value.shape[1]) * value).astype(BF)
    ns.deep[...] = deep_value
    keep("pieces", "deep")
    do("over", "m0", "m1", "r1")
    do("plane", "w1_1", "w2_1")
    whole("m0", "m1", "r1")
    rows = up_w.shape[0] * up_w.shape[2]
    lifted = [dot(deep_value, up_w[:, i].reshape(rows, -1)).astype(BF) for i in range(2)]
    for b in range(blocks):
        at = slice(256 * b, 256 * b + 256)
        stacked = jnp.concatenate(
            [lifted[i][64 * b : 64 * b + 64, wide * j : wide * j + wide] for i in range(2) for j in range(2)], axis=0
        )
        ns.up[at] = dot(ns.unpatch[...], stacked).astype(BF)
    for b in range(blocks):
        at = slice(256 * b, 256 * b + 256)
        joined = dot(ns.up[at], merge[0][...]) + dot(skip[at], merge[1][...])
        ns.h[at] = joined
        low = joined.astype(BF)
        ns.a1[at] = low
        for k in range(2):
            ends = dot(ns.edges[...], low[128 * k : 128 * k + 128]).astype(BF)
            ns.packed[0, 2 * b + k] = ends[:48]
            ns.packed[1, 2 * b + k] = ends[48:]
    do("onward", "w1_1", "w2_1")
    cot_begin()
    swap_rows(ns.packed, ns.halo, ns.es, ns.er, count)
    keep("up", "a1")
    keeps["z0"]().wait()

    conv_phase(1, cols, ns, script(nothing, nothing, lambda: do("over", "w1_1", "w2_1")))
    ns.st1[...] = all_sum(ns.stats, ns.slots1, ns.send1, ns.recv1, count)
    keep("z1")
    whole("w1_1", "w2_1")
    ff_phase(1, ns, ns.st1, ns.w1_1, ns.w2_1, ns.h, ns.y1, ns.nat1, nothing)
    keep("nat1")

    cot_end()
    for name, save in saves.items():
        save().wait()
        do("finish", name)
    for name, copy in keeps.items():
        if name != "z0":
            copy().wait()
    for k in range(len(swapped)):
        swap(k).wait_send()
    pl.when(p > 0)(edge(True).wait_send)
    pl.when(p < count - 1)(edge(False).wait_send)


class Reduce:
    def __init__(self, sec, partial, bank, out, send, recv):
        self.sec, self.partial, self.out, self.send, self.recv = sec, partial, out, send, recv
        self.own, self.core, self.one, self.two, self.row, self.mine = bank
        self.s, self.d, self.g, self.m, _ = where_am_i()
        self.bit = 1 + self.s
        self.rest = self.m ^ (3 - self.bit)

    def near(self):
        return pltpu.make_async_copy(half(self.partial, self.s), self.own, self.send.at[0])

    def over(self):
        return remote(half(self.partial, 1 - self.s), self.core, self.send.at[1], self.recv.at[1], (1 - self.s, self.d))

    def first(self, index):
        col = (self.m ^ self.bit, self.m ^ 3)[index]
        return remote(self.own.at[:, col], self.one.at[:, index], self.send.at[2 + index], self.recv.at[2 + index], (self.s, self.d ^ self.bit))

    def second(self):
        return remote(self.own.at[:, self.rest], self.two, self.send.at[4], self.recv.at[4], (self.s, self.d ^ (3 - self.bit)))

    def along(self, step):
        to = (self.g + step) % 4
        return remote(self.own.at[to, self.m], self.row.at[step - 1], self.send.at[4 + step], self.recv.at[4 + step], (self.s, 4 * to + self.m))

    def give(self):
        return remote(self.mine, self.out.at[self.s], self.send.at[8], self.recv.at[8], (1 - self.s, self.d))

    def start(self):
        self.over().start()
        self.near().start()

    def plane(self):
        self.near().wait()
        arrived(self.core, self.recv.at[1])
        own, core, m, bit = self.own, self.core, self.m, self.bit

        def add(k, carry):
            z, col = k % 4, (m ^ 3, m ^ bit, m ^ (3 - bit), m)
            for c in col:
                own[z, c] = (own[z, c].astype(F32) + core[z, c].astype(F32)).astype(BF)
            return carry

        lax.fori_loop(0, 4, add, 0)
        self.first(1).start()
        self.first(0).start()

    def onward(self):
        own, one, rest = self.own, self.one, self.rest
        arrived(one.at[:, 1], self.recv.at[3])

        def add(z, carry):
            own[z, rest] = (own[z, rest].astype(F32) + one[z, 1].astype(F32)).astype(BF)
            return carry

        lax.fori_loop(0, 4, add, 0)
        self.second().start()

    def line(self):
        own, one, two, m = self.own, self.one, self.two, self.m
        arrived(one.at[:, 0], self.recv.at[2])
        arrived(two, self.recv.at[4])

        def add(z, carry):
            own[z, m] = (own[z, m].astype(F32) + one[z, 0].astype(F32) + two[z].astype(F32)).astype(BF)
            return carry

        lax.fori_loop(0, 4, add, 0)
        for step in range(1, 4):
            self.along(step).start()

    def total(self):
        for step in range(1, 4):
            arrived(self.row.at[step - 1], self.recv.at[4 + step])
        row = self.row
        self.mine[...] = self.own[self.g, self.m].astype(F32) + row[0].astype(F32) + row[1].astype(F32) + row[2].astype(F32)
        pl.when(self.s != self.sec)(lambda: self.give().start())

        @pl.when(self.s == self.sec)
        def _():
            self.out[self.s] = self.mine[...]

    def finish(self):
        self.over().wait_send()
        for index in range(2):
            self.first(index).wait_send()
        self.second().wait_send()
        for step in range(1, 4):
            self.along(step).wait_send()
        pl.when(self.s != self.sec)(lambda: self.give().wait_send())
        pl.when(self.s == self.sec)(lambda: arrived(self.out.at[1 - self.s], self.recv.at[8]))


def reduce_bank(name, shape):
    part = half_shape(shape)
    out = {f"{name}_{k}": pltpu.VMEM(lead + part, BF) for k, lead in (("own", (4, 4)), ("core", (4, 4)), ("one", (4, 2)), ("two", (4,)), ("row", (3,)))}
    out.update({f"{name}_mine": pltpu.VMEM(part, F32), f"{name}_s": DMA((9,)), f"{name}_r": DMA((9,))})
    return out


def reducer(ns, name, sec, partial, out):
    bank = [getattr(ns, f"{name}_{k}") for k in ("own", "core", "one", "two", "row", "mine")]
    return Reduce(sec, partial, bank, out, getattr(ns, f"{name}_s"), getattr(ns, f"{name}_r"))


def loads(pairs, sems, first=0):
    copies = [pltpu.make_async_copy(src, dst, sems.at[first + k]) for k, (src, dst) in enumerate(pairs)]
    for c in copies:
        c.start()
    return [c.wait for c in copies]


def back_ff_phase(sec, count, ns, top, kept, w_in, w_out, hook, done, between):
    z_in, st = kept
    cells, wide = ns.dym.shape
    hidden = w_in.shape[1]
    chunks = cells // 128
    ocean, small, dym = ns.ocean, ns.small, ns.dym
    counted, mean, inverse, gain, shift = norm_terms(st, ns.par[sec])

    def phase(w1, w2, z, n, de, dn, dr):
        got_z, got_w1, got_w2 = loads([(z_in, z), (w_in, w1), (w_out, w2)], ns.load_sem)

        def begin(c, total):
            at = pl.ds(pl.multiple_of(c * 128, 128), 128)
            if sec == 1:
                block = top[:, c]
                block = dot(block.reshape(-1, block.shape[-1]), ns.spread[...]).astype(BF)
                grad = dot(ns.turn[...], block)
            else:
                grad = top[at]
            grad = grad * lanes4(ocean[at], wide)
            dym[at] = grad
            low = grad.astype(BF)
            dr[at] = low
            return total + rows8(low.astype(F32))

        total = lax.fori_loop(0, chunks, begin, jnp.zeros((8, wide), F32), unroll=True)
        small[2:3] = total.sum(0, keepdims=True)
        small[3:8] = jnp.zeros((5, wide), F32)
        got_z()

        def norm(c, carry):
            at = pl.ds(pl.multiple_of(c * 128, 128), 128)
            n[at] = ((z[at] - mean) * inverse * gain + shift).astype(BF)
            return carry

        lax.fori_loop(0, chunks, norm, 0, unroll=True)
        got_w1()
        got_w2()
        for h in range(hidden // 256):
            at = slice(256 * h, 256 * h + 256)
            e = dot(n[...], w1[:, at]) + ns.bias[sec, 0:1, at]
            phi, slope = gelu_terms(e)
            ns.dw2[at] = dot_tn((e * phi).astype(BF), dr[...]).astype(BF)
            low = (dot_nt(dr[...], w2[at]) * slope).astype(BF)
            de[:, at] = low
            row, col = 3 + 256 * h // wide, 256 * h % wide
            small[row : row + 1, col : col + 256] = low.astype(F32).sum(0, keepdims=True)
            ns.dw1[:, at] = dot_tn(n[...], low).astype(BF)
            hook(h)
        done()
        dn[...] = dot_nt(de[...], w1[...])

        def sums(c, carry):
            at = pl.ds(pl.multiple_of(c * 128, 128), 128)
            grad = dn[at]
            return carry[0] + rows8(grad), carry[1] + rows8(grad * ((z[at] - mean) * inverse))

        zero = jnp.zeros((8, wide), F32)
        plain, scaled = lax.fori_loop(0, chunks, sums, (zero, zero), unroll=True)
        small[0:1] = plain.sum(0, keepdims=True)
        small[1:2] = scaled.sum(0, keepdims=True)
        ns.stats[...] = small[...]
        summed = all_sum(ns.stats, ns.slots, ns.send, ns.recv, count)
        first = -inverse * gain * summed[0:1] / counted
        second = -inverse * inverse * gain * summed[1:2] / counted

        def end(c, carry):
            at = pl.ds(pl.multiple_of(c * 128, 128), 128)
            grad = inverse * gain * dn[at] + lanes4(ocean[at], wide) * (first + second * (z[at] - mean))
            low = grad.astype(BF)
            ns.dz[at] = low
            ends = dot(ns.edges[...], low).astype(BF)
            ns.packed[0, c] = ends[:48]
            ns.packed[1, c] = ends[48:]
            return carry

        lax.fori_loop(0, chunks, end, 0, unroll=True)

    field = lambda t: pltpu.VMEM((cells, wide), t)
    pl.run_scoped(
        phase, pltpu.VMEM(w_in.shape, BF), pltpu.VMEM(w_out.shape, BF), field(F32), field(BF), pltpu.VMEM((cells, hidden), BF), field(F32), field(BF),
    )
    swap_rows(ns.packed, ns.halo, ns.hsend, ns.hrecv, count, between)


def back_conv_phase(sec, cols, ns, a_in, tiny, hook):
    cells, wide = ns.dz.shape
    dz = ns.dz

    def phase(S, kb, a, field, acc_dk):
        (got_a,) = loads([(a_in, a)], ns.load_sem)
        taps_to(kb, ns.par[sec], True)
        lanes = S.shape[1]
        for group in range(wide // 128 // lanes):
            part = slice(group * lanes * 128, (group + 1) * lanes * 128)

            def chunk(c, carry):
                block = jnp.concatenate([dz[pl.ds(pl.multiple_of(c * 128, 128), 128), part], ns.halo[0, c, :, part], ns.halo[1, c, :, part]], axis=0)
                shifted(block, ns.shifts[...], S, c)
                return carry

            lax.fori_loop(0, cols // 16, chunk, 0, unroll=5)
            wrap(S, cols)
            hook()
            if group == 0:
                got_a()
            tiles = [(lane, slice((group * lanes + lane) * 128, (group * lanes + lane + 1) * 128)) for lane in range(lanes)]
            for lane, at in tiles:

                def step(b, carry):
                    rows = pl.ds(pl.multiple_of(b * 128, 128), 128)
                    above = ns.dym[rows, at].reshape(16, 8, 128)
                    sums = taps_at(S, kb, lane, group * lanes + lane, b * 16, [above[k] for k in range(16)])
                    dz[rows, at] = jnp.concatenate(sums, axis=0).astype(BF)
                    return carry

                lax.fori_loop(0, cols // 16, step, 0, unroll=2)
            hook()
            for lane, at in tiles:
                field[...] = a[:, at].astype(F32).reshape(field.shape)
                acc_dk[...] = jnp.zeros(acc_dk.shape, F32)

                def tap_sums(b, carry):
                    here = [field[b * 16 + k] for k in range(16)]
                    for i in range(7):
                        window = [S[i, lane, b * 16 + t] for t in range(22)]
                        for j in range(7):
                            total = window[j] * here[0]
                            for k in range(1, 16):
                                total = total + window[j + k] * here[k]
                            acc_dk[7 * i + j] += total
                    return carry

                lax.fori_loop(0, cols // 16, tap_sums, 0, unroll=2)
                for k in range(49):
                    tiny[48 - k : 49 - k, at] = acc_dk[k].sum(0, keepdims=True)
            hook()
        tiny[49:56] = jnp.zeros((7, wide), F32)

    pl.run_scoped(
        phase, pltpu.VMEM((7, 2, cols + 6, 8, 128), F32), pltpu.VMEM((wide // 128, 49, 8, 128), F32), pltpu.VMEM((cells, wide), BF),
        pltpu.VMEM((cols, 8, 128), F32), pltpu.VMEM((49, 8, 128), F32),
    )


def back_mid_phase(ns, hook):
    dh = ns.dz
    cells, wide = dh.shape
    blocks = cells // 256

    def phase(skip, up, merge0, merge1, up_w, deep, down, pieces, dups, spreads, dskip):
        got = loads(
            [(ns.m1, merge1), (ns.m0, merge0), (ns.up, up), (ns.skip, skip), (ns.r1, up_w), (ns.deep, deep), (ns.pieces, pieces), (ns.r0, down)],
            ns.load_sem,
        )
        for k in range(2):
            got[k]()
        for b in range(blocks):
            at = slice(256 * b, 256 * b + 256)
            low = dot_nt(dh[at], merge1[...]).astype(BF)
            ns.dym[at] = low.astype(F32)
            dskip[at] = low
            lifted = dot_nt(dh[at], merge0[...]).astype(BF)
            moved = dot(ns.patch[...], lifted).astype(BF)
            for k in range(4):
                dups[k // 2, 64 * b : 64 * b + 64, wide * (k % 2) : wide * (k % 2) + wide] = moved[64 * k : 64 * k + 64]
        to_natural(dskip[...], ns.back[...], ns.gather[...], ns.nat)
        hook(0)
        got[2]()
        got[3]()
        ns.dm0[...] = dot_tn(up[...], dh[...]).astype(BF)
        ns.dm1[...] = dot_tn(skip[...], dh[...]).astype(BF)
        hook(1)
        rows = up_w.shape[0] * up_w.shape[2]
        got[4]()
        ddeep = dot_nt(dups[0], up_w[:, 0].reshape(rows, -1)) + dot_nt(dups[1], up_w[:, 1].reshape(rows, -1))
        got[5]()
        for i in range(2):
            up_w[:, i] = dot_tn(deep[...], dups[i]).astype(BF).reshape(up_w.shape[0], up_w.shape[2], -1)
        saves = [pltpu.make_async_copy(up_w, ns.dr1, ns.load_sem.at[0]), pltpu.make_async_copy(down, ns.dr0, ns.load_sem.at[1])]
        saves[0].start()
        masked = (lanes4(ns.coarse[...], ddeep.shape[1]) * ddeep).astype(BF)
        hook(2)
        got[6]()
        got[7]()
        for k in range(4):
            spreads[k] = dot_nt(masked, down[wide * k : wide * k + wide])
            down[wide * k : wide * k + wide] = dot_tn(pieces[k], masked).astype(BF)
        saves[1].start()
        saves[0].wait()
        hook(3)
        for b in range(blocks):
            value = jnp.concatenate([spreads[k, 64 * b : 64 * b + 64] for k in range(4)], axis=0)
            high = value.astype(BF)
            rest = (value - high.astype(F32)).astype(BF)
            at = slice(256 * b, 256 * b + 256)
            ns.dym[at] += dot(ns.unpatch[...], high) + dot(ns.unpatch[...], rest)
        saves[1].wait()

    like = lambda ref: pltpu.VMEM(ref.shape, BF)
    deep_cells = ns.deep.shape[0]
    pl.run_scoped(
        phase, like(ns.skip), like(ns.up), like(ns.m0), like(ns.m1), like(ns.r1), like(ns.deep), like(ns.r0), like(ns.pieces),
        pltpu.VMEM((2, deep_cells, 2 * wide), BF), pltpu.VMEM((4, deep_cells, wide), F32), pltpu.VMEM((cells, wide), BF),
    )


def with_names(ns, **names):
    out = Names()
    out.__dict__.update(ns.__dict__)
    out.__dict__.update(names)
    return out


def back_kernel(fast, count, cols, ns):
    s, d, g, m, p = where_am_i()
    greet_near(count)
    acts = [deliver(k, getattr(ns, f"nat{k}"), ns.act, getattr(ns, f"bounce{k}"), ns.ds.at[k], ns.dr.at[k], ns.db.at[k]) for k in range(2)]
    gi1, gi0 = (deliver(1 - k, ns.nat, ns.gi, getattr(ns, f"bounce{2 + k}"), ns.ds.at[2 + k], ns.dr.at[2 + k], ns.db.at[2 + k]) for k in range(2))
    w_dec = w_enc = m_all = r_up = r_down = []
    if fast:
        cut = lambda ref: ref.reshape(4, 4, ref.shape[0] // 16, ref.shape[1])
        w_dec = [reducer(ns, "w0", 1, cut(ns.dw1), ns.gw1), reducer(ns, "w1", 1, cut(ns.dw2), ns.gw2)]
        w_enc = [reducer(ns, "w0", 0, cut(ns.dw1), ns.gw1), reducer(ns, "w1", 0, cut(ns.dw2), ns.gw2)]
        m_all = [reducer(ns, f"m{k}", k, cut(getattr(ns, f"dm{k}")), ns.gm) for k in range(2)]
        r_up = [reducer(ns, "r1", 1, ns.dr1.reshape(4, 4, -1, ns.dr1.shape[3]), ns.gr)]
        r_down = [reducer(ns, "r0", 0, ns.dr0.reshape(4, 4, -1, ns.dr0.shape[1]), ns.gr)]

    def do(*steps):
        def action(*_):
            for step in steps:
                if isinstance(step, tuple):
                    for r in step[0]:
                        getattr(r, step[1])()
                else:
                    step()

        return action

    def keep_dw(sec):
        if not fast:
            copies = [pltpu.make_async_copy(ns.dw1, getattr(ns, f"dw1_{sec}"), ns.ps.at[0]), pltpu.make_async_copy(ns.dw2, getattr(ns, f"dw2_{sec}"), ns.ps.at[1])]
            for copy in copies:
                copy.start()
            for copy in copies:
                copy.wait()

    def at_step(**actions):
        return lambda h: actions.get(f"h{h}", nothing)()

    do(*(act[0] for act in acts))()
    dec = with_names(ns, halo=ns.halo1, slots=ns.slots1, send=ns.send1, recv=ns.recv1, hsend=ns.hsend1, hrecv=ns.hrecv1)
    back_ff_phase(1, count, dec, ns.top, (ns.z1, ns.st1), ns.w1_1, ns.w2_1, at_step(h3=do(*(act[1] for act in acts))), do((w_dec, "start"), lambda: keep_dw(1)), do((w_dec, "plane")))
    back_conv_phase(1, cols, dec, ns.a1, ns.tiny1, script(
        nothing, nothing, do(*(act[3] for act in acts)), do((w_dec, "onward")), nothing, do((w_dec, "line"))))
    ns.tiny1[56:64] = ns.small[...]
    back_mid_phase(ns, script(gi1[0], do((m_all, "start")), do((w_dec, "total"), gi1[1]), do((r_up, "start"), (m_all, "plane"))))
    do((r_down, "start"), (w_dec, "finish"))()

    back_ff_phase(0, count, ns, ns.dym, (ns.z0, ns.st0), ns.w1_0, ns.w2_0, at_step(
        h0=do((r_up, "plane")), h2=do((m_all, "onward")), h4=do((r_down, "plane")),
    ), do((w_enc, "start"), (m_all, "line"), lambda: keep_dw(0)), do((r_up, "onward"), (w_enc, "plane")))
    def give_dh():
        to_natural(ns.dz[...], ns.back[...], ns.gather[...], ns.nat)
        gi0[0]()

    back_conv_phase(0, cols, ns, ns.a0, ns.tiny0, script(
        do((r_down, "onward"), (r_up, "line")), do((m_all, "total"), gi1[3]), do((w_enc, "onward"), (r_down, "line")), do((r_up, "total")),
        do(give_dh, (w_enc, "line")), gi0[1]))
    ns.tiny0[56:64] = ns.small[...]
    if fast:
        sm, tiny, ts, tr = ns.sm, ns.tiny, ns.ts, ns.tr
        peers = {1: lambda step: (s, 4 * ((g + step) % 4) + m), 5: lambda step: (s, d ^ step)}

        def send(base, step):
            return remote(tiny.at[base], tiny.at[base + step], ts.at[base + step], tr.at[base + step], peers[base](step))

        def gather(base):
            for step in range(1, 4):
                arrived(tiny.at[base + step], tr.at[base + step])
            for step in range(1, 4):
                send(base, step).wait_send()
            return tiny[base] + tiny[base + 1] + tiny[base + 2] + tiny[base + 3]

        def deep_ready():
            sm[0] = ns.tiny0[...]
            sm[1] = ns.tiny1[...]
            over = remote(sm.at[1 - s], tiny.at[0], ts.at[0], tr.at[0], (1 - s, d))
            over.start()
            do((r_down, "total"))()
            arrived(tiny.at[0], tr.at[0])
            over.wait_send()
            tiny[1] = sm[s] + tiny[0]
            for step in range(1, 4):
                send(1, step).start()
            do((m_all + r_up + r_down, "finish"))()

        def mats_ready():
            tiny[5] = gather(1)
            for step in range(1, 4):
                send(5, step).start()
            do((w_enc, "total"), (w_enc, "finish"))()

        def small_ready():
            ns.total[...] = gather(5)

        unpack_sums(ns, deep_ready, mats_ready, small_ready)
    gi0[3]()


class Names:
    pass


def build(name, body, ins, outs, scratch, alias, cid, limit):
    ins = {k: v if isinstance(v, tuple) else (v, VM) for k, v in ins.items()}
    outs = {k: v if len(v) == 3 else v + (VM,) for k, v in outs.items()}
    names = list(ins) + list(outs) + list(scratch)

    def kernel(*refs):
        ns = Names()
        for k, ref in zip(names, refs):
            setattr(ns, k, ref)
        body(ns)

    order_in, order_out = list(ins), list(outs)
    results = pl.pallas_call(
        kernel, name=name, out_shape=[jax.ShapeDtypeStruct(v[0], v[1]) for v in outs.values()],
        in_specs=[v[1] for v in ins.values()], out_specs=[v[2] for v in outs.values()], scratch_shapes=list(scratch.values()),
        input_output_aliases={order_in.index(a): order_out.index(b) for a, b in alias.items()},
        compiler_params=pltpu.CompilerParams(vmem_limit_bytes=limit * MEGA, collective_id=cid, has_side_effects=True),
    )(*[v[0] for v in ins.values()])
    out = Names()
    for k, v in zip(order_out, results):
        setattr(out, k, v)
    return out


def on_device(sections, dps, inputs, cotangent, land, kernel, bn_gain, bn_bias, bias_in, bias_out, w_in, w_out, resample, merge):
    batches, height, cols, c = inputs.shape
    hid = bias_in.shape[1]
    n = resample.shape[1] * dps // (4 * c)
    cw, hw, nw = (GROUPS * padded(v) for v in (c, hid, n))
    cells, deep_cells = cols * 8, cols * 2
    count = 2 * (dps // 4)
    fast = dps == GROUPS
    assert batches == 4 and height == 4 and dps % 4 == 0 and sections == 2 and cols % 32 == 0
    s = lax.axis_index("section")
    mats = {k: jnp.asarray(v) for k, v in matrices(c, hid, n).items()}
    tiles = cols // 16
    both = ("section", "dp")

    def packs(parts, w1, w2, rd, ru):
        return pack_in(w1, parts, c, hid), pack_in(w2, parts, hid, c), pack_down(rd, parts, c, n), pack_up(ru, parts, c, n)

    if not fast:
        flat = [lax.all_gather(v.astype(BF).reshape(-1), both, axis=0, tiled=True) for v in (w_in, w_out, resample, merge)]
        halves = [v.reshape(2, -1) for v in flat]
        whole = [packs(GROUPS, halves[0][k], halves[1][k], halves[2][k], halves[2][k]) for k in range(2)]
        rows = jnp.concatenate([kernel[0], bn_gain, bn_bias, bias_out], axis=0)
        mine = grow(grow(rows.reshape(-1, GROUPS, c // GROUPS), (52, GROUPS, padded(c))).reshape(52, cw), (56, cw))
        mine_bias = grow(grow(bias_in.reshape(GROUPS, -1), (GROUPS, padded(hid))).reshape(1, hw), (8, hw))

    x = inputs.reshape(batches, height, tiles, 16, c)
    cot = cotangent.reshape(batches, height, tiles, 16, c)
    land_cols = -(-cols // 128) * 128
    at_any = lambda v: (v, ANY)
    field = lambda t: ((cells, cw), t)
    natural = ((8, tiles, 16, c), BF)
    edge_rows = ((2, tiles, 48, cw), BF)
    shapes = [(padded(c), hw), (padded(hid), cw), (4 * padded(c), nw), (padded(c), cw)]
    names = dict(w1_0=0, w2_0=1, r0=2, m0=3, m1=3, r1=2, w1_1=0, w2_1=1)
    ins = dict(x=x, land=grow(land, (8, land_cols)), cot=cot)
    if fast:
        ins.update(half_hidden=mats["half_hidden"], deep_spread=mats["deep_spread"])
    else:
        ins.update(mine=mine, mine_bias=mine_bias)
        given = dict(w1_0=whole[0][0], w2_0=whole[0][1], r0=whole[0][2], r1=whole[1][3], w1_1=whole[1][0], w2_1=whole[1][1])
        given.update(m0=pack_in(halves[3][0], GROUPS, c, c), m1=pack_in(halves[3][1], GROUPS, c, c))
        ins.update({k + "_in": v.reshape((4, 4) + shapes[names[k]]) for k, v in given.items()})
    ins = {k: at_any(v) for k, v in ins.items()}
    ins.update({k: mats[k] for k in ("spread", "gather", "natural", "shifts", "patch", "unpatch", "edges", "back", "pick", "rows")})
    if fast:
        ins.update(w_in=w_in, w_out=w_out, resample=resample, merge=merge.reshape(1, -1), kernel=kernel, bn_gain=bn_gain, bn_bias=bn_bias, bias_in=bias_in, bias_out=bias_out)
    outs = dict(
        par=((2, 56, cw), F32), bias=((2, 8, hw), F32), ocean=((cells, 128), F32), coarse=((deep_cells, 128), F32),
        st0=((8, cw), F32), st1=((8, cw), F32), cot8=natural + (ANY,),
    )
    held = dict(
        a0=field(BF), a1=field(BF), skip=field(BF), up=field(BF), pieces=((4, deep_cells, cw), BF), deep=((deep_cells, nw), BF), nat0=natural, nat1=natural,
    )
    outs.update({k + "_out": v + (ANY,) for k, v in held.items()}, z0_out=((cols, 8, cw), F32, ANY), z1_out=((cols, 8, cw), F32, ANY))
    outs.update({k + "_out": ((4, 4) + shapes[v], BF, ANY) for k, v in names.items()})
    scratch = dict(
        x14=pltpu.VMEM((14, tiles, 16, c), BF), land2=pltpu.VMEM((2, 8, land_cols), jnp.int32),
        z=pltpu.VMEM((cols, 8, cw), F32),
        h=pltpu.VMEM((cells, cw), F32),
        halo=pltpu.VMEM(*edge_rows), packed=pltpu.VMEM(*edge_rows), y1=pltpu.VMEM(*field(BF)),
        stats=pltpu.VMEM((8, cw), F32), slots=pltpu.VMEM((count // 2 + 1, 8, cw), F32), slots1=pltpu.VMEM((count // 2 + 1, 8, cw), F32),
        send=DMA((count,)), recv=DMA((count,)), send1=DMA((count,)), recv1=DMA((count,)),
        xs=DMA((4,)), xr=DMA((2,)), ls=DMA((4,)), lr=DMA((2,)), hs=DMA((2,)), hr=DMA((2,)), ps=DMA((6,)), pr=DMA((6,)), cs=DMA((4,)), cr=DMA((2,)),
        es=DMA((2,)), er=DMA((2,)), gs=DMA((8, 12)), gr=DMA((8, 12)), save=DMA((8,)), keep=DMA((10,)),
    )
    scratch.update({k: pltpu.VMEM((4, 4) + shapes[v], BF) for k, v in names.items()}, **{k: pltpu.VMEM(*v) for k, v in held.items()})
    if fast:
        scratch.update({f"shard{k}": pltpu.VMEM((2,) + shapes[k], BF) for k in range(4)})
    fw = build("forward", lambda ns: forward_kernel(fast, count, cols, ns), ins, outs, scratch, {}, 1, 63)
    wide_w = dict(dw1=((cw, hw), BF), dw2=((hw, cw), BF))
    bounce = natural + (ANY,)
    names = ("par", "ocean", "coarse", "bias", "st0", "st1")
    ins = dict(top=fw.cot8, **{k: getattr(fw, k) for k in names})
    ins.update({k: mats[k] for k in ("shifts", "edges", "back", "gather", "spread", "turn", "patch", "unpatch")})
    ins.update({k: at_any(getattr(fw, k + "_out")) for k in ("nat0", "nat1", "a0", "a1", "up", "skip", "deep", "pieces")})
    ins.update({k: at_any(getattr(fw, k + "_out").reshape(cells, cw)) for k in ("z0", "z1")})
    views = dict(w1_0=(cw, hw), w2_0=(hw, cw), w1_1=(cw, hw), w2_1=(hw, cw), m0=(cw, cw), m1=(cw, cw), r0=(4 * cw, nw), r1=(GROUPS, 2, padded(n), 2 * cw))
    ins.update({k: at_any(getattr(fw, k + "_out").reshape(v)) for k, v in views.items()})
    outs = dict(
        act=((4, 4, tiles, 16, c), BF, ANY), gi=((4, 4, tiles, 16, c), BF, ANY), tiny0=((64, cw), F32), tiny1=((64, cw), F32),
        dm0=((cw, cw), BF), dm1=((cw, cw), BF), dr0=(views["r0"], BF, ANY), dr1=(views["r1"], BF, ANY), **{f"bounce{k}": bounce for k in range(4)},
    )
    space = {k: pltpu.VMEM(*v) for k, v in dict(dym=field(F32), dz=field(BF), packed=edge_rows, halo=edge_rows, halo1=edge_rows, nat=natural, **wide_w).items()}
    space.update(small=pltpu.VMEM((8, cw), F32), stats=pltpu.VMEM((8, cw), F32))
    for k in ("", "1"):
        space.update({"slots" + k: pltpu.VMEM((count // 2 + 1, 8, cw), F32), "send" + k: DMA((count,)), "recv" + k: DMA((count,)), "hsend" + k: DMA((2,)), "hrecv" + k: DMA((2,))})
    space.update(load_sem=DMA((8,)), ds=DMA((4, 2, 2)), dr=DMA((4, 4)), db=DMA((4, 2)), ps=DMA((2,)))
    if fast:
        for name, k in (("w0", 0), ("w1", 1), ("m0", 3), ("m1", 3), ("r0", 2), ("r1", 2)):
            space.update(reduce_bank(name, shapes[k]))
        for name, k in (("gw1", 0), ("gw2", 1), ("gr", 2), ("gm", 3)):
            space[name] = pltpu.VMEM((2,) + half_shape(shapes[k]), F32)
        space["total"] = pltpu.VMEM((64, cw), F32)
        outs.update(gwi=(w_in.shape, F32), gwo=(w_out.shape, F32), gres=(resample.shape, F32), gmm=((1, merge.shape[0]), F32))
        outs.update(gk=((1, 49, c), F32), gg=((1, c), F32), gs=((1, c), F32), gbo=((1, c), F32), gbi=((1, hid), F32))
        ins.update(half_hidden_back=at_any(mats["half_hidden_back"]), deep_back=at_any(mats["deep_back"]))
        space.update(sm=pltpu.VMEM((2, 64, cw), F32), tiny=pltpu.VMEM((9, 64, cw), F32), ts=DMA((9,)), tr=DMA((9,)))
    else:
        outs.update({f"{k}_{sec}": v + (ANY,) for k, v in wide_w.items() for sec in range(2)})
    bw = build("backward", lambda ns: back_kernel(fast, count, cols, ns), ins, outs, space, {}, 2, 63)
    activations = bw.act.reshape(1, batches, height, cols, c)
    grad_input = bw.gi.astype(F32).reshape(1, batches, height, cols, c)
    if fast:
        return activations, grad_input, bw.gk, bw.gg, bw.gs, bw.gbi, bw.gbo, bw.gwi, bw.gwo, bw.gres, bw.gmm.reshape(-1)
    scatter = lambda v: lax.psum_scatter(v.astype(F32).reshape(-1), both, scatter_dimension=0, tiled=True)
    gw1 = scatter(jnp.stack([unpack_in(v, c, hid) for v in (bw.dw1_0, bw.dw1_1)]))
    gw2 = scatter(jnp.stack([unpack_in(v, hid, c) for v in (bw.dw2_0, bw.dw2_1)]))
    gres = scatter(jnp.stack([unpack_down(bw.dr0, c, n), unpack_up(bw.dr1, c, n)]))
    gmm = scatter(jnp.stack([unpack_in(v, c, c) for v in (bw.dm0, bw.dm1)]))
    tiny = lax.psum(jnp.stack([bw.tiny0, bw.tiny1]), both)[s]
    narrow = lambda v: v.reshape(-1, GROUPS, padded(c))[:, :, : c // GROUPS].reshape(-1, c)
    fine = narrow(tiny[:59])
    grad_bias_in = tiny[59:63].reshape(-1)[:hw].reshape(GROUPS, -1)[:, : hid // GROUPS].reshape(1, hid)
    return (
        activations, grad_input, fine[None, :49], fine[57:58], fine[56:57], grad_bias_in, fine[58:59],
        gw1[None], gw2[None], gres[None], gmm,
    )


def solution(mesh):
    sections, dps = mesh.shape["section"], mesh.shape["dp"]
    flat, both = P("section", "dp"), P(("section", "dp"))
    per = P("section", None)
    rows = P(None, "dp", None, None)
    taps = P("section", None, None)
    fields = P("section", None, "dp", None, None)
    return jax.shard_map(
        functools.partial(on_device, sections, dps), mesh=mesh,
        in_specs=(rows, rows, P("dp", None), taps, per, per, per, per, flat, flat, flat, both),
        out_specs=(fields, fields, taps, per, per, per, per, flat, flat, flat, both), check_vma=False,
    )
```

```python
import functools

import jax
import jax.numpy as jnp
import ml_dtypes
import numpy as np
from jax import lax
from jax.experimental import pallas as pl
from jax.experimental.pallas import tpu as pltpu
from jax.sharding import PartitionSpec as P

BF = jnp.bfloat16
F32 = jnp.float32
MESH = pl.DeviceIdType.MESH
ANY = pl.BlockSpec(memory_space=pl.ANY)
VM = pl.BlockSpec(memory_space=pltpu.VMEM)
DMA = pltpu.SemaphoreType.DMA
EPS = 1e-05
GROUPS = 16
MEGA = 1 << 20


def padded(width):
    return -(-(width // GROUPS) // 16) * 16


def selector(rows, cols, pairs):
    out = np.zeros((rows, cols), np.float32)
    for r, c in pairs:
        out[r, c] = 1
    return out.astype(ml_dtypes.bfloat16)


def matrices(channels, hidden, deep):
    group, wide = channels // GROUPS, padded(channels)
    spread = selector(channels, GROUPS * wide, [(c, c // group * wide + c % group) for c in range(channels)])
    natural = selector(896, 224, [(i * 128 + q * 8 + p, (p + i) * 16 + q) for i in range(7) for q in range(16) for p in range(8)])

    def place(q, row):
        if row < 0:
            return 128 + q * 3 + row + 3
        return q * 8 + row if row < 8 else 176 + q * 3 + row - 8

    shifts = selector(896, 224, [(i * 128 + q * 8 + p, place(q, p + i - 3)) for i in range(7) for q in range(16) for p in range(8)])
    turn = selector(128, 128, [(q * 8 + p, p * 16 + q) for q in range(16) for p in range(8)])
    edges = selector(96, 128, [(48 * e + q * 3 + k, q * 8 + 5 * e + k) for e in range(2) for q in range(16) for k in range(3)])
    patch = selector(
        256, 256,
        [((i * 2 + j) * 64 + b * 4 + a, (2 * b + j) * 8 + 2 * a + i) for i in range(2) for j in range(2) for b in range(16) for a in range(4)],
    )
    pick = selector(128, 16, [(q * 8 + p, p // 4 * 8 + p % 4) for q in range(16) for p in range(8)])

    def widen(width):
        group, wide = width // GROUPS, padded(width)
        return selector(width, GROUPS * wide, [(v, v // group * wide + v % group) for v in range(width)])

    half_hidden = widen(hidden)[: hidden // 2, : GROUPS * padded(hidden) // 2]
    deep_spread = widen(deep)
    band = channels // GROUPS
    rows = selector(4 * wide, -(-4 * band // 16) * 16, [(k * wide + r, k * band + r) for k in range(4) for r in range(band)])
    return dict(
        half_hidden=half_hidden, half_hidden_back=np.ascontiguousarray(half_hidden.T), deep_spread=deep_spread,
        deep_back=np.ascontiguousarray(deep_spread.T), rows=rows, pick=pick, spread=spread, gather=np.ascontiguousarray(spread.T), natural=natural, shifts=shifts, turn=turn,
        back=np.ascontiguousarray(turn.T), edges=edges, patch=patch, unpatch=np.ascontiguousarray(patch.T),
    )


def grow(value, sizes):
    return jnp.pad(value, [(0, n - o) for n, o in zip(sizes, value.shape)])


def pack_in(value, parts, c, h):
    value = value.reshape(parts, c // GROUPS, GROUPS, h // GROUPS)
    return grow(value, (parts, padded(c), GROUPS, padded(h))).reshape(parts, padded(c), -1)


def pack_down(value, parts, c, n):
    value = value.reshape(parts, 4, c // GROUPS, GROUPS, n // GROUPS)
    return grow(value, (parts, 4, padded(c), GROUPS, padded(n))).reshape(parts, 4 * padded(c), -1)


def pack_up(value, parts, c, n):
    value = value.reshape(parts, n // GROUPS, 2, 2 * GROUPS, c // GROUPS)
    value = grow(value, (parts, padded(n), 2, 2 * GROUPS, padded(c)))
    return value.transpose(0, 2, 1, 3, 4).reshape(parts, 2 * padded(n), -1)


def unpack_in(value, c, h):
    value = value.reshape(-1, padded(c), GROUPS, padded(h))
    return value[:, : c // GROUPS, :, : h // GROUPS].reshape(-1)


def unpack_down(value, c, n):
    value = value.reshape(-1, 4, padded(c), GROUPS, padded(n))
    return value[:, :, : c // GROUPS, :, : n // GROUPS].reshape(-1)


def unpack_up(value, c, n):
    value = value.reshape(-1, 2, padded(n), 2 * GROUPS, padded(c))
    return value.transpose(0, 2, 1, 3, 4)[:, : n // GROUPS, :, :, : c // GROUPS].reshape(-1)


def device(p, m):
    g = p // 2
    return (p + g) % 2, 4 * g + m


def where_am_i():
    s, d = lax.axis_index("section"), lax.axis_index("dp")
    g = d // 4
    return s, d, g, d % 4, 2 * g + (s + g) % 2


def greet_near(count):
    s, d, g, m, p = where_am_i()
    barrier = pltpu.get_barrier_semaphore()

    def one(k, carry):
        q = (p + k) % count
        pl.semaphore_signal(barrier, inc=1, device_id=device(q, m), device_id_type=MESH)
        return carry

    lax.fori_loop(1, count, one, 0)
    for k in range(1, 4):
        for sec in range(2):
            pl.semaphore_signal(barrier, inc=1, device_id=(sec, 4 * g + (m + k) % 4), device_id_type=MESH)
    pl.semaphore_wait(barrier, count + 5)


def remote(src, dst, send, recv, peer):
    return pltpu.make_async_remote_copy(src_ref=src, dst_ref=dst, send_sem=send, recv_sem=recv, device_id=peer, device_id_type=MESH)


def arrived(ref, sem):
    pltpu.make_async_copy(ref, ref, sem).wait()


def all_sum(mine, slots, send, recv, count, between=None):
    s, d, g, m, p = where_am_i()
    groups = count // 2
    over = remote(mine, slots.at[groups], send.at[0], recv.at[0], (1 - s, d))
    over.start()
    arrived(slots.at[groups], recv.at[0])
    slots[g] = mine[...] + slots[groups]
    over.wait_send()

    def copy(k):
        return remote(slots.at[g], slots.at[g], send.at[k], recv.at[k], (s, 4 * ((g + k) % groups) + m))

    lax.fori_loop(1, groups, lambda k, c: (copy(k).start(), c)[1], 0)
    if between is not None:
        between()

    def wait(k, carry):
        arrived(slots.at[(g + groups - k) % groups], recv.at[k])
        copy(k).wait_send()
        return carry

    lax.fori_loop(1, groups, wait, 0)
    return lax.fori_loop(0, groups, lambda k, total: total + slots[k], jnp.zeros(mine.shape, F32))


def swap_rows(packed, halo, send, recv, count, between=None):
    s, d, g, m, p = where_am_i()

    def peer(q):
        return device(q, m)

    @pl.when(p > 0)
    def _():
        remote(packed.at[0], halo.at[1], send.at[0], recv.at[1], peer(p - 1)).start()

    @pl.when(p < count - 1)
    def _():
        remote(packed.at[1], halo.at[0], send.at[1], recv.at[0], peer(p + 1)).start()

    if between is not None:
        between()

    @pl.when(p > 0)
    def _():
        arrived(halo.at[0], recv.at[0])
        remote(packed.at[0], halo.at[1], send.at[0], recv.at[1], peer(p - 1)).wait_send()

    @pl.when(p < count - 1)
    def _():
        arrived(halo.at[1], recv.at[1])
        remote(packed.at[1], halo.at[0], send.at[1], recv.at[0], peer(p + 1)).wait_send()

    @pl.when(p == 0)
    def _():
        halo[0] = jnp.zeros(halo.shape[1:], BF)

    @pl.when(p == count - 1)
    def _():
        halo[1] = jnp.zeros(halo.shape[1:], BF)


def dot(a, b):
    return jnp.dot(a, b, preferred_element_type=F32)


def dot_nt(a, b):
    return lax.dot_general(a, b, (((1,), (1,)), ((), ())), preferred_element_type=F32)


def dot_tn(a, b):
    return lax.dot_general(a, b, (((0,), (0,)), ((), ())), preferred_element_type=F32)


def lanes4(mask, width):
    return jnp.concatenate([mask] * (width // 128), axis=1)


def rows8(value):
    return value.reshape(-1, 8, value.shape[-1]).sum(0)


def to_natural(cells, back, gather, out):
    narrow = dot(cells, gather).astype(BF)
    for c in range(out.shape[1]):
        out[:, c] = dot(back, narrow[128 * c : 128 * c + 128]).astype(BF).reshape(8, 16, narrow.shape[1])


def shifted(chunk, perm, S, c):
    moved = dot(perm, chunk)
    for lane in range(S.shape[1]):
        S[:, lane, pl.ds(3 + 16 * c, 16)] = moved[:, lane * 128 : lane * 128 + 128].reshape(7, 16, 8, 128)
    return moved


def wrap(S, cols):
    S[:, :, 0:3] = S[:, :, cols : cols + 3]
    S[:, :, cols + 3 : cols + 6] = S[:, :, 3:6]


def taps_to(kb, par, flip):
    for lane in range(kb.shape[0]):
        at = slice(128 * lane, 128 * lane + 128)
        for k in range(49):
            tap = 48 - k if flip else k
            kb[lane, k] = jnp.broadcast_to(par[tap : tap + 1, at], (8, 128))


def taps_at(S, kb, lane, tile, first, sums):
    for i in range(7):
        window = [S[i, lane, first + t] for t in range(len(sums) + 6)]
        taps = [kb[tile, 7 * i + j] for j in range(7)]
        for k in range(len(sums)):
            total = window[k] * taps[0]
            for j in range(1, 7):
                total = total + window[k + j] * taps[j]
            sums[k] = sums[k] + total
    return sums


def norm_terms(st, par):
    counted = st[2:3]
    mean = st[0:1] / counted
    inverse = lax.rsqrt(st[1:2] / counted - mean * mean + EPS)
    return counted, mean, inverse, par[49:50], par[50:51]


def start_either(self, src, dst, send, recv, peer):
    pl.when(jnp.logical_not(self))(lambda: remote(src, dst, send, recv, peer).start())
    pl.when(self)(lambda: pltpu.make_async_copy(src, dst, recv).start())


def deliver(sec, nat, out, bounce, send, recv, b):
    s, d, g, m, p = where_am_i()

    def target(which, j):
        dp = 4 * g + 2 * ((p + which) % 2) + j
        part = (nat, bounce)[which].at[pl.ds(4 * j, 4)]
        return dp == d, part, out.at[m], send.at[which, j], recv.at[m], (s, dp)

    def over():
        return remote(nat, bounce, b.at[0], b.at[1], (1 - s, d))

    def sends(which):
        for j in range(2):
            start_either(*target(which, j))

    def begin():
        pl.when(s != sec)(lambda: over().start())
        pl.when(s == sec)(lambda: sends(0))

    def middle():
        @pl.when(s == sec)
        def _():
            arrived(bounce, b.at[1])
            sends(1)

    def end():
        @pl.when(s == sec)
        def _():
            for mb in range(4):
                arrived(out.at[mb], recv.at[mb])
            for which in range(2):
                for j in range(2):
                    self_, *rest = target(which, j)
                    pl.when(jnp.logical_not(self_))(lambda rest=rest: remote(*rest).wait_send())

        pl.when(s != sec)(lambda: over().wait_send())

    return [begin, middle, lambda: None, end]


def collect(field, out, first, send, recv):
    s, d, g, m, p = where_am_i()
    core, dp = device(d // 2, 0)
    j = d % 2

    def parts(step):
        mb = (m + step) % 4
        return field.at[mb], out.at[pl.ds(first + 4 * j, 4)], send.at[step], recv.at[j], (s, dp + mb)

    def begin():
        @pl.when(s == core)
        def _():
            for step in range(1, 4):
                remote(*parts(step)).start()
            src, dst, _, sem, _ = parts(0)
            pltpu.make_async_copy(src, dst, sem).start()

    def end():
        for jj in range(2):
            arrived(out.at[pl.ds(first + 4 * jj, 4)], recv.at[jj])

        @pl.when(s == core)
        def _():
            for step in range(1, 4):
                remote(*parts(step)).wait_send()

    return begin, end


def half(ref, c):
    rows, lanes = ref.shape[-2:]
    lead = (slice(None),) * (len(ref.shape) - 2)
    if rows % 32 == 0:
        return ref.at[lead + (pl.ds(pl.multiple_of(c * (rows // 2), 16), rows // 2),)]
    return ref.at[lead + (slice(None), pl.ds(pl.multiple_of(c * (lanes // 2), 128), lanes // 2))]


def half_shape(shape):
    rows, lanes = shape[-2:]
    return shape[:-2] + ((rows // 2, lanes) if rows % 32 == 0 else (rows, lanes // 2))


def collect_land(land, out, send, recv):
    s, d, g, m, p = where_am_i()
    core, dp = device(d // 2, 0)

    def part(step):
        return remote(land, out.at[d % 2], send.at[step], recv.at[d % 2], (s, dp + (m + step) % 4))

    def begin():
        @pl.when(s == core)
        def _():
            for step in range(1, 4):
                part(step).start()
            pltpu.make_async_copy(land, out.at[d % 2], recv.at[d % 2]).start()

    def end():
        for jj in range(2):
            arrived(out.at[jj], recv.at[jj])

        @pl.when(s == core)
        def _():
            for step in range(1, 4):
                part(step).wait_send()

    return begin, end


def script(*actions):
    queue = list(actions)

    def hook(*_):
        if queue:
            queue.pop(0)()

    return hook


def nothing(*_):
    pass


class Gather:
    def __init__(self, shard, full, send, recv):
        self.shard, self.full, self.send, self.recv = shard, full, send, recv
        self.s, self.d, self.g, self.m, _ = where_am_i()
        self.bit = 1 + self.s

    def block(self, col, c):
        return half(self.full.at[:, col], c)

    def near(self):
        return pltpu.make_async_copy(half(self.shard, self.s), half(self.full.at[self.g, self.m], self.s), self.send.at[0])

    def line(self, step):
        src, dst = half(self.shard, self.s), half(self.full.at[self.g, self.m], self.s)
        return remote(src, dst, self.send.at[step], self.recv.at[step], (self.s, 4 * ((self.g + step) % 4) + self.m))

    def column(self, slot, col, peer):
        block = self.block(col, self.s)
        return remote(block, block, self.send.at[slot], self.recv.at[slot], peer)

    def first(self):
        return self.column(4, self.m, (self.s, self.d ^ self.bit))

    def second(self, index):
        return self.column(5 + index, (self.m, self.m ^ self.bit)[index], (self.s, self.d ^ (3 - self.bit)))

    def cols(self, way):
        return (self.m, self.m ^ way, self.m ^ (3 - way), self.m ^ 3)

    def hand(self, index):
        return self.column(7 + index, self.cols(self.bit)[index], (1 - self.s, self.d))

    def start(self):
        self.near().start()
        for step in range(1, 4):
            self.line(step).start()

    def plane(self):
        self.near().wait()
        for step in range(1, 4):
            arrived(half(self.full.at[(self.g + 4 - step) % 4, self.m], self.s), self.recv.at[step])
        self.first().start()
        self.second(0).start()
        self.hand(0).start()

    def onward(self):
        arrived(self.block(self.m ^ self.bit, self.s), self.recv.at[4])
        self.second(1).start()
        self.hand(1).start()

    def over(self):
        for index in range(2):
            arrived(self.block((self.m ^ (3 - self.bit), self.m ^ 3)[index], self.s), self.recv.at[5 + index])
            self.hand(2 + index).start()

    def whole(self):
        for index, col in enumerate(self.cols(3 - self.bit)):
            arrived(self.block(col, 1 - self.s), self.recv.at[7 + index])

    def finish(self):
        for step in range(1, 4):
            self.line(step).wait_send()
        self.first().wait_send()
        for index in range(2):
            self.second(index).wait_send()
        for index in range(4):
            self.hand(index).wait_send()


class Load:
    def __init__(self, src, full, sem):
        self.copy = lambda: pltpu.make_async_copy(src, full, sem.at[0])

    def start(self):
        self.copy().start()

    def whole(self):
        self.copy().wait()

    def plane(self):
        pass

    onward = over = finish = plane


def masks(land, ocean, coarse, pick, patch):
    rows, across = land.shape[0] * land.shape[1], land.shape[2]
    flat = land[...].reshape(rows, across).astype(F32).astype(BF)
    spread = dot(pick, flat)
    at = lax.broadcasted_iota(jnp.int32, spread.shape, 1) - lax.broadcasted_iota(jnp.int32, spread.shape, 0) // 8
    ones = jnp.ones((across, 128), BF)

    def chunk(c, carry):
        ocean[pl.ds(pl.multiple_of(c * 128, 128), 128)] = dot(jnp.where(at == 16 * c, spread, 0.0).astype(BF), ones)
        return carry

    lax.fori_loop(0, ocean.shape[0] // 128, chunk, 0, unroll=True)
    for b in range(ocean.shape[0] // 256):
        moved = dot(patch, ocean[256 * b : 256 * b + 256].astype(BF))
        coarse[64 * b : 64 * b + 64] = moved[:64] * moved[64:128] * moved[128:192] * moved[192:]


def conv_phase(sec, cols, ns, hook):
    ocean, z, stats = ns.ocean, ns.z, ns.stats
    wide, tiles = z.shape[2], cols // 16

    def count_cells(b, t):
        return t + ocean[pl.ds(pl.multiple_of(b * 64, 64), 64)].reshape(8, 8, 128).sum(0)

    def phase(S, kb, *laid):
        taps_to(kb, ns.par[sec], False)
        tally = lax.fori_loop(0, cols // 8, count_cells, jnp.zeros((8, 128), F32))
        lanes = S.shape[1]
        if sec == 0:
            (laid,) = laid

            def lay(r, carry):
                row = ns.x14[r]
                laid[r] = dot(row.reshape(cols, row.shape[2]), ns.spread[...]).astype(BF).reshape(tiles, 16, wide)
                return carry

            lax.fori_loop(0, 14, lay, 0, unroll=True)
        for group in range(wide // 128 // lanes):
            part = slice(group * lanes * 128, (group + 1) * lanes * 128)

            def chunk(c, carry):
                cells = pl.ds(pl.multiple_of(c * 128, 128), 128)
                if sec == 0:
                    moved = shifted(laid[:, c, :, part].reshape(224, lanes * 128), ns.natural[...], S, c)
                    ns.a0[cells, part] = moved[384:512].astype(BF)
                else:
                    shifted(jnp.concatenate([ns.a1[cells, part], ns.halo[0, c, :, part], ns.halo[1, c, :, part]], axis=0), ns.shifts[...], S, c)
                return carry

            lax.fori_loop(0, tiles, chunk, 0, unroll=5)
            wrap(S, cols)
            hook()
            for lane in range(lanes):
                at = slice((group * lanes + lane) * 128, (group * lanes + lane + 1) * 128)

                def step(b, carry):
                    first, second = carry
                    sums = taps_at(S, kb, lane, group * lanes + lane, b * 16, [jnp.zeros((8, 128), F32)] * 16)
                    for k, total in enumerate(sums):
                        z[b * 16 + k, :, at] = total
                        kept = total * ocean[pl.ds(pl.multiple_of(b * 128 + 8 * k, 8), 8)]
                        first = first + kept
                        second = second + kept * total
                    return first, second

                zero = jnp.zeros((8, 128), F32)
                first, second = lax.fori_loop(0, tiles, step, (zero, zero), unroll=2)
                stats[0:1, at] = first.sum(0, keepdims=True)
                stats[1:2, at] = second.sum(0, keepdims=True)
                stats[2:3, at] = tally.sum(0, keepdims=True)
                stats[3:8, at] = jnp.zeros((5, 128), F32)
                hook()

    space = [pltpu.VMEM((7, 2, cols + 6, 8, 128), F32), pltpu.VMEM((wide // 128, 49, 8, 128), F32)]
    pl.run_scoped(phase, *space, *([pltpu.VMEM((14, tiles, 16, wide), BF)] if sec == 0 else []))


def gelu_terms(e):
    phi = 0.5 + 0.5 * lax.erf(e * np.float32(0.5**0.5))
    return phi, phi + e * (np.float32((2 * np.pi) ** -0.5) * jnp.exp(-0.5 * e * e))


def ff_phase(sec, ns, st, w1, w2, res, y, nat, hook):
    par = ns.par[sec]
    counted, mean, inverse, gain, shift = norm_terms(st, par)
    cells, wide = res.shape
    w1, w2 = w1.reshape(wide, -1), w2.reshape(-1, wide)
    hidden = w1.shape[1]

    def phase(n, g, r):
        def norm(b, carry):
            z = ns.z[pl.ds(b * 32, 32)].reshape(256, wide)
            n[pl.ds(pl.multiple_of(b * 256, 256), 256)] = ((z - mean) * inverse * gain + shift).astype(BF)
            return carry

        lax.fori_loop(0, cells // 256, norm, 0, unroll=True)
        for h in range(hidden // 256):
            at = slice(256 * h, 256 * h + 256)
            e = dot(n[...], w1[:, at]) + ns.bias[sec, 0:1, at]
            g[:, at] = (e * gelu_terms(e)[0]).astype(BF)
            hook(h)
        r[...] = dot(g[...], w2[...])
        hook(hidden // 256)

        def end(b, carry):
            at = pl.ds(pl.multiple_of(b * 256, 256), 256)
            y[at] = (lanes4(ns.ocean[at], wide) * (res[at].astype(F32) + (r[at] + par[51:52]))).astype(BF)
            return carry

        lax.fori_loop(0, cells // 256, end, 0, unroll=True)
        to_natural(y[...], ns.back[...], ns.gather[...], nat)

    pl.run_scoped(phase, pltpu.VMEM((cells, wide), BF), pltpu.VMEM((cells, hidden), BF), pltpu.VMEM((cells, wide), F32))


def parts3(value):
    high = value.astype(BF)
    rest = value - high.astype(F32)
    middle = rest.astype(BF)
    return high, middle, (rest - middle.astype(F32)).astype(BF)


def select(value, matrix):
    return sum(dot(v, matrix) for v in parts3(value))


def pack_shards(ns, swap):
    s = lax.axis_index("section")
    c, wide = ns.spread.shape
    hid, n = 2 * ns.half_hidden.shape[0], ns.deep_spread.shape[0]

    def phase(nat, half_hidden, deep_spread):
        got = loads([(ns.half_hidden, half_hidden), (ns.deep_spread, deep_spread)], ns.keep)

        def rows(flat, width):
            count = flat.shape[1] // width
            tall = -(-count // 16) * 16
            nat[tall - 16 : tall] = jnp.zeros((16, nat.shape[1]), F32)
            for r in range(count):
                nat[r : r + 1, 0:width] = flat[0:1, r * width : r * width + width]
            return tall

        tall = rows(ns.w_in, hid)
        got[0]()
        size = half_hidden.shape[1]
        for q in range(2):
            ns.shard0[s, :, size * q : size * q + size] = dot(nat[0:tall, hid // 2 * q : hid // 2 * q + hid // 2].astype(BF), half_hidden[...]).astype(BF)
        swap(0)
        tall = rows(ns.w_out, c)
        ns.shard1[s] = dot(nat[0:tall, 0:c].astype(BF), ns.spread[...]).astype(BF)
        swap(1)
        got[1]()

        @pl.when(s == 0)
        def _():
            tall = rows(ns.resample, n)
            laid = dot(nat[0:tall, 0:n].astype(BF), deep_spread[...]).astype(BF)
            ns.shard2[0] = dot(ns.rows[...], laid).astype(BF)

        @pl.when(s == 1)
        def _():
            tall = rows(ns.resample, 4 * c)
            for q in range(4):
                ns.shard2[1, tall * (q // 2) : tall * (q // 2) + tall, wide * (q % 2) : wide * (q % 2) + wide] = dot(
                    nat[0:tall, c * q : c * q + c].astype(BF), ns.spread[...]).astype(BF)

        swap(2)
        tall = rows(ns.merge, c)
        ns.shard3[s] = dot(nat[0:tall, 0:c].astype(BF), ns.spread[...]).astype(BF)
        swap(3)
        nat[48:64] = jnp.zeros((16, nat.shape[1]), F32)
        nat[0:49, 0:c] = ns.kernel[0]
        for k, ref in enumerate((ns.bn_gain, ns.bn_bias, ns.bias_out)):
            nat[49 + k : 50 + k, 0:c] = ref[...]
        ns.par[s] = select(nat[0:56, 0:c], ns.spread[...])
        swap(4)
        nat[0:8] = jnp.zeros((8, nat.shape[1]), F32)
        nat[0:1, 0:hid] = ns.bias_in[...]
        for q in range(2):
            ns.bias[s, :, size * q : size * q + size] = select(nat[0:8, hid // 2 * q : hid // 2 * q + hid // 2], half_hidden[...])
        swap(5)

    pl.run_scoped(phase, pltpu.VMEM((112, max(hid, 4 * c)), F32), pltpu.VMEM(ns.half_hidden.shape, BF), pltpu.VMEM(ns.deep_spread.shape, BF))


def unpack_sums(ns, deep_ready, mats_ready, small_ready):
    s = lax.axis_index("section")
    wide, c = ns.gather.shape
    hid, n = 2 * ns.half_hidden_back.shape[1], ns.deep_back.shape[1]

    def phase(nat, half_back, deep_back):
        got = loads([(ns.half_hidden_back, half_back), (ns.deep_back, deep_back)], ns.load_sem)
        got[0]()
        got[1]()

        def narrow(value, matrix):
            return dot(value.astype(BF), matrix) + dot((value - value.astype(BF).astype(F32)).astype(BF), matrix)

        def rows(out, width, count):
            for r in range(count):
                out[0:1, r * width : r * width + width] = nat[r : r + 1, 0:width]

        size = half_back.shape[0]
        deep_ready()
        merge = ns.gm.reshape(-1, wide)
        nat[0 : merge.shape[0], 0:c] = narrow(merge[...], ns.gather[...])
        rows(ns.gmm, c, ns.gmm.shape[1] // c)
        deep = ns.gr.reshape(-1, ns.gr.shape[2])

        @pl.when(s == 0)
        def _():
            nat[0 : deep.shape[0], 0:n] = narrow(deep[...], deep_back[...])
            band, high = c // GROUPS, deep.shape[0] // 4
            for k in range(4):
                for r in range(band):
                    at = n * (band * k + r)
                    ns.gres[0:1, at : at + n] = nat[high * k + r : high * k + r + 1, 0:n]

        @pl.when(s == 1)
        def _():
            high = deep.shape[0] // 2
            for j in range(2):
                nat[0 : deep.shape[0], 0:c] = narrow(deep[:, wide * j : wide * j + wide], ns.gather[...])
                for i in range(2):
                    for r in range(n // GROUPS):
                        at = 4 * c * r + c * (2 * i + j)
                        ns.gres[0:1, at : at + c] = nat[high * i + r : high * i + r + 1, 0:c]

        mats_ready()
        grad = ns.gw1.reshape(-1, ns.gw1.shape[2])
        for q in range(2):
            nat[0 : grad.shape[0], hid // 2 * q : hid // 2 * q + hid // 2] = narrow(grad[:, size * q : size * q + size], half_back[...])
        rows(ns.gwi, hid, ns.gwi.shape[1] // hid)
        for k in range(2):
            lanes = wide // 2
            part = narrow(ns.gw2[k], ns.gather[lanes * k : lanes * k + lanes])
            if k == 0:
                nat[0 : ns.gw2.shape[1], 0:c] = part
            else:
                nat[0 : ns.gw2.shape[1], 0:c] += part
        rows(ns.gwo, c, ns.gwo.shape[1] // c)
        small_ready()
        nat[0:64, 0:c] = narrow(ns.total[...], ns.gather[...])
        ns.gk[0] = nat[0:49, 0:c]
        ns.gs[...] = nat[56:57, 0:c]
        ns.gg[...] = nat[57:58, 0:c]
        ns.gbo[...] = nat[58:59, 0:c]
        flat = jnp.concatenate([ns.total[59 + k : 60 + k] for k in range(-(-2 * size // wide))], axis=1)
        for q in range(2):
            ns.gbi[0:1, hid // 2 * q : hid // 2 * q + hid // 2] = narrow(jnp.broadcast_to(flat[:, size * q : size * q + size], (8, size)), half_back[...])[0:1]

    pl.run_scoped(phase, pltpu.VMEM((128, max(hid, 4 * c)), F32), pltpu.VMEM(ns.half_hidden_back.shape, BF), pltpu.VMEM(ns.deep_back.shape, BF))


def forward_kernel(fast, count, cols, ns):
    s, d, g, m, p = where_am_i()
    greet_near(count)
    x14 = ns.x14
    x_begin, x_end = collect(ns.x, x14, 3, ns.xs, ns.xr)
    land_begin, land_end = collect_land(ns.land, ns.land2, ns.ls, ns.lr)
    x_begin()
    land_begin()
    swapped = [getattr(ns, f"shard{k}") for k in range(4)] + [ns.par, ns.bias] if fast else [ns.par, ns.bias]

    def swap(k):
        return remote(swapped[k].at[s], swapped[k].at[s], ns.ps.at[k], ns.pr.at[k], (1 - s, d))

    def swap_in(k):
        arrived(swapped[k].at[1 - s], ns.pr.at[k])

    fulls = dict(w1_0=ns.w1_0, w2_0=ns.w2_0, r0=ns.r0, m0=ns.m0, m1=ns.m1, r1=ns.r1, w1_1=ns.w1_1, w2_1=ns.w2_1)
    which = dict(w1_0=(0, 0), w2_0=(1, 0), r0=(2, 0), r1=(2, 1), m0=(3, 0), m1=(3, 1), w1_1=(0, 1), w2_1=(1, 1))
    mats = {}
    for k, (name, full) in enumerate(fulls.items()):
        if fast:
            index, sec = which[name]
            mats[name] = Gather(getattr(ns, f"shard{index}").at[sec], full, ns.gs.at[k], ns.gr.at[k])
        else:
            mats[name] = Load(getattr(ns, name + "_in"), full, ns.gs.at[k])
    kept = dict(z0=ns.z, z1=ns.z, a0=ns.a0, a1=ns.a1, skip=ns.skip, up=ns.up, pieces=ns.pieces, deep=ns.deep, nat0=ns.nat0, nat1=ns.nat1)
    keeps = {name: lambda k=k, name=name, ref=ref: pltpu.make_async_copy(ref, getattr(ns, name + "_out"), ns.keep.at[k]) for k, (name, ref) in enumerate(kept.items())}

    def keep(*names):
        for name in names:
            keeps[name]().start()

    saves = {name: lambda k=k, name=name, full=full: pltpu.make_async_copy(full, getattr(ns, name + "_out"), ns.save.at[k]) for k, (name, full) in enumerate(fulls.items())}

    def do(step, *names):
        for name in names:
            getattr(mats[name], step)()

    def whole(*names):
        do("whole", *names)
        for name in names:
            saves[name]().start()

    def give(k):
        swap(k).start()
        if k == 1:
            swap_in(0)
            do("start", "w1_0")
        if k == 2:
            swap_in(1)
            do("start", "w2_0")

    if fast:
        pack_shards(ns, give)
        swap_in(2)
        swap_in(3)
    else:
        near = [pltpu.make_async_copy(src, dst.at[s], ns.keep.at[k]) for k, (src, dst) in enumerate(((ns.mine, ns.par), (ns.mine_bias, ns.bias)))]
        for c in near:
            c.start()
        for c in near:
            c.wait()
        for k in range(2):
            swap(k).start()
        do("start", "w1_0", "w2_0")
    do("start", "r0")
    land_end()
    masks(ns.land2, ns.ocean, ns.coarse, ns.pick[...], ns.patch[...])
    x_end()

    def edge(up):
        src, dst = (x14.at[pl.ds(3, 3)], x14.at[pl.ds(11, 3)]) if up else (x14.at[pl.ds(8, 3)], x14.at[pl.ds(0, 3)])
        return remote(src, dst, ns.hs.at[int(up)], ns.hr.at[int(up)], device(p - 1 if up else p + 1, m))

    pl.when(p > 0)(edge(True).start)
    pl.when(p < count - 1)(edge(False).start)
    do("plane", "w1_0", "w2_0")
    swap_in(len(swapped) - 2)
    swap_in(len(swapped) - 1)

    @pl.when(p == 0)
    def _():
        x14[0:3] = jnp.zeros((3,) + x14.shape[1:], BF)

    @pl.when(p == count - 1)
    def _():
        x14[11:14] = jnp.zeros((3,) + x14.shape[1:], BF)

    pl.when(p > 0)(lambda: arrived(x14.at[pl.ds(0, 3)], ns.hr.at[0]))
    pl.when(p < count - 1)(lambda: arrived(x14.at[pl.ds(11, 3)], ns.hr.at[1]))

    cot_begin, cot_end = collect(ns.cot, ns.cot8, 0, ns.cs, ns.cr)

    do("onward", "w1_0", "w2_0")

    conv_phase(0, cols, ns, script(
        nothing,
        lambda: (do("plane", "r0"), do("start", "r1", "m0", "m1")),
        nothing,
        lambda: do("over", "w1_0", "w2_0"),
        lambda: do("onward", "r0"),
        nothing,
    ))
    ns.st0[...] = all_sum(ns.stats, ns.slots, ns.send, ns.recv, count)
    keep("z0", "a0")
    whole("w1_0", "w2_0")
    ff0 = {1: lambda: (do("plane", "r1", "m0", "m1"), do("start", "w1_1", "w2_1")), 7: lambda: do("over", "r0")}
    ff_phase(0, ns, ns.st0, ns.w1_0, ns.w2_0, ns.a0, ns.skip, ns.nat0, lambda k: ff0.get(k, nothing)())
    keep("skip", "nat0")

    skip, pieces, wide = ns.skip, ns.pieces, ns.skip.shape[1]
    blocks = skip.shape[0] // 256
    down, up_w = ns.r0.reshape(4 * wide, -1), ns.r1.reshape(GROUPS, 2, ns.r1.shape[2] // 2, -1)
    merge = [v.reshape(wide, wide) for v in (ns.m0, ns.m1)]
    for b in range(blocks):
        moved = dot(ns.patch[...], skip[256 * b : 256 * b + 256]).astype(BF)
        for k in range(4):
            pieces[k, 64 * b : 64 * b + 64] = moved[64 * k : 64 * k + 64]
    do("onward", "r1", "m0", "m1")
    whole("r0")
    value = sum(dot(pieces[k], down[wide * k : wide * k + wide]) for k in range(4))
    deep_value = (lanes4(ns.coarse[...], value.shape[1]) * value).astype(BF)
    ns.deep[...] = deep_value
    keep("pieces", "deep")
    do("over", "m0", "m1", "r1")
    do("plane", "w1_1", "w2_1")
    whole("m0", "m1", "r1")
    rows = up_w.shape[0] * up_w.shape[2]
    lifted = [dot(deep_value, up_w[:, i].reshape(rows, -1)).astype(BF) for i in range(2)]
    for b in range(blocks):
        at = slice(256 * b, 256 * b + 256)
        stacked = jnp.concatenate(
            [lifted[i][64 * b : 64 * b + 64, wide * j : wide * j + wide] for i in range(2) for j in range(2)], axis=0
        )
        ns.up[at] = dot(ns.unpatch[...], stacked).astype(BF)
    for b in range(blocks):
        at = slice(256 * b, 256 * b + 256)
        joined = dot(ns.up[at], merge[0][...]) + dot(skip[at], merge[1][...])
        ns.h[at] = joined
        low = joined.astype(BF)
        ns.a1[at] = low
        for k in range(2):
            ends = dot(ns.edges[...], low[128 * k : 128 * k + 128]).astype(BF)
            ns.packed[0, 2 * b + k] = ends[:48]
            ns.packed[1, 2 * b + k] = ends[48:]
    do("onward", "w1_1", "w2_1")
    cot_begin()
    swap_rows(ns.packed, ns.halo, ns.es, ns.er, count)
    keep("up", "a1")
    keeps["z0"]().wait()

    conv_phase(1, cols, ns, script(nothing, nothing, lambda: do("over", "w1_1", "w2_1")))
    ns.st1[...] = all_sum(ns.stats, ns.slots1, ns.send1, ns.recv1, count)
    keep("z1")
    whole("w1_1", "w2_1")
    ff_phase(1, ns, ns.st1, ns.w1_1, ns.w2_1, ns.h, ns.y1, ns.nat1, nothing)
    keep("nat1")

    cot_end()
    for name, save in saves.items():
        save().wait()
        do("finish", name)
    for name, copy in keeps.items():
        if name != "z0":
            copy().wait()
    for k in range(len(swapped)):
        swap(k).wait_send()
    pl.when(p > 0)(edge(True).wait_send)
    pl.when(p < count - 1)(edge(False).wait_send)


class Reduce:
    def __init__(self, sec, partial, bank, out, send, recv):
        self.sec, self.partial, self.out, self.send, self.recv = sec, partial, out, send, recv
        self.own, self.core, self.one, self.two, self.row, self.mine = bank
        self.s, self.d, self.g, self.m, _ = where_am_i()
        self.bit = 1 + self.s
        self.rest = self.m ^ (3 - self.bit)

    def near(self):
        return pltpu.make_async_copy(half(self.partial, self.s), self.own, self.send.at[0])

    def over(self):
        return remote(half(self.partial, 1 - self.s), self.core, self.send.at[1], self.recv.at[1], (1 - self.s, self.d))

    def first(self, index):
        col = (self.m ^ self.bit, self.m ^ 3)[index]
        return remote(self.own.at[:, col], self.one.at[:, index], self.send.at[2 + index], self.recv.at[2 + index], (self.s, self.d ^ self.bit))

    def second(self):
        return remote(self.own.at[:, self.rest], self.two, self.send.at[4], self.recv.at[4], (self.s, self.d ^ (3 - self.bit)))

    def along(self, step):
        to = (self.g + step) % 4
        return remote(self.own.at[to, self.m], self.row.at[step - 1], self.send.at[4 + step], self.recv.at[4 + step], (self.s, 4 * to + self.m))

    def give(self):
        return remote(self.mine, self.out.at[self.s], self.send.at[8], self.recv.at[8], (1 - self.s, self.d))

    def start(self):
        self.over().start()
        self.near().start()

    def plane(self):
        self.near().wait()
        arrived(self.core, self.recv.at[1])
        own, core, m, bit = self.own, self.core, self.m, self.bit

        def add(k, carry):
            z, col = k % 4, (m ^ 3, m ^ bit, m ^ (3 - bit), m)
            for c in col:
                own[z, c] = (own[z, c].astype(F32) + core[z, c].astype(F32)).astype(BF)
            return carry

        lax.fori_loop(0, 4, add, 0)
        self.first(1).start()
        self.first(0).start()

    def onward(self):
        own, one, rest = self.own, self.one, self.rest
        arrived(one.at[:, 1], self.recv.at[3])

        def add(z, carry):
            own[z, rest] = (own[z, rest].astype(F32) + one[z, 1].astype(F32)).astype(BF)
            return carry

        lax.fori_loop(0, 4, add, 0)
        self.second().start()

    def line(self):
        own, one, two, m = self.own, self.one, self.two, self.m
        arrived(one.at[:, 0], self.recv.at[2])
        arrived(two, self.recv.at[4])

        def add(z, carry):
            own[z, m] = (own[z, m].astype(F32) + one[z, 0].astype(F32) + two[z].astype(F32)).astype(BF)
            return carry

        lax.fori_loop(0, 4, add, 0)
        for step in range(1, 4):
            self.along(step).start()

    def total(self):
        for step in range(1, 4):
            arrived(self.row.at[step - 1], self.recv.at[4 + step])
        row = self.row
        self.mine[...] = self.own[self.g, self.m].astype(F32) + row[0].astype(F32) + row[1].astype(F32) + row[2].astype(F32)
        pl.when(self.s != self.sec)(lambda: self.give().start())

        @pl.when(self.s == self.sec)
        def _():
            self.out[self.s] = self.mine[...]

    def finish(self):
        self.over().wait_send()
        for index in range(2):
            self.first(index).wait_send()
        self.second().wait_send()
        for step in range(1, 4):
            self.along(step).wait_send()
        pl.when(self.s != self.sec)(lambda: self.give().wait_send())
        pl.when(self.s == self.sec)(lambda: arrived(self.out.at[1 - self.s], self.recv.at[8]))


def reduce_bank(name, shape):
    part = half_shape(shape)
    out = {f"{name}_{k}": pltpu.VMEM(lead + part, BF) for k, lead in (("own", (4, 4)), ("core", (4, 4)), ("one", (4, 2)), ("two", (4,)), ("row", (3,)))}
    out.update({f"{name}_mine": pltpu.VMEM(part, F32), f"{name}_s": DMA((9,)), f"{name}_r": DMA((9,))})
    return out


def reducer(ns, name, sec, partial, out):
    bank = [getattr(ns, f"{name}_{k}") for k in ("own", "core", "one", "two", "row", "mine")]
    return Reduce(sec, partial, bank, out, getattr(ns, f"{name}_s"), getattr(ns, f"{name}_r"))


def loads(pairs, sems, first=0):
    copies = [pltpu.make_async_copy(src, dst, sems.at[first + k]) for k, (src, dst) in enumerate(pairs)]
    for c in copies:
        c.start()
    return [c.wait for c in copies]


def back_ff_phase(sec, count, ns, top, kept, w_in, w_out, hook, done, between, meanwhile=None):
    z_in, st = kept
    cells, wide = ns.dym.shape
    hidden = w_in.shape[1]
    chunks = cells // 128
    ocean, small, dym = ns.ocean, ns.small, ns.dym
    counted, mean, inverse, gain, shift = norm_terms(st, ns.par[sec])

    def phase(w1, w2, z, n, de, dn, dr):
        got_z, got_w1, got_w2 = loads([(z_in, z), (w_in, w1), (w_out, w2)], ns.load_sem)

        def begin(c, total):
            at = pl.ds(pl.multiple_of(c * 128, 128), 128)
            if sec == 1:
                block = top[:, c]
                block = dot(block.reshape(-1, block.shape[-1]), ns.spread[...]).astype(BF)
                grad = dot(ns.turn[...], block)
            else:
                grad = top[at]
            grad = grad * lanes4(ocean[at], wide)
            dym[at] = grad
            low = grad.astype(BF)
            dr[at] = low
            return total + rows8(low.astype(F32))

        total = lax.fori_loop(0, chunks, begin, jnp.zeros((8, wide), F32), unroll=True)
        small[2:3] = total.sum(0, keepdims=True)
        small[3:8] = jnp.zeros((5, wide), F32)
        got_z()

        def norm(c, carry):
            at = pl.ds(pl.multiple_of(c * 128, 128), 128)
            n[at] = ((z[at] - mean) * inverse * gain + shift).astype(BF)
            return carry

        lax.fori_loop(0, chunks, norm, 0, unroll=True)
        got_w1()
        got_w2()
        for h in range(hidden // 256):
            at = slice(256 * h, 256 * h + 256)
            e = dot(n[...], w1[:, at]) + ns.bias[sec, 0:1, at]
            phi, slope = gelu_terms(e)
            ns.dw2[at] = dot_tn((e * phi).astype(BF), dr[...]).astype(BF)
            low = (dot_nt(dr[...], w2[at]) * slope).astype(BF)
            de[:, at] = low
            row, col = 3 + 256 * h // wide, 256 * h % wide
            small[row : row + 1, col : col + 256] = low.astype(F32).sum(0, keepdims=True)
            ns.dw1[:, at] = dot_tn(n[...], low).astype(BF)
            hook(h)
        done()
        dn[...] = dot_nt(de[...], w1[...])

        def sums(c, carry):
            at = pl.ds(pl.multiple_of(c * 128, 128), 128)
            grad = dn[at]
            return carry[0] + rows8(grad), carry[1] + rows8(grad * ((z[at] - mean) * inverse))

        zero = jnp.zeros((8, wide), F32)
        plain, scaled = lax.fori_loop(0, chunks, sums, (zero, zero), unroll=True)
        small[0:1] = plain.sum(0, keepdims=True)
        small[1:2] = scaled.sum(0, keepdims=True)
        ns.stats[...] = small[...]
        summed = all_sum(ns.stats, ns.slots, ns.send, ns.recv, count, meanwhile)
        first = -inverse * gain * summed[0:1] / counted
        second = -inverse * inverse * gain * summed[1:2] / counted

        def end(c, carry):
            at = pl.ds(pl.multiple_of(c * 128, 128), 128)
            grad = inverse * gain * dn[at] + lanes4(ocean[at], wide) * (first + second * (z[at] - mean))
            low = grad.astype(BF)
            ns.dz[at] = low
            ends = dot(ns.edges[...], low).astype(BF)
            ns.packed[0, c] = ends[:48]
            ns.packed[1, c] = ends[48:]
            return carry

        lax.fori_loop(0, chunks, end, 0, unroll=True)

    field = lambda t: pltpu.VMEM((cells, wide), t)
    pl.run_scoped(
        phase, pltpu.VMEM(w_in.shape, BF), pltpu.VMEM(w_out.shape, BF), field(F32), field(BF), pltpu.VMEM((cells, hidden), BF), field(F32), field(BF),
    )
    swap_rows(ns.packed, ns.halo, ns.hsend, ns.hrecv, count, between)


def back_conv_phase(sec, cols, ns, a_in, tiny, hook):
    cells, wide = ns.dz.shape
    dz = ns.dz

    def phase(S, kb, a, field, acc_dk):
        (got_a,) = loads([(a_in, a)], ns.load_sem)
        taps_to(kb, ns.par[sec], True)
        lanes = S.shape[1]
        for group in range(wide // 128 // lanes):
            part = slice(group * lanes * 128, (group + 1) * lanes * 128)

            def chunk(c, carry):
                block = jnp.concatenate([dz[pl.ds(pl.multiple_of(c * 128, 128), 128), part], ns.halo[0, c, :, part], ns.halo[1, c, :, part]], axis=0)
                shifted(block, ns.shifts[...], S, c)
                return carry

            lax.fori_loop(0, cols // 16, chunk, 0, unroll=5)
            wrap(S, cols)
            hook()
            if group == 0:
                got_a()
            tiles = [(lane, slice((group * lanes + lane) * 128, (group * lanes + lane + 1) * 128)) for lane in range(lanes)]
            for lane, at in tiles:

                def step(b, carry):
                    rows = pl.ds(pl.multiple_of(b * 128, 128), 128)
                    above = ns.dym[rows, at].reshape(16, 8, 128)
                    sums = taps_at(S, kb, lane, group * lanes + lane, b * 16, [above[k] for k in range(16)])
                    dz[rows, at] = jnp.concatenate(sums, axis=0).astype(BF)
                    return carry

                lax.fori_loop(0, cols // 16, step, 0, unroll=2)
            hook()
            for lane, at in tiles:
                field[...] = a[:, at].astype(F32).reshape(field.shape)
                acc_dk[...] = jnp.zeros(acc_dk.shape, F32)

                def tap_sums(b, carry):
                    here = [field[b * 16 + k] for k in range(16)]
                    for i in range(7):
                        window = [S[i, lane, b * 16 + t] for t in range(22)]
                        for j in range(7):
                            total = window[j] * here[0]
                            for k in range(1, 16):
                                total = total + window[j + k] * here[k]
                            acc_dk[7 * i + j] += total
                    return carry

                lax.fori_loop(0, cols // 16, tap_sums, 0, unroll=2)
                for k in range(49):
                    tiny[48 - k : 49 - k, at] = acc_dk[k].sum(0, keepdims=True)
            hook()
        tiny[49:56] = jnp.zeros((7, wide), F32)

    pl.run_scoped(
        phase, pltpu.VMEM((7, 2, cols + 6, 8, 128), F32), pltpu.VMEM((wide // 128, 49, 8, 128), F32), pltpu.VMEM((cells, wide), BF),
        pltpu.VMEM((cols, 8, 128), F32), pltpu.VMEM((49, 8, 128), F32),
    )


def back_mid_phase(ns, hook):
    dh = ns.dz
    cells, wide = dh.shape
    blocks = cells // 256

    def phase(skip, up, merge0, merge1, up_w, deep, down, pieces, dups, spreads, dskip):
        got = loads(
            [(ns.m1, merge1), (ns.m0, merge0), (ns.up, up), (ns.skip, skip), (ns.r1, up_w), (ns.deep, deep), (ns.pieces, pieces), (ns.r0, down)],
            ns.load_sem,
        )
        for k in range(2):
            got[k]()
        for b in range(blocks):
            at = slice(256 * b, 256 * b + 256)
            low = dot_nt(dh[at], merge1[...]).astype(BF)
            ns.dym[at] = low.astype(F32)
            dskip[at] = low
            lifted = dot_nt(dh[at], merge0[...]).astype(BF)
            moved = dot(ns.patch[...], lifted).astype(BF)
            for k in range(4):
                dups[k // 2, 64 * b : 64 * b + 64, wide * (k % 2) : wide * (k % 2) + wide] = moved[64 * k : 64 * k + 64]
        to_natural(dskip[...], ns.back[...], ns.gather[...], ns.nat)
        hook(0)
        got[2]()
        got[3]()
        ns.dm0[...] = dot_tn(up[...], dh[...]).astype(BF)
        ns.dm1[...] = dot_tn(skip[...], dh[...]).astype(BF)
        hook(1)
        rows = up_w.shape[0] * up_w.shape[2]
        got[4]()
        ddeep = dot_nt(dups[0], up_w[:, 0].reshape(rows, -1)) + dot_nt(dups[1], up_w[:, 1].reshape(rows, -1))
        got[5]()
        for i in range(2):
            up_w[:, i] = dot_tn(deep[...], dups[i]).astype(BF).reshape(up_w.shape[0], up_w.shape[2], -1)
        saves = [pltpu.make_async_copy(up_w, ns.dr1, ns.load_sem.at[0]), pltpu.make_async_copy(down, ns.dr0, ns.load_sem.at[1])]
        saves[0].start()
        masked = (lanes4(ns.coarse[...], ddeep.shape[1]) * ddeep).astype(BF)
        hook(2)
        got[6]()
        got[7]()
        for k in range(4):
            spreads[k] = dot_nt(masked, down[wide * k : wide * k + wide])
            down[wide * k : wide * k + wide] = dot_tn(pieces[k], masked).astype(BF)
        saves[1].start()
        saves[0].wait()
        hook(3)
        for b in range(blocks):
            value = jnp.concatenate([spreads[k, 64 * b : 64 * b + 64] for k in range(4)], axis=0)
            high = value.astype(BF)
            rest = (value - high.astype(F32)).astype(BF)
            at = slice(256 * b, 256 * b + 256)
            ns.dym[at] += dot(ns.unpatch[...], high) + dot(ns.unpatch[...], rest)
        saves[1].wait()

    like = lambda ref: pltpu.VMEM(ref.shape, BF)
    deep_cells = ns.deep.shape[0]
    pl.run_scoped(
        phase, like(ns.skip), like(ns.up), like(ns.m0), like(ns.m1), like(ns.r1), like(ns.deep), like(ns.r0), like(ns.pieces),
        pltpu.VMEM((2, deep_cells, 2 * wide), BF), pltpu.VMEM((4, deep_cells, wide), F32), pltpu.VMEM((cells, wide), BF),
    )


def with_names(ns, **names):
    out = Names()
    out.__dict__.update(ns.__dict__)
    out.__dict__.update(names)
    return out


def back_kernel(fast, count, cols, ns):
    s, d, g, m, p = where_am_i()
    greet_near(count)
    acts = [deliver(k, getattr(ns, f"nat{k}"), ns.act, getattr(ns, f"bounce{k}"), ns.ds.at[k], ns.dr.at[k], ns.db.at[k]) for k in range(2)]
    gi1, gi0 = (deliver(1 - k, ns.nat, ns.gi, getattr(ns, f"bounce{2 + k}"), ns.ds.at[2 + k], ns.dr.at[2 + k], ns.db.at[2 + k]) for k in range(2))
    w_dec = w_enc = m_all = r_up = r_down = []
    if fast:
        cut = lambda ref: ref.reshape(4, 4, ref.shape[0] // 16, ref.shape[1])
        w_dec = [reducer(ns, "w0", 1, cut(ns.dw1), ns.gw1), reducer(ns, "w1", 1, cut(ns.dw2), ns.gw2)]
        w_enc = [reducer(ns, "w0", 0, cut(ns.dw1), ns.gw1), reducer(ns, "w1", 0, cut(ns.dw2), ns.gw2)]
        m_all = [reducer(ns, f"m{k}", k, cut(getattr(ns, f"dm{k}")), ns.gm) for k in range(2)]
        r_up = [reducer(ns, "r1", 1, ns.dr1.reshape(4, 4, -1, ns.dr1.shape[3]), ns.gr)]
        r_down = [reducer(ns, "r0", 0, ns.dr0.reshape(4, 4, -1, ns.dr0.shape[1]), ns.gr)]

    def do(*steps):
        def action(*_):
            for step in steps:
                if isinstance(step, tuple):
                    for r in step[0]:
                        getattr(r, step[1])()
                else:
                    step()

        return action

    def keep_dw(sec):
        if not fast:
            copies = [pltpu.make_async_copy(ns.dw1, getattr(ns, f"dw1_{sec}"), ns.ps.at[0]), pltpu.make_async_copy(ns.dw2, getattr(ns, f"dw2_{sec}"), ns.ps.at[1])]
            for copy in copies:
                copy.start()
            for copy in copies:
                copy.wait()

    def at_step(**actions):
        return lambda h: actions.get(f"h{h}", nothing)()

    do(*(act[0] for act in acts))()
    dec = with_names(ns, halo=ns.halo1, slots=ns.slots1, send=ns.send1, recv=ns.recv1, hsend=ns.hsend1, hrecv=ns.hrecv1)
    back_ff_phase(1, count, dec, ns.top, (ns.z1, ns.st1), ns.w1_1, ns.w2_1, at_step(h3=do(*(act[1] for act in acts))), do((w_dec, "start"), lambda: keep_dw(1)), do((w_dec, "plane")))
    back_conv_phase(1, cols, dec, ns.a1, ns.tiny1, script(
        nothing, nothing, do(*(act[3] for act in acts)), do((w_dec, "onward")), nothing, do((w_dec, "line"))))
    ns.tiny1[56:64] = ns.small[...]
    back_mid_phase(ns, script(gi1[0], do((m_all, "start")), do((w_dec, "total"), gi1[1]), do((r_up, "start"), (m_all, "plane"))))
    do((r_down, "start"), (w_dec, "finish"))()

    back_ff_phase(0, count, ns, ns.dym, (ns.z0, ns.st0), ns.w1_0, ns.w2_0, at_step(
        h0=do((r_up, "plane")), h2=do((m_all, "onward")), h4=do((r_down, "plane")),
    ), do((w_enc, "start"), (m_all, "line"), lambda: keep_dw(0)), do((w_enc, "plane")), do((r_up, "onward")))
    def give_dh():
        to_natural(ns.dz[...], ns.back[...], ns.gather[...], ns.nat)
        gi0[0]()

    back_conv_phase(0, cols, ns, ns.a0, ns.tiny0, script(
        do((r_down, "onward"), (r_up, "line")), do((m_all, "total"), gi1[3]), do((w_enc, "onward"), (r_down, "line")), do((r_up, "total")),
        do(give_dh, (w_enc, "line")), gi0[1]))
    ns.tiny0[56:64] = ns.small[...]
    if fast:
        sm, tiny, ts, tr = ns.sm, ns.tiny, ns.ts, ns.tr
        peers = {1: lambda step: (s, 4 * ((g + step) % 4) + m), 5: lambda step: (s, d ^ step)}

        def send(base, step):
            return remote(tiny.at[base], tiny.at[base + step], ts.at[base + step], tr.at[base + step], peers[base](step))

        def gather(base):
            for step in range(1, 4):
                arrived(tiny.at[base + step], tr.at[base + step])
            for step in range(1, 4):
                send(base, step).wait_send()
            return tiny[base] + tiny[base + 1] + tiny[base + 2] + tiny[base + 3]

        def deep_ready():
            sm[0] = ns.tiny0[...]
            sm[1] = ns.tiny1[...]
            over = remote(sm.at[1 - s], tiny.at[0], ts.at[0], tr.at[0], (1 - s, d))
            over.start()
            do((r_down, "total"))()
            arrived(tiny.at[0], tr.at[0])
            over.wait_send()
            tiny[1] = sm[s] + tiny[0]
            for step in range(1, 4):
                send(1, step).start()
            do((m_all + r_up + r_down, "finish"))()

        def mats_ready():
            tiny[5] = gather(1)
            for step in range(1, 4):
                send(5, step).start()
            do((w_enc, "total"), (w_enc, "finish"))()

        def small_ready():
            ns.total[...] = gather(5)

        unpack_sums(ns, deep_ready, mats_ready, small_ready)
    gi0[3]()


class Names:
    pass


def build(name, body, ins, outs, scratch, alias, cid, limit):
    ins = {k: v if isinstance(v, tuple) else (v, VM) for k, v in ins.items()}
    outs = {k: v if len(v) == 3 else v + (VM,) for k, v in outs.items()}
    names = list(ins) + list(outs) + list(scratch)

    def kernel(*refs):
        ns = Names()
        for k, ref in zip(names, refs):
            setattr(ns, k, ref)
        body(ns)

    order_in, order_out = list(ins), list(outs)
    results = pl.pallas_call(
        kernel, name=name, out_shape=[jax.ShapeDtypeStruct(v[0], v[1]) for v in outs.values()],
        in_specs=[v[1] for v in ins.values()], out_specs=[v[2] for v in outs.values()], scratch_shapes=list(scratch.values()),
        input_output_aliases={order_in.index(a): order_out.index(b) for a, b in alias.items()},
        compiler_params=pltpu.CompilerParams(vmem_limit_bytes=limit * MEGA, collective_id=cid, has_side_effects=True),
    )(*[v[0] for v in ins.values()])
    out = Names()
    for k, v in zip(order_out, results):
        setattr(out, k, v)
    return out


def on_device(sections, dps, inputs, cotangent, land, kernel, bn_gain, bn_bias, bias_in, bias_out, w_in, w_out, resample, merge):
    batches, height, cols, c = inputs.shape
    hid = bias_in.shape[1]
    n = resample.shape[1] * dps // (4 * c)
    cw, hw, nw = (GROUPS * padded(v) for v in (c, hid, n))
    cells, deep_cells = cols * 8, cols * 2
    count = 2 * (dps // 4)
    fast = dps == GROUPS
    assert batches == 4 and height == 4 and dps % 4 == 0 and sections == 2 and cols % 32 == 0
    s = lax.axis_index("section")
    mats = {k: jnp.asarray(v) for k, v in matrices(c, hid, n).items()}
    tiles = cols // 16
    both = ("section", "dp")

    def packs(parts, w1, w2, rd, ru):
        return pack_in(w1, parts, c, hid), pack_in(w2, parts, hid, c), pack_down(rd, parts, c, n), pack_up(ru, parts, c, n)

    if not fast:
        flat = [lax.all_gather(v.astype(BF).reshape(-1), both, axis=0, tiled=True) for v in (w_in, w_out, resample, merge)]
        halves = [v.reshape(2, -1) for v in flat]
        whole = [packs(GROUPS, halves[0][k], halves[1][k], halves[2][k], halves[2][k]) for k in range(2)]
        rows = jnp.concatenate([kernel[0], bn_gain, bn_bias, bias_out], axis=0)
        mine = grow(grow(rows.reshape(-1, GROUPS, c // GROUPS), (52, GROUPS, padded(c))).reshape(52, cw), (56, cw))
        mine_bias = grow(grow(bias_in.reshape(GROUPS, -1), (GROUPS, padded(hid))).reshape(1, hw), (8, hw))

    x = inputs.reshape(batches, height, tiles, 16, c)
    cot = cotangent.reshape(batches, height, tiles, 16, c)
    land_cols = -(-cols // 128) * 128
    at_any = lambda v: (v, ANY)
    field = lambda t: ((cells, cw), t)
    natural = ((8, tiles, 16, c), BF)
    edge_rows = ((2, tiles, 48, cw), BF)
    shapes = [(padded(c), hw), (padded(hid), cw), (4 * padded(c), nw), (padded(c), cw)]
    names = dict(w1_0=0, w2_0=1, r0=2, m0=3, m1=3, r1=2, w1_1=0, w2_1=1)
    ins = dict(x=x, land=grow(land, (8, land_cols)), cot=cot)
    if fast:
        ins.update(half_hidden=mats["half_hidden"], deep_spread=mats["deep_spread"])
    else:
        ins.update(mine=mine, mine_bias=mine_bias)
        given = dict(w1_0=whole[0][0], w2_0=whole[0][1], r0=whole[0][2], r1=whole[1][3], w1_1=whole[1][0], w2_1=whole[1][1])
        given.update(m0=pack_in(halves[3][0], GROUPS, c, c), m1=pack_in(halves[3][1], GROUPS, c, c))
        ins.update({k + "_in": v.reshape((4, 4) + shapes[names[k]]) for k, v in given.items()})
    ins = {k: at_any(v) for k, v in ins.items()}
    ins.update({k: mats[k] for k in ("spread", "gather", "natural", "shifts", "patch", "unpatch", "edges", "back", "pick", "rows")})
    if fast:
        ins.update(w_in=w_in, w_out=w_out, resample=resample, merge=merge.reshape(1, -1), kernel=kernel, bn_gain=bn_gain, bn_bias=bn_bias, bias_in=bias_in, bias_out=bias_out)
    outs = dict(
        par=((2, 56, cw), F32), bias=((2, 8, hw), F32), ocean=((cells, 128), F32), coarse=((deep_cells, 128), F32),
        st0=((8, cw), F32), st1=((8, cw), F32), cot8=natural + (ANY,),
    )
    held = dict(
        a0=field(BF), a1=field(BF), skip=field(BF), up=field(BF), pieces=((4, deep_cells, cw), BF), deep=((deep_cells, nw), BF), nat0=natural, nat1=natural,
    )
    outs.update({k + "_out": v + (ANY,) for k, v in held.items()}, z0_out=((cols, 8, cw), F32, ANY), z1_out=((cols, 8, cw), F32, ANY))
    outs.update({k + "_out": ((4, 4) + shapes[v], BF, ANY) for k, v in names.items()})
    scratch = dict(
        x14=pltpu.VMEM((14, tiles, 16, c), BF), land2=pltpu.VMEM((2, 8, land_cols), jnp.int32),
        z=pltpu.VMEM((cols, 8, cw), F32),
        h=pltpu.VMEM((cells, cw), F32),
        halo=pltpu.VMEM(*edge_rows), packed=pltpu.VMEM(*edge_rows), y1=pltpu.VMEM(*field(BF)),
        stats=pltpu.VMEM((8, cw), F32), slots=pltpu.VMEM((count // 2 + 1, 8, cw), F32), slots1=pltpu.VMEM((count // 2 + 1, 8, cw), F32),
        send=DMA((count,)), recv=DMA((count,)), send1=DMA((count,)), recv1=DMA((count,)),
        xs=DMA((4,)), xr=DMA((2,)), ls=DMA((4,)), lr=DMA((2,)), hs=DMA((2,)), hr=DMA((2,)), ps=DMA((6,)), pr=DMA((6,)), cs=DMA((4,)), cr=DMA((2,)),
        es=DMA((2,)), er=DMA((2,)), gs=DMA((8, 12)), gr=DMA((8, 12)), save=DMA((8,)), keep=DMA((10,)),
    )
    scratch.update({k: pltpu.VMEM((4, 4) + shapes[v], BF) for k, v in names.items()}, **{k: pltpu.VMEM(*v) for k, v in held.items()})
    if fast:
        scratch.update({f"shard{k}": pltpu.VMEM((2,) + shapes[k], BF) for k in range(4)})
    fw = build("forward", lambda ns: forward_kernel(fast, count, cols, ns), ins, outs, scratch, {}, 1, 63)
    wide_w = dict(dw1=((cw, hw), BF), dw2=((hw, cw), BF))
    bounce = natural + (ANY,)
    names = ("par", "ocean", "coarse", "bias", "st0", "st1")
    ins = dict(top=fw.cot8, **{k: getattr(fw, k) for k in names})
    ins.update({k: mats[k] for k in ("shifts", "edges", "back", "gather", "spread", "turn", "patch", "unpatch")})
    ins.update({k: at_any(getattr(fw, k + "_out")) for k in ("nat0", "nat1", "a0", "a1", "up", "skip", "deep", "pieces")})
    ins.update({k: at_any(getattr(fw, k + "_out").reshape(cells, cw)) for k in ("z0", "z1")})
    views = dict(w1_0=(cw, hw), w2_0=(hw, cw), w1_1=(cw, hw), w2_1=(hw, cw), m0=(cw, cw), m1=(cw, cw), r0=(4 * cw, nw), r1=(GROUPS, 2, padded(n), 2 * cw))
    ins.update({k: at_any(getattr(fw, k + "_out").reshape(v)) for k, v in views.items()})
    outs = dict(
        act=((4, 4, tiles, 16, c), BF, ANY), gi=((4, 4, tiles, 16, c), BF, ANY), tiny0=((64, cw), F32), tiny1=((64, cw), F32),
        dm0=((cw, cw), BF), dm1=((cw, cw), BF), dr0=(views["r0"], BF, ANY), dr1=(views["r1"], BF, ANY), **{f"bounce{k}": bounce for k in range(4)},
    )
    space = {k: pltpu.VMEM(*v) for k, v in dict(dym=field(F32), dz=field(BF), packed=edge_rows, halo=edge_rows, halo1=edge_rows, nat=natural, **wide_w).items()}
    space.update(small=pltpu.VMEM((8, cw), F32), stats=pltpu.VMEM((8, cw), F32))
    for k in ("", "1"):
        space.update({"slots" + k: pltpu.VMEM((count // 2 + 1, 8, cw), F32), "send" + k: DMA((count,)), "recv" + k: DMA((count,)), "hsend" + k: DMA((2,)), "hrecv" + k: DMA((2,))})
    space.update(load_sem=DMA((8,)), ds=DMA((4, 2, 2)), dr=DMA((4, 4)), db=DMA((4, 2)), ps=DMA((2,)))
    if fast:
        for name, k in (("w0", 0), ("w1", 1), ("m0", 3), ("m1", 3), ("r0", 2), ("r1", 2)):
            space.update(reduce_bank(name, shapes[k]))
        for name, k in (("gw1", 0), ("gw2", 1), ("gr", 2), ("gm", 3)):
            space[name] = pltpu.VMEM((2,) + half_shape(shapes[k]), F32)
        space["total"] = pltpu.VMEM((64, cw), F32)
        outs.update(gwi=(w_in.shape, F32), gwo=(w_out.shape, F32), gres=(resample.shape, F32), gmm=((1, merge.shape[0]), F32))
        outs.update(gk=((1, 49, c), F32), gg=((1, c), F32), gs=((1, c), F32), gbo=((1, c), F32), gbi=((1, hid), F32))
        ins.update(half_hidden_back=at_any(mats["half_hidden_back"]), deep_back=at_any(mats["deep_back"]))
        space.update(sm=pltpu.VMEM((2, 64, cw), F32), tiny=pltpu.VMEM((9, 64, cw), F32), ts=DMA((9,)), tr=DMA((9,)))
    else:
        outs.update({f"{k}_{sec}": v + (ANY,) for k, v in wide_w.items() for sec in range(2)})
    bw = build("backward", lambda ns: back_kernel(fast, count, cols, ns), ins, outs, space, {}, 2, 63)
    activations = bw.act.reshape(1, batches, height, cols, c)
    grad_input = bw.gi.astype(F32).reshape(1, batches, height, cols, c)
    if fast:
        return activations, grad_input, bw.gk, bw.gg, bw.gs, bw.gbi, bw.gbo, bw.gwi, bw.gwo, bw.gres, bw.gmm.reshape(-1)
    scatter = lambda v: lax.psum_scatter(v.astype(F32).reshape(-1), both, scatter_dimension=0, tiled=True)
    gw1 = scatter(jnp.stack([unpack_in(v, c, hid) for v in (bw.dw1_0, bw.dw1_1)]))
    gw2 = scatter(jnp.stack([unpack_in(v, hid, c) for v in (bw.dw2_0, bw.dw2_1)]))
    gres = scatter(jnp.stack([unpack_down(bw.dr0, c, n), unpack_up(bw.dr1, c, n)]))
    gmm = scatter(jnp.stack([unpack_in(v, c, c) for v in (bw.dm0, bw.dm1)]))
    tiny = lax.psum(jnp.stack([bw.tiny0, bw.tiny1]), both)[s]
    narrow = lambda v: v.reshape(-1, GROUPS, padded(c))[:, :, : c // GROUPS].reshape(-1, c)
    fine = narrow(tiny[:59])
    grad_bias_in = tiny[59:63].reshape(-1)[:hw].reshape(GROUPS, -1)[:, : hid // GROUPS].reshape(1, hid)
    return (
        activations, grad_input, fine[None, :49], fine[57:58], fine[56:57], grad_bias_in, fine[58:59],
        gw1[None], gw2[None], gres[None], gmm,
    )


def solution(mesh):
    sections, dps = mesh.shape["section"], mesh.shape["dp"]
    flat, both = P("section", "dp"), P(("section", "dp"))
    per = P("section", None)
    rows = P(None, "dp", None, None)
    taps = P("section", None, None)
    fields = P("section", None, "dp", None, None)
    return jax.shard_map(
        functools.partial(on_device, sections, dps), mesh=mesh,
        in_specs=(rows, rows, P("dp", None), taps, per, per, per, per, flat, flat, flat, both),
        out_specs=(fields, fields, taps, per, per, per, per, flat, flat, flat, both), check_vma=False,
    )
```
